32 devices in a mesh: clip: 8 (over y, x, core), frame: 4 (over z).
Axes of the slice: x: 2, y: 2, z: 4, core: 2. Of those that a mesh axis runs over, the one named last changes fastest.
Arguments:
- tokens: bfloat16 [32, 4, 256, 768], P('clip', 'frame'), may hold values from -6 to 6
- target: bfloat16 [32, 4, 256, 768], P('clip', 'frame'), may hold values from -6 to 6
- loss_weight: float32 [32], P('clip'), may hold values from 0.5 to 2
- timesteps: int32 [32], replicated, may hold values from 0 to 999
- offsets: int32 [32], P('clip'), may hold values from 0 to 63
- cond_table: float32 [1000, 768], replicated, may hold values from -6 to 6
- modulate_w: bfloat16 [768, 6912], replicated, may hold values from -0.21875 to 0.21875
- spatial_qkv: bfloat16 [768, 2304], replicated, may hold values from -0.21875 to 0.21875
- spatial_out: bfloat16 [768, 768], replicated, may hold values from -0.875 to 0.875
- temporal_qkv: bfloat16 [768, 2304], replicated, may hold values from -0.21875 to 0.21875
- temporal_out: bfloat16 [768, 768], replicated, may hold values from -0.3125 to 0.3125
- mlp_in: bfloat16 [768, 3072], replicated, may hold values from -0.21875 to 0.21875
- mlp_out: bfloat16 [3072, 768], replicated, may hold values from -0.109375 to 0.109375
Outputs:
- output: bfloat16 [32, 4, 256, 768], P('clip', 'frame')
- grad_tokens: float32 [32, 4, 256, 768], P('clip', 'frame')
- grad_table: float32 [1000, 768], replicated
- grad_modulate: float32 [768, 6912], P('clip', 'frame')
- grad_spatial_qkv: float32 [768, 2304], P('clip', 'frame')
- grad_spatial_out: float32 [768, 768], P('clip', 'frame')
- grad_temporal_qkv: float32 [768, 2304], P('clip', 'frame')
- grad_temporal_out: float32 [768, 768], P('clip', 'frame')
- grad_mlp_in: float32 [768, 3072], P('clip', 'frame')
- grad_mlp_out: float32 [3072, 768], P('clip', 'frame')
The draws below stay inside these ranges and needn't reach their ends.
All inputs are finite; a program needn't handle non-finite values.
Results may differ from the reference program's by a relative error of at most 0.012.
The reference program's roundings to bfloat16 on the way count: a program that leaves them out, or rounds other values in their place, can miss the bound.
Values may be sent and summed in bfloat16 or wider, within the bound.
A program may use at most 256 MiB of HBM per device.

```python
import math
import jax
import jax.numpy as jnp
from jax import lax

D = 768
HEAD_DIM = 64
FF = 3072
PATCHES = 256
STEPS = 1000
CLIPS = 32
FRAMES = 4


def plant(entries, key, least, largest):
    longest = entries.shape.index(max(entries.shape))
    spots = []
    for shift in (0, 1):
        where = [jax.random.randint(jax.random.fold_in(key, axis), (), 0, length) for axis, length in enumerate(entries.shape)]
        where[longest] = (where[longest] + shift) % entries.shape[longest]
        spots.append(tuple(where))
    return entries.at[spots[0]].set(least).at[spots[1]].set(largest)


def steps_of(rng, dims, pieces, smallest, largest):
    level = 1.0
    for dim, parts in pieces:
        heights = jax.random.uniform(jax.random.fold_in(jax.random.fold_in(rng, 6), dim), (parts,), jnp.float32, smallest / len(pieces), largest / len(pieces))
        level = level * jnp.repeat(jnp.exp(heights), dims[dim] // parts).reshape((-1,) + (1,) * (len(dims) - 1 - dim))
    return level


def normal_values(stream_key, shape, scale, bound, pieces=(), kind=jnp.bfloat16):
    drawn = jax.random.normal(stream_key, shape, jnp.float32) * scale
    if len(pieces) > 0:
        drawn = steps_of(stream_key, shape, pieces, -0.22, 0.18) * drawn
    return jnp.clip(drawn, min=-bound, max=bound).astype(kind)


def setup_inputs(seed: int = 0) -> dict:
    key_of = jax.random.split(jax.random.key(seed), 14)
    return {
        "tokens": normal_values(key_of[0], (CLIPS, FRAMES, PATCHES, D), 1.0, 6.0, ((0, 8), (1, 4))),
        "target": normal_values(key_of[1], (CLIPS, FRAMES, PATCHES, D), 1.0, 6.0, ((0, 8), (1, 4))),
        "loss_weight": jnp.clip(jnp.exp(math.log(2.0) - 1.3862944 * jax.random.uniform(key_of[2], (CLIPS,), jnp.float32) ** steps_of(key_of[2], (CLIPS,), ((0, 8),), -0.2, 0.2)), 0.5, 2.0),
        "timesteps": plant(jax.random.randint(key_of[3], (CLIPS,), 0, STEPS), jax.random.fold_in(key_of[3], 1), 0, STEPS - 1).astype(jnp.int32),
        "offsets": plant(jax.random.randint(key_of[4], (CLIPS,), 0, 64), jax.random.fold_in(key_of[4], 1), 0, 63).astype(jnp.int32),
        "cond_table": normal_values(key_of[5], (STEPS, D), 1.0, 6.0, (), jnp.float32),
        "modulate_w": normal_values(key_of[6], (D, 9 * D), D ** -0.5, 0.21875),
        "spatial_qkv": normal_values(key_of[7], (D, 3 * D), D ** -0.5, 0.21875),
        "spatial_out": normal_values(key_of[8], (D, D), (D // 16) ** -0.5, 0.875),
        "temporal_qkv": normal_values(key_of[9], (D, 3 * D), D ** -0.5, 0.21875),
        "temporal_out": normal_values(key_of[10], (D, D), (D // 2) ** -0.5, 0.3125),
        "mlp_in": normal_values(key_of[11], (D, FF), D ** -0.5, 0.21875),
        "mlp_out": normal_values(key_of[12], (FF, D), FF ** -0.5, 0.109375),
    }


@jax.custom_vjp
def low(v):
    return lax.optimization_barrier(v.astype(jnp.bfloat16)).astype(jnp.float32)

@jax.custom_vjp
def low_back(v):
    return v

def low_keep(v):
    return (low(v), None)

def low_pass(kept, grad):
    return (grad,)

def back_keep(v):
    return (v, None)

def back_low(kept, grad):
    return (low(grad),)
low.defvjp(low_keep, low_pass)
low_back.defvjp(back_keep, back_low)
NORM_EPSILON = 1e-06
HIGHEST_PRECISION = lax.Precision.HIGHEST

def layer_norm(values):
    centred = values - lax.optimization_barrier(jnp.mean(values, axis=-1, keepdims=True))
    return centred * lax.rsqrt(lax.optimization_barrier(jnp.mean(centred * centred, axis=-1, keepdims=True)) + NORM_EPSILON)

def product(left, right):
    return jnp.dot(left, right, precision=HIGHEST_PRECISION)

def clip_forward(clip_tokens, step_index, first_frame, table, modulate_w, spatial_qkv, spatial_out, temporal_qkv, temporal_out, mlp_in, mlp_out):
    frames, patches, model_width = clip_tokens.shape
    head_count = model_width // HEAD_DIM
    scale_qk = HEAD_DIM ** (-0.5)
    condition = lax.dynamic_index_in_dim(table, step_index, 0, keepdims=False)
    modulation = product(low(jax.nn.silu(condition))[None, :], modulate_w).reshape(9, model_width)
    normed_a = layer_norm(clip_tokens)
    hidden_a = low(normed_a * (1.0 + modulation[1]) + modulation[0])
    proj_a = low_back(low(product(hidden_a.reshape(-1, model_width), spatial_qkv)))
    proj_a = proj_a.reshape(frames, patches, 3, head_count, HEAD_DIM)
    queries_a, keyset_a, valueset_a = (proj_a[:, :, 0], proj_a[:, :, 1], proj_a[:, :, 2])
    scores_a = low_back(jnp.einsum('fqhd,fkhd->fhqk', queries_a, keyset_a, precision=HIGHEST_PRECISION) * scale_qk)
    soft_a = jax.nn.softmax(scores_a, axis=-1)
    mixed_a = jnp.einsum('fhqk,fkhd->fqhd', low(soft_a), valueset_a, precision=HIGHEST_PRECISION)
    mixed_a = low_back(low(mixed_a.reshape(-1, model_width)))
    branch_a = low_back(product(mixed_a, spatial_out)).reshape(clip_tokens.shape)
    after_a = clip_tokens + modulation[2] * branch_a
    half_width = model_width // 2
    positions = (first_frame + jnp.arange(frames, dtype=jnp.int32)).astype(jnp.float32)
    freqs = jnp.exp(jnp.arange(half_width, dtype=jnp.float32) * (-math.log(10000.0) / half_width))
    angles = positions[:, None] * freqs[None, :]
    posenc = jnp.concatenate((jnp.sin(angles), jnp.cos(angles)), axis=-1)[:, None, :]
    hidden_b = low(layer_norm(after_a) * (1.0 + modulation[4]) + modulation[3] + posenc)
    proj_b = low_back(low(product(hidden_b.reshape(-1, model_width), temporal_qkv)))
    proj_b = proj_b.reshape(frames, patches, 3, model_width)
    queries_b = proj_b[:, :, 0].reshape(frames, patches, head_count, HEAD_DIM)
    keys_padded = jnp.pad(proj_b[:, :, 1], ((1, 1), (0, 0), (0, 0)))
    values_padded = jnp.pad(proj_b[:, :, 2], ((1, 1), (0, 0), (0, 0)))
    frame_ids = jnp.arange(frames, dtype=jnp.int32)
    raw_list = []
    valid_list = []
    value_list = []
    for offset_key in range(3):
        key_here = keys_padded[offset_key:offset_key + frames].reshape(frames, patches, head_count, HEAD_DIM)
        raw_list.append(jnp.einsum('fphd,fphd->fph', queries_b, key_here, precision=HIGHEST_PRECISION))
        value_list.append(values_padded[offset_key:offset_key + frames].reshape(frames, patches, head_count, HEAD_DIM))
        shifted = frame_ids + offset_key - 1
        valid_list.append((shifted >= 0) & (shifted < frames))
    scores_b = low_back(jnp.stack(raw_list) * scale_qk)
    valid_keys = jnp.stack(valid_list)
    masked_b = jnp.where(valid_keys[:, :, None, None], scores_b, -1e+30)
    soft_b = jax.nn.softmax(masked_b, axis=0)
    mixed_b = jnp.einsum('jfph,jfphd->fphd', low(soft_b), jnp.stack(value_list), precision=HIGHEST_PRECISION)
    mixed_b = low_back(low(mixed_b.reshape(-1, model_width)))
    branch_b = low_back(product(mixed_b, temporal_out)).reshape(clip_tokens.shape)
    after_b = after_a + modulation[5] * branch_b
    hidden_c = low(layer_norm(after_b) * (1.0 + modulation[7]) + modulation[6])
    upward = low_back(product(hidden_c.reshape(-1, model_width), mlp_in))
    act_low = low(jax.nn.gelu(upward, approximate=True))
    branch_c = low_back(product(act_low, mlp_out)).reshape(clip_tokens.shape)
    return after_b + modulation[8] * branch_c

def reference(tokens, target, loss_weight, timesteps, offsets, cond_table, modulate_w, spatial_qkv, spatial_out, temporal_qkv, temporal_out, mlp_in, mlp_out):
    matrices = tuple((matrix.astype(jnp.float32) for matrix in (modulate_w, spatial_qkv, spatial_out, temporal_qkv, temporal_out, mlp_in, mlp_out)))
    checkpointed = jax.checkpoint(clip_forward)

    def run(inputs, table, *weights):

        def advance(carry, item):
            clip_tokens, step_index, first_frame = item
            return (carry, checkpointed(clip_tokens, step_index, first_frame, table, *weights))
        _, outputs = lax.scan(advance, None, (inputs, timesteps, offsets))
        return outputs
    result, pullback = jax.vjp(run, tokens.astype(jnp.float32), cond_table, *matrices)
    cotangent = loss_weight[:, None, None, None] * (result - target.astype(jnp.float32))
    gradients = pullback(cotangent)
    return (result.astype(jnp.bfloat16), gradients[0], gradients[1], gradients[2], gradients[3], gradients[4], gradients[5], gradients[6], gradients[7], gradients[8])
```

```python
import functools
import math

import jax
import jax.numpy as jnp
from jax import lax
from jax.experimental import pallas as pl
from jax.experimental.pallas import tpu as pltpu
from jax.sharding import PartitionSpec as P

HEAD_DIM = 64
NORM_EPSILON = 1e-06
F32 = jnp.float32
BF16 = jnp.bfloat16
LANES = 128
SLOT = 16
NO_KEY = -1e30
VMEM_LIMIT = 60 * 2**20
GELU_A = math.sqrt(2.0 / math.pi)
GELU_B = 0.044715


def dot(left, right):
    return lax.dot_general(left, right, (((1,), (0,)), ((), ())), preferred_element_type=F32)


def dot_nt(left, right):
    return lax.dot_general(left, right, (((1,), (1,)), ((), ())), preferred_element_type=F32)


def dot_tn(left, right):
    return lax.dot_general(left, right, (((0,), (0,)), ((), ())), preferred_element_type=F32)


def norm(values):
    centred = values - jnp.mean(values, axis=-1, keepdims=True)
    inv_std = lax.rsqrt(jnp.mean(centred * centred, axis=-1, keepdims=True) + NORM_EPSILON)
    return centred * inv_std, inv_std


def norm_back(grad_hidden, normed, inv_std, scale_plus):
    grad_normed = grad_hidden * scale_plus
    mean_grad = jnp.mean(grad_normed, axis=-1, keepdims=True)
    mean_cross = jnp.mean(grad_normed * normed, axis=-1, keepdims=True)
    return inv_std * (grad_normed - mean_grad - normed * mean_cross)


def column_sum(values):
    return jnp.sum(values, axis=0, keepdims=True)


def side_masks(dtype, value):
    lane = lax.broadcasted_iota(jnp.int32, (1, LANES), 1)
    return [jnp.where((lane < HEAD_DIM) == (side == 0), value, 0.0).astype(dtype) for side in (0, 1)]


def spatial_forward(
    heads, tokens, mod, posenc, w_qkv, w_out, hidden_a, qkv, mixed, branch, after, hidden_b, lse
):
    width = tokens.shape[-1]
    rows = tokens.shape[1]
    inputs = tokens[0].astype(F32)
    normed, _ = norm(inputs)
    hidden = (normed * (1.0 + mod[0, 1:2]) + mod[0, 0:1]).astype(BF16)
    hidden_a[0] = hidden
    for part in range(3):
        cols = slice(part * width, (part + 1) * width)
        qkv[0, :, cols] = dot(hidden, w_qkv[:, cols]).astype(BF16)
    masks = side_masks(BF16, HEAD_DIM**-0.5)
    lane = lax.broadcasted_iota(jnp.int32, (1, LANES), 1)
    table = jnp.zeros((rows, LANES), F32)
    for pair in range(heads // 2):
        cols = pl.ds(pair * LANES, LANES)
        query = qkv[0, :, cols]
        key = qkv[0, :, pl.ds(width + pair * LANES, LANES)]
        value = qkv[0, :, pl.ds(2 * width + pair * LANES, LANES)]
        out = []
        for side in range(2):
            scores = dot_nt(query * masks[side], key)
            top = jnp.max(scores, axis=-1, keepdims=True)
            grown = jnp.exp(scores - top)
            total = jnp.sum(grown, axis=-1, keepdims=True)
            soft = (grown * (1.0 / total)).astype(BF16)
            out.append(dot(soft, value))
            table = jnp.where(lane == 2 * pair + side, top + jnp.log(total), table)
        mixed[0, :, cols] = jnp.where(lane < HEAD_DIM, out[0], out[1]).astype(BF16)
    lse[0] = table
    branch_a = dot(mixed[0], w_out[...])
    branch[0] = branch_a.astype(BF16)
    after_a = inputs + mod[0, 2:3] * branch_a
    after[0] = after_a
    normed_b, _ = norm(after_a)
    hidden_b[0] = (normed_b * (1.0 + mod[0, 4:5]) + (mod[0, 3:4] + posenc[0])).astype(BF16)


def by_head(left, right, to_heads):
    full = left.astype(F32) * right.astype(F32)
    high = full.astype(BF16)
    rest = (full - high.astype(F32)).astype(BF16)
    return dot(high, to_heads) + dot(rest, to_heads)


def middle(
    hb_own, hb_prev, hb_next, after_a, target, mod, weight, masks, to_heads, spread, pack,
    w_qkv, w_out, w_in, w_mlp,
    output, grad_b, hidden_c, act, grad_branch_c, grad_up, mixed_b, grad_branch_b, sent, q_own,
    grad_q, sums, slope,
):
    width = after_a.shape[-1]
    ff = act.shape[-1]
    scale_qk = HEAD_DIM**-0.5
    own = hb_own[0]
    query = dot(own, w_qkv[:, :width]).astype(BF16)
    q_own[0] = query
    keys, values, scores = [], [], []
    for number, hidden in enumerate((hb_prev, hb_own, hb_next)):
        keys.append(dot(hidden[0], w_qkv[:, width : 2 * width]).astype(BF16))
        values.append(dot(hidden[0], w_qkv[:, 2 * width :]).astype(BF16))
        raw = by_head(query, keys[number], to_heads[...]) * scale_qk
        scores.append(raw + masks[number : number + 1])
    top = jnp.maximum(jnp.maximum(scores[0], scores[1]), scores[2])
    grown = [jnp.exp(entry - top) for entry in scores]
    inverse = 1.0 / (grown[0] + grown[1] + grown[2])
    soft = [entry * inverse for entry in grown]
    soft_low = [entry.astype(BF16) for entry in soft]
    to_width = spread[LANES : 2 * LANES]
    total = None
    for number in range(3):
        term = dot(soft_low[number], to_width) * values[number].astype(F32)
        total = term if total is None else total + term
    mixed = total.astype(BF16)
    mixed_b[0] = mixed
    branch_b = dot(mixed, w_out[...])
    after_b = after_a[0] + mod[0, 5:6] * branch_b
    normed_c, inv_c = norm(after_b)
    hidden = (normed_c * (1.0 + mod[0, 7:8]) + mod[0, 6:7]).astype(BF16)
    hidden_c[0] = hidden
    for part in range(ff // width):
        cols = slice(part * width, (part + 1) * width)
        upward = dot(hidden, w_in[:, cols])
        squared = upward * upward
        bent = jnp.tanh(GELU_A * upward * (1.0 + GELU_B * squared))
        act[0, :, cols] = (0.5 * upward * (1.0 + bent)).astype(BF16)
        slope[:, cols] = 0.5 * (1.0 + bent) + (0.5 * GELU_A) * upward * (1.0 - bent * bent) * (
            1.0 + 3.0 * GELU_B * squared
        )
    branch_c = dot(act[0], w_mlp[...])
    result = after_b + mod[0, 8:9] * branch_c
    output[0] = result.astype(BF16)
    grad_result = weight[0, :, :1] * (result - target[0].astype(F32))
    sums[0, 2:3] = column_sum(grad_result * branch_c)
    low_c = (mod[0, 8:9] * grad_result).astype(BF16)
    grad_branch_c[0] = low_c
    for part in range(ff // width):
        cols = slice(part * width, (part + 1) * width)
        grad_act = dot_nt(low_c, w_mlp[cols, :])
        grad_up[0, :, cols] = (grad_act * slope[:, cols]).astype(BF16)
    grad_hidden = dot_nt(grad_up[0], w_in[...])
    sums[0, 0:1] = column_sum(grad_hidden)
    sums[0, 1:2] = column_sum(grad_hidden * normed_c)
    grad_after = grad_result + norm_back(grad_hidden, normed_c, inv_c, 1.0 + mod[0, 7:8])
    grad_b[0] = grad_after
    sums[0, 3:4] = column_sum(grad_after * branch_b)
    low_b = (mod[0, 5:6] * grad_after).astype(BF16)
    grad_branch_b[0] = low_b
    grad_mixed = dot_nt(low_b, w_out[...]).astype(BF16)
    grad_soft = [by_head(grad_mixed, values[number], to_heads[...]) for number in range(3)]
    inner = soft[0] * grad_soft[0] + soft[1] * grad_soft[1] + soft[2] * grad_soft[2]
    grad_scores = [(soft[number] * (grad_soft[number] - inner)).astype(BF16) for number in range(3)]
    total = None
    for number in range(3):
        term = dot(grad_scores[number], to_width) * keys[number].astype(F32)
        total = term if total is None else total + term
    grad_q[0] = (total * scale_qk).astype(BF16)
    sent[0, :, :width] = grad_mixed
    sent[0, :, width:] = dot(
        jnp.concatenate(soft_low + grad_scores, axis=1), pack[...]
    ).astype(BF16)


def spatial_backward(
    heads, hb_prev, hb_next, sent_own, sent_prev, sent_next, q_own, grad_q, grad_b, after_a,
    tokens, branch, qkv, lse, mod, spread, w_qkv_b, w_out, w_qkv_a,
    grad_tokens, grad_qkv_b, grad_qkv_a, grad_branch_a, sums,
):
    width = after_a.shape[-1]
    scale_qk = HEAD_DIM**-0.5
    w_query = w_qkv_b[:, :width]
    queries = (
        dot(hb_prev[0], w_query).astype(BF16).astype(F32),
        q_own[0].astype(F32),
        dot(hb_next[0], w_query).astype(BF16).astype(F32),
    )
    grad_key = None
    grad_value = None
    for number, source in enumerate((sent_prev, sent_own, sent_next)):
        other = 2 - number
        table = source[0, :, width:]
        low = LANES - SLOT * other
        soft = dot(table, spread[low : low + LANES])
        low = LANES - SLOT * (3 + other)
        score = dot(table, spread[low : low + LANES])
        key_term = score * queries[number]
        value_term = soft * source[0, :, :width].astype(F32)
        grad_key = key_term if grad_key is None else grad_key + key_term
        grad_value = value_term if grad_value is None else grad_value + value_term
    grad_qkv_b[0, :, :width] = grad_q[0]
    grad_qkv_b[0, :, width : 2 * width] = (grad_key * scale_qk).astype(BF16)
    grad_qkv_b[0, :, 2 * width :] = grad_value.astype(BF16)
    grad_hidden = dot_nt(grad_qkv_b[0], w_qkv_b[...])
    normed_b, inv_b = norm(after_a[0])
    sums[0, 3:4] = column_sum(grad_hidden)
    sums[0, 4:5] = column_sum(grad_hidden * normed_b)
    grad_after = grad_b[0] + norm_back(grad_hidden, normed_b, inv_b, 1.0 + mod[0, 4:5])
    sums[0, 2:3] = column_sum(grad_after * branch[0].astype(F32))
    low_a = (mod[0, 2:3] * grad_after).astype(BF16)
    grad_branch_a[0] = low_a
    grad_mixed = dot_nt(low_a, w_out[...]).astype(BF16)
    masks = side_masks(BF16, 1.0)
    lane = lax.broadcasted_iota(jnp.int32, (1, LANES), 1)
    scale_low = jnp.asarray(scale_qk, BF16)
    for pair in range(heads // 2):
        cols = slice(pair * LANES, (pair + 1) * LANES)
        query = qkv[0, :, cols]
        key = qkv[0, :, pl.ds(width + pair * LANES, LANES)]
        value = qkv[0, :, pl.ds(2 * width + pair * LANES, LANES)]
        gm = grad_mixed[:, cols]
        parts = []
        for side in range(2):
            head = 2 * pair + side
            scores = dot_nt(query * (masks[side] * scale_low), key)
            soft = jnp.exp(scores - lse[0, :, head : head + 1])
            grad_soft = dot_nt(gm * masks[side], value)
            inner = jnp.sum(soft * grad_soft, axis=-1, keepdims=True)
            grad_scores = (soft * (grad_soft - inner)).astype(BF16)
            parts.append(
                (dot(grad_scores, key), dot_tn(grad_scores, query), dot_tn(soft.astype(BF16), gm))
            )
        for number, factor in ((0, scale_qk), (1, scale_qk), (2, 1.0)):
            both = jnp.where(lane < HEAD_DIM, parts[0][number], parts[1][number])
            start = number * width + pair * LANES
            grad_qkv_a[0, :, start : start + LANES] = (both * factor).astype(BF16)
    grad_hidden = dot_nt(grad_qkv_a[0], w_qkv_a[...])
    normed_a, inv_a = norm(tokens[0].astype(F32))
    sums[0, 0:1] = column_sum(grad_hidden)
    sums[0, 1:2] = column_sum(grad_hidden * normed_a)
    grad_tokens[0] = grad_after + norm_back(grad_hidden, normed_a, inv_a, 1.0 + mod[0, 1:2])


def weight_term(left, right, out):
    out[...] = dot_tn(left[...], right[...]).astype(BF16)


def weight_grad(left, right, tile_m, tile_n):
    rows, height = left.shape
    width = right.shape[1]
    return pl.pallas_call(
        weight_term,
        grid=(height // tile_m, width // tile_n),
        in_specs=[
            pl.BlockSpec((rows, tile_m), lambda i, j: (0, i)),
            pl.BlockSpec((rows, tile_n), lambda i, j: (0, j)),
        ],
        out_specs=pl.BlockSpec((tile_m, tile_n), lambda i, j: (i, j)),
        out_shape=jax.ShapeDtypeStruct((height, width), BF16),
        compiler_params=pltpu.CompilerParams(vmem_limit_bytes=VMEM_LIMIT),
        cost_estimate=pl.CostEstimate(
            flops=2 * rows * height * width,
            bytes_accessed=2 * (rows * height + rows * width + height * width),
            transcendentals=0,
        ),
    )(left, right)


def clip_block(array):
    rest = array.shape[1:]
    return pl.BlockSpec((1,) + rest, lambda c: (c,) + (0,) * len(rest))


def whole(array):
    return pl.BlockSpec(
        array.shape, lambda c: (0,) * array.ndim, pipeline_mode=pl.Buffered(1)
    )


def per_clip(body, blocks, wholes, outs, flops, scratch=()):
    clips = blocks[0].shape[0]
    operands = [(a, clip_block(a)) for a in blocks] + [(a, whole(a)) for a in wholes]
    touched = sum(math.prod(a.shape) * a.dtype.itemsize for a in [*blocks, *wholes, *outs])
    return pl.pallas_call(
        body,
        grid=(clips,),
        in_specs=[spec for _, spec in operands],
        out_specs=[clip_block(a) for a in outs],
        out_shape=list(outs),
        scratch_shapes=list(scratch),
        compiler_params=pltpu.CompilerParams(vmem_limit_bytes=VMEM_LIMIT),
        cost_estimate=pl.CostEstimate(flops=flops, bytes_accessed=touched, transcendentals=0),
    )(*[a for a, _ in operands])


def scatter_sum(parts, axis, bits):
    count = lax.axis_size(axis)
    me = lax.axis_index(axis)
    shape = parts.shape[1:]
    left = list(range(count.bit_length() - 1))[::-1]
    held = parts.reshape((2,) * len(left) + shape)
    for bit in bits:
        dim = left.index(bit)
        left.remove(bit)
        mine = (me >> bit) & 1
        away = lax.dynamic_index_in_dim(held, 1 - mine, dim, keepdims=False)
        keep = lax.dynamic_index_in_dim(held, mine, dim, keepdims=False)
        came = lax.ppermute(away, axis, [(i, i ^ (1 << bit)) for i in range(count)])
        total = keep.astype(F32) + came.astype(F32)
        held = total.astype(parts.dtype)
    return total.reshape(shape)


def clip_bits(first):
    bits = list(range(1, lax.axis_size("clip").bit_length() - 1))
    return [0] + (bits if first == 0 else bits[::-1])


def frame_bits():
    return list(range(lax.axis_size("frame").bit_length() - 1))


def thirds(values):
    high = values.astype(BF16)
    rest = values - high.astype(F32)
    mid = rest.astype(BF16)
    low = (rest - mid.astype(F32)).astype(BF16)
    return jnp.concatenate((high, mid, low), axis=0)


def local(
    tokens, target, loss_weight, timesteps, offsets, cond_table, modulate_w,
    spatial_qkv, spatial_out, temporal_qkv, temporal_out, mlp_in, mlp_out,
):
    clips, frames, patches, width = tokens.shape
    steps = cond_table.shape[0]
    ff = mlp_in.shape[1]
    heads = width // HEAD_DIM
    rows = clips * frames * patches
    n_clip = lax.axis_size("clip")
    n_frame = lax.axis_size("frame")
    clip_at = lax.axis_index("clip")
    frame_at = lax.axis_index("frame")
    flat = (clips, patches, width)
    tok = tokens.reshape(flat)
    tgt = target.reshape(flat)

    condition = jnp.take(cond_table, timesteps, axis=0, mode="clip")
    cond_low = jax.nn.silu(condition).astype(BF16)
    cond_here = lax.dynamic_slice_in_dim(condition, clip_at * clips, clips)
    _, silu_pull = jax.vjp(jax.nn.silu, cond_here)
    low_here = lax.dynamic_slice_in_dim(cond_low, clip_at * clips, clips)
    mod = jnp.dot(low_here, modulate_w, preferred_element_type=F32).reshape(clips, 9, width)

    half = width // 2
    positions = (offsets + frame_at).astype(F32)
    freqs = jnp.exp(jnp.arange(half, dtype=F32) * (-math.log(10000.0) / half))
    angles = positions[:, None] * freqs
    posenc = jnp.concatenate((jnp.sin(angles), jnp.cos(angles)), axis=-1)[:, None, :]

    head_of = jnp.arange(width, dtype=jnp.int32) // HEAD_DIM
    lane_ids = jnp.arange(LANES, dtype=jnp.int32)
    to_heads = (head_of[:, None] == lane_ids[None, :]).astype(BF16)
    tall = jnp.arange(2 * LANES, dtype=jnp.int32) - LANES
    spread = (tall[:, None] == head_of[None, :]).astype(BF16)
    group, inside = jnp.divmod(jnp.arange(6 * LANES, dtype=jnp.int32), LANES)
    slot_at = jnp.where(inside < heads, group * SLOT + inside, -1)
    pack = (slot_at[:, None] == lane_ids[None, :]).astype(BF16)
    side_ok = jnp.stack((frame_at > 0, frame_at >= 0, frame_at < n_frame - 1))
    masks = jnp.where(side_ok[:, None], 0.0, NO_KEY) * jnp.ones((1, LANES), F32)
    masks = jnp.pad(masks, ((0, 5), (0, 0)))
    weight = jnp.broadcast_to(loss_weight[:, None, None], (clips, 1, LANES))

    def struct(last, dtype):
        return jax.ShapeDtypeStruct((clips, patches, last), dtype)

    macs = rows * width * width
    hidden_a, qkv_a, mixed_a, branch_a, after_a, hidden_b, lse = per_clip(
        functools.partial(spatial_forward, heads),
        [tok, mod, posenc],
        [spatial_qkv, spatial_out],
        [
            struct(width, BF16), struct(3 * width, BF16), struct(width, BF16),
            struct(width, BF16), struct(width, F32), struct(width, BF16), struct(LANES, F32),
        ],
        flops=2 * macs * 7,
    )
    up = [(i, i + 1) for i in range(n_frame - 1)]
    down = [(i + 1, i) for i in range(n_frame - 1)]
    hb_prev = lax.ppermute(hidden_b, "frame", up)
    hb_next = lax.ppermute(hidden_b, "frame", down)
    (
        output, grad_b, hidden_c, act, grad_branch_c, grad_up, mixed_b, grad_branch_b, sent,
        q_own, grad_q, sums_mid,
    ) = per_clip(
        middle,
        [hidden_b, hb_prev, hb_next, after_a, tgt, mod, weight],
        [masks, to_heads, spread, pack, temporal_qkv, temporal_out, mlp_in, mlp_out],
        [
            struct(width, BF16), struct(width, F32), struct(width, BF16), struct(ff, BF16),
            struct(width, BF16), struct(ff, BF16), struct(width, BF16), struct(width, BF16),
            struct(width + LANES, BF16), struct(width, BF16), struct(width, BF16),
            jax.ShapeDtypeStruct((clips, 8, width), F32),
        ],
        flops=2 * macs * 31,
        scratch=[pltpu.VMEM((patches, ff), F32)],
    )
    sent_prev = lax.ppermute(sent, "frame", up)
    sent_next = lax.ppermute(sent, "frame", down)

    def flat_rows(array):
        return array.reshape(rows, array.shape[-1])

    weight_in = weight_grad(flat_rows(hidden_c), flat_rows(grad_up), width, width)
    weight_mlp = weight_grad(flat_rows(act), flat_rows(grad_branch_c), width, width)
    grad_tok, grad_qkv_b, grad_qkv_a, grad_branch_a, sums_back = per_clip(
        functools.partial(spatial_backward, heads),
        [
            hb_prev, hb_next, sent, sent_prev, sent_next, q_own, grad_q, grad_b, after_a,
            tok, branch_a, qkv_a, lse, mod,
        ],
        [spread, temporal_qkv, spatial_out, spatial_qkv],
        [
            struct(width, F32), struct(3 * width, BF16), struct(3 * width, BF16),
            struct(width, BF16), jax.ShapeDtypeStruct((clips, 8, width), F32),
        ],
        flops=2 * macs * 16,
    )
    weight_qkv_b = weight_grad(flat_rows(hidden_b), flat_rows(grad_qkv_b), width, width)
    weight_out_b = weight_grad(flat_rows(mixed_b), flat_rows(grad_branch_b), width, width)
    weight_qkv_a = weight_grad(flat_rows(hidden_a), flat_rows(grad_qkv_a), width, width)
    weight_out_a = weight_grad(flat_rows(mixed_a), flat_rows(grad_branch_a), width, width)

    def over_frames(by_clip):
        tall_rows, cols = by_clip.shape
        shares = by_clip.reshape(tall_rows, n_frame, cols // n_frame).transpose(1, 0, 2)
        return scatter_sum(shares.astype(BF16), "frame", frame_bits())

    def reduce_weight(term, first):
        shares = term.reshape(n_clip, term.shape[0] // n_clip, term.shape[1])
        return over_frames(scatter_sum(shares, "clip", clip_bits(first)))

    grad_mlp_in = reduce_weight(weight_in, 0)
    grad_mlp_out = reduce_weight(weight_mlp, 1)

    def reduce_pair(qkv_term, out_term):
        both = jnp.concatenate((qkv_term, out_term), axis=1)
        shares = both.reshape(n_clip, both.shape[0] // n_clip, both.shape[1])
        cut = both.shape[1] // 2
        first = scatter_sum(shares[:, :, :cut], "clip", clip_bits(0))
        second = scatter_sum(shares[:, :, cut:], "clip", clip_bits(1))
        joined = jnp.concatenate((first, second), axis=1)
        qkv_cols = qkv_term.shape[1]
        tall_rows = joined.shape[0]
        frame_shares = jnp.concatenate(
            (
                joined[:, :qkv_cols].reshape(tall_rows, n_frame, -1),
                joined[:, qkv_cols:].reshape(tall_rows, n_frame, -1),
            ),
            axis=2,
        ).transpose(1, 0, 2)
        done = scatter_sum(frame_shares.astype(BF16), "frame", frame_bits())
        return done[:, : qkv_cols // n_frame], done[:, qkv_cols // n_frame :]

    grad_temporal_qkv, grad_temporal_out = reduce_pair(weight_qkv_b, weight_out_b)
    grad_spatial_qkv, grad_spatial_out = reduce_pair(weight_qkv_a, weight_out_a)

    grad_mod = jnp.concatenate(
        (sums_back[:, :5], sums_mid[:, 3:4], sums_mid[:, :3]), axis=1
    ).reshape(clips, 9 * width)
    by_term = dot_nt(thirds(grad_mod), modulate_w).reshape(3, clips, width)
    grad_cond = silu_pull(by_term[0] + by_term[1] + by_term[2])[0]
    grad_cond = lax.psum(grad_cond, "frame")
    grad_cond = lax.all_gather(grad_cond, "clip", axis=0, tiled=True)
    onehot = (timesteps[:, None] == jnp.arange(steps, dtype=jnp.int32)[None, :]).astype(BF16)
    grad_table = dot_tn(jnp.concatenate((onehot,) * 3, axis=0), thirds(grad_cond))
    mod_cols = 9 * width // n_frame
    mod_share = scatter_sum(
        grad_mod.reshape(clips, n_frame, mod_cols).transpose(1, 0, 2), "frame", frame_bits()
    )
    mod_all = lax.all_gather(mod_share, "clip", axis=0, tiled=True)
    mod_rows = width // n_clip
    low_rows = lax.dynamic_slice_in_dim(cond_low, clip_at * mod_rows, mod_rows, axis=1)
    grad_modulate = dot_tn(jnp.concatenate((low_rows,) * 3, axis=0), thirds(mod_all))
    return (
        output.reshape(tokens.shape),
        grad_tok.reshape(tokens.shape),
        grad_table,
        grad_modulate,
        grad_spatial_qkv,
        grad_spatial_out,
        grad_temporal_qkv,
        grad_temporal_out,
        grad_mlp_in,
        grad_mlp_out,
    )


def solution(mesh):
    placed = (
        P("clip", "frame", None, None), P("clip", "frame", None, None), P("clip"), P(), P("clip"),
    ) + (P(),) * 8
    return jax.shard_map(
        local,
        mesh=mesh,
        in_specs=placed,
        out_specs=(
            P("clip", "frame", None, None), P("clip", "frame", None, None), P(),
        ) + (P("clip", "frame"),) * 7,
        check_vma=False,
    )
```

```python
import functools
import math

import jax
import jax.numpy as jnp
from jax import lax
from jax.experimental import pallas as pl
from jax.experimental.pallas import tpu as pltpu
from jax.sharding import PartitionSpec as P

HEAD_DIM = 64
NORM_EPSILON = 1e-06
F32 = jnp.float32
BF16 = jnp.bfloat16
LANES = 128
SLOT = 16
NO_KEY = -1e30
VMEM_LIMIT = 60 * 2**20
GELU_A = math.sqrt(2.0 / math.pi)
GELU_B = 0.044715


def dot(left, right):
    return lax.dot_general(left, right, (((1,), (0,)), ((), ())), preferred_element_type=F32)


def dot_nt(left, right):
    return lax.dot_general(left, right, (((1,), (1,)), ((), ())), preferred_element_type=F32)


def dot_tn(left, right):
    return lax.dot_general(left, right, (((0,), (0,)), ((), ())), preferred_element_type=F32)


def norm(values):
    centred = values - jnp.mean(values, axis=-1, keepdims=True)
    inv_std = lax.rsqrt(jnp.mean(centred * centred, axis=-1, keepdims=True) + NORM_EPSILON)
    return centred * inv_std, inv_std


def norm_back(grad_hidden, normed, inv_std, scale_plus):
    grad_normed = grad_hidden * scale_plus
    mean_grad = jnp.mean(grad_normed, axis=-1, keepdims=True)
    mean_cross = jnp.mean(grad_normed * normed, axis=-1, keepdims=True)
    return inv_std * (grad_normed - mean_grad - normed * mean_cross)


def column_sum(values):
    return jnp.sum(values, axis=0, keepdims=True)


def side_masks(dtype, value):
    lane = lax.broadcasted_iota(jnp.int32, (1, LANES), 1)
    return [jnp.where((lane < HEAD_DIM) == (side == 0), value, 0.0).astype(dtype) for side in (0, 1)]


def spatial_forward(
    heads, tokens, mod, posenc, w_qkv, w_out, hidden_a, qkv, mixed, branch, after, hidden_b, lse,
    from_prev, from_next, held, blank, send_sems, recv_sems, blank_sems,
):
    clip = pl.program_id(0)
    clips = pl.num_programs(0)
    me = lax.axis_index("frame")
    count = lax.axis_size("frame")
    has_prev = me > 0
    has_next = me < count - 1
    barrier = pltpu.get_barrier_semaphore()

    def move(way, number):
        return pltpu.make_async_remote_copy(
            src_ref=held.at[number],
            dst_ref=(from_prev, from_next)[way].at[number],
            send_sem=send_sems.at[way, number],
            recv_sem=recv_sems.at[way, number],
            device_id={"frame": me + 1 if way == 0 else me - 1},
            device_id_type=pl.DeviceIdType.MESH,
        )

    def fill(way, number):
        return pltpu.make_async_copy(
            blank, (from_prev, from_next)[way].at[number], blank_sems.at[number]
        )

    @pl.when(clip == 0)
    def _():
        blank[...] = jnp.zeros_like(blank)

        @pl.when(has_prev)
        def _():
            pl.semaphore_signal(
                barrier, inc=1, device_id={"frame": me - 1}, device_id_type=pl.DeviceIdType.MESH
            )

        @pl.when(has_next)
        def _():
            pl.semaphore_signal(
                barrier, inc=1, device_id={"frame": me + 1}, device_id_type=pl.DeviceIdType.MESH
            )
    width = tokens.shape[-1]
    rows = tokens.shape[1]
    inputs = tokens[0].astype(F32)
    normed, _ = norm(inputs)
    hidden = (normed * (1.0 + mod[0, 1:2]) + mod[0, 0:1]).astype(BF16)
    hidden_a[0] = hidden
    for part in range(3):
        cols = slice(part * width, (part + 1) * width)
        qkv[0, :, cols] = dot(hidden, w_qkv[:, cols]).astype(BF16)
    masks = side_masks(BF16, HEAD_DIM**-0.5)
    lane = lax.broadcasted_iota(jnp.int32, (1, LANES), 1)
    table = jnp.zeros((rows, LANES), F32)
    for pair in range(heads // 2):
        cols = pl.ds(pair * LANES, LANES)
        query = qkv[0, :, cols]
        key = qkv[0, :, pl.ds(width + pair * LANES, LANES)]
        value = qkv[0, :, pl.ds(2 * width + pair * LANES, LANES)]
        out = []
        for side in range(2):
            scores = dot_nt(query * masks[side], key)
            top = jnp.max(scores, axis=-1, keepdims=True)
            grown = jnp.exp(scores - top)
            total = jnp.sum(grown, axis=-1, keepdims=True)
            soft = (grown * (1.0 / total)).astype(BF16)
            out.append(dot(soft, value))
            table = jnp.where(lane == 2 * pair + side, top + jnp.log(total), table)
        mixed[0, :, cols] = jnp.where(lane < HEAD_DIM, out[0], out[1]).astype(BF16)
    lse[0] = table
    branch_a = dot(mixed[0], w_out[...])
    branch[0] = branch_a.astype(BF16)
    after_a = inputs + mod[0, 2:3] * branch_a
    after[0] = after_a
    normed_b, _ = norm(after_a)
    hidden = (normed_b * (1.0 + mod[0, 4:5]) + (mod[0, 3:4] + posenc[0])).astype(BF16)
    hidden_b[0] = hidden
    held[clip] = hidden

    @pl.when(clip == 0)
    def _():
        pl.semaphore_wait(barrier, jnp.where(has_prev, 1, 0) + jnp.where(has_next, 1, 0))

    @pl.when(has_next)
    def _():
        move(0, clip).start()

    @pl.when(has_prev)
    def _():
        move(1, clip).start()

    @pl.when(jnp.logical_not(has_prev))
    def _():
        fill(0, clip).start()

    @pl.when(jnp.logical_not(has_next))
    def _():
        fill(1, clip).start()

    @pl.when(clip == clips - 1)
    def _():
        for number in range(held.shape[0]):

            @pl.when(has_next)
            def _():
                move(0, number).wait_send()
                move(1, number).wait_recv()

            @pl.when(has_prev)
            def _():
                move(1, number).wait_send()
                move(0, number).wait_recv()

            @pl.when(jnp.logical_not(has_prev))
            def _():
                fill(0, number).wait()

            @pl.when(jnp.logical_not(has_next))
            def _():
                fill(1, number).wait()


def by_head(left, right, to_heads):
    full = left.astype(F32) * right.astype(F32)
    high = full.astype(BF16)
    rest = (full - high.astype(F32)).astype(BF16)
    return dot(high, to_heads) + dot(rest, to_heads)


def middle(
    hb_own, hb_prev, hb_next, after_a, target, mod, weight, masks, to_heads, spread, pack,
    w_qkv, w_out, w_in, w_mlp,
    output, grad_b, hidden_c, act, grad_branch_c, grad_up, mixed_b, grad_branch_b, sent, q_own,
    grad_q, sums, slope,
):
    width = after_a.shape[-1]
    ff = act.shape[-1]
    scale_qk = HEAD_DIM**-0.5
    own = hb_own[0]
    query = dot(own, w_qkv[:, :width]).astype(BF16)
    q_own[0] = query
    keys, values, scores = [], [], []
    for number, hidden in enumerate((hb_prev, hb_own, hb_next)):
        keys.append(dot(hidden[0], w_qkv[:, width : 2 * width]).astype(BF16))
        values.append(dot(hidden[0], w_qkv[:, 2 * width :]).astype(BF16))
        raw = by_head(query, keys[number], to_heads[...]) * scale_qk
        scores.append(raw + masks[number : number + 1])
    top = jnp.maximum(jnp.maximum(scores[0], scores[1]), scores[2])
    grown = [jnp.exp(entry - top) for entry in scores]
    inverse = 1.0 / (grown[0] + grown[1] + grown[2])
    soft = [entry * inverse for entry in grown]
    soft_low = [entry.astype(BF16) for entry in soft]
    to_width = spread[LANES : 2 * LANES]
    total = None
    for number in range(3):
        term = dot(soft_low[number], to_width) * values[number].astype(F32)
        total = term if total is None else total + term
    mixed = total.astype(BF16)
    mixed_b[0] = mixed
    branch_b = dot(mixed, w_out[...])
    after_b = after_a[0] + mod[0, 5:6] * branch_b
    normed_c, inv_c = norm(after_b)
    hidden = (normed_c * (1.0 + mod[0, 7:8]) + mod[0, 6:7]).astype(BF16)
    hidden_c[0] = hidden
    for part in range(ff // width):
        cols = slice(part * width, (part + 1) * width)
        upward = dot(hidden, w_in[:, cols])
        squared = upward * upward
        bent = jnp.tanh(GELU_A * upward * (1.0 + GELU_B * squared))
        act[0, :, cols] = (0.5 * upward * (1.0 + bent)).astype(BF16)
        slope[:, cols] = 0.5 * (1.0 + bent) + (0.5 * GELU_A) * upward * (1.0 - bent * bent) * (
            1.0 + 3.0 * GELU_B * squared
        )
    branch_c = dot(act[0], w_mlp[...])
    result = after_b + mod[0, 8:9] * branch_c
    output[0] = result.astype(BF16)
    grad_result = weight[0, :, :1] * (result - target[0].astype(F32))
    sums[0, 2:3] = column_sum(grad_result * branch_c)
    low_c = (mod[0, 8:9] * grad_result).astype(BF16)
    grad_branch_c[0] = low_c
    for part in range(ff // width):
        cols = slice(part * width, (part + 1) * width)
        grad_act = dot_nt(low_c, w_mlp[cols, :])
        grad_up[0, :, cols] = (grad_act * slope[:, cols]).astype(BF16)
    grad_hidden = dot_nt(grad_up[0], w_in[...])
    sums[0, 0:1] = column_sum(grad_hidden)
    sums[0, 1:2] = column_sum(grad_hidden * normed_c)
    grad_after = grad_result + norm_back(grad_hidden, normed_c, inv_c, 1.0 + mod[0, 7:8])
    grad_b[0] = grad_after
    sums[0, 3:4] = column_sum(grad_after * branch_b)
    low_b = (mod[0, 5:6] * grad_after).astype(BF16)
    grad_branch_b[0] = low_b
    grad_mixed = dot_nt(low_b, w_out[...]).astype(BF16)
    grad_soft = [by_head(grad_mixed, values[number], to_heads[...]) for number in range(3)]
    inner = soft[0] * grad_soft[0] + soft[1] * grad_soft[1] + soft[2] * grad_soft[2]
    grad_scores = [(soft[number] * (grad_soft[number] - inner)).astype(BF16) for number in range(3)]
    total = None
    for number in range(3):
        term = dot(grad_scores[number], to_width) * keys[number].astype(F32)
        total = term if total is None else total + term
    grad_q[0] = (total * scale_qk).astype(BF16)
    sent[0, :, :width] = grad_mixed
    sent[0, :, width:] = dot(
        jnp.concatenate(soft_low + grad_scores, axis=1), pack[...]
    ).astype(BF16)


def spatial_backward(
    heads, hb_prev, hb_next, sent_own, sent_prev, sent_next, q_own, grad_q, grad_b, after_a,
    tokens, branch, qkv, lse, mod, spread, w_qkv_b, w_out, w_qkv_a,
    grad_tokens, grad_qkv_b, grad_qkv_a, grad_branch_a, sums,
):
    width = after_a.shape[-1]
    scale_qk = HEAD_DIM**-0.5
    w_query = w_qkv_b[:, :width]
    queries = (
        dot(hb_prev[0], w_query).astype(BF16).astype(F32),
        q_own[0].astype(F32),
        dot(hb_next[0], w_query).astype(BF16).astype(F32),
    )
    grad_key = None
    grad_value = None
    for number, source in enumerate((sent_prev, sent_own, sent_next)):
        other = 2 - number
        table = source[0, :, width:]
        low = LANES - SLOT * other
        soft = dot(table, spread[low : low + LANES])
        low = LANES - SLOT * (3 + other)
        score = dot(table, spread[low : low + LANES])
        key_term = score * queries[number]
        value_term = soft * source[0, :, :width].astype(F32)
        grad_key = key_term if grad_key is None else grad_key + key_term
        grad_value = value_term if grad_value is None else grad_value + value_term
    grad_qkv_b[0, :, :width] = grad_q[0]
    grad_qkv_b[0, :, width : 2 * width] = (grad_key * scale_qk).astype(BF16)
    grad_qkv_b[0, :, 2 * width :] = grad_value.astype(BF16)
    grad_hidden = dot_nt(grad_qkv_b[0], w_qkv_b[...])
    normed_b, inv_b = norm(after_a[0])
    sums[0, 3:4] = column_sum(grad_hidden)
    sums[0, 4:5] = column_sum(grad_hidden * normed_b)
    grad_after = grad_b[0] + norm_back(grad_hidden, normed_b, inv_b, 1.0 + mod[0, 4:5])
    sums[0, 2:3] = column_sum(grad_after * branch[0].astype(F32))
    low_a = (mod[0, 2:3] * grad_after).astype(BF16)
    grad_branch_a[0] = low_a
    grad_mixed = dot_nt(low_a, w_out[...]).astype(BF16)
    masks = side_masks(BF16, 1.0)
    lane = lax.broadcasted_iota(jnp.int32, (1, LANES), 1)
    scale_low = jnp.asarray(scale_qk, BF16)
    for pair in range(heads // 2):
        cols = slice(pair * LANES, (pair + 1) * LANES)
        query = qkv[0, :, cols]
        key = qkv[0, :, pl.ds(width + pair * LANES, LANES)]
        value = qkv[0, :, pl.ds(2 * width + pair * LANES, LANES)]
        gm = grad_mixed[:, cols]
        parts = []
        for side in range(2):
            head = 2 * pair + side
            scores = dot_nt(query * (masks[side] * scale_low), key)
            soft = jnp.exp(scores - lse[0, :, head : head + 1])
            grad_soft = dot_nt(gm * masks[side], value)
            inner = jnp.sum(soft * grad_soft, axis=-1, keepdims=True)
            grad_scores = (soft * (grad_soft - inner)).astype(BF16)
            parts.append(
                (dot(grad_scores, key), dot_tn(grad_scores, query), dot_tn(soft.astype(BF16), gm))
            )
        for number, factor in ((0, scale_qk), (1, scale_qk), (2, 1.0)):
            both = jnp.where(lane < HEAD_DIM, parts[0][number], parts[1][number])
            start = number * width + pair * LANES
            grad_qkv_a[0, :, start : start + LANES] = (both * factor).astype(BF16)
    grad_hidden = dot_nt(grad_qkv_a[0], w_qkv_a[...])
    normed_a, inv_a = norm(tokens[0].astype(F32))
    sums[0, 0:1] = column_sum(grad_hidden)
    sums[0, 1:2] = column_sum(grad_hidden * normed_a)
    grad_tokens[0] = grad_after + norm_back(grad_hidden, normed_a, inv_a, 1.0 + mod[0, 1:2])


def weight_term(left, right, out):
    out[...] = dot_tn(left[...], right[...]).astype(BF16)


def weight_grad(left, right, tile_m, tile_n):
    rows, height = left.shape
    width = right.shape[1]
    return pl.pallas_call(
        weight_term,
        grid=(height // tile_m, width // tile_n),
        in_specs=[
            pl.BlockSpec((rows, tile_m), lambda i, j: (0, i)),
            pl.BlockSpec((rows, tile_n), lambda i, j: (0, j)),
        ],
        out_specs=pl.BlockSpec((tile_m, tile_n), lambda i, j: (i, j)),
        out_shape=jax.ShapeDtypeStruct((height, width), BF16),
        compiler_params=pltpu.CompilerParams(vmem_limit_bytes=VMEM_LIMIT),
        cost_estimate=pl.CostEstimate(
            flops=2 * rows * height * width,
            bytes_accessed=2 * (rows * height + rows * width + height * width),
            transcendentals=0,
        ),
    )(left, right)


def clip_block(array):
    rest = array.shape[1:]
    return pl.BlockSpec((1,) + rest, lambda c: (c,) + (0,) * len(rest))


def whole(array):
    return pl.BlockSpec(
        array.shape, lambda c: (0,) * array.ndim, pipeline_mode=pl.Buffered(1)
    )


def per_clip(body, blocks, wholes, outs, flops, scratch=(), landing=()):
    clips = blocks[0].shape[0]
    operands = [(a, clip_block(a)) for a in blocks] + [(a, whole(a)) for a in wholes]
    touched = sum(math.prod(a.shape) * a.dtype.itemsize for a in [*blocks, *wholes, *outs])
    return pl.pallas_call(
        body,
        grid=(clips,),
        in_specs=[spec for _, spec in operands],
        out_specs=[clip_block(a) for a in outs] + [pl.BlockSpec(memory_space=pl.ANY)] * len(landing),
        out_shape=[*outs, *landing],
        scratch_shapes=list(scratch),
        compiler_params=pltpu.CompilerParams(
            vmem_limit_bytes=VMEM_LIMIT,
            **({"collective_id": 1, "has_side_effects": True} if landing else {}),
        ),
        cost_estimate=pl.CostEstimate(flops=flops, bytes_accessed=touched, transcendentals=0),
    )(*[a for a, _ in operands])


def scatter_sum(parts, axis, bits):
    count = lax.axis_size(axis)
    me = lax.axis_index(axis)
    shape = parts.shape[1:]
    left = list(range(count.bit_length() - 1))[::-1]
    held = parts.reshape((2,) * len(left) + shape)
    for bit in bits:
        dim = left.index(bit)
        left.remove(bit)
        mine = (me >> bit) & 1
        away = lax.dynamic_index_in_dim(held, 1 - mine, dim, keepdims=False)
        keep = lax.dynamic_index_in_dim(held, mine, dim, keepdims=False)
        came = lax.ppermute(away, axis, [(i, i ^ (1 << bit)) for i in range(count)])
        total = keep.astype(F32) + came.astype(F32)
        held = total.astype(parts.dtype)
    return total.reshape(shape)


def clip_bits(first):
    bits = list(range(1, lax.axis_size("clip").bit_length() - 1))
    return [0] + (bits if first == 0 else bits[::-1])


def frame_bits():
    return list(range(lax.axis_size("frame").bit_length() - 1))


def thirds(values):
    high = values.astype(BF16)
    rest = values - high.astype(F32)
    mid = rest.astype(BF16)
    low = (rest - mid.astype(F32)).astype(BF16)
    return jnp.concatenate((high, mid, low), axis=0)


def local(
    tokens, target, loss_weight, timesteps, offsets, cond_table, modulate_w,
    spatial_qkv, spatial_out, temporal_qkv, temporal_out, mlp_in, mlp_out,
):
    clips, frames, patches, width = tokens.shape
    steps = cond_table.shape[0]
    ff = mlp_in.shape[1]
    heads = width // HEAD_DIM
    rows = clips * frames * patches
    n_clip = lax.axis_size("clip")
    n_frame = lax.axis_size("frame")
    clip_at = lax.axis_index("clip")
    frame_at = lax.axis_index("frame")
    flat = (clips, patches, width)
    tok = tokens.reshape(flat)
    tgt = target.reshape(flat)

    condition = jnp.take(cond_table, timesteps, axis=0, mode="clip")
    cond_low = jax.nn.silu(condition).astype(BF16)
    cond_here = lax.dynamic_slice_in_dim(condition, clip_at * clips, clips)
    _, silu_pull = jax.vjp(jax.nn.silu, cond_here)
    low_here = lax.dynamic_slice_in_dim(cond_low, clip_at * clips, clips)
    mod = jnp.dot(low_here, modulate_w, preferred_element_type=F32).reshape(clips, 9, width)

    half = width // 2
    positions = (offsets + frame_at).astype(F32)
    freqs = jnp.exp(jnp.arange(half, dtype=F32) * (-math.log(10000.0) / half))
    angles = positions[:, None] * freqs
    posenc = jnp.concatenate((jnp.sin(angles), jnp.cos(angles)), axis=-1)[:, None, :]

    head_of = jnp.arange(width, dtype=jnp.int32) // HEAD_DIM
    lane_ids = jnp.arange(LANES, dtype=jnp.int32)
    to_heads = (head_of[:, None] == lane_ids[None, :]).astype(BF16)
    tall = jnp.arange(2 * LANES, dtype=jnp.int32) - LANES
    spread = (tall[:, None] == head_of[None, :]).astype(BF16)
    group, inside = jnp.divmod(jnp.arange(6 * LANES, dtype=jnp.int32), LANES)
    slot_at = jnp.where(inside < heads, group * SLOT + inside, -1)
    pack = (slot_at[:, None] == lane_ids[None, :]).astype(BF16)
    side_ok = jnp.stack((frame_at > 0, frame_at >= 0, frame_at < n_frame - 1))
    masks = jnp.where(side_ok[:, None], 0.0, NO_KEY) * jnp.ones((1, LANES), F32)
    masks = jnp.pad(masks, ((0, 5), (0, 0)))
    weight = jnp.broadcast_to(loss_weight[:, None, None], (clips, 1, LANES))

    def struct(last, dtype):
        return jax.ShapeDtypeStruct((clips, patches, last), dtype)

    macs = rows * width * width
    hidden_a, qkv_a, mixed_a, branch_a, after_a, hidden_b, lse, hb_prev, hb_next = per_clip(
        functools.partial(spatial_forward, heads),
        [tok, mod, posenc],
        [spatial_qkv, spatial_out],
        [
            struct(width, BF16), struct(3 * width, BF16), struct(width, BF16),
            struct(width, BF16), struct(width, F32), struct(width, BF16), struct(LANES, F32),
        ],
        flops=2 * macs * 7,
        scratch=[
            pltpu.VMEM(flat, BF16), pltpu.VMEM((patches, width), BF16),
            pltpu.SemaphoreType.DMA((2, clips)), pltpu.SemaphoreType.DMA((2, clips)),
            pltpu.SemaphoreType.DMA((clips,)),
        ],
        landing=[struct(width, BF16)] * 2,
    )
    up = [(i, i + 1) for i in range(n_frame - 1)]
    down = [(i + 1, i) for i in range(n_frame - 1)]
    (
        output, grad_b, hidden_c, act, grad_branch_c, grad_up, mixed_b, grad_branch_b, sent,
        q_own, grad_q, sums_mid,
    ) = per_clip(
        middle,
        [hidden_b, hb_prev, hb_next, after_a, tgt, mod, weight],
        [masks, to_heads, spread, pack, temporal_qkv, temporal_out, mlp_in, mlp_out],
        [
            struct(width, BF16), struct(width, F32), struct(width, BF16), struct(ff, BF16),
            struct(width, BF16), struct(ff, BF16), struct(width, BF16), struct(width, BF16),
            struct(width + LANES, BF16), struct(width, BF16), struct(width, BF16),
            jax.ShapeDtypeStruct((clips, 8, width), F32),
        ],
        flops=2 * macs * 31,
        scratch=[pltpu.VMEM((patches, ff), F32)],
    )
    sent_prev = lax.ppermute(sent, "frame", up)
    sent_next = lax.ppermute(sent, "frame", down)

    def flat_rows(array):
        return array.reshape(rows, array.shape[-1])

    weight_in = weight_grad(flat_rows(hidden_c), flat_rows(grad_up), width, width)
    weight_mlp = weight_grad(flat_rows(act), flat_rows(grad_branch_c), width, width)
    grad_tok, grad_qkv_b, grad_qkv_a, grad_branch_a, sums_back = per_clip(
        functools.partial(spatial_backward, heads),
        [
            hb_prev, hb_next, sent, sent_prev, sent_next, q_own, grad_q, grad_b, after_a,
            tok, branch_a, qkv_a, lse, mod,
        ],
        [spread, temporal_qkv, spatial_out, spatial_qkv],
        [
            struct(width, F32), struct(3 * width, BF16), struct(3 * width, BF16),
            struct(width, BF16), jax.ShapeDtypeStruct((clips, 8, width), F32),
        ],
        flops=2 * macs * 16,
    )
    weight_qkv_b = weight_grad(flat_rows(hidden_b), flat_rows(grad_qkv_b), width, width)
    weight_out_b = weight_grad(flat_rows(mixed_b), flat_rows(grad_branch_b), width, width)
    weight_qkv_a = weight_grad(flat_rows(hidden_a), flat_rows(grad_qkv_a), width, width)
    weight_out_a = weight_grad(flat_rows(mixed_a), flat_rows(grad_branch_a), width, width)

    def over_frames(by_clip):
        tall_rows, cols = by_clip.shape
        shares = by_clip.reshape(tall_rows, n_frame, cols // n_frame).transpose(1, 0, 2)
        return scatter_sum(shares.astype(BF16), "frame", frame_bits())

    def reduce_weight(term, first):
        shares = term.reshape(n_clip, term.shape[0] // n_clip, term.shape[1])
        return over_frames(scatter_sum(shares, "clip", clip_bits(first)))

    grad_mlp_in = reduce_weight(weight_in, 0)
    grad_mlp_out = reduce_weight(weight_mlp, 1)

    def reduce_pair(qkv_term, out_term):
        both = jnp.concatenate((qkv_term, out_term), axis=1)
        shares = both.reshape(n_clip, both.shape[0] // n_clip, both.shape[1])
        cut = both.shape[1] // 2
        first = scatter_sum(shares[:, :, :cut], "clip", clip_bits(0))
        second = scatter_sum(shares[:, :, cut:], "clip", clip_bits(1))
        joined = jnp.concatenate((first, second), axis=1)
        qkv_cols = qkv_term.shape[1]
        tall_rows = joined.shape[0]
        frame_shares = jnp.concatenate(
            (
                joined[:, :qkv_cols].reshape(tall_rows, n_frame, -1),
                joined[:, qkv_cols:].reshape(tall_rows, n_frame, -1),
            ),
            axis=2,
        ).transpose(1, 0, 2)
        done = scatter_sum(frame_shares.astype(BF16), "frame", frame_bits())
        return done[:, : qkv_cols // n_frame], done[:, qkv_cols // n_frame :]

    grad_temporal_qkv, grad_temporal_out = reduce_pair(weight_qkv_b, weight_out_b)
    grad_spatial_qkv, grad_spatial_out = reduce_pair(weight_qkv_a, weight_out_a)

    grad_mod = jnp.concatenate(
        (sums_back[:, :5], sums_mid[:, 3:4], sums_mid[:, :3]), axis=1
    ).reshape(clips, 9 * width)
    by_term = dot_nt(thirds(grad_mod), modulate_w).reshape(3, clips, width)
    grad_cond = silu_pull(by_term[0] + by_term[1] + by_term[2])[0]
    grad_cond = lax.psum(grad_cond, "frame")
    grad_cond = lax.all_gather(grad_cond, "clip", axis=0, tiled=True)
    onehot = (timesteps[:, None] == jnp.arange(steps, dtype=jnp.int32)[None, :]).astype(BF16)
    grad_table = dot_tn(jnp.concatenate((onehot,) * 3, axis=0), thirds(grad_cond))
    mod_cols = 9 * width // n_frame
    mod_share = scatter_sum(
        grad_mod.reshape(clips, n_frame, mod_cols).transpose(1, 0, 2), "frame", frame_bits()
    )
    mod_all = lax.all_gather(mod_share, "clip", axis=0, tiled=True)
    mod_rows = width // n_clip
    low_rows = lax.dynamic_slice_in_dim(cond_low, clip_at * mod_rows, mod_rows, axis=1)
    grad_modulate = dot_tn(jnp.concatenate((low_rows,) * 3, axis=0), thirds(mod_all))
    return (
        output.reshape(tokens.shape),
        grad_tok.reshape(tokens.shape),
        grad_table,
        grad_modulate,
        grad_spatial_qkv,
        grad_spatial_out,
        grad_temporal_qkv,
        grad_temporal_out,
        grad_mlp_in,
        grad_mlp_out,
    )


def solution(mesh):
    placed = (
        P("clip", "frame", None, None), P("clip", "frame", None, None), P("clip"), P(), P("clip"),
    ) + (P(),) * 8
    return jax.shard_map(
        local,
        mesh=mesh,
        in_specs=placed,
        out_specs=(
            P("clip", "frame", None, None), P("clip", "frame", None, None), P(),
        ) + (P("clip", "frame"),) * 7,
        check_vma=False,
    )
```

```python
import functools
import math

import jax
import jax.numpy as jnp
from jax import lax
from jax.experimental import pallas as pl
from jax.experimental.pallas import tpu as pltpu
from jax.sharding import PartitionSpec as P

HEAD_DIM = 64
NORM_EPSILON = 1e-06
F32 = jnp.float32
BF16 = jnp.bfloat16
LANES = 128
SLOT = 16
NO_KEY = -1e30
VMEM_LIMIT = 60 * 2**20
GELU_A = math.sqrt(2.0 / math.pi)
GELU_B = 0.044715


def dot(left, right):
    return lax.dot_general(left, right, (((1,), (0,)), ((), ())), preferred_element_type=F32)


def dot_nt(left, right):
    return lax.dot_general(left, right, (((1,), (1,)), ((), ())), preferred_element_type=F32)


def dot_tn(left, right):
    return lax.dot_general(left, right, (((0,), (0,)), ((), ())), preferred_element_type=F32)


def norm(values):
    centred = values - jnp.mean(values, axis=-1, keepdims=True)
    inv_std = lax.rsqrt(jnp.mean(centred * centred, axis=-1, keepdims=True) + NORM_EPSILON)
    return centred * inv_std, inv_std


def norm_back(grad_hidden, normed, inv_std, scale_plus):
    grad_normed = grad_hidden * scale_plus
    mean_grad = jnp.mean(grad_normed, axis=-1, keepdims=True)
    mean_cross = jnp.mean(grad_normed * normed, axis=-1, keepdims=True)
    return inv_std * (grad_normed - mean_grad - normed * mean_cross)


def column_sum(values):
    return jnp.sum(values, axis=0, keepdims=True)


def side_masks(dtype, value):
    lane = lax.broadcasted_iota(jnp.int32, (1, LANES), 1)
    return [jnp.where((lane < HEAD_DIM) == (side == 0), value, 0.0).astype(dtype) for side in (0, 1)]


class Refs:
    def __init__(self, names, refs):
        self.__dict__.update(zip(names, refs, strict=True))


class Late:
    def __init__(self, source, ref, sem, step):
        self.ref = ref
        self.copy = pltpu.make_async_copy(source, ref, sem)
        self.step = step
        self.waited = False

    def __getitem__(self, index):
        if not self.waited:
            pl.when(pl.program_id(0) == self.step)(self.copy.wait)
            self.waited = True
        return self.ref[index]


def partner(axis, bit):
    me = lax.axis_index(axis)
    return me + (1 << bit) - (2 << bit) * lax.rem(me // (1 << bit), 2)


def remote(source, target, send_sem, recv_sem, **where):
    return pltpu.make_async_remote_copy(
        src_ref=source, dst_ref=target, send_sem=send_sem, recv_sem=recv_sem,
        device_id=where, device_id_type=pl.DeviceIdType.MESH,
    )


def greet(barrier, **where):
    pl.semaphore_signal(barrier, inc=1, device_id=where, device_id_type=pl.DeviceIdType.MESH)


def run_kernel(body, steps, ins, weights, outs, scratch, flops, collective=None):
    anywhere = pl.BlockSpec(memory_space=pl.ANY)
    names = [name for name, *_ in ins] + [name + "_hbm" for name, *_ in weights]
    names += [name for name, *_ in outs]
    names += [name + "_vmem" for name, *_ in weights] + ["weight_sems"]
    names += [name for name, _ in scratch]

    def kernel(*refs):
        r = Refs(names, refs)
        lates = []
        for number, (name, _, step) in enumerate(weights):
            late = Late(
                getattr(r, name + "_hbm"), getattr(r, name + "_vmem"), r.weight_sems.at[number], step
            )
            lates.append(late)
            setattr(r, name, late)

        @pl.when(pl.program_id(0) == 0)
        def _():
            for late in lates:
                if late.step == 0:
                    late.copy.start()

        body(r)

        @pl.when(pl.program_id(0) == 0)
        def _():
            for late in lates:
                if late.step > 0:
                    late.copy.start()

    arrays = [array for _, array, _ in ins] + [array for _, array, _ in weights]
    shapes = [shape for _, shape, _ in outs]
    touched = sum(math.prod(a.shape) * a.dtype.itemsize for a in arrays + shapes)
    params = {} if collective is None else {"collective_id": collective, "has_side_effects": True}
    done = pl.pallas_call(
        kernel,
        grid=(steps,),
        in_specs=[spec for *_, spec in ins] + [anywhere] * len(weights),
        out_specs=[spec or anywhere for *_, spec in outs],
        out_shape=shapes,
        scratch_shapes=[pltpu.VMEM(a.shape, a.dtype) for _, a, _ in weights]
        + [pltpu.SemaphoreType.DMA((max(len(weights), 1),))]
        + [shape for _, shape in scratch],
        compiler_params=pltpu.CompilerParams(vmem_limit_bytes=VMEM_LIMIT, **params),
        cost_estimate=pl.CostEstimate(flops=flops, bytes_accessed=touched, transcendentals=0),
    )(*arrays)
    return Refs([name for name, *_ in outs], done)


def clip_spec(array, first, clips, depth=None):
    rest = array.shape[1:]
    mode = {} if depth is None else {"pipeline_mode": pl.Buffered(depth)}
    return pl.BlockSpec(
        (1,) + rest, lambda s: (jnp.clip(s - first, 0, clips - 1),) + (0,) * len(rest), **mode
    )


def spatial_forward(r, heads, clip):
    width = r.tokens.shape[-1]
    rows = r.tokens.shape[1]
    mod = r.mod
    inputs = r.tokens[0].astype(F32)
    normed, _ = norm(inputs)
    hidden = (normed * (1.0 + mod[0, 1:2]) + mod[0, 0:1]).astype(BF16)
    r.hidden_a[0] = hidden
    for part in range(3):
        cols = slice(part * width, (part + 1) * width)
        r.qkv_a[0, :, cols] = dot(hidden, r.w_qkv_a[:, cols]).astype(BF16)
    masks = side_masks(BF16, HEAD_DIM**-0.5)
    lane = lax.broadcasted_iota(jnp.int32, (1, LANES), 1)
    table = jnp.zeros((rows, LANES), F32)
    for pair in range(heads // 2):
        query, key, value = (
            r.qkv_a[0, :, pl.ds(part * width + pair * LANES, LANES)] for part in range(3)
        )
        out = []
        for side in range(2):
            scores = dot_nt(query * masks[side], key)
            top = jnp.max(scores, axis=-1, keepdims=True)
            grown = jnp.exp(scores - top)
            total = jnp.sum(grown, axis=-1, keepdims=True)
            soft = (grown * (1.0 / total)).astype(BF16)
            out.append(dot(soft, value))
            table = jnp.where(lane == 2 * pair + side, top + jnp.log(total), table)
        cols = slice(pair * LANES, (pair + 1) * LANES)
        r.mixed_a[0, :, cols] = jnp.where(lane < HEAD_DIM, out[0], out[1]).astype(BF16)
    r.lse[0] = table
    branch_a = dot(r.mixed_a[0], r.w_out_a[...])
    r.branch_a[0] = branch_a.astype(BF16)
    after_a = inputs + mod[0, 2:3] * branch_a
    r.after_held[clip] = after_a
    normed_b, _ = norm(after_a)
    r.hidden_held[clip] = (
        normed_b * (1.0 + mod[0, 4:5]) + (mod[0, 3:4] + r.posenc[0])
    ).astype(BF16)


def by_head(left, right, to_heads):
    return dot(left * right, to_heads)


def middle(r, clip, rows_at):
    width = r.target.shape[-1]
    rows = r.target.shape[1]
    ff = r.act.shape[-1]
    scale_qk = HEAD_DIM**-0.5
    mod = r.mod
    own_rows = pl.ds(rows_at, rows)
    store = r.w_qkv_a_vmem

    def kept(number, part):
        return store[number * rows : (number + 1) * rows, part * width : (part + 1) * width]

    for number, (hidden, out) in enumerate(
        ((r.hidden_prev, r.q_prev), (r.hidden_held, r.q_own), (r.hidden_next, r.q_next))
    ):
        for part in range(3):
            cols = slice(part * width, (part + 1) * width)
            value = dot(hidden[clip], r.w_qkv_b[:, cols]).astype(BF16)
            store[number * rows : (number + 1) * rows, cols] = value
            if part == 0:
                out[0] = value
    scores = []
    for number in range(3):
        raw = by_head(kept(1, 0), kept(number, 1), r.to_heads[...]) * scale_qk
        scores.append(raw + r.masks[number : number + 1])
    top = jnp.maximum(jnp.maximum(scores[0], scores[1]), scores[2])
    grown = [jnp.exp(entry - top) for entry in scores]
    inverse = 1.0 / (grown[0] + grown[1] + grown[2])
    soft = [entry * inverse for entry in grown]
    soft_low = [entry.astype(BF16) for entry in soft]
    to_width = r.spread[LANES : 2 * LANES]
    total = None
    for number in range(3):
        term = dot(soft_low[number], to_width) * kept(number, 2).astype(F32)
        total = term if total is None else total + term
    mixed = total.astype(BF16)
    r.mixed_b[0] = mixed
    branch_b = dot(mixed, r.w_out_b[...])
    r.grad_b[0] = branch_b
    after_b = r.after_held[clip] + mod[0, 5:6] * branch_b
    normed_c, inv_c = norm(after_b)
    hidden = (normed_c * (1.0 + mod[0, 7:8]) + mod[0, 6:7]).astype(BF16)
    r.hidden_c[own_rows, :] = hidden
    parts = ff // width
    ahead = dot(hidden, r.w_in[:, :width])
    for part in range(parts):
        cols = slice(part * width, (part + 1) * width)
        upward = ahead
        if part + 1 < parts:
            ahead = dot(hidden, r.w_in[:, (part + 1) * width : (part + 2) * width])
        squared = upward * upward
        bent = jnp.tanh(upward * (GELU_A + (GELU_A * GELU_B) * squared))
        share = 0.5 + 0.5 * bent
        r.act[own_rows, cols] = (upward * share).astype(BF16)
        steep = (1.0 - bent * bent) * (0.5 * GELU_A + (1.5 * GELU_A * GELU_B) * squared)
        r.grad_up[own_rows, cols] = (share + upward * steep).astype(BF16)
    branch_c = dot(r.act[own_rows, :], r.w_mlp[...])
    result = after_b + mod[0, 8:9] * branch_c
    r.output[0] = result.astype(BF16)
    grad_result = r.weight[0, :, :1] * (result - r.target[0].astype(F32))
    r.sums[0, 2:3] = column_sum(grad_result * branch_c)
    low_c = (mod[0, 8:9] * grad_result).astype(BF16)
    r.grad_branch_c[own_rows, :] = low_c
    ahead = dot_nt(low_c, r.w_mlp[:width, :])
    for part in range(parts):
        cols = slice(part * width, (part + 1) * width)
        grad_act = ahead
        if part + 1 < parts:
            ahead = dot_nt(low_c, r.w_mlp[(part + 1) * width : (part + 2) * width, :])
        r.grad_up[own_rows, cols] = (grad_act * r.grad_up[own_rows, cols].astype(F32)).astype(BF16)
    grad_hidden = dot_nt(r.grad_up[own_rows, :], r.w_in[...])
    r.sums[0, 0:1] = column_sum(grad_hidden)
    r.sums[0, 1:2] = column_sum(grad_hidden * normed_c)
    grad_after = grad_result + norm_back(grad_hidden, normed_c, inv_c, 1.0 + mod[0, 7:8])
    r.sums[0, 3:4] = column_sum(grad_after * r.grad_b[0])
    r.grad_b[0] = grad_after
    low_b = (mod[0, 5:6] * grad_after).astype(BF16)
    r.grad_branch_b[0] = low_b
    grad_mixed = dot_nt(low_b, r.w_out_b[...]).astype(BF16)
    grad_soft = [by_head(grad_mixed, kept(number, 2), r.to_heads[...]) for number in range(3)]
    inner = soft[0] * grad_soft[0] + soft[1] * grad_soft[1] + soft[2] * grad_soft[2]
    grad_scores = [(soft[number] * (grad_soft[number] - inner)).astype(BF16) for number in range(3)]
    total = None
    for number in range(3):
        term = dot(grad_scores[number], to_width) * kept(number, 1).astype(F32)
        total = term if total is None else total + term
    r.grad_q[0] = (total * scale_qk).astype(BF16)
    r.sent_held[clip, :, :width] = grad_mixed
    r.sent_held[clip, :, width:] = dot(
        jnp.concatenate(soft_low + grad_scores, axis=1), r.pack[...]
    ).astype(BF16)


def turn(left, n, turned, sorted_rows):
    core = lax.rem(lax.axis_index("clip"), 2)
    turned[...] = left.T
    share = turned.shape[0] // n
    for number in range(n):
        spot = 2 * number + 1 - core if number < n // 2 else 2 * number - n + core
        at = pl.multiple_of(spot * share, share)
        sorted_rows[number * share : (number + 1) * share] = turned[pl.ds(at, share)]


def forward_kernel(heads, clips, n, r):
    step = pl.program_id(0)
    rows, width = r.tokens.shape[1:]
    ff = r.act.shape[-1]
    in_steps = ff // width
    out_steps = n // 2
    share = ff // n
    last = 2 * clips + in_steps + out_steps - 1
    frame = lax.axis_index("frame")
    has_prev = frame > 0
    has_next = frame < lax.axis_size("frame") - 1
    no_prev = jnp.logical_not(has_prev)
    no_next = jnp.logical_not(has_next)
    core = lax.rem(lax.axis_index("clip"), 2)
    sibling = partner("clip", 0)
    barrier = pltpu.get_barrier_semaphore()

    def halo(way, clip):
        return remote(
            r.hidden_held.at[clip], (r.hidden_prev, r.hidden_next)[way].at[clip],
            r.halo_send.at[way, clip], r.halo_recv.at[way, clip],
            frame=frame + 1 if way == 0 else frame - 1,
        )

    def packet(way, clip):
        return remote(
            r.sent_held.at[clip], (r.sent_prev, r.sent_next)[way].at[clip],
            r.sent_send.at[way, clip], r.sent_recv.at[way, clip],
            frame=frame + 1 if way == 0 else frame - 1,
        )

    half = width // 2

    def in_tile(tile):
        return remote(
            r.stage.at[lax.rem(tile, 2), pl.ds(0, half)], r.came_in.at[tile],
            r.tile_send.at[tile], r.tile_recv.at[tile], clip=sibling,
        )

    def in_kept(tile):
        return pltpu.make_async_copy(
            r.stage.at[lax.rem(tile, 2), pl.ds(half, half)], r.keep_in.at[tile],
            r.keep_sems.at[tile],
        )

    def out_part(tile, which):
        return r.stage.at[
            lax.rem(tile + in_steps, 2), pl.ds(pl.multiple_of(which * share, share), share)
        ]

    def out_tile(tile):
        return remote(
            out_part(tile, 1 - core), r.came_out.at[tile],
            r.tile_send.at[tile + in_steps], r.tile_recv.at[tile + in_steps], clip=sibling,
        )

    def out_kept(tile):
        return pltpu.make_async_copy(
            out_part(tile, core), r.keep_out.at[tile], r.keep_sems.at[tile + in_steps]
        )

    def save(clip):
        return [
            pltpu.make_async_copy(r.after_held.at[clip], r.after_a.at[clip], r.save_sems.at[0, clip]),
            pltpu.make_async_copy(
                r.hidden_held.at[clip], r.hidden_b.at[clip], r.save_sems.at[1, clip]
            ),
        ]

    def save_sent(clip):
        return pltpu.make_async_copy(r.sent_held.at[clip], r.sent.at[clip], r.save_sems.at[2, clip])

    def fill(way, clip):
        zeros = (r.hidden_prev, r.hidden_next)[way].at[clip]
        target = (r.sent_prev, r.sent_next)[way].at[clip]
        return [
            pltpu.make_async_copy(zeros, target.at[:, pl.ds(0, width)], r.save_sems.at[3, clip]),
            pltpu.make_async_copy(
                zeros.at[:, pl.ds(0, LANES)], target.at[:, pl.ds(width, LANES)],
                r.save_sems.at[4, clip],
            ),
        ]

    @pl.when(step == 0)
    def _():
        greet(barrier, clip=sibling)
        pl.when(has_prev)(lambda: greet(barrier, frame=frame - 1))
        pl.when(has_next)(lambda: greet(barrier, frame=frame + 1))

        @pl.when(no_prev)
        def _():
            r.hidden_prev[...] = jnp.zeros_like(r.hidden_prev)
            for clip in range(clips):
                for copy in fill(0, clip):
                    copy.start()

        @pl.when(no_next)
        def _():
            r.hidden_next[...] = jnp.zeros_like(r.hidden_next)
            for clip in range(clips):
                for copy in fill(1, clip):
                    copy.start()

    @pl.when(step < clips)
    def _():
        spatial_forward(r, heads, step)

        @pl.when(step == 0)
        def _():
            pl.semaphore_wait(
                barrier, 1 + jnp.where(has_prev, 1, 0) + jnp.where(has_next, 1, 0)
            )

        pl.when(has_next)(lambda: halo(0, step).start())
        pl.when(has_prev)(lambda: halo(1, step).start())
        for copy in save(step):
            copy.start()

    @pl.when((step >= clips) & (step < 2 * clips))
    def _():
        clip = step - clips
        pl.when(has_prev)(lambda: halo(0, clip).wait_recv())
        pl.when(has_next)(lambda: halo(1, clip).wait_recv())
        middle(r, clip, pl.multiple_of(clip * rows, rows))
        pl.when(has_next)(lambda: packet(0, clip).start())
        pl.when(has_prev)(lambda: packet(1, clip).start())
        save_sent(clip).start()

    turned = r.w_qkv_a_vmem.at[:, pl.ds(0, clips * rows)]
    sorted_rows = r.w_qkv_a_vmem.at[:, pl.ds(clips * rows, clips * rows)]

    @pl.when((step >= 2 * clips) & (step < 2 * clips + in_steps))
    def _():
        tile = step - 2 * clips

        @pl.when(tile == 0)
        def _():
            turn(r.hidden_c[...], n, turned, sorted_rows)

        @pl.when(tile >= 2)
        def _():
            in_tile(tile - 2).wait_send()
            in_kept(tile - 2).wait()

        cols = pl.ds(pl.multiple_of(tile * width, width), width)
        r.stage[lax.rem(tile, 2)] = dot(sorted_rows[...], r.grad_up[:, cols]).astype(BF16)
        in_tile(tile).start()
        in_kept(tile).start()

    @pl.when(step >= 2 * clips + in_steps)
    def _():
        tile = step - 2 * clips - in_steps

        @pl.when(tile < 2)
        def _():
            in_tile(in_steps + tile - 2).wait_send()
            in_kept(in_steps + tile - 2).wait()

        @pl.when(tile >= 2)
        def _():
            out_tile(tile - 2).wait_send()
            out_kept(tile - 2).wait()

        cols = pl.ds(pl.multiple_of(tile * 2 * share, 2 * share), 2 * share)
        r.stage[lax.rem(tile + in_steps, 2), : 2 * share] = dot_tn(
            r.act[:, cols], r.grad_branch_c[...]
        ).astype(BF16)
        out_tile(tile).start()
        out_kept(tile).start()

    @pl.when(step == last)
    def _():
        for clip in range(clips):
            for copy in save(clip):
                copy.wait()
            save_sent(clip).wait()

            @pl.when(has_next)
            def _():
                halo(0, clip).wait_send()
                packet(0, clip).wait_send()
                packet(1, clip).wait_recv()

            @pl.when(has_prev)
            def _():
                halo(1, clip).wait_send()
                packet(1, clip).wait_send()
                packet(0, clip).wait_recv()

            for way, absent in ((0, no_prev), (1, no_next)):

                @pl.when(absent)
                def _():
                    for copy in fill(way, clip):
                        copy.wait()

        for tile in range(in_steps):
            in_tile(tile).wait_recv()
        for tile in range(out_steps):
            out_tile(tile).wait_recv()
        for tile in range(out_steps - 2, out_steps):
            out_tile(tile).wait_send()
            out_kept(tile).wait()


def forward_call(tok, target, mod, posenc, weight, masks, tables, weights, n):
    clips, rows, width = tok.shape
    ff = weights["mlp_in"].shape[1]
    heads = width // HEAD_DIM
    tokens_here = clips * rows
    half = width // 2
    in_steps, out_steps, share = ff // width, n // 2, ff // n
    to_heads, spread, pack = tables

    def struct(last, dtype=BF16):
        return jax.ShapeDtypeStruct((clips, rows, last), dtype)

    def early(array):
        return clip_spec(array, 0, clips)

    def late(array):
        return clip_spec(array, clips, clips)

    mod_spec = pl.BlockSpec(
        (1,) + mod.shape[1:],
        lambda s: (jnp.where(s < clips, s, jnp.minimum(s - clips, clips - 1)), 0, 0),
    )
    ins = [
        ("tokens", tok, early(tok)), ("posenc", posenc, early(posenc)), ("mod", mod, mod_spec),
        ("target", target, clip_spec(target, clips, clips, 1)), ("weight", weight, late(weight)),
    ]
    held = [
        ("w_qkv_a", weights["spatial_qkv"], 0), ("w_out_a", weights["spatial_out"], 0),
        ("w_qkv_b", weights["temporal_qkv"], clips), ("to_heads", to_heads, clips),
        ("masks", masks, clips), ("spread", spread, clips), ("w_out_b", weights["temporal_out"], clips),
        ("w_in", weights["mlp_in"], clips), ("w_mlp", weights["mlp_out"], clips), ("pack", pack, clips),
    ]
    outs = []
    for name, shape in (
        ("hidden_a", struct(width)), ("qkv_a", struct(3 * width)), ("mixed_a", struct(width)),
        ("branch_a", struct(width)), ("lse", struct(LANES, F32)),
    ):
        outs.append((name, shape, clip_spec(shape, 0, clips, 1)))
    for name, shape in (
        ("output", struct(width)), ("grad_b", struct(width, F32)), ("mixed_b", struct(width)),
        ("grad_branch_b", struct(width)), ("q_own", struct(width)), ("q_prev", struct(width)),
        ("q_next", struct(width)), ("grad_q", struct(width)),
        ("sums", jax.ShapeDtypeStruct((clips, 8, width), F32)),
    ):
        outs.append((name, shape, clip_spec(shape, clips, clips, 1)))
    outs += [
        ("after_a", struct(width, F32), None), ("hidden_b", struct(width), None),
        ("sent", struct(width + LANES), None), ("sent_prev", struct(width + LANES), None),
        ("sent_next", struct(width + LANES), None),
    ]
    tile_in = jax.ShapeDtypeStruct((in_steps, half, width), BF16)
    tile_out = jax.ShapeDtypeStruct((out_steps, share, width), BF16)
    outs += [
        ("keep_in", tile_in, None), ("came_in", tile_in, None), ("keep_out", tile_out, None),
        ("came_out", tile_out, None),
    ]
    dma = pltpu.SemaphoreType.DMA
    scratch = [
        ("after_held", pltpu.VMEM((clips, rows, width), F32)),
        ("hidden_held", pltpu.VMEM((clips, rows, width), BF16)),
        ("hidden_prev", pltpu.VMEM((clips, rows, width), BF16)),
        ("hidden_next", pltpu.VMEM((clips, rows, width), BF16)),
        ("sent_held", pltpu.VMEM((clips, rows, width + LANES), BF16)),
        ("act", pltpu.VMEM((tokens_here, ff), BF16)),
        ("grad_up", pltpu.VMEM((tokens_here, ff), BF16)),
        ("hidden_c", pltpu.VMEM((tokens_here, width), BF16)),
        ("grad_branch_c", pltpu.VMEM((tokens_here, width), BF16)),
        ("stage", pltpu.VMEM((2, max(width, 2 * share), width), BF16)),
        ("halo_send", dma((2, clips))), ("halo_recv", dma((2, clips))),
        ("sent_send", dma((2, clips))), ("sent_recv", dma((2, clips))),
        ("tile_send", dma((in_steps + out_steps,))), ("tile_recv", dma((in_steps + out_steps,))),
        ("keep_sems", dma((in_steps + out_steps,))), ("save_sems", dma((5, clips))),
    ]
    return run_kernel(
        functools.partial(forward_kernel, heads, clips, n), 2 * clips + in_steps + out_steps,
        ins, held, outs, scratch, 2 * tokens_here * width * width * 46, collective=1,
    )


def spatial_backward(
    heads, q_prev, q_next, sent_own, sent_prev, sent_next, q_own, grad_q, grad_b, after_a,
    tokens, branch, qkv, lse, mod, spread, w_qkv_b, w_out, w_qkv_a,
    grad_tokens, grad_qkv_b, grad_qkv_a, grad_branch_a, sums,
):
    width = after_a.shape[-1]
    scale_qk = HEAD_DIM**-0.5
    queries = [query[0].astype(F32) for query in (q_prev, q_own, q_next)]
    grad_key = None
    grad_value = None
    for number, source in enumerate((sent_prev, sent_own, sent_next)):
        other = 2 - number
        table = source[0, :, width:]
        low = LANES - SLOT * other
        soft = dot(table, spread[low : low + LANES])
        low = LANES - SLOT * (3 + other)
        score = dot(table, spread[low : low + LANES])
        key_term = score * queries[number]
        value_term = soft * source[0, :, :width].astype(F32)
        grad_key = key_term if grad_key is None else grad_key + key_term
        grad_value = value_term if grad_value is None else grad_value + value_term
    grad_qkv_b[0, :, :width] = grad_q[0]
    grad_qkv_b[0, :, width : 2 * width] = (grad_key * scale_qk).astype(BF16)
    grad_qkv_b[0, :, 2 * width :] = grad_value.astype(BF16)
    grad_hidden = dot_nt(grad_qkv_b[0], w_qkv_b[...])
    normed_b, inv_b = norm(after_a[0])
    sums[0, 3:4] = column_sum(grad_hidden)
    sums[0, 4:5] = column_sum(grad_hidden * normed_b)
    grad_after = grad_b[0] + norm_back(grad_hidden, normed_b, inv_b, 1.0 + mod[0, 4:5])
    sums[0, 2:3] = column_sum(grad_after * branch[0].astype(F32))
    low_a = (mod[0, 2:3] * grad_after).astype(BF16)
    grad_branch_a[0] = low_a
    grad_mixed = dot_nt(low_a, w_out[...]).astype(BF16)
    masks = side_masks(BF16, 1.0)
    lane = lax.broadcasted_iota(jnp.int32, (1, LANES), 1)
    scale_low = jnp.asarray(scale_qk, BF16)
    for pair in range(heads // 2):
        cols = slice(pair * LANES, (pair + 1) * LANES)
        query = qkv[0, :, cols]
        key = qkv[0, :, pl.ds(width + pair * LANES, LANES)]
        value = qkv[0, :, pl.ds(2 * width + pair * LANES, LANES)]
        gm = grad_mixed[:, cols]
        parts = []
        for side in range(2):
            head = 2 * pair + side
            scores = dot_nt(query * (masks[side] * scale_low), key)
            soft = jnp.exp(scores - lse[0, :, head : head + 1])
            grad_soft = dot_nt(gm * masks[side], value)
            inner = jnp.sum(soft * grad_soft, axis=-1, keepdims=True)
            grad_scores = (soft * (grad_soft - inner)).astype(BF16)
            parts.append(
                (dot(grad_scores, key), dot_tn(grad_scores, query), dot_tn(soft.astype(BF16), gm))
            )
        for number, factor in ((0, scale_qk), (1, scale_qk), (2, 1.0)):
            both = jnp.where(lane < HEAD_DIM, parts[0][number], parts[1][number])
            start = number * width + pair * LANES
            grad_qkv_a[0, :, start : start + LANES] = (both * factor).astype(BF16)
    grad_hidden = dot_nt(grad_qkv_a[0], w_qkv_a[...])
    normed_a, inv_a = norm(tokens[0].astype(F32))
    sums[0, 0:1] = column_sum(grad_hidden)
    sums[0, 1:2] = column_sum(grad_hidden * normed_a)
    grad_tokens[0] = grad_after + norm_back(grad_hidden, normed_a, inv_a, 1.0 + mod[0, 1:2])


def weight_term(left, right, out):
    out[...] = dot_tn(left[...], right[...]).astype(BF16)


def weight_grad(left, right, tile_m, tile_n):
    rows, height = left.shape
    width = right.shape[1]
    return pl.pallas_call(
        weight_term,
        grid=(height // tile_m, width // tile_n),
        in_specs=[
            pl.BlockSpec((rows, tile_m), lambda i, j: (0, i)),
            pl.BlockSpec((rows, tile_n), lambda i, j: (0, j)),
        ],
        out_specs=pl.BlockSpec((tile_m, tile_n), lambda i, j: (i, j)),
        out_shape=jax.ShapeDtypeStruct((height, width), BF16),
        compiler_params=pltpu.CompilerParams(vmem_limit_bytes=VMEM_LIMIT),
        cost_estimate=pl.CostEstimate(
            flops=2 * rows * height * width,
            bytes_accessed=2 * (rows * height + rows * width + height * width),
            transcendentals=0,
        ),
    )(left, right)


def clip_block(array):
    rest = array.shape[1:]
    return pl.BlockSpec((1,) + rest, lambda c: (c,) + (0,) * len(rest))


def whole(array):
    return pl.BlockSpec(
        array.shape, lambda c: (0,) * array.ndim, pipeline_mode=pl.Buffered(1)
    )


def per_clip(body, blocks, wholes, outs, flops, scratch=(), landing=()):
    clips = blocks[0].shape[0]
    operands = [(a, clip_block(a)) for a in blocks] + [(a, whole(a)) for a in wholes]
    touched = sum(math.prod(a.shape) * a.dtype.itemsize for a in [*blocks, *wholes, *outs])
    return pl.pallas_call(
        body,
        grid=(clips,),
        in_specs=[spec for _, spec in operands],
        out_specs=[clip_block(a) for a in outs] + [pl.BlockSpec(memory_space=pl.ANY)] * len(landing),
        out_shape=[*outs, *landing],
        scratch_shapes=list(scratch),
        compiler_params=pltpu.CompilerParams(
            vmem_limit_bytes=VMEM_LIMIT,
            **({"collective_id": 1, "has_side_effects": True} if landing else {}),
        ),
        cost_estimate=pl.CostEstimate(flops=flops, bytes_accessed=touched, transcendentals=0),
    )(*[a for a, _ in operands])


def scatter_sum(parts, axis, bits, base=0):
    count = lax.axis_size(axis)
    me = lax.axis_index(axis)
    shape = parts.shape[1:]
    left = list(range(base, count.bit_length() - 1))[::-1]
    held = parts.reshape((2,) * len(left) + shape)
    for bit in bits:
        dim = left.index(bit)
        left.remove(bit)
        mine = (me >> bit) & 1
        away = lax.dynamic_index_in_dim(held, 1 - mine, dim, keepdims=False)
        keep = lax.dynamic_index_in_dim(held, mine, dim, keepdims=False)
        came = lax.ppermute(away, axis, [(i, i ^ (1 << bit)) for i in range(count)])
        total = keep.astype(F32) + came.astype(F32)
        held = total.astype(parts.dtype)
    return total.reshape(shape)


def clip_bits(first):
    bits = list(range(1, lax.axis_size("clip").bit_length() - 1))
    return [0] + (bits if first == 0 else bits[::-1])


def frame_bits():
    return list(range(lax.axis_size("frame").bit_length() - 1))


def thirds(values):
    high = values.astype(BF16)
    rest = values - high.astype(F32)
    mid = rest.astype(BF16)
    low = (rest - mid.astype(F32)).astype(BF16)
    return jnp.concatenate((high, mid, low), axis=0)


def local(
    tokens, target, loss_weight, timesteps, offsets, cond_table, modulate_w,
    spatial_qkv, spatial_out, temporal_qkv, temporal_out, mlp_in, mlp_out,
):
    clips, frames, patches, width = tokens.shape
    steps = cond_table.shape[0]
    ff = mlp_in.shape[1]
    heads = width // HEAD_DIM
    rows = clips * frames * patches
    n_clip = lax.axis_size("clip")
    n_frame = lax.axis_size("frame")
    clip_at = lax.axis_index("clip")
    frame_at = lax.axis_index("frame")
    flat = (clips, patches, width)
    tok = tokens.reshape(flat)
    tgt = target.reshape(flat)

    condition = jnp.take(cond_table, timesteps, axis=0, mode="clip")
    cond_low = jax.nn.silu(condition).astype(BF16)
    cond_here = lax.dynamic_slice_in_dim(condition, clip_at * clips, clips)
    _, silu_pull = jax.vjp(jax.nn.silu, cond_here)
    low_here = lax.dynamic_slice_in_dim(cond_low, clip_at * clips, clips)
    mod = jnp.dot(low_here, modulate_w, preferred_element_type=F32).reshape(clips, 9, width)

    half = width // 2
    positions = (offsets + frame_at).astype(F32)
    freqs = jnp.exp(jnp.arange(half, dtype=F32) * (-math.log(10000.0) / half))
    angles = positions[:, None] * freqs
    posenc = jnp.concatenate((jnp.sin(angles), jnp.cos(angles)), axis=-1)[:, None, :]

    head_of = jnp.arange(width, dtype=jnp.int32) // HEAD_DIM
    lane_ids = jnp.arange(LANES, dtype=jnp.int32)
    to_heads = (head_of[:, None] == lane_ids[None, :]).astype(BF16)
    tall = jnp.arange(2 * LANES, dtype=jnp.int32) - LANES
    spread = (tall[:, None] == head_of[None, :]).astype(BF16)
    group, inside = jnp.divmod(jnp.arange(6 * LANES, dtype=jnp.int32), LANES)
    slot_at = jnp.where(inside < heads, group * SLOT + inside, -1)
    pack = (slot_at[:, None] == lane_ids[None, :]).astype(BF16)
    side_ok = jnp.stack((frame_at > 0, frame_at >= 0, frame_at < n_frame - 1))
    masks = jnp.where(side_ok[:, None], 0.0, NO_KEY) * jnp.ones((1, LANES), F32)
    masks = jnp.pad(masks, ((0, 5), (0, 0)))
    weight = jnp.broadcast_to(loss_weight[:, None, None], (clips, 1, LANES))

    def struct(last, dtype):
        return jax.ShapeDtypeStruct((clips, patches, last), dtype)

    macs = rows * width * width
    weights = {
        "spatial_qkv": spatial_qkv, "spatial_out": spatial_out, "temporal_qkv": temporal_qkv,
        "temporal_out": temporal_out, "mlp_in": mlp_in, "mlp_out": mlp_out,
    }
    fwd = forward_call(
        tok, tgt, mod, posenc, weight, masks, (to_heads, spread, pack), weights, n_clip
    )

    def flat_rows(array):
        return array.reshape(rows, array.shape[-1])

    grad_tok, grad_qkv_b, grad_qkv_a, grad_branch_a, sums_back = per_clip(
        functools.partial(spatial_backward, heads),
        [
            fwd.q_prev, fwd.q_next, fwd.sent, fwd.sent_prev, fwd.sent_next, fwd.q_own, fwd.grad_q,
            fwd.grad_b, fwd.after_a, tok, fwd.branch_a, fwd.qkv_a, fwd.lse, mod,
        ],
        [spread, temporal_qkv, spatial_out, spatial_qkv],
        [
            struct(width, F32), struct(3 * width, BF16), struct(3 * width, BF16),
            struct(width, BF16), jax.ShapeDtypeStruct((clips, 8, width), F32),
        ],
        flops=2 * macs * 16,
    )
    weight_qkv_b = weight_grad(flat_rows(fwd.hidden_b), flat_rows(grad_qkv_b), width, width)
    weight_out_b = weight_grad(flat_rows(fwd.mixed_b), flat_rows(fwd.grad_branch_b), width, width)
    weight_qkv_a = weight_grad(flat_rows(fwd.hidden_a), flat_rows(grad_qkv_a), width, width)
    weight_out_a = weight_grad(flat_rows(fwd.mixed_a), flat_rows(grad_branch_a), width, width)

    def over_frames(by_clip):
        tall_rows, cols = by_clip.shape
        shares = by_clip.reshape(tall_rows, n_frame, cols // n_frame).transpose(1, 0, 2)
        return scatter_sum(shares.astype(BF16), "frame", frame_bits())

    def add(keep, came):
        return (keep.astype(F32) + came.astype(F32)).astype(BF16)

    in_sum = add(fwd.keep_in, fwd.came_in).reshape(ff // width, n_clip // 2, width // n_clip, width)
    in_sum = in_sum.transpose(1, 2, 0, 3).reshape(n_clip // 2, width // n_clip, ff)
    out_sum = add(fwd.keep_out, fwd.came_out)
    grad_mlp_in = over_frames(scatter_sum(in_sum, "clip", clip_bits(0)[1:], 1))
    grad_mlp_out = over_frames(scatter_sum(out_sum, "clip", clip_bits(1)[1:], 1))

    def reduce_pair(qkv_term, out_term):
        both = jnp.concatenate((qkv_term, out_term), axis=1)
        shares = both.reshape(n_clip, both.shape[0] // n_clip, both.shape[1])
        cut = both.shape[1] // 2
        first = scatter_sum(shares[:, :, :cut], "clip", clip_bits(0))
        second = scatter_sum(shares[:, :, cut:], "clip", clip_bits(1))
        joined = jnp.concatenate((first, second), axis=1)
        qkv_cols = qkv_term.shape[1]
        tall_rows = joined.shape[0]
        frame_shares = jnp.concatenate(
            (
                joined[:, :qkv_cols].reshape(tall_rows, n_frame, -1),
                joined[:, qkv_cols:].reshape(tall_rows, n_frame, -1),
            ),
            axis=2,
        ).transpose(1, 0, 2)
        done = scatter_sum(frame_shares.astype(BF16), "frame", frame_bits())
        return done[:, : qkv_cols // n_frame], done[:, qkv_cols // n_frame :]

    grad_temporal_qkv, grad_temporal_out = reduce_pair(weight_qkv_b, weight_out_b)
    grad_spatial_qkv, grad_spatial_out = reduce_pair(weight_qkv_a, weight_out_a)

    grad_mod = jnp.concatenate(
        (sums_back[:, :5], fwd.sums[:, 3:4], fwd.sums[:, :3]), axis=1
    ).reshape(clips, 9 * width)
    by_term = dot_nt(thirds(grad_mod), modulate_w).reshape(3, clips, width)
    grad_cond = silu_pull(by_term[0] + by_term[1] + by_term[2])[0]
    grad_cond = lax.psum(grad_cond, "frame")
    grad_cond = lax.all_gather(grad_cond, "clip", axis=0, tiled=True)
    onehot = (timesteps[:, None] == jnp.arange(steps, dtype=jnp.int32)[None, :]).astype(BF16)
    grad_table = dot_tn(jnp.concatenate((onehot,) * 3, axis=0), thirds(grad_cond))
    mod_cols = 9 * width // n_frame
    mod_share = scatter_sum(
        grad_mod.reshape(clips, n_frame, mod_cols).transpose(1, 0, 2), "frame", frame_bits()
    )
    mod_all = lax.all_gather(mod_share, "clip", axis=0, tiled=True)
    mod_rows = width // n_clip
    low_rows = lax.dynamic_slice_in_dim(cond_low, clip_at * mod_rows, mod_rows, axis=1)
    grad_modulate = dot_tn(jnp.concatenate((low_rows,) * 3, axis=0), thirds(mod_all))
    return (
        fwd.output.reshape(tokens.shape),
        grad_tok.reshape(tokens.shape),
        grad_table,
        grad_modulate,
        grad_spatial_qkv,
        grad_spatial_out,
        grad_temporal_qkv,
        grad_temporal_out,
        grad_mlp_in,
        grad_mlp_out,
    )


def solution(mesh):
    placed = (
        P("clip", "frame", None, None), P("clip", "frame", None, None), P("clip"), P(), P("clip"),
    ) + (P(),) * 8
    return jax.shard_map(
        local,
        mesh=mesh,
        in_specs=placed,
        out_specs=(
            P("clip", "frame", None, None), P("clip", "frame", None, None), P(),
        ) + (P("clip", "frame"),) * 7,
        check_vma=False,
    )
```

```python
import functools
import math

import jax
import jax.numpy as jnp
from jax import lax
from jax.experimental import pallas as pl
from jax.experimental.pallas import tpu as pltpu
from jax.sharding import PartitionSpec as P

HEAD_DIM = 64
NORM_EPSILON = 1e-06
F32 = jnp.float32
BF16 = jnp.bfloat16
LANES = 128
SLOT = 16
NO_KEY = -1e30
VMEM_LIMIT = 60 * 2**20
IN_DEPTH = 1
GELU_A = math.sqrt(2.0 / math.pi)
GELU_B = 0.044715


def dot(left, right):
    return lax.dot_general(left, right, (((1,), (0,)), ((), ())), preferred_element_type=F32)


def dot_nt(left, right):
    return lax.dot_general(left, right, (((1,), (1,)), ((), ())), preferred_element_type=F32)


def dot_tn(left, right):
    return lax.dot_general(left, right, (((0,), (0,)), ((), ())), preferred_element_type=F32)


def norm(values):
    centred = values - jnp.mean(values, axis=-1, keepdims=True)
    inv_std = lax.rsqrt(jnp.mean(centred * centred, axis=-1, keepdims=True) + NORM_EPSILON)
    return centred * inv_std, inv_std


def norm_back(grad_hidden, normed, inv_std, scale_plus):
    grad_normed = grad_hidden * scale_plus
    mean_grad = jnp.mean(grad_normed, axis=-1, keepdims=True)
    mean_cross = jnp.mean(grad_normed * normed, axis=-1, keepdims=True)
    return inv_std * (grad_normed - mean_grad - normed * mean_cross)


def column_sum(values):
    return jnp.sum(values, axis=0, keepdims=True)


def side_masks(dtype, value):
    lane = lax.broadcasted_iota(jnp.int32, (1, LANES), 1)
    return [jnp.where((lane < HEAD_DIM) == (side == 0), value, 0.0).astype(dtype) for side in (0, 1)]


class Refs:
    def __init__(self, names, refs):
        self.__dict__.update(zip(names, refs, strict=True))


class Late:
    def __init__(self, source, ref, sem, step):
        self.ref = ref
        self.copy = pltpu.make_async_copy(source, ref, sem)
        self.step = step
        self.waited = False

    def __getitem__(self, index):
        if not self.waited:
            pl.when(pl.program_id(0) == self.step)(self.copy.wait)
            self.waited = True
        return self.ref[index]


def partner(axis, bit):
    me = lax.axis_index(axis)
    return me + (1 << bit) - (2 << bit) * lax.rem(me // (1 << bit), 2)


def remote(source, target, send_sem, recv_sem, **where):
    return pltpu.make_async_remote_copy(
        src_ref=source, dst_ref=target, send_sem=send_sem, recv_sem=recv_sem,
        device_id=where, device_id_type=pl.DeviceIdType.MESH,
    )


def greet(barrier, **where):
    pl.semaphore_signal(barrier, inc=1, device_id=where, device_id_type=pl.DeviceIdType.MESH)


def run_kernel(body, steps, ins, weights, outs, scratch, flops, collective=None):
    anywhere = pl.BlockSpec(memory_space=pl.ANY)
    names = [name for name, *_ in ins] + [name + "_hbm" for name, *_ in weights]
    names += [name for name, *_ in outs]
    names += [name + "_vmem" for name, *_ in weights] + ["weight_sems"]
    names += [name for name, _ in scratch]

    def kernel(*refs):
        r = Refs(names, refs)
        lates = []
        for number, (name, _, step) in enumerate(weights):
            late = Late(
                getattr(r, name + "_hbm"), getattr(r, name + "_vmem"), r.weight_sems.at[number], step
            )
            lates.append(late)
            setattr(r, name, late)

        @pl.when(pl.program_id(0) == 0)
        def _():
            for late in lates:
                if late.step == 0:
                    late.copy.start()

        body(r)

        @pl.when(pl.program_id(0) == 0)
        def _():
            for late in lates:
                if late.step > 0:
                    late.copy.start()

    arrays = [array for _, array, _ in ins] + [array for _, array, _ in weights]
    shapes = [shape for _, shape, _ in outs]
    touched = sum(math.prod(a.shape) * a.dtype.itemsize for a in arrays + shapes)
    params = {} if collective is None else {"collective_id": collective, "has_side_effects": True}
    done = pl.pallas_call(
        kernel,
        grid=(steps,),
        in_specs=[spec for *_, spec in ins] + [anywhere] * len(weights),
        out_specs=[spec or anywhere for *_, spec in outs],
        out_shape=shapes,
        scratch_shapes=[pltpu.VMEM(a.shape, a.dtype) for _, a, _ in weights]
        + [pltpu.SemaphoreType.DMA((max(len(weights), 1),))]
        + [shape for _, shape in scratch],
        compiler_params=pltpu.CompilerParams(vmem_limit_bytes=VMEM_LIMIT, **params),
        cost_estimate=pl.CostEstimate(flops=flops, bytes_accessed=touched, transcendentals=0),
    )(*arrays)
    return Refs([name for name, *_ in outs], done)


def clip_spec(array, first, clips, depth=None):
    rest = array.shape[1:]
    mode = {} if depth is None else {"pipeline_mode": pl.Buffered(depth)}
    return pl.BlockSpec(
        (1,) + rest, lambda s: (jnp.clip(s - first, 0, clips - 1),) + (0,) * len(rest), **mode
    )


def spatial_forward(r, heads, clip):
    width = r.tokens.shape[-1]
    rows = r.tokens.shape[1]
    mod = r.mod
    inputs = r.tokens[0].astype(F32)
    normed, _ = norm(inputs)
    hidden = (normed * (1.0 + mod[0, 1:2]) + mod[0, 0:1]).astype(BF16)
    r.hidden_a[0] = hidden
    for part in range(3):
        cols = slice(part * width, (part + 1) * width)
        r.qkv_a[0, :, cols] = dot(hidden, r.w_qkv_a[:, cols]).astype(BF16)
    masks = side_masks(BF16, HEAD_DIM**-0.5)
    lane = lax.broadcasted_iota(jnp.int32, (1, LANES), 1)
    table = jnp.zeros((rows, LANES), F32)
    for pair in range(heads // 2):
        query, key, value = (
            r.qkv_a[0, :, pl.ds(part * width + pair * LANES, LANES)] for part in range(3)
        )
        out = []
        for side in range(2):
            scores = dot_nt(query * masks[side], key)
            top = jnp.max(scores, axis=-1, keepdims=True)
            grown = jnp.exp(scores - top)
            total = jnp.sum(grown, axis=-1, keepdims=True)
            soft = (grown * (1.0 / total)).astype(BF16)
            out.append(dot(soft, value))
            table = jnp.where(lane == 2 * pair + side, top + jnp.log(total), table)
        cols = slice(pair * LANES, (pair + 1) * LANES)
        r.mixed_a[0, :, cols] = jnp.where(lane < HEAD_DIM, out[0], out[1]).astype(BF16)
    r.lse[0] = table
    branch_a = dot(r.mixed_a[0], r.w_out_a[...])
    r.branch_a[0] = branch_a.astype(BF16)
    after_a = inputs + mod[0, 2:3] * branch_a
    r.after_held[clip] = after_a
    normed_b, _ = norm(after_a)
    r.hidden_held[clip] = (
        normed_b * (1.0 + mod[0, 4:5]) + (mod[0, 3:4] + r.posenc[0])
    ).astype(BF16)


def by_head(left, right, to_heads):
    return dot(left * right, to_heads)


def middle(r, clip, rows_at):
    width = r.target.shape[-1]
    rows = r.target.shape[1]
    ff = r.act.shape[-1]
    scale_qk = HEAD_DIM**-0.5
    mod = r.mod
    own_rows = pl.ds(rows_at, rows)
    store = r.w_qkv_a_vmem

    def kept(number, part):
        return store[number * rows : (number + 1) * rows, part * width : (part + 1) * width]

    for number, (hidden, out) in enumerate(
        ((r.hidden_prev, r.q_prev), (r.hidden_held, r.q_own), (r.hidden_next, r.q_next))
    ):
        for part in range(3):
            cols = slice(part * width, (part + 1) * width)
            value = dot(hidden[clip], r.w_qkv_b[:, cols]).astype(BF16)
            store[number * rows : (number + 1) * rows, cols] = value
            if part == 0:
                out[0] = value
    scores = []
    for number in range(3):
        raw = by_head(kept(1, 0), kept(number, 1), r.to_heads[...]) * scale_qk
        scores.append(raw + r.masks[number : number + 1])
    top = jnp.maximum(jnp.maximum(scores[0], scores[1]), scores[2])
    grown = [jnp.exp(entry - top) for entry in scores]
    inverse = 1.0 / (grown[0] + grown[1] + grown[2])
    soft = [entry * inverse for entry in grown]
    soft_low = [entry.astype(BF16) for entry in soft]
    to_width = r.spread[LANES : 2 * LANES]
    total = None
    for number in range(3):
        term = dot(soft_low[number], to_width) * kept(number, 2).astype(F32)
        total = term if total is None else total + term
    mixed = total.astype(BF16)
    r.mixed_b[0] = mixed
    branch_b = dot(mixed, r.w_out_b[...])
    r.grad_b[0] = branch_b
    after_b = r.after_held[clip] + mod[0, 5:6] * branch_b
    normed_c, inv_c = norm(after_b)
    hidden = (normed_c * (1.0 + mod[0, 7:8]) + mod[0, 6:7]).astype(BF16)
    r.hidden_c[own_rows, :] = hidden
    parts = ff // width
    ahead = dot(hidden, r.w_in[:, :width])
    for part in range(parts):
        cols = slice(part * width, (part + 1) * width)
        upward = ahead
        if part + 1 < parts:
            ahead = dot(hidden, r.w_in[:, (part + 1) * width : (part + 2) * width])
        squared = upward * upward
        bent = jnp.tanh(upward * (GELU_A + (GELU_A * GELU_B) * squared))
        share = 0.5 + 0.5 * bent
        r.act[own_rows, cols] = (upward * share).astype(BF16)
        steep = (1.0 - bent * bent) * (0.5 * GELU_A + (1.5 * GELU_A * GELU_B) * squared)
        r.grad_up[own_rows, cols] = (share + upward * steep).astype(BF16)
    branch_c = dot(r.act[own_rows, :], r.w_mlp[...])
    result = after_b + mod[0, 8:9] * branch_c
    r.output[0] = result.astype(BF16)
    grad_result = r.weight[0, :, :1] * (result - r.target[0].astype(F32))
    r.sums[0, 2:3] = column_sum(grad_result * branch_c)
    low_c = (mod[0, 8:9] * grad_result).astype(BF16)
    r.grad_branch_c[own_rows, :] = low_c
    ahead = dot_nt(low_c, r.w_mlp[:width, :])
    for part in range(parts):
        cols = slice(part * width, (part + 1) * width)
        grad_act = ahead
        if part + 1 < parts:
            ahead = dot_nt(low_c, r.w_mlp[(part + 1) * width : (part + 2) * width, :])
        r.grad_up[own_rows, cols] = (grad_act * r.grad_up[own_rows, cols].astype(F32)).astype(BF16)
    grad_hidden = dot_nt(r.grad_up[own_rows, :], r.w_in[...])
    r.sums[0, 0:1] = column_sum(grad_hidden)
    r.sums[0, 1:2] = column_sum(grad_hidden * normed_c)
    grad_after = grad_result + norm_back(grad_hidden, normed_c, inv_c, 1.0 + mod[0, 7:8])
    r.sums[0, 3:4] = column_sum(grad_after * r.grad_b[0])
    r.grad_b[0] = grad_after
    low_b = (mod[0, 5:6] * grad_after).astype(BF16)
    r.grad_branch_b[0] = low_b
    grad_mixed = dot_nt(low_b, r.w_out_b[...]).astype(BF16)
    grad_soft = [by_head(grad_mixed, kept(number, 2), r.to_heads[...]) for number in range(3)]
    inner = soft[0] * grad_soft[0] + soft[1] * grad_soft[1] + soft[2] * grad_soft[2]
    grad_scores = [(soft[number] * (grad_soft[number] - inner)).astype(BF16) for number in range(3)]
    total = None
    for number in range(3):
        term = dot(grad_scores[number], to_width) * kept(number, 1).astype(F32)
        total = term if total is None else total + term
    r.grad_q[0] = (total * scale_qk).astype(BF16)
    r.sent_held[clip, :, :width] = grad_mixed
    r.sent_held[clip, :, width:] = dot(
        jnp.concatenate(soft_low + grad_scores, axis=1), r.pack[...]
    ).astype(BF16)


def turn(left, n, turned, sorted_rows):
    core = lax.rem(lax.axis_index("clip"), 2)
    turned[...] = left.T
    share = turned.shape[0] // n
    for number in range(n):
        spot = 2 * number + 1 - core if number < n // 2 else 2 * number - n + core
        at = pl.multiple_of(spot * share, share)
        sorted_rows[number * share : (number + 1) * share] = turned[pl.ds(at, share)]


def forward_kernel(heads, clips, n, r):
    step = pl.program_id(0)
    rows, width = r.tokens.shape[1:]
    ff = r.act.shape[-1]
    in_steps = ff // width
    out_steps = n // 2
    share = ff // n
    last = 2 * clips + in_steps + out_steps - 1
    frame = lax.axis_index("frame")
    has_prev = frame > 0
    has_next = frame < lax.axis_size("frame") - 1
    no_prev = jnp.logical_not(has_prev)
    no_next = jnp.logical_not(has_next)
    core = lax.rem(lax.axis_index("clip"), 2)
    sibling = partner("clip", 0)
    barrier = pltpu.get_barrier_semaphore()

    def halo(way, clip):
        return remote(
            r.hidden_held.at[clip], (r.hidden_prev, r.hidden_next)[way].at[clip],
            r.halo_send.at[way, clip], r.halo_recv.at[way, clip],
            frame=frame + 1 if way == 0 else frame - 1,
        )

    def packet(way, clip):
        return remote(
            r.sent_held.at[clip], (r.sent_prev, r.sent_next)[way].at[clip],
            r.sent_send.at[way, clip], r.sent_recv.at[way, clip],
            frame=frame + 1 if way == 0 else frame - 1,
        )

    half = width // 2

    def in_tile(tile):
        return remote(
            r.stage.at[lax.rem(tile, 2), pl.ds(0, half)], r.came_in.at[tile],
            r.tile_send.at[tile], r.tile_recv.at[tile], clip=sibling,
        )

    def in_kept(tile):
        return pltpu.make_async_copy(
            r.stage.at[lax.rem(tile, 2), pl.ds(half, half)], r.keep_in.at[tile],
            r.keep_sems.at[tile],
        )

    def out_part(tile, which):
        return r.stage.at[
            lax.rem(tile + in_steps, 2), pl.ds(pl.multiple_of(which * share, share), share)
        ]

    def out_tile(tile):
        return remote(
            out_part(tile, 1 - core), r.came_out.at[tile],
            r.tile_send.at[tile + in_steps], r.tile_recv.at[tile + in_steps], clip=sibling,
        )

    def out_kept(tile):
        return pltpu.make_async_copy(
            out_part(tile, core), r.keep_out.at[tile], r.keep_sems.at[tile + in_steps]
        )

    def save(clip):
        return [
            pltpu.make_async_copy(r.after_held.at[clip], r.after_a.at[clip], r.save_sems.at[0, clip]),
            pltpu.make_async_copy(
                r.hidden_held.at[clip], r.hidden_b.at[clip], r.save_sems.at[1, clip]
            ),
        ]

    def save_sent(clip):
        return pltpu.make_async_copy(r.sent_held.at[clip], r.sent.at[clip], r.save_sems.at[2, clip])

    def fill(way, clip):
        zeros = (r.hidden_prev, r.hidden_next)[way].at[clip]
        target = (r.sent_prev, r.sent_next)[way].at[clip]
        return [
            pltpu.make_async_copy(zeros, target.at[:, pl.ds(0, width)], r.save_sems.at[3, clip]),
            pltpu.make_async_copy(
                zeros.at[:, pl.ds(0, LANES)], target.at[:, pl.ds(width, LANES)],
                r.save_sems.at[4, clip],
            ),
        ]

    @pl.when(step == 0)
    def _():
        greet(barrier, clip=sibling)
        pl.when(has_prev)(lambda: greet(barrier, frame=frame - 1))
        pl.when(has_next)(lambda: greet(barrier, frame=frame + 1))

        @pl.when(no_prev)
        def _():
            r.hidden_prev[...] = jnp.zeros_like(r.hidden_prev)
            for clip in range(clips):
                for copy in fill(0, clip):
                    copy.start()

        @pl.when(no_next)
        def _():
            r.hidden_next[...] = jnp.zeros_like(r.hidden_next)
            for clip in range(clips):
                for copy in fill(1, clip):
                    copy.start()

    @pl.when(step < clips)
    def _():
        spatial_forward(r, heads, step)

        @pl.when(step == 0)
        def _():
            pl.semaphore_wait(
                barrier, 1 + jnp.where(has_prev, 1, 0) + jnp.where(has_next, 1, 0)
            )

        pl.when(has_next)(lambda: halo(0, step).start())
        pl.when(has_prev)(lambda: halo(1, step).start())
        for copy in save(step):
            copy.start()

    @pl.when((step >= clips) & (step < 2 * clips))
    def _():
        clip = step - clips
        pl.when(has_prev)(lambda: halo(0, clip).wait_recv())
        pl.when(has_next)(lambda: halo(1, clip).wait_recv())
        middle(r, clip, pl.multiple_of(clip * rows, rows))
        pl.when(has_next)(lambda: packet(0, clip).start())
        pl.when(has_prev)(lambda: packet(1, clip).start())
        save_sent(clip).start()

    turned = r.w_qkv_a_vmem.at[:, pl.ds(0, clips * rows)]
    sorted_rows = r.w_qkv_a_vmem.at[:, pl.ds(clips * rows, clips * rows)]

    @pl.when((step >= 2 * clips) & (step < 2 * clips + in_steps))
    def _():
        tile = step - 2 * clips

        @pl.when(tile == 0)
        def _():
            turn(r.hidden_c[...], n, turned, sorted_rows)

        @pl.when(tile >= 2)
        def _():
            in_tile(tile - 2).wait_send()
            in_kept(tile - 2).wait()

        cols = pl.ds(pl.multiple_of(tile * width, width), width)
        r.stage[lax.rem(tile, 2)] = dot(sorted_rows[...], r.grad_up[:, cols]).astype(BF16)
        in_tile(tile).start()
        in_kept(tile).start()

    @pl.when(step >= 2 * clips + in_steps)
    def _():
        tile = step - 2 * clips - in_steps

        @pl.when(tile < 2)
        def _():
            in_tile(in_steps + tile - 2).wait_send()
            in_kept(in_steps + tile - 2).wait()

        @pl.when(tile >= 2)
        def _():
            out_tile(tile - 2).wait_send()
            out_kept(tile - 2).wait()

        cols = pl.ds(pl.multiple_of(tile * 2 * share, 2 * share), 2 * share)
        r.stage[lax.rem(tile + in_steps, 2), : 2 * share] = dot_tn(
            r.act[:, cols], r.grad_branch_c[...]
        ).astype(BF16)
        out_tile(tile).start()
        out_kept(tile).start()

    @pl.when(step == last)
    def _():
        for clip in range(clips):
            for copy in save(clip):
                copy.wait()
            save_sent(clip).wait()

            @pl.when(has_next)
            def _():
                halo(0, clip).wait_send()
                packet(0, clip).wait_send()
                packet(1, clip).wait_recv()

            @pl.when(has_prev)
            def _():
                halo(1, clip).wait_send()
                packet(1, clip).wait_send()
                packet(0, clip).wait_recv()

            for way, absent in ((0, no_prev), (1, no_next)):

                @pl.when(absent)
                def _():
                    for copy in fill(way, clip):
                        copy.wait()

        for tile in range(in_steps):
            in_tile(tile).wait_recv()
        for tile in range(out_steps):
            out_tile(tile).wait_recv()
        for tile in range(out_steps - 2, out_steps):
            out_tile(tile).wait_send()
            out_kept(tile).wait()


def forward_call(tok, target, mod, posenc, weight, masks, tables, weights, n):
    clips, rows, width = tok.shape
    ff = weights["mlp_in"].shape[1]
    heads = width // HEAD_DIM
    tokens_here = clips * rows
    half = width // 2
    in_steps, out_steps, share = ff // width, n // 2, ff // n
    to_heads, spread, pack = tables

    def struct(last, dtype=BF16):
        return jax.ShapeDtypeStruct((clips, rows, last), dtype)

    def early(array):
        return clip_spec(array, 0, clips)

    def late(array):
        return clip_spec(array, clips, clips)

    mod_spec = pl.BlockSpec(
        (1,) + mod.shape[1:],
        lambda s: (jnp.where(s < clips, s, jnp.minimum(s - clips, clips - 1)), 0, 0),
    )
    ins = [
        ("tokens", tok, early(tok)), ("posenc", posenc, early(posenc)), ("mod", mod, mod_spec),
        ("target", target, clip_spec(target, clips, clips, 1)), ("weight", weight, late(weight)),
    ]
    held = [
        ("w_qkv_a", weights["spatial_qkv"], 0), ("w_out_a", weights["spatial_out"], 0),
        ("w_qkv_b", weights["temporal_qkv"], clips), ("to_heads", to_heads, clips),
        ("masks", masks, clips), ("spread", spread, clips), ("w_out_b", weights["temporal_out"], clips),
        ("w_in", weights["mlp_in"], clips), ("w_mlp", weights["mlp_out"], clips), ("pack", pack, clips),
    ]
    outs = []
    for name, shape in (
        ("hidden_a", struct(width)), ("qkv_a", struct(3 * width)), ("mixed_a", struct(width)),
        ("branch_a", struct(width)), ("lse", struct(LANES, F32)),
    ):
        outs.append((name, shape, clip_spec(shape, 0, clips, 1)))
    for name, shape in (
        ("output", struct(width)), ("grad_b", struct(width, F32)), ("mixed_b", struct(width)),
        ("grad_branch_b", struct(width)), ("q_own", struct(width)), ("q_prev", struct(width)),
        ("q_next", struct(width)), ("grad_q", struct(width)),
        ("sums", jax.ShapeDtypeStruct((clips, 8, width), F32)),
    ):
        outs.append((name, shape, clip_spec(shape, clips, clips, 1)))
    outs += [
        ("after_a", struct(width, F32), None), ("hidden_b", struct(width), None),
        ("sent", struct(width + LANES), None), ("sent_prev", struct(width + LANES), None),
        ("sent_next", struct(width + LANES), None),
    ]
    tile_in = jax.ShapeDtypeStruct((in_steps, half, width), BF16)
    tile_out = jax.ShapeDtypeStruct((out_steps, share, width), BF16)
    outs += [
        ("keep_in", tile_in, None), ("came_in", tile_in, None), ("keep_out", tile_out, None),
        ("came_out", tile_out, None),
    ]
    dma = pltpu.SemaphoreType.DMA
    scratch = [
        ("after_held", pltpu.VMEM((clips, rows, width), F32)),
        ("hidden_held", pltpu.VMEM((clips, rows, width), BF16)),
        ("hidden_prev", pltpu.VMEM((clips, rows, width), BF16)),
        ("hidden_next", pltpu.VMEM((clips, rows, width), BF16)),
        ("sent_held", pltpu.VMEM((clips, rows, width + LANES), BF16)),
        ("act", pltpu.VMEM((tokens_here, ff), BF16)),
        ("grad_up", pltpu.VMEM((tokens_here, ff), BF16)),
        ("hidden_c", pltpu.VMEM((tokens_here, width), BF16)),
        ("grad_branch_c", pltpu.VMEM((tokens_here, width), BF16)),
        ("stage", pltpu.VMEM((2, max(width, 2 * share), width), BF16)),
        ("halo_send", dma((2, clips))), ("halo_recv", dma((2, clips))),
        ("sent_send", dma((2, clips))), ("sent_recv", dma((2, clips))),
        ("tile_send", dma((in_steps + out_steps,))), ("tile_recv", dma((in_steps + out_steps,))),
        ("keep_sems", dma((in_steps + out_steps,))), ("save_sems", dma((5, clips))),
    ]
    return run_kernel(
        functools.partial(forward_kernel, heads, clips, n), 2 * clips + in_steps + out_steps,
        ins, held, outs, scratch, 2 * tokens_here * width * width * 46, collective=1,
    )


def temporal_backward(r, clip, rows_at):
    width = r.tokens.shape[-1]
    rows = r.tokens.shape[1]
    scale_qk = HEAD_DIM**-0.5
    own_rows = pl.ds(rows_at, rows)
    grad_key = None
    grad_value = None
    for number, (source, query) in enumerate(
        ((r.sent_prev, r.q_prev), (r.sent, r.q_own), (r.sent_next, r.q_next))
    ):
        other = 2 - number
        table = source[0, :, width:]
        low = LANES - SLOT * other
        soft = dot(table, r.spread[low : low + LANES])
        low = LANES - SLOT * (3 + other)
        score = dot(table, r.spread[low : low + LANES])
        key_term = score * query[0].astype(F32)
        value_term = soft * source[0, :, :width].astype(F32)
        grad_key = key_term if grad_key is None else grad_key + key_term
        grad_value = value_term if grad_value is None else grad_value + value_term
    r.grad_qkv[own_rows, :width] = r.grad_q[0]
    r.grad_qkv[own_rows, width : 2 * width] = (grad_key * scale_qk).astype(BF16)
    r.grad_qkv[own_rows, 2 * width :] = grad_value.astype(BF16)
    grad_hidden = dot_nt(r.grad_qkv[own_rows, :], r.w_qkv_b[...])
    normed_b, inv_b = norm(r.after_a[0])
    r.sums_b[0, 0:1] = column_sum(grad_hidden)
    r.sums_b[0, 1:2] = column_sum(grad_hidden * normed_b)
    r.grad_a[clip] = r.grad_b[0] + norm_back(grad_hidden, normed_b, inv_b, 1.0 + r.mod[0, 4:5])


def spatial_backward(r, heads, clip, rows_at):
    width = r.tokens.shape[-1]
    rows = r.tokens.shape[1]
    scale_qk = HEAD_DIM**-0.5
    own_rows = pl.ds(rows_at, rows)
    mod = r.mod
    r.sums_a[0, 2:3] = column_sum(r.grad_a[clip] * r.branch_a[0].astype(F32))
    low_a = (mod[0, 2:3] * r.grad_a[clip]).astype(BF16)
    r.grad_branch[own_rows, :] = low_a
    grad_mixed = dot_nt(low_a, r.w_out_a[...]).astype(BF16)
    masks = side_masks(BF16, 1.0)
    lane = lax.broadcasted_iota(jnp.int32, (1, LANES), 1)
    scale_low = jnp.asarray(scale_qk, BF16)
    for pair in range(heads // 2):
        query, key, value = (
            r.qkv_a[0, :, pl.ds(part * width + pair * LANES, LANES)] for part in range(3)
        )
        gm = grad_mixed[:, pair * LANES : (pair + 1) * LANES]
        parts = []
        for side in range(2):
            head = 2 * pair + side
            scores = dot_nt(query * (masks[side] * scale_low), key)
            soft = jnp.exp(scores - r.lse[0, :, head : head + 1])
            grad_soft = dot_nt(gm * masks[side], value)
            inner = jnp.sum(soft * grad_soft, axis=-1, keepdims=True)
            grad_scores = (soft * (grad_soft - inner)).astype(BF16)
            parts.append(
                (dot(grad_scores, key), dot_tn(grad_scores, query), dot_tn(soft.astype(BF16), gm))
            )
        for number, factor in ((0, scale_qk), (1, scale_qk), (2, 1.0)):
            both = jnp.where(lane < HEAD_DIM, parts[0][number], parts[1][number])
            start = number * width + pair * LANES
            r.grad_qkv[own_rows, start : start + LANES] = (both * factor).astype(BF16)
    grad_hidden = dot_nt(r.grad_qkv[own_rows, :], r.w_qkv_a[...])
    normed_a, inv_a = norm(r.tokens[0].astype(F32))
    r.sums_a[0, 0:1] = column_sum(grad_hidden)
    r.sums_a[0, 1:2] = column_sum(grad_hidden * normed_a)
    r.grad_tokens[0] = r.grad_a[clip] + norm_back(
        grad_hidden, normed_a, inv_a, 1.0 + mod[0, 1:2]
    )


class Halving:
    def __init__(self, sums, landings, sends, recvs, bits):
        self.sums, self.landings, self.sends, self.recvs = sums, landings, sends, recvs
        self.bits = bits

    def share(self, stage, number, keep):
        me = lax.axis_index("clip")
        later = sorted(self.bits[stage + 1 :])
        spot = sum(((number >> i) & 1) << (bit - 1) for i, bit in enumerate(later))
        for bit in self.bits[: stage + 1]:
            mine = lax.rem(me // (1 << bit), 2)
            if bit == self.bits[stage] and not keep:
                mine = 1 - mine
            spot = spot + mine * (1 << (bit - 1))
        return spot

    def count(self, stage):
        return 1 << (len(self.bits) - 1 - stage)

    def copy(self, stage, number):
        at = sum(self.count(i) for i in range(stage)) + number
        return remote(
            self.sums.at[:, self.share(stage, number, False)],
            self.landings.at[:, at], self.sends.at[at], self.recvs.at[at],
            clip=partner("clip", self.bits[stage]),
        )

    def send(self, stage):
        for number in range(self.count(stage)):
            self.copy(stage, number).start()

    def fold(self, stage):
        for number in range(self.count(stage)):
            self.copy(stage, number).wait_recv()
            at = sum(self.count(i) for i in range(stage)) + number
            spot = self.share(stage, number, True)
            self.sums[:, spot] = (
                self.sums[:, spot].astype(F32) + self.landings[:, at].astype(F32)
            ).astype(BF16)

    def own(self):
        return self.sums[:, self.share(len(self.bits) - 1, 0, True)]

    def drain(self):
        for stage in range(len(self.bits)):
            for number in range(self.count(stage)):
                self.copy(stage, number).wait_send()


class Frames:
    def __init__(self, away, landing, sends, recvs, out):
        self.away, self.landing, self.sends, self.recvs, self.out = away, landing, sends, recvs, out

    def copy(self, distance):
        count = self.away.shape[0]
        frame = lax.rem(lax.axis_index("frame") + distance, count)
        return remote(
            self.away.at[frame], self.landing.at[distance - 1],
            self.sends.at[distance - 1], self.recvs.at[distance - 1], frame=frame,
        )

    def send(self, rows):
        count, _, cols = self.away.shape
        for frame in range(count):
            self.away[frame] = rows[:, frame * cols : (frame + 1) * cols]
        for distance in range(1, count):
            self.copy(distance).start()

    def finish(self):
        total = self.away[lax.axis_index("frame")].astype(F32)
        for distance in range(1, self.away.shape[0]):
            self.copy(distance).wait_recv()
            total = total + self.landing[distance - 1].astype(F32)
        self.out[...] = total

    def drain(self):
        for distance in range(1, self.away.shape[0]):
            self.copy(distance).wait_send()


def side_by_side(tiles):
    return jnp.concatenate([tiles[i] for i in range(tiles.shape[0])], axis=1)


def backward_kernel(heads, clips, n, n_frame, r):
    step = pl.program_id(0)
    rows, width = r.tokens.shape[1:]
    tiles = 4
    half = n // 2
    share = width // n
    first_t = clips
    first_s = clips + tiles
    first_w = 2 * clips + tiles
    last = first_w + tiles - 1
    sibling = partner("clip", 0)
    barrier = pltpu.get_barrier_semaphore()
    bits = list(range(1, n.bit_length() - 1))
    frame = lax.axis_index("frame")

    feed_in = Halving(r.sum_in, r.land_in, r.in_send, r.in_recv, bits)
    feed_out = Halving(r.sum_out, r.land_out, r.out_send, r.out_recv, bits[::-1])

    def pair(name):
        sums, land = getattr(r, "sum_" + name), getattr(r, "land_" + name)
        sends, recvs = getattr(r, name + "_send"), getattr(r, name + "_recv")
        return [
            Halving(
                sums.at[pl.ds(2 * i, 2)], land.at[pl.ds(2 * i, 2)], sends.at[i], recvs.at[i],
                bits[:: 1 - 2 * i],
            )
            for i in range(2)
        ]

    temporal, spatial = pair("t"), pair("s")
    stages = len(bits)

    def tile_copy(name, tile):
        return remote(
            r.stage.at[lax.rem(tile, 2)], getattr(r, "core_" + name).at[tile],
            getattr(r, name + "_core_send").at[tile], getattr(r, name + "_core_recv").at[tile],
            clip=sibling,
        )

    def fold_core(name, which):
        sums, core = getattr(r, "sum_" + name), getattr(r, "core_" + name)
        for tile in which:
            tile_copy(name, tile).wait_recv()
            sums[tile] = (sums[tile].astype(F32) + core[tile].astype(F32)).astype(BF16)

    frames = {
        name: Frames(
            getattr(r, "away_" + name), getattr(r, "near_" + name),
            getattr(r, name + "_z_send"), getattr(r, name + "_z_recv"), getattr(r, "done_" + name),
        )
        for name in ("in", "out", "tq", "to", "sq", "so")
    }

    def to_frames(units, wide, narrow):
        left = units[0].own()
        right = units[1].own()
        frames[wide].send(jnp.concatenate((side_by_side(left), right[0]), axis=1))
        frames[narrow].send(right[1])

    loads = [
        pltpu.make_async_copy(r.keep_in, r.sum_in, r.load_sems.at[0]),
        pltpu.make_async_copy(r.came_in, r.core_t, r.load_sems.at[1]),
        pltpu.make_async_copy(r.keep_out, r.sum_out, r.load_sems.at[2]),
        pltpu.make_async_copy(r.came_out, r.core_s, r.load_sems.at[3]),
    ]
    lefts_t = [
        pltpu.make_async_copy(r.hidden_b, r.left, r.load_sems.at[4]),
        pltpu.make_async_copy(r.mixed_b, r.left_out, r.load_sems.at[5]),
        pltpu.make_async_copy(r.grad_branch_b, r.grad_branch, r.load_sems.at[6]),
    ]
    lefts_s = [
        pltpu.make_async_copy(r.hidden_a, r.left, r.load_sems.at[7]),
        pltpu.make_async_copy(r.mixed_a, r.left_out, r.load_sems.at[8]),
    ]
    load_w = pltpu.make_async_copy(r.w_qkv_a_hbm, r.w_qkv_a, r.load_sems.at[9])

    @pl.when(step == 0)
    def _():
        for bit in range(n.bit_length() - 1):
            greet(barrier, clip=partner("clip", bit))
        for distance in range(1, n_frame):
            greet(barrier, frame=lax.rem(frame + distance, n_frame))
        for copy in loads + lefts_t:
            copy.start()

    @pl.when(step < clips)
    def _():
        temporal_backward(r, step, pl.multiple_of(step * rows, rows))

    @pl.when(step == 0)
    def _():
        for copy in loads:
            copy.wait()
        for tile in range(tiles):
            r.sum_in[tile] = (
                r.sum_in[tile].astype(F32) + r.core_t[tile].astype(F32)
            ).astype(BF16)
        per = r.sum_out.shape[1] // tiles
        for tile in range(tiles):
            which = slice(tile * per, (tile + 1) * per)
            came = r.core_s[tile].reshape(r.sum_out[0, which].shape)
            r.sum_out[0, which] = (
                r.sum_out[0, which].astype(F32) + came.astype(F32)
            ).astype(BF16)
        pl.semaphore_wait(barrier, n.bit_length() - 1 + n_frame - 1)
        pl.semaphore_signal(
            r.free, inc=1, device_id={"clip": sibling}, device_id_type=pl.DeviceIdType.MESH
        )
        feed_in.send(0)
        feed_out.send(0)

    def weight_tile(name, tile, turned, sorted_rows):
        @pl.when(tile == 0)
        def _():
            turn(r.left[...], n, turned, sorted_rows)

        @pl.when(tile == tiles - 1)
        def _():
            turn(r.left_out[...], n, turned, sorted_rows)

        def put(right):
            total = dot(sorted_rows[...], right).astype(BF16)
            r.stage[lax.rem(tile, 2)] = total[: half * share].reshape(half, share, width)
            getattr(r, "sum_" + name)[tile] = total[half * share :].reshape(half, share, width)

        @pl.when(tile < tiles - 1)
        def _():
            put(r.grad_qkv[:, pl.ds(pl.multiple_of(tile * width, width), width)])

        @pl.when(tile == tiles - 1)
        def _():
            put(r.grad_branch[...])

        tile_copy(name, tile).start()

    tokens_here = clips * rows

    @pl.when((step >= first_t) & (step < first_s))
    def _():
        tile = step - first_t

        @pl.when(tile == 0)
        def _():
            for copy in lefts_t:
                copy.wait()
            pl.semaphore_wait(r.free, 1)

        pl.when(tile >= 2)(lambda: tile_copy("t", tile - 2).wait_send())
        weight_tile(
            "t", tile, r.w_qkv_a.at[:, pl.ds(0, tokens_here)],
            r.w_qkv_a.at[:, pl.ds(tokens_here, tokens_here)],
        )

        @pl.when(tile == tiles - 1)
        def _():
            load_w.start()
            for copy in lefts_s:
                copy.start()

    @pl.when((step >= first_s) & (step < first_w))
    def _():
        clip = step - first_s

        pl.when(clip == 0)(load_w.wait)
        spatial_backward(r, heads, clip, pl.multiple_of(clip * rows, rows))

    @pl.when(step == first_s)
    def _():
        feed_in.fold(0)
        feed_out.fold(0)
        if stages > 1:
            feed_in.send(1)
            feed_out.send(1)
        fold_core("t", range(tiles))
        for unit in temporal:
            unit.send(0)

    @pl.when(step == first_w - 2)
    def _():
        for stage in range(1, stages):
            for unit in (feed_in, feed_out):
                unit.fold(stage)
                if stage + 1 < stages:
                    unit.send(stage + 1)
        frames["in"].send(side_by_side(feed_in.own()))
        frames["out"].send(feed_out.own()[0])

    @pl.when(step == first_w - 1)
    def _():
        for unit in temporal:
            unit.fold(0)
            if stages > 1:
                unit.send(1)

    @pl.when(step >= first_w)
    def _():
        tile = step - first_w

        @pl.when(tile == 0)
        def _():
            for copy in lefts_s:
                copy.wait()

        @pl.when(tile < 2)
        def _():
            tile_copy("t", tiles + tile - 2).wait_send()

        pl.when(tile >= 2)(lambda: tile_copy("s", tile - 2).wait_send())
        weight_tile(
            "s", tile, r.w_qkv_b_vmem.at[:, pl.ds(0, tokens_here)],
            r.w_qkv_b_vmem.at[:, pl.ds(tokens_here, tokens_here)],
        )

    @pl.when(step == last - 1)
    def _():
        fold_core("s", (0, 1))
        spatial[0].send(0)

    @pl.when(step == last)
    def _():
        fold_core("s", (2, 3))
        spatial[1].send(0)
        for stage in range(1, stages):
            for unit in temporal:
                unit.fold(stage)
                if stage + 1 < stages:
                    unit.send(stage + 1)
        to_frames(temporal, "tq", "to")
        for name in ("in", "out"):
            frames[name].finish()
        for stage in range(stages):
            for unit in spatial:
                unit.fold(stage)
                if stage + 1 < stages:
                    unit.send(stage + 1)
        to_frames(spatial, "sq", "so")
        for name in ("tq", "to", "sq", "so"):
            frames[name].finish()
        for unit in (feed_in, feed_out, *temporal, *spatial):
            unit.drain()
        for name in frames:
            frames[name].drain()
        for tile in range(tiles - 2, tiles):
            tile_copy("s", tile).wait_send()


def backward_call(fwd, tok, mod, spread, weights, n, n_frame):
    clips, rows, width = tok.shape
    ff = weights["mlp_in"].shape[1]
    heads = width // HEAD_DIM
    tokens_here = clips * rows
    tiles = 4
    half, share, tall = n // 2, width // n, ff // n
    first_s, first_w = clips + tiles, 2 * clips + tiles

    def struct(last, dtype=BF16):
        return jax.ShapeDtypeStruct((clips, rows, last), dtype)

    mod_spec = pl.BlockSpec(
        (1,) + mod.shape[1:],
        lambda s: (
            jnp.where(s < first_s, jnp.minimum(s, clips - 1), jnp.minimum(s - first_s, clips - 1)),
            0, 0,
        ),
    )
    anywhere = pl.BlockSpec(memory_space=pl.ANY)
    ins = [("mod", mod, mod_spec)]
    for name in ("q_prev", "q_own", "q_next", "sent_prev", "sent", "sent_next", "grad_q", "grad_b", "after_a"):
        array = getattr(fwd, name)
        ins.append((name, array, clip_spec(array, 0, clips, IN_DEPTH)))
    for name, array in (
        ("tokens", tok), ("branch_a", fwd.branch_a), ("qkv_a", fwd.qkv_a), ("lse", fwd.lse)
    ):
        ins.append((name, array, clip_spec(array, first_s, clips, IN_DEPTH)))
    flat = (tokens_here, width)
    for name in ("hidden_b", "mixed_b", "grad_branch_b", "hidden_a", "mixed_a"):
        ins.append((name, getattr(fwd, name).reshape(flat), anywhere))
    core_shape = (tiles, half, share, width)
    ins += [
        ("keep_in", fwd.keep_in.reshape(core_shape), anywhere),
        ("came_in", fwd.came_in.reshape(core_shape), anywhere),
        ("keep_out", fwd.keep_out.reshape(1, half, tall, width), anywhere),
        ("came_out", fwd.came_out.reshape(core_shape), anywhere),
        ("w_qkv_a_hbm", weights["spatial_qkv"], anywhere),
    ]
    held = [
        ("spread", spread, 0), ("w_qkv_b", weights["temporal_qkv"], 0),
        ("w_out_a", weights["spatial_out"], first_s),
    ]
    sums = jax.ShapeDtypeStruct((clips, 8, width), F32)
    grad_tokens = struct(width, F32)
    outs = [
        ("grad_tokens", grad_tokens, clip_spec(grad_tokens, first_s, clips, 1)),
        ("sums_b", sums, clip_spec(sums, 0, clips)), ("sums_a", sums, clip_spec(sums, first_s, clips)),
    ]
    dma = pltpu.SemaphoreType.DMA
    pieces = {
        "in": (share, ff // n_frame), "out": (tall, width // n_frame),
        "tq": (share, 3 * width // n_frame), "to": (share, width // n_frame),
        "sq": (share, 3 * width // n_frame), "so": (share, width // n_frame),
    }
    moved = half - 1
    scratch = [
        ("grad_a", pltpu.VMEM((clips, rows, width), F32)),
        ("grad_qkv", pltpu.VMEM((tokens_here, 3 * width), BF16)),
        ("grad_branch", pltpu.VMEM(flat, BF16)), ("left", pltpu.VMEM(flat, BF16)),
        ("left_out", pltpu.VMEM(flat, BF16)),
        ("w_qkv_a", pltpu.VMEM(weights["spatial_qkv"].shape, BF16)),
        ("stage", pltpu.VMEM((2, half, share, width), BF16)),
        ("sum_in", pltpu.VMEM(core_shape, BF16)), ("land_in", pltpu.VMEM((tiles, moved, share, width), BF16)),
        ("in_send", dma((moved,))), ("in_recv", dma((moved,))),
        ("sum_out", pltpu.VMEM((1, half, tall, width), BF16)),
        ("land_out", pltpu.VMEM((1, moved, tall, width), BF16)),
        ("out_send", dma((moved,))), ("out_recv", dma((moved,))),
        ("load_sems", dma((10,))), ("free", pltpu.SemaphoreType.REGULAR),
    ]
    for name in ("t", "s"):
        scratch += [
            ("sum_" + name, pltpu.VMEM(core_shape, BF16)), ("core_" + name, pltpu.VMEM(core_shape, BF16)),
            ("land_" + name, pltpu.VMEM((tiles, moved, share, width), BF16)),
            (name + "_send", dma((2, moved))), (name + "_recv", dma((2, moved))),
            (name + "_core_send", dma((tiles,))), (name + "_core_recv", dma((tiles,))),
        ]
    for name, (height, cols) in pieces.items():
        shape = jax.ShapeDtypeStruct((height, cols), F32)
        outs.append(("done_" + name, shape, pl.BlockSpec(shape.shape, lambda s: (0, 0))))
        scratch += [
            ("away_" + name, pltpu.VMEM((n_frame, height, cols), BF16)),
            ("near_" + name, pltpu.VMEM((n_frame - 1, height, cols), BF16)),
            (name + "_z_send", dma((n_frame - 1,))), (name + "_z_recv", dma((n_frame - 1,))),
        ]
    return run_kernel(
        functools.partial(backward_kernel, heads, clips, n, n_frame), first_w + tiles,
        ins, held, outs, scratch, 2 * tokens_here * width * width * 20, collective=2,
    )


def swap(array, axis, bit):
    return lax.ppermute(array, axis, [(i, i ^ (1 << bit)) for i in range(lax.axis_size(axis))])


def scatter_frames(parts):
    count = lax.axis_size("frame")
    me = lax.axis_index("frame")
    left = list(range(count.bit_length() - 1))[::-1]
    shape = parts.shape[1:]
    held = parts.reshape((2,) * len(left) + shape)
    for bit in reversed(list(left)):
        dim = left.index(bit)
        left.remove(bit)
        mine = (me >> bit) & 1
        away = lax.dynamic_index_in_dim(held, 1 - mine, dim, keepdims=False)
        keep = lax.dynamic_index_in_dim(held, mine, dim, keepdims=False)
        held = keep + swap(away, "frame", bit)
    return held.reshape(shape)


def sum_frames(values):
    for bit in range(lax.axis_size("frame").bit_length() - 1):
        values = values + swap(values, "frame", bit)
    return values


def gather_clips(values):
    me = lax.axis_index("clip")
    for bit in range(lax.axis_size("clip").bit_length() - 1):
        other = swap(values, "clip", bit)
        mine = (me >> bit) & 1
        values = jnp.concatenate(
            (jnp.where(mine == 1, other, values), jnp.where(mine == 1, values, other)), axis=0
        )
    return values


def thirds(values):
    high = values.astype(BF16)
    rest = values - high.astype(F32)
    mid = rest.astype(BF16)
    low = (rest - mid.astype(F32)).astype(BF16)
    return jnp.concatenate((high, mid, low), axis=0)


def local(
    tokens, target, loss_weight, timesteps, offsets, cond_table, modulate_w,
    spatial_qkv, spatial_out, temporal_qkv, temporal_out, mlp_in, mlp_out,
):
    clips, frames, patches, width = tokens.shape
    steps = cond_table.shape[0]
    heads = width // HEAD_DIM
    n_clip = lax.axis_size("clip")
    n_frame = lax.axis_size("frame")
    clip_at = lax.axis_index("clip")
    frame_at = lax.axis_index("frame")
    flat = (clips, patches, width)
    tok = tokens.reshape(flat)
    tgt = target.reshape(flat)

    condition = jnp.take(cond_table, timesteps, axis=0, mode="clip")
    cond_low = jax.nn.silu(condition).astype(BF16)
    cond_here = lax.dynamic_slice_in_dim(condition, clip_at * clips, clips)
    _, silu_pull = jax.vjp(jax.nn.silu, cond_here)
    low_here = lax.dynamic_slice_in_dim(cond_low, clip_at * clips, clips)
    mod = jnp.dot(low_here, modulate_w, preferred_element_type=F32).reshape(clips, 9, width)

    half = width // 2
    positions = (offsets + frame_at).astype(F32)
    freqs = jnp.exp(jnp.arange(half, dtype=F32) * (-math.log(10000.0) / half))
    angles = positions[:, None] * freqs
    posenc = jnp.concatenate((jnp.sin(angles), jnp.cos(angles)), axis=-1)[:, None, :]

    head_of = jnp.arange(width, dtype=jnp.int32) // HEAD_DIM
    lane_ids = jnp.arange(LANES, dtype=jnp.int32)
    to_heads = (head_of[:, None] == lane_ids[None, :]).astype(BF16)
    tall = jnp.arange(2 * LANES, dtype=jnp.int32) - LANES
    spread = (tall[:, None] == head_of[None, :]).astype(BF16)
    group, inside = jnp.divmod(jnp.arange(6 * LANES, dtype=jnp.int32), LANES)
    slot_at = jnp.where(inside < heads, group * SLOT + inside, -1)
    pack = (slot_at[:, None] == lane_ids[None, :]).astype(BF16)
    side_ok = jnp.stack((frame_at > 0, frame_at >= 0, frame_at < n_frame - 1))
    masks = jnp.where(side_ok[:, None], 0.0, NO_KEY) * jnp.ones((1, LANES), F32)
    masks = jnp.pad(masks, ((0, 5), (0, 0)))
    weight = jnp.broadcast_to(loss_weight[:, None, None], (clips, 1, LANES))

    weights = {
        "spatial_qkv": spatial_qkv, "spatial_out": spatial_out, "temporal_qkv": temporal_qkv,
        "temporal_out": temporal_out, "mlp_in": mlp_in, "mlp_out": mlp_out,
    }
    fwd = forward_call(
        tok, tgt, mod, posenc, weight, masks, (to_heads, spread, pack), weights, n_clip
    )

    bwd = backward_call(fwd, tok, mod, spread, weights, n_clip, n_frame)

    grad_mod = jnp.concatenate(
        (bwd.sums_a[:, :3], bwd.sums_b[:, :2], fwd.sums[:, 3:4], fwd.sums[:, :3]), axis=1
    ).reshape(clips, 9 * width)
    by_term = dot_nt(thirds(grad_mod), modulate_w).reshape(3, clips, width)
    grad_cond = sum_frames(silu_pull(by_term[0] + by_term[1] + by_term[2])[0])
    mod_cols = 9 * width // n_frame
    mod_share = scatter_frames(grad_mod.reshape(clips, n_frame, mod_cols).transpose(1, 0, 2))
    gathered = gather_clips(jnp.concatenate((grad_cond, mod_share), axis=1))
    onehot = (timesteps[:, None] == jnp.arange(steps, dtype=jnp.int32)[None, :]).astype(BF16)
    grad_table = dot_tn(jnp.concatenate((onehot,) * 3, axis=0), thirds(gathered[:, :width]))
    mod_rows = width // n_clip
    low_rows = lax.dynamic_slice_in_dim(cond_low, clip_at * mod_rows, mod_rows, axis=1)
    grad_modulate = dot_tn(jnp.concatenate((low_rows,) * 3, axis=0), thirds(gathered[:, width:]))
    return (
        fwd.output.reshape(tokens.shape),
        bwd.grad_tokens.reshape(tokens.shape),
        grad_table,
        grad_modulate,
        bwd.done_sq,
        bwd.done_so,
        bwd.done_tq,
        bwd.done_to,
        bwd.done_in,
        bwd.done_out,
    )


def solution(mesh):
    placed = (
        P("clip", "frame", None, None), P("clip", "frame", None, None), P("clip"), P(), P("clip"),
    ) + (P(),) * 8
    return jax.shard_map(
        local,
        mesh=mesh,
        in_specs=placed,
        out_specs=(
            P("clip", "frame", None, None), P("clip", "frame", None, None), P(),
        ) + (P("clip", "frame"),) * 7,
        check_vma=False,
    )
```

```python
import functools
import math

import jax
import jax.numpy as jnp
from jax import lax
from jax.experimental import pallas as pl
from jax.experimental.pallas import tpu as pltpu
from jax.sharding import PartitionSpec as P

HEAD_DIM = 64
NORM_EPSILON = 1e-06
F32 = jnp.float32
BF16 = jnp.bfloat16
LANES = 128
SLOT = 16
NO_KEY = -1e30
VMEM_LIMIT = 60 * 2**20
GROUP = 2
GELU_A = math.sqrt(2.0 / math.pi)
GELU_B = 0.044715


def dot(left, right):
    return lax.dot_general(left, right, (((1,), (0,)), ((), ())), preferred_element_type=F32)


def dot_nt(left, right):
    return lax.dot_general(left, right, (((1,), (1,)), ((), ())), preferred_element_type=F32)


def dot_tn(left, right):
    return lax.dot_general(left, right, (((0,), (0,)), ((), ())), preferred_element_type=F32)


def norm(values):
    centred = values - jnp.mean(values, axis=-1, keepdims=True)
    inv_std = lax.rsqrt(jnp.mean(centred * centred, axis=-1, keepdims=True) + NORM_EPSILON)
    return centred * inv_std, inv_std


def norm_back(grad_hidden, normed, inv_std, scale_plus):
    grad_normed = grad_hidden * scale_plus
    mean_grad = jnp.mean(grad_normed, axis=-1, keepdims=True)
    mean_cross = jnp.mean(grad_normed * normed, axis=-1, keepdims=True)
    return inv_std * (grad_normed - mean_grad - normed * mean_cross)


def column_sum(values):
    return jnp.sum(values, axis=0, keepdims=True)


def side_masks(dtype, value):
    lane = lax.broadcasted_iota(jnp.int32, (1, LANES), 1)
    return [jnp.where((lane < HEAD_DIM) == (side == 0), value, 0.0).astype(dtype) for side in (0, 1)]


class Refs:
    def __init__(self, names, refs):
        self.__dict__.update(zip(names, refs, strict=True))


class Late:
    def __init__(self, source, ref, sem, step):
        self.ref = ref
        self.copy = pltpu.make_async_copy(source, ref, sem)
        self.step = step
        self.waited = False

    def __getitem__(self, index):
        if not self.waited:
            pl.when(pl.program_id(0) == self.step)(self.copy.wait)
            self.waited = True
        return self.ref[index]


def partner(axis, bit):
    me = lax.axis_index(axis)
    return me + (1 << bit) - (2 << bit) * lax.rem(me // (1 << bit), 2)


def remote(source, target, send_sem, recv_sem, **where):
    return pltpu.make_async_remote_copy(
        src_ref=source, dst_ref=target, send_sem=send_sem, recv_sem=recv_sem,
        device_id=where, device_id_type=pl.DeviceIdType.MESH,
    )


def greet(barrier, **where):
    pl.semaphore_signal(barrier, inc=1, device_id=where, device_id_type=pl.DeviceIdType.MESH)


def run_kernel(body, steps, ins, weights, outs, scratch, flops, collective=None):
    anywhere = pl.BlockSpec(memory_space=pl.ANY)
    names = [name for name, *_ in ins] + [name + "_hbm" for name, *_ in weights]
    names += [name for name, *_ in outs]
    names += [name + "_vmem" for name, *_ in weights] + ["weight_sems"]
    names += [name for name, _ in scratch]

    def kernel(*refs):
        r = Refs(names, refs)
        lates = []
        for number, (name, _, step) in enumerate(weights):
            late = Late(
                getattr(r, name + "_hbm"), getattr(r, name + "_vmem"), r.weight_sems.at[number], step
            )
            lates.append(late)
            setattr(r, name, late)

        @pl.when(pl.program_id(0) == 0)
        def _():
            for late in lates:
                if late.step == 0:
                    late.copy.start()

        body(r)

        @pl.when(pl.program_id(0) == 0)
        def _():
            for late in lates:
                if late.step > 0:
                    late.copy.start()

    arrays = [array for _, array, _ in ins] + [array for _, array, _ in weights]
    shapes = [shape for _, shape, _ in outs]
    touched = sum(math.prod(a.shape) * a.dtype.itemsize for a in arrays + shapes)
    params = {} if collective is None else {"collective_id": collective, "has_side_effects": True}
    done = pl.pallas_call(
        kernel,
        grid=(steps,),
        in_specs=[spec for *_, spec in ins] + [anywhere] * len(weights),
        out_specs=[spec or anywhere for *_, spec in outs],
        out_shape=shapes,
        scratch_shapes=[pltpu.VMEM(a.shape, a.dtype) for _, a, _ in weights]
        + [pltpu.SemaphoreType.DMA((max(len(weights), 1),))]
        + [shape for _, shape in scratch],
        compiler_params=pltpu.CompilerParams(vmem_limit_bytes=VMEM_LIMIT, **params),
        cost_estimate=pl.CostEstimate(flops=flops, bytes_accessed=touched, transcendentals=0),
    )(*arrays)
    return Refs([name for name, *_ in outs], done)


def clip_spec(array, first, clips, depth=None):
    rest = array.shape[1:]
    mode = {} if depth is None else {"pipeline_mode": pl.Buffered(depth)}
    return pl.BlockSpec(
        (1,) + rest, lambda s: (jnp.clip(s - first, 0, clips - 1),) + (0,) * len(rest), **mode
    )


def spatial_forward(r, heads, clip):
    width = r.tokens.shape[-1]
    rows = r.tokens.shape[1]
    mod = r.mod
    inputs = r.tokens[0].astype(F32)
    normed, _ = norm(inputs)
    hidden = (normed * (1.0 + mod[0, 1:2]) + mod[0, 0:1]).astype(BF16)
    r.hidden_a[0] = hidden
    for part in range(3):
        cols = slice(part * width, (part + 1) * width)
        r.qkv_a[0, :, cols] = dot(hidden, r.w_qkv_a[:, cols]).astype(BF16)
    scaled, plain = side_masks(BF16, HEAD_DIM**-0.5), side_masks(BF16, 1.0)
    for first in range(0, heads // 2, GROUP):
        pairs = range(first, min(first + GROUP, heads // 2))
        scores, softs = [], []
        for pair in pairs:
            query, key = (columns(r.qkv_a, part, pair) for part in (0, 1))
            scores.append(dot_nt(both_sides(key, scaled), query))
        for pair, score in zip(pairs, scores):
            halves = []
            for side in range(2):
                mine = score[side * rows : (side + 1) * rows]
                top = jnp.max(mine, axis=0, keepdims=True)
                grown = jnp.exp(mine - top)
                total = jnp.sum(grown, axis=0, keepdims=True)
                halves.append((grown * (1.0 / total)).astype(BF16))
                head = 2 * pair + side
                r.lse[0, head : head + 1] = top + jnp.log(total)
            softs.append(jnp.concatenate(halves, axis=0))
        for pair, soft in zip(pairs, softs):
            value = columns(r.qkv_a, 2, pair)
            r.mixed_a[0, :, pair * LANES : (pair + 1) * LANES] = dot_tn(
                soft, both_sides(value, plain)
            ).astype(BF16)
    branch_a = dot(r.mixed_a[0], r.w_out_a[...])
    r.branch_a[0] = branch_a.astype(BF16)
    after_a = inputs + mod[0, 2:3] * branch_a
    r.after_held[clip] = after_a
    normed_b, _ = norm(after_a)
    r.hidden_held[clip] = (
        normed_b * (1.0 + mod[0, 4:5]) + (mod[0, 3:4] + r.posenc[0])
    ).astype(BF16)


def both_sides(array, masks):
    return jnp.concatenate((array * masks[0], array * masks[1]), axis=0)


def columns(ref, part, pair):
    start = part * (ref.shape[-1] // 3) + pair * LANES
    return ref[0, :, start : start + LANES]


def by_head(left, right, to_heads):
    return dot(left * right, to_heads)


def middle(r, clip, rows_at):
    width = r.target.shape[-1]
    rows = r.target.shape[1]
    ff = r.act.shape[-1]
    scale_qk = HEAD_DIM**-0.5
    mod = r.mod
    own_rows = pl.ds(rows_at, rows)
    store = r.w_qkv_a_vmem

    def kept(number, part):
        return store[number * rows : (number + 1) * rows, part * width : (part + 1) * width]

    for number, (hidden, out) in enumerate(
        ((r.hidden_prev, r.q_prev), (r.hidden_held, r.q_own), (r.hidden_next, r.q_next))
    ):
        for part in range(3):
            cols = slice(part * width, (part + 1) * width)
            value = dot(hidden[clip], r.w_qkv_b[:, cols]).astype(BF16)
            store[number * rows : (number + 1) * rows, cols] = value
            if part == 0:
                out[0] = value
    scores = []
    for number in range(3):
        raw = by_head(kept(1, 0), kept(number, 1), r.to_heads[...]) * scale_qk
        scores.append(raw + r.masks[number : number + 1])
    top = jnp.maximum(jnp.maximum(scores[0], scores[1]), scores[2])
    grown = [jnp.exp(entry - top) for entry in scores]
    inverse = 1.0 / (grown[0] + grown[1] + grown[2])
    soft = [entry * inverse for entry in grown]
    soft_low = [entry.astype(BF16) for entry in soft]
    to_width = r.spread[LANES : 2 * LANES]
    total = None
    for number in range(3):
        term = dot(soft_low[number], to_width) * kept(number, 2).astype(F32)
        total = term if total is None else total + term
    mixed = total.astype(BF16)
    r.mixed_b[0] = mixed
    branch_b = dot(mixed, r.w_out_b[...])
    r.grad_b[0] = branch_b
    after_b = r.after_held[clip] + mod[0, 5:6] * branch_b
    normed_c, inv_c = norm(after_b)
    hidden = (normed_c * (1.0 + mod[0, 7:8]) + mod[0, 6:7]).astype(BF16)
    r.hidden_c[own_rows, :] = hidden
    parts = ff // width
    ahead = dot(hidden, r.w_in[:, :width])
    for part in range(parts):
        cols = slice(part * width, (part + 1) * width)
        upward = ahead
        if part + 1 < parts:
            ahead = dot(hidden, r.w_in[:, (part + 1) * width : (part + 2) * width])
        squared = upward * upward
        bent = jnp.tanh(upward * (GELU_A + (GELU_A * GELU_B) * squared))
        share = 0.5 + 0.5 * bent
        r.act[own_rows, cols] = (upward * share).astype(BF16)
        steep = (1.0 - bent * bent) * (0.5 * GELU_A + (1.5 * GELU_A * GELU_B) * squared)
        r.grad_up[own_rows, cols] = (share + upward * steep).astype(BF16)
    branch_c = dot(r.act[own_rows, :], r.w_mlp[...])
    result = after_b + mod[0, 8:9] * branch_c
    r.output[0] = result.astype(BF16)
    grad_result = r.weight[0, :, :1] * (result - r.target[0].astype(F32))
    r.sums[0, 2:3] = column_sum(grad_result * branch_c)
    low_c = (mod[0, 8:9] * grad_result).astype(BF16)
    r.grad_branch_c[own_rows, :] = low_c
    ahead = dot_nt(low_c, r.w_mlp[:width, :])
    for part in range(parts):
        cols = slice(part * width, (part + 1) * width)
        grad_act = ahead
        if part + 1 < parts:
            ahead = dot_nt(low_c, r.w_mlp[(part + 1) * width : (part + 2) * width, :])
        r.grad_up[own_rows, cols] = (grad_act * r.grad_up[own_rows, cols].astype(F32)).astype(BF16)
    grad_hidden = dot_nt(r.grad_up[own_rows, :], r.w_in[...])
    r.sums[0, 0:1] = column_sum(grad_hidden)
    r.sums[0, 1:2] = column_sum(grad_hidden * normed_c)
    grad_after = grad_result + norm_back(grad_hidden, normed_c, inv_c, 1.0 + mod[0, 7:8])
    r.sums[0, 3:4] = column_sum(grad_after * r.grad_b[0])
    r.grad_b[0] = grad_after
    low_b = (mod[0, 5:6] * grad_after).astype(BF16)
    r.grad_branch_b[0] = low_b
    grad_mixed = dot_nt(low_b, r.w_out_b[...]).astype(BF16)
    grad_soft = [by_head(grad_mixed, kept(number, 2), r.to_heads[...]) for number in range(3)]
    inner = soft[0] * grad_soft[0] + soft[1] * grad_soft[1] + soft[2] * grad_soft[2]
    grad_scores = [(soft[number] * (grad_soft[number] - inner)).astype(BF16) for number in range(3)]
    total = None
    for number in range(3):
        term = dot(grad_scores[number], to_width) * kept(number, 1).astype(F32)
        total = term if total is None else total + term
    r.grad_q[0] = (total * scale_qk).astype(BF16)
    r.sent_held[clip, :, :width] = grad_mixed
    r.sent_held[clip, :, width:] = dot(
        jnp.concatenate(soft_low + grad_scores, axis=1), r.pack[...]
    ).astype(BF16)


def share_rows(number, keep, share):
    core = lax.rem(lax.axis_index("clip"), 2)
    spot = 2 * number + (core if keep else 1 - core)
    return pl.ds(pl.multiple_of(spot * share, share), share)


def forward_kernel(heads, clips, n, r):
    step = pl.program_id(0)
    rows, width = r.tokens.shape[1:]
    ff = r.act.shape[-1]
    in_steps = ff // width
    out_steps = n // 2
    share = ff // n
    last = 2 * clips + in_steps + out_steps - 1
    frame = lax.axis_index("frame")
    has_prev = frame > 0
    has_next = frame < lax.axis_size("frame") - 1
    no_prev = jnp.logical_not(has_prev)
    no_next = jnp.logical_not(has_next)
    core = lax.rem(lax.axis_index("clip"), 2)
    sibling = partner("clip", 0)
    barrier = pltpu.get_barrier_semaphore()

    def halo(way, clip):
        return remote(
            r.hidden_held.at[clip], (r.hidden_prev, r.hidden_next)[way].at[clip],
            r.halo_send.at[way, clip], r.halo_recv.at[way, clip],
            frame=frame + 1 if way == 0 else frame - 1,
        )

    def packet(way, clip):
        return remote(
            r.sent_held.at[clip], (r.sent_prev, r.sent_next)[way].at[clip],
            r.sent_send.at[way, clip], r.sent_recv.at[way, clip],
            frame=frame + 1 if way == 0 else frame - 1,
        )

    low_share = width // n

    def in_tile(tile):
        return [
            remote(
                r.stage.at[lax.rem(tile, 2), share_rows(number, False, low_share)],
                r.came_in.at[tile, number],
                r.in_send.at[tile, number], r.in_recv.at[tile, number], clip=sibling,
            )
            for number in range(n // 2)
        ]

    def in_kept(tile):
        return [
            pltpu.make_async_copy(
                r.stage.at[lax.rem(tile, 2), share_rows(number, True, low_share)],
                r.keep_in.at[tile, number], r.in_keep.at[tile, number],
            )
            for number in range(n // 2)
        ]

    def in_sent(tile):
        for copy in in_tile(tile):
            copy.wait_send()
        for copy in in_kept(tile):
            copy.wait()

    def out_part(tile, which):
        return r.stage.at[
            lax.rem(tile + in_steps, 2), pl.ds(pl.multiple_of(which * share, share), share)
        ]

    def out_tile(tile):
        return remote(
            out_part(tile, 1 - core), r.came_out.at[tile],
            r.out_send.at[tile], r.out_recv.at[tile], clip=sibling,
        )

    def out_kept(tile):
        return pltpu.make_async_copy(
            out_part(tile, core), r.keep_out.at[tile], r.out_keep.at[tile]
        )

    def save(clip):
        return [
            pltpu.make_async_copy(r.after_held.at[clip], r.after_a.at[clip], r.save_sems.at[0, clip]),
            pltpu.make_async_copy(
                r.hidden_held.at[clip], r.hidden_b.at[clip], r.save_sems.at[1, clip]
            ),
        ]

    def save_sent(clip):
        return pltpu.make_async_copy(r.sent_held.at[clip], r.sent.at[clip], r.save_sems.at[2, clip])

    def fill(way, clip):
        zeros = (r.hidden_prev, r.hidden_next)[way].at[clip]
        target = (r.sent_prev, r.sent_next)[way].at[clip]
        return [
            pltpu.make_async_copy(zeros, target.at[:, pl.ds(0, width)], r.save_sems.at[3, clip]),
            pltpu.make_async_copy(
                zeros.at[:, pl.ds(0, LANES)], target.at[:, pl.ds(width, LANES)],
                r.save_sems.at[4, clip],
            ),
        ]

    @pl.when(step == 0)
    def _():
        greet(barrier, clip=sibling)
        pl.when(has_prev)(lambda: greet(barrier, frame=frame - 1))
        pl.when(has_next)(lambda: greet(barrier, frame=frame + 1))

        @pl.when(no_prev)
        def _():
            r.hidden_prev[...] = jnp.zeros_like(r.hidden_prev)
            for clip in range(clips):
                for copy in fill(0, clip):
                    copy.start()

        @pl.when(no_next)
        def _():
            r.hidden_next[...] = jnp.zeros_like(r.hidden_next)
            for clip in range(clips):
                for copy in fill(1, clip):
                    copy.start()

    @pl.when(step < clips)
    def _():
        spatial_forward(r, heads, step)

        @pl.when(step == 0)
        def _():
            pl.semaphore_wait(
                barrier, 1 + jnp.where(has_prev, 1, 0) + jnp.where(has_next, 1, 0)
            )

        pl.when(has_next)(lambda: halo(0, step).start())
        pl.when(has_prev)(lambda: halo(1, step).start())
        for copy in save(step):
            copy.start()

    @pl.when((step >= clips) & (step < 2 * clips))
    def _():
        clip = step - clips
        pl.when(has_prev)(lambda: halo(0, clip).wait_recv())
        pl.when(has_next)(lambda: halo(1, clip).wait_recv())
        middle(r, clip, pl.multiple_of(clip * rows, rows))
        pl.when(has_next)(lambda: packet(0, clip).start())
        pl.when(has_prev)(lambda: packet(1, clip).start())
        save_sent(clip).start()

    @pl.when((step >= 2 * clips) & (step < 2 * clips + in_steps))
    def _():
        tile = step - 2 * clips

        pl.when(tile >= 2)(lambda: in_sent(tile - 2))
        cols = pl.ds(pl.multiple_of(tile * width, width), width)
        r.stage[lax.rem(tile, 2), :width] = dot_tn(r.hidden_c[...], r.grad_up[:, cols]).astype(BF16)
        for copy in in_tile(tile) + in_kept(tile):
            copy.start()

    @pl.when(step >= 2 * clips + in_steps)
    def _():
        tile = step - 2 * clips - in_steps

        pl.when(tile < 2)(lambda: in_sent(in_steps + tile - 2))

        @pl.when(tile >= 2)
        def _():
            out_tile(tile - 2).wait_send()
            out_kept(tile - 2).wait()

        cols = pl.ds(pl.multiple_of(tile * 2 * share, 2 * share), 2 * share)
        r.stage[lax.rem(tile + in_steps, 2), : 2 * share] = dot_tn(
            r.act[:, cols], r.grad_branch_c[...]
        ).astype(BF16)
        out_tile(tile).start()
        out_kept(tile).start()

    @pl.when(step == last)
    def _():
        for clip in range(clips):
            for copy in save(clip):
                copy.wait()
            save_sent(clip).wait()

            @pl.when(has_next)
            def _():
                halo(0, clip).wait_send()
                packet(0, clip).wait_send()
                packet(1, clip).wait_recv()

            @pl.when(has_prev)
            def _():
                halo(1, clip).wait_send()
                packet(1, clip).wait_send()
                packet(0, clip).wait_recv()

            for way, absent in ((0, no_prev), (1, no_next)):

                @pl.when(absent)
                def _():
                    for copy in fill(way, clip):
                        copy.wait()

        for tile in range(in_steps):
            for copy in in_tile(tile):
                copy.wait_recv()
        for tile in range(out_steps):
            out_tile(tile).wait_recv()
        for tile in range(out_steps - 2, out_steps):
            out_tile(tile).wait_send()
            out_kept(tile).wait()


def forward_call(tok, target, mod, posenc, weight, masks, tables, weights, n):
    clips, rows, width = tok.shape
    ff = weights["mlp_in"].shape[1]
    heads = width // HEAD_DIM
    tokens_here = clips * rows
    in_steps, out_steps, share = ff // width, n // 2, ff // n
    to_heads, spread, pack = tables

    def struct(last, dtype=BF16):
        return jax.ShapeDtypeStruct((clips, rows, last), dtype)

    def early(array):
        return clip_spec(array, 0, clips)

    def late(array):
        return clip_spec(array, clips, clips)

    mod_spec = pl.BlockSpec(
        (1,) + mod.shape[1:],
        lambda s: (jnp.where(s < clips, s, jnp.minimum(s - clips, clips - 1)), 0, 0),
    )
    ins = [
        ("tokens", tok, early(tok)), ("posenc", posenc, early(posenc)), ("mod", mod, mod_spec),
        ("target", target, clip_spec(target, clips, clips, 1)), ("weight", weight, late(weight)),
    ]
    held = [
        ("w_qkv_a", weights["spatial_qkv"], 0), ("w_out_a", weights["spatial_out"], 0),
        ("w_qkv_b", weights["temporal_qkv"], clips), ("to_heads", to_heads, clips),
        ("masks", masks, clips), ("spread", spread, clips), ("w_out_b", weights["temporal_out"], clips),
        ("w_in", weights["mlp_in"], clips), ("w_mlp", weights["mlp_out"], clips), ("pack", pack, clips),
    ]
    outs = []
    for name, shape in (
        ("hidden_a", struct(width)), ("qkv_a", struct(3 * width)), ("mixed_a", struct(width)),
        ("branch_a", struct(width)),
        ("lse", jax.ShapeDtypeStruct((clips, -(-heads // 8) * 8, rows), F32)),
    ):
        outs.append((name, shape, clip_spec(shape, 0, clips, 1)))
    for name, shape in (
        ("output", struct(width)), ("grad_b", struct(width, F32)), ("mixed_b", struct(width)),
        ("grad_branch_b", struct(width)), ("q_own", struct(width)), ("q_prev", struct(width)),
        ("q_next", struct(width)), ("grad_q", struct(width)),
        ("sums", jax.ShapeDtypeStruct((clips, 8, width), F32)),
    ):
        outs.append((name, shape, clip_spec(shape, clips, clips, 1)))
    outs += [
        ("after_a", struct(width, F32), None), ("hidden_b", struct(width), None),
        ("sent", struct(width + LANES), None), ("sent_prev", struct(width + LANES), None),
        ("sent_next", struct(width + LANES), None),
    ]
    tile_in = jax.ShapeDtypeStruct((in_steps, n // 2, width // n, width), BF16)
    tile_out = jax.ShapeDtypeStruct((out_steps, share, width), BF16)
    outs += [
        ("keep_in", tile_in, None), ("came_in", tile_in, None), ("keep_out", tile_out, None),
        ("came_out", tile_out, None),
    ]
    dma = pltpu.SemaphoreType.DMA
    scratch = [
        ("after_held", pltpu.VMEM((clips, rows, width), F32)),
        ("hidden_held", pltpu.VMEM((clips, rows, width), BF16)),
        ("hidden_prev", pltpu.VMEM((clips, rows, width), BF16)),
        ("hidden_next", pltpu.VMEM((clips, rows, width), BF16)),
        ("sent_held", pltpu.VMEM((clips, rows, width + LANES), BF16)),
        ("act", pltpu.VMEM((tokens_here, ff), BF16)),
        ("grad_up", pltpu.VMEM((tokens_here, ff), BF16)),
        ("hidden_c", pltpu.VMEM((tokens_here, width), BF16)),
        ("grad_branch_c", pltpu.VMEM((tokens_here, width), BF16)),
        ("stage", pltpu.VMEM((2, max(width, 2 * share), width), BF16)),
        ("halo_send", dma((2, clips))), ("halo_recv", dma((2, clips))),
        ("sent_send", dma((2, clips))), ("sent_recv", dma((2, clips))),
        ("in_send", dma((in_steps, n // 2))), ("in_recv", dma((in_steps, n // 2))),
        ("in_keep", dma((in_steps, n // 2))), ("out_send", dma((out_steps,))),
        ("out_recv", dma((out_steps,))), ("out_keep", dma((out_steps,))),
        ("save_sems", dma((5, clips))),
    ]
    return run_kernel(
        functools.partial(forward_kernel, heads, clips, n), 2 * clips + in_steps + out_steps,
        ins, held, outs, scratch, 2 * tokens_here * width * width * 46, collective=1,
    )


def temporal_backward(r, clip, rows_at):
    width = r.tokens.shape[-1]
    rows = r.tokens.shape[1]
    scale_qk = HEAD_DIM**-0.5
    own_rows = pl.ds(rows_at, rows)
    grad_key = None
    grad_value = None
    for number, (source, query) in enumerate(
        ((r.sent_prev, r.q_prev), (r.sent, r.q_own), (r.sent_next, r.q_next))
    ):
        other = 2 - number
        table = source[0, :, width:]
        low = LANES - SLOT * other
        soft = dot(table, r.spread[low : low + LANES])
        low = LANES - SLOT * (3 + other)
        score = dot(table, r.spread[low : low + LANES])
        key_term = score * query[0].astype(F32)
        value_term = soft * source[0, :, :width].astype(F32)
        grad_key = key_term if grad_key is None else grad_key + key_term
        grad_value = value_term if grad_value is None else grad_value + value_term
    r.grad_qkv[own_rows, :width] = r.grad_q[0]
    r.grad_qkv[own_rows, width : 2 * width] = (grad_key * scale_qk).astype(BF16)
    r.grad_qkv[own_rows, 2 * width :] = grad_value.astype(BF16)
    grad_hidden = dot_nt(r.grad_qkv[own_rows, :], r.w_qkv_b[...])
    normed_b, inv_b = norm(r.after_a[0])
    r.sums_b[0, 0:1] = column_sum(grad_hidden)
    r.sums_b[0, 1:2] = column_sum(grad_hidden * normed_b)
    r.grad_a[clip] = r.grad_b[0] + norm_back(grad_hidden, normed_b, inv_b, 1.0 + r.mod[0, 4:5])


def spatial_backward(r, heads, clip, rows_at):
    width = r.tokens.shape[-1]
    rows = r.tokens.shape[1]
    scale_qk = HEAD_DIM**-0.5
    own_rows = pl.ds(rows_at, rows)
    mod = r.mod
    r.sums_a[0, 2:3] = column_sum(r.grad_a[clip] * r.branch_a[0].astype(F32))
    low_a = (mod[0, 2:3] * r.grad_a[clip]).astype(BF16)
    r.grad_branch[own_rows, :] = low_a
    grad_mixed = dot_nt(low_a, r.w_out_a[...]).astype(BF16)
    scaled, plain = side_masks(BF16, scale_qk), side_masks(BF16, 1.0)
    lane = lax.broadcasted_iota(jnp.int32, (1, LANES), 1)
    for first in range(0, heads // 2, GROUP):
        pairs = range(first, min(first + GROUP, heads // 2))
        scores, grads, softs, backs = [], [], [], []
        for pair in pairs:
            gm = grad_mixed[:, pair * LANES : (pair + 1) * LANES]
            scores.append(
                dot_nt(both_sides(columns(r.qkv_a, 1, pair), scaled), columns(r.qkv_a, 0, pair))
            )
            grads.append(dot_nt(both_sides(columns(r.qkv_a, 2, pair), plain), gm))
        for pair, score, grad in zip(pairs, scores, grads):
            low, back = [], []
            for side in range(2):
                mine = slice(side * rows, (side + 1) * rows)
                head = 2 * pair + side
                soft = jnp.exp(score[mine] - r.lse[0, head : head + 1])
                inner = jnp.sum(soft * grad[mine], axis=0, keepdims=True)
                back.append((soft * (grad[mine] - inner)).astype(BF16))
                low.append(soft.astype(BF16))
            softs.append(jnp.concatenate(low, axis=0))
            backs.append(jnp.concatenate(back, axis=0))
        for pair, soft, back in zip(pairs, softs, backs):
            gm = grad_mixed[:, pair * LANES : (pair + 1) * LANES]
            query, key = (columns(r.qkv_a, part, pair) for part in (0, 1))
            start = pair * LANES
            r.grad_qkv[own_rows, start : start + LANES] = dot_tn(
                back, both_sides(key, scaled)
            ).astype(BF16)
            for part, total, factor in ((1, dot(back, query), scale_qk), (2, dot(soft, gm), 1.0)):
                joined = jnp.where(lane < HEAD_DIM, total[:rows], total[rows:])
                start = part * width + pair * LANES
                r.grad_qkv[own_rows, start : start + LANES] = (joined * factor).astype(BF16)
    grad_hidden = dot_nt(r.grad_qkv[own_rows, :], r.w_qkv_a[...])
    normed_a, inv_a = norm(r.tokens[0].astype(F32))
    r.sums_a[0, 0:1] = column_sum(grad_hidden)
    r.sums_a[0, 1:2] = column_sum(grad_hidden * normed_a)
    r.grad_tokens[0] = r.grad_a[clip] + norm_back(
        grad_hidden, normed_a, inv_a, 1.0 + mod[0, 1:2]
    )


class Halving:
    def __init__(self, sums, landings, sends, recvs, bits):
        self.sums, self.landings, self.sends, self.recvs = sums, landings, sends, recvs
        self.bits = bits

    def share(self, stage, number, keep):
        me = lax.axis_index("clip")
        later = sorted(self.bits[stage + 1 :])
        spot = sum(((number >> i) & 1) << (bit - 1) for i, bit in enumerate(later))
        for bit in self.bits[: stage + 1]:
            mine = lax.rem(me // (1 << bit), 2)
            if bit == self.bits[stage] and not keep:
                mine = 1 - mine
            spot = spot + mine * (1 << (bit - 1))
        return spot

    def count(self, stage):
        return 1 << (len(self.bits) - 1 - stage)

    def copy(self, stage, number):
        at = sum(self.count(i) for i in range(stage)) + number
        return remote(
            self.sums.at[:, self.share(stage, number, False)],
            self.landings.at[:, at], self.sends.at[at], self.recvs.at[at],
            clip=partner("clip", self.bits[stage]),
        )

    def send(self, stage):
        for number in range(self.count(stage)):
            self.copy(stage, number).start()

    def fold(self, stage):
        for number in range(self.count(stage)):
            self.copy(stage, number).wait_recv()
            at = sum(self.count(i) for i in range(stage)) + number
            spot = self.share(stage, number, True)
            self.sums[:, spot] = (
                self.sums[:, spot].astype(F32) + self.landings[:, at].astype(F32)
            ).astype(BF16)

    def own(self):
        return self.sums[:, self.share(len(self.bits) - 1, 0, True)]

    def drain(self):
        for stage in range(len(self.bits)):
            for number in range(self.count(stage)):
                self.copy(stage, number).wait_send()


class Frames:
    def __init__(self, away, landing, sends, recvs, out):
        self.away, self.landing, self.sends, self.recvs, self.out = away, landing, sends, recvs, out

    def copy(self, distance):
        count = self.away.shape[0]
        frame = lax.rem(lax.axis_index("frame") + distance, count)
        return remote(
            self.away.at[frame], self.landing.at[distance - 1],
            self.sends.at[distance - 1], self.recvs.at[distance - 1], frame=frame,
        )

    def send(self, rows):
        count, _, cols = self.away.shape
        for frame in range(count):
            self.away[frame] = rows[:, frame * cols : (frame + 1) * cols]
        for distance in range(1, count):
            self.copy(distance).start()

    def finish(self):
        total = self.away[lax.axis_index("frame")].astype(F32)
        for distance in range(1, self.away.shape[0]):
            self.copy(distance).wait_recv()
            total = total + self.landing[distance - 1].astype(F32)
        self.out[...] = total

    def drain(self):
        for distance in range(1, self.away.shape[0]):
            self.copy(distance).wait_send()


def side_by_side(tiles):
    return jnp.concatenate([tiles[i] for i in range(tiles.shape[0])], axis=1)


def backward_kernel(heads, clips, n, n_frame, r):
    step = pl.program_id(0)
    rows, width = r.tokens.shape[1:]
    tiles = 4
    half = n // 2
    share = width // n
    first_t = clips
    first_s = clips + tiles
    first_w = 2 * clips + tiles
    last = first_w + tiles - 1
    sibling = partner("clip", 0)
    barrier = pltpu.get_barrier_semaphore()
    bits = list(range(1, n.bit_length() - 1))
    frame = lax.axis_index("frame")

    feed_in = Halving(r.sum_in, r.land_in, r.in_send, r.in_recv, bits)
    feed_out = Halving(r.sum_out, r.land_out, r.out_send, r.out_recv, bits[::-1])

    def pair(name):
        sums, land = getattr(r, "sum_" + name), getattr(r, "land_" + name)
        sends, recvs = getattr(r, name + "_send"), getattr(r, name + "_recv")
        return [
            Halving(
                sums.at[pl.ds(2 * i, 2)], land.at[pl.ds(2 * i, 2)], sends.at[i], recvs.at[i],
                bits[:: 1 - 2 * i],
            )
            for i in range(2)
        ]

    temporal, spatial = pair("t"), pair("s")
    stages = len(bits)

    regions = {"t": r.w_qkv_a_vmem, "s": r.w_qkv_b_vmem}

    def tile_cols(tile):
        return pl.ds(pl.multiple_of(lax.rem(tile, 3) * width, width), width)

    def tile_copies(name, tile):
        sends, recvs = getattr(r, name + "_core_send"), getattr(r, name + "_core_recv")
        return [
            remote(
                regions[name].at[share_rows(number, False, share), tile_cols(tile)],
                getattr(r, "core_" + name).at[tile, number],
                sends.at[tile, number], recvs.at[tile, number], clip=sibling,
            )
            for number in range(half)
        ]

    def tile_sent(name, tile):
        for copy in tile_copies(name, tile):
            copy.wait_send()

    def fold_core(name, which):
        sums, core = getattr(r, "sum_" + name), getattr(r, "core_" + name)
        for tile in which:
            for copy in tile_copies(name, tile):
                copy.wait_recv()
            sums[tile] = (sums[tile].astype(F32) + core[tile].astype(F32)).astype(BF16)

    frames = {
        name: Frames(
            getattr(r, "away_" + name), getattr(r, "near_" + name),
            getattr(r, name + "_z_send"), getattr(r, name + "_z_recv"), getattr(r, "done_" + name),
        )
        for name in ("in", "out", "tq", "to", "sq", "so")
    }

    def to_frames(units, wide, narrow):
        left = units[0].own()
        right = units[1].own()
        frames[wide].send(jnp.concatenate((side_by_side(left), right[0]), axis=1))
        frames[narrow].send(right[1])

    loads = [
        pltpu.make_async_copy(r.keep_in, r.sum_in, r.load_sems.at[0]),
        pltpu.make_async_copy(r.came_in, r.core_t, r.load_sems.at[1]),
        pltpu.make_async_copy(r.keep_out, r.sum_out, r.load_sems.at[2]),
        pltpu.make_async_copy(r.came_out, r.core_s, r.load_sems.at[3]),
    ]
    lefts_t = [
        pltpu.make_async_copy(r.hidden_b, r.left, r.load_sems.at[4]),
        pltpu.make_async_copy(r.mixed_b, r.left_out, r.load_sems.at[5]),
        pltpu.make_async_copy(r.grad_branch_b, r.grad_branch, r.load_sems.at[6]),
    ]
    lefts_s = [
        pltpu.make_async_copy(r.hidden_a, r.left, r.load_sems.at[7]),
        pltpu.make_async_copy(r.mixed_a, r.left_out, r.load_sems.at[8]),
    ]
    r.w_qkv_a = Late(r.w_qkv_a_hbm, r.w_qkv_a_vmem, r.load_sems.at[9], first_s)

    @pl.when(step == 0)
    def _():
        for bit in range(n.bit_length() - 1):
            greet(barrier, clip=partner("clip", bit))
        for distance in range(1, n_frame):
            greet(barrier, frame=lax.rem(frame + distance, n_frame))
        for copy in loads + lefts_t:
            copy.start()

    @pl.when(step < clips)
    def _():
        temporal_backward(r, step, pl.multiple_of(step * rows, rows))

    @pl.when(step == 0)
    def _():
        for copy in loads:
            copy.wait()
        for tile in range(tiles):
            r.sum_in[tile] = (
                r.sum_in[tile].astype(F32) + r.core_t[tile].astype(F32)
            ).astype(BF16)
        per = r.sum_out.shape[1] // tiles
        for tile in range(tiles):
            which = slice(tile * per, (tile + 1) * per)
            came = r.core_s[tile].reshape(r.sum_out[0, which].shape)
            r.sum_out[0, which] = (
                r.sum_out[0, which].astype(F32) + came.astype(F32)
            ).astype(BF16)
        pl.semaphore_wait(barrier, n.bit_length() - 1 + n_frame - 1)
        pl.semaphore_signal(
            r.free, inc=1, device_id={"clip": sibling}, device_id_type=pl.DeviceIdType.MESH
        )
        feed_in.send(0)
        feed_out.send(0)

    def weight_tile(name, tile):
        region = regions[name]

        @pl.when(tile < tiles - 1)
        def _():
            cols = pl.ds(pl.multiple_of(tile * width, width), width)
            region[:, tile_cols(tile)] = dot_tn(r.left[...], r.grad_qkv[:, cols]).astype(BF16)

        @pl.when(tile == tiles - 1)
        def _():
            region[:, tile_cols(tile)] = dot_tn(r.left_out[...], r.grad_branch[...]).astype(BF16)

        for copy in tile_copies(name, tile):
            copy.start()
        for number in range(half):
            getattr(r, "sum_" + name)[tile, number] = region[
                share_rows(number, True, share), tile_cols(tile)
            ]

    @pl.when((step >= first_t) & (step < first_s))
    def _():
        tile = step - first_t

        @pl.when(tile == 0)
        def _():
            for copy in lefts_t:
                copy.wait()
            pl.semaphore_wait(r.free, 1)

        pl.when(tile == 3)(lambda: tile_sent("t", 0))
        weight_tile("t", tile)

        @pl.when(tile == tiles - 1)
        def _():
            for copy in lefts_s:
                copy.start()

    @pl.when((step >= first_s) & (step < first_w))
    def _():
        clip = step - first_s

        @pl.when(clip == 0)
        def _():
            for tile in range(1, tiles):
                tile_sent("t", tile)
            r.w_qkv_a.copy.start()

        spatial_backward(r, heads, clip, pl.multiple_of(clip * rows, rows))

    @pl.when(step == first_s)
    def _():
        feed_in.fold(0)
        feed_out.fold(0)
        if stages > 1:
            feed_in.send(1)
            feed_out.send(1)
        fold_core("t", range(tiles))
        for unit in temporal:
            unit.send(0)

    @pl.when(step == first_w - 2)
    def _():
        for stage in range(1, stages):
            for unit in (feed_in, feed_out):
                unit.fold(stage)
                if stage + 1 < stages:
                    unit.send(stage + 1)
        frames["in"].send(side_by_side(feed_in.own()))
        frames["out"].send(feed_out.own()[0])

    @pl.when(step == first_w - 1)
    def _():
        for unit in temporal:
            unit.fold(0)
            if stages > 1:
                unit.send(1)

    @pl.when(step >= first_w)
    def _():
        tile = step - first_w

        @pl.when(tile == 0)
        def _():
            for copy in lefts_s:
                copy.wait()

        pl.when(tile == 3)(lambda: tile_sent("s", 0))
        weight_tile("s", tile)

    @pl.when(step == last - 1)
    def _():
        fold_core("s", (0, 1))
        spatial[0].send(0)

    @pl.when(step == last)
    def _():
        fold_core("s", (2, 3))
        spatial[1].send(0)
        for stage in range(1, stages):
            for unit in temporal:
                unit.fold(stage)
                if stage + 1 < stages:
                    unit.send(stage + 1)
        to_frames(temporal, "tq", "to")
        for name in ("in", "out"):
            frames[name].finish()
        for stage in range(stages):
            for unit in spatial:
                unit.fold(stage)
                if stage + 1 < stages:
                    unit.send(stage + 1)
        to_frames(spatial, "sq", "so")
        for name in ("tq", "to", "sq", "so"):
            frames[name].finish()
        for unit in (feed_in, feed_out, *temporal, *spatial):
            unit.drain()
        for name in frames:
            frames[name].drain()
        for tile in range(1, tiles):
            tile_sent("s", tile)


def backward_call(fwd, tok, mod, spread, weights, n, n_frame):
    clips, rows, width = tok.shape
    ff = weights["mlp_in"].shape[1]
    heads = width // HEAD_DIM
    tokens_here = clips * rows
    tiles = 4
    half, share, tall = n // 2, width // n, ff // n
    first_s, first_w = clips + tiles, 2 * clips + tiles

    def struct(last, dtype=BF16):
        return jax.ShapeDtypeStruct((clips, rows, last), dtype)

    mod_spec = pl.BlockSpec(
        (1,) + mod.shape[1:],
        lambda s: (
            jnp.where(s < first_s, jnp.minimum(s, clips - 1), jnp.minimum(s - first_s, clips - 1)),
            0, 0,
        ),
    )
    anywhere = pl.BlockSpec(memory_space=pl.ANY)
    ins = [("mod", mod, mod_spec)]
    for name in ("q_prev", "q_own", "q_next", "sent_prev", "sent", "sent_next", "grad_q", "grad_b", "after_a"):
        array = getattr(fwd, name)
        ins.append((name, array, clip_spec(array, 0, clips, 1 if array.dtype == F32 else 2)))
    for name, array in (
        ("tokens", tok), ("branch_a", fwd.branch_a), ("qkv_a", fwd.qkv_a), ("lse", fwd.lse)
    ):
        ins.append((name, array, clip_spec(array, first_s, clips, 1)))
    flat = (tokens_here, width)
    for name in ("hidden_b", "mixed_b", "grad_branch_b", "hidden_a", "mixed_a"):
        ins.append((name, getattr(fwd, name).reshape(flat), anywhere))
    core_shape = (tiles, half, share, width)
    ins += [
        ("keep_in", fwd.keep_in.reshape(core_shape), anywhere),
        ("came_in", fwd.came_in.reshape(core_shape), anywhere),
        ("keep_out", fwd.keep_out.reshape(1, half, tall, width), anywhere),
        ("came_out", fwd.came_out.reshape(core_shape), anywhere),
        ("w_qkv_a_hbm", weights["spatial_qkv"], anywhere),
    ]
    held = [
        ("spread", spread, 0), ("w_qkv_b", weights["temporal_qkv"], 0),
        ("w_out_a", weights["spatial_out"], first_s),
    ]
    sums = jax.ShapeDtypeStruct((clips, 8, width), F32)
    grad_tokens = struct(width, F32)
    outs = [
        ("grad_tokens", grad_tokens, clip_spec(grad_tokens, first_s, clips, 1)),
        ("sums_b", sums, clip_spec(sums, 0, clips)), ("sums_a", sums, clip_spec(sums, first_s, clips)),
    ]
    dma = pltpu.SemaphoreType.DMA
    pieces = {
        "in": (share, ff // n_frame), "out": (tall, width // n_frame),
        "tq": (share, 3 * width // n_frame), "to": (share, width // n_frame),
        "sq": (share, 3 * width // n_frame), "so": (share, width // n_frame),
    }
    moved = half - 1
    scratch = [
        ("grad_a", pltpu.VMEM((clips, rows, width), F32)),
        ("grad_qkv", pltpu.VMEM((tokens_here, 3 * width), BF16)),
        ("grad_branch", pltpu.VMEM(flat, BF16)), ("left", pltpu.VMEM(flat, BF16)),
        ("left_out", pltpu.VMEM(flat, BF16)),
        ("w_qkv_a_vmem", pltpu.VMEM(weights["spatial_qkv"].shape, BF16)),
        ("sum_in", pltpu.VMEM(core_shape, BF16)), ("land_in", pltpu.VMEM((tiles, moved, share, width), BF16)),
        ("in_send", dma((moved,))), ("in_recv", dma((moved,))),
        ("sum_out", pltpu.VMEM((1, half, tall, width), BF16)),
        ("land_out", pltpu.VMEM((1, moved, tall, width), BF16)),
        ("out_send", dma((moved,))), ("out_recv", dma((moved,))),
        ("load_sems", dma((10,))), ("free", pltpu.SemaphoreType.REGULAR),
    ]
    for name in ("t", "s"):
        scratch += [
            ("sum_" + name, pltpu.VMEM(core_shape, BF16)), ("core_" + name, pltpu.VMEM(core_shape, BF16)),
            ("land_" + name, pltpu.VMEM((tiles, moved, share, width), BF16)),
            (name + "_send", dma((2, moved))), (name + "_recv", dma((2, moved))),
            (name + "_core_send", dma((tiles, half))), (name + "_core_recv", dma((tiles, half))),
        ]
    for name, (height, cols) in pieces.items():
        shape = jax.ShapeDtypeStruct((height, cols), F32)
        outs.append(("done_" + name, shape, pl.BlockSpec(shape.shape, lambda s: (0, 0))))
        scratch += [
            ("away_" + name, pltpu.VMEM((n_frame, height, cols), BF16)),
            ("near_" + name, pltpu.VMEM((n_frame - 1, height, cols), BF16)),
            (name + "_z_send", dma((n_frame - 1,))), (name + "_z_recv", dma((n_frame - 1,))),
        ]
    return run_kernel(
        functools.partial(backward_kernel, heads, clips, n, n_frame), first_w + tiles,
        ins, held, outs, scratch, 2 * tokens_here * width * width * 20, collective=2,
    )


def swap(array, axis, bit):
    return lax.ppermute(array, axis, [(i, i ^ (1 << bit)) for i in range(lax.axis_size(axis))])


def scatter_frames(parts):
    count = lax.axis_size("frame")
    me = lax.axis_index("frame")
    left = list(range(count.bit_length() - 1))[::-1]
    shape = parts.shape[1:]
    held = parts.reshape((2,) * len(left) + shape)
    for bit in reversed(list(left)):
        dim = left.index(bit)
        left.remove(bit)
        mine = (me >> bit) & 1
        away = lax.dynamic_index_in_dim(held, 1 - mine, dim, keepdims=False)
        keep = lax.dynamic_index_in_dim(held, mine, dim, keepdims=False)
        held = keep + swap(away, "frame", bit)
    return held.reshape(shape)


def sum_frames(values):
    for bit in range(lax.axis_size("frame").bit_length() - 1):
        values = values + swap(values, "frame", bit)
    return values


def gather_clips(values):
    me = lax.axis_index("clip")
    for bit in range(lax.axis_size("clip").bit_length() - 1):
        other = swap(values, "clip", bit)
        mine = (me >> bit) & 1
        values = jnp.concatenate(
            (jnp.where(mine == 1, other, values), jnp.where(mine == 1, values, other)), axis=0
        )
    return values


def thirds(values):
    high = values.astype(BF16)
    rest = values - high.astype(F32)
    mid = rest.astype(BF16)
    low = (rest - mid.astype(F32)).astype(BF16)
    return jnp.concatenate((high, mid, low), axis=0)


def local(
    tokens, target, loss_weight, timesteps, offsets, cond_table, modulate_w,
    spatial_qkv, spatial_out, temporal_qkv, temporal_out, mlp_in, mlp_out,
):
    clips, frames, patches, width = tokens.shape
    steps = cond_table.shape[0]
    heads = width // HEAD_DIM
    n_clip = lax.axis_size("clip")
    n_frame = lax.axis_size("frame")
    clip_at = lax.axis_index("clip")
    frame_at = lax.axis_index("frame")
    flat = (clips, patches, width)
    tok = tokens.reshape(flat)
    tgt = target.reshape(flat)

    condition = jnp.take(cond_table, timesteps, axis=0, mode="clip")
    cond_low = jax.nn.silu(condition).astype(BF16)
    cond_here = lax.dynamic_slice_in_dim(condition, clip_at * clips, clips)
    _, silu_pull = jax.vjp(jax.nn.silu, cond_here)
    low_here = lax.dynamic_slice_in_dim(cond_low, clip_at * clips, clips)
    mod = jnp.dot(low_here, modulate_w, preferred_element_type=F32).reshape(clips, 9, width)

    half = width // 2
    positions = (offsets + frame_at).astype(F32)
    freqs = jnp.exp(jnp.arange(half, dtype=F32) * (-math.log(10000.0) / half))
    angles = positions[:, None] * freqs
    posenc = jnp.concatenate((jnp.sin(angles), jnp.cos(angles)), axis=-1)[:, None, :]

    head_of = jnp.arange(width, dtype=jnp.int32) // HEAD_DIM
    lane_ids = jnp.arange(LANES, dtype=jnp.int32)
    to_heads = (head_of[:, None] == lane_ids[None, :]).astype(BF16)
    tall = jnp.arange(2 * LANES, dtype=jnp.int32) - LANES
    spread = (tall[:, None] == head_of[None, :]).astype(BF16)
    group, inside = jnp.divmod(jnp.arange(6 * LANES, dtype=jnp.int32), LANES)
    slot_at = jnp.where(inside < heads, group * SLOT + inside, -1)
    pack = (slot_at[:, None] == lane_ids[None, :]).astype(BF16)
    side_ok = jnp.stack((frame_at > 0, frame_at >= 0, frame_at < n_frame - 1))
    masks = jnp.where(side_ok[:, None], 0.0, NO_KEY) * jnp.ones((1, LANES), F32)
    masks = jnp.pad(masks, ((0, 5), (0, 0)))
    weight = jnp.broadcast_to(loss_weight[:, None, None], (clips, 1, LANES))

    weights = {
        "spatial_qkv": spatial_qkv, "spatial_out": spatial_out, "temporal_qkv": temporal_qkv,
        "temporal_out": temporal_out, "mlp_in": mlp_in, "mlp_out": mlp_out,
    }
    fwd = forward_call(
        tok, tgt, mod, posenc, weight, masks, (to_heads, spread, pack), weights, n_clip
    )

    bwd = backward_call(fwd, tok, mod, spread, weights, n_clip, n_frame)

    grad_mod = jnp.concatenate(
        (bwd.sums_a[:, :3], bwd.sums_b[:, :2], fwd.sums[:, 3:4], fwd.sums[:, :3]), axis=1
    ).reshape(clips, 9 * width)
    by_term = dot_nt(thirds(grad_mod), modulate_w).reshape(3, clips, width)
    grad_cond = sum_frames(silu_pull(by_term[0] + by_term[1] + by_term[2])[0])
    mod_cols = 9 * width // n_frame
    mod_share = scatter_frames(grad_mod.reshape(clips, n_frame, mod_cols).transpose(1, 0, 2))
    gathered = gather_clips(jnp.concatenate((grad_cond, mod_share), axis=1))
    onehot = (timesteps[:, None] == jnp.arange(steps, dtype=jnp.int32)[None, :]).astype(BF16)
    grad_table = dot_tn(jnp.concatenate((onehot,) * 3, axis=0), thirds(gathered[:, :width]))
    mod_rows = width // n_clip
    low_rows = lax.dynamic_slice_in_dim(cond_low, clip_at * mod_rows, mod_rows, axis=1)
    grad_modulate = dot_tn(jnp.concatenate((low_rows,) * 3, axis=0), thirds(gathered[:, width:]))
    return (
        fwd.output.reshape(tokens.shape),
        bwd.grad_tokens.reshape(tokens.shape),
        grad_table,
        grad_modulate,
        bwd.done_sq,
        bwd.done_so,
        bwd.done_tq,
        bwd.done_to,
        bwd.done_in,
        bwd.done_out,
    )


def solution(mesh):
    placed = (
        P("clip", "frame", None, None), P("clip", "frame", None, None), P("clip"), P(), P("clip"),
    ) + (P(),) * 8
    return jax.shard_map(
        local,
        mesh=mesh,
        in_specs=placed,
        out_specs=(
            P("clip", "frame", None, None), P("clip", "frame", None, None), P(),
        ) + (P("clip", "frame"),) * 7,
        check_vma=False,
    )
```

```python
import functools
import math

import jax
import jax.numpy as jnp
import numpy as np
from jax import lax
from jax.experimental import pallas as pl
from jax.experimental.pallas import tpu as pltpu
from jax.sharding import PartitionSpec as P

HEAD_DIM = 64
NORM_EPSILON = 1e-06
F32 = jnp.float32
BF16 = jnp.bfloat16
LANES = 128
SLOT = 16
NO_KEY = -1e30
VMEM_LIMIT = 60 * 2**20
GROUP = 2
GELU_A = math.sqrt(2.0 / math.pi)
GELU_B = 0.044715


def dot(left, right):
    return lax.dot_general(left, right, (((1,), (0,)), ((), ())), preferred_element_type=F32)


def dot_nt(left, right):
    return lax.dot_general(left, right, (((1,), (1,)), ((), ())), preferred_element_type=F32)


def dot_tn(left, right):
    return lax.dot_general(left, right, (((0,), (0,)), ((), ())), preferred_element_type=F32)


def norm(values):
    centred = values - jnp.mean(values, axis=-1, keepdims=True)
    inv_std = lax.rsqrt(jnp.mean(centred * centred, axis=-1, keepdims=True) + NORM_EPSILON)
    return centred * inv_std, inv_std


def norm_back(grad_hidden, normed, inv_std, scale_plus):
    grad_normed = grad_hidden * scale_plus
    mean_grad = jnp.mean(grad_normed, axis=-1, keepdims=True)
    mean_cross = jnp.mean(grad_normed * normed, axis=-1, keepdims=True)
    return inv_std * (grad_normed - mean_grad - normed * mean_cross)


def column_sum(values):
    return jnp.sum(values, axis=0, keepdims=True)


def side_masks(dtype, value):
    lane = lax.broadcasted_iota(jnp.int32, (1, LANES), 1)
    return [jnp.where((lane < HEAD_DIM) == (side == 0), value, 0.0).astype(dtype) for side in (0, 1)]


class Refs:
    def __init__(self, names, refs):
        self.__dict__.update(zip(names, refs, strict=True))


class Late:
    def __init__(self, source, ref, sem, step):
        self.ref = ref
        self.copy = pltpu.make_async_copy(source, ref, sem)
        self.step = step
        self.waited = False

    def __getitem__(self, index):
        if not self.waited:
            pl.when(pl.program_id(0) == self.step)(self.copy.wait)
            self.waited = True
        return self.ref[index]


def partner(axis, bit):
    me = lax.axis_index(axis)
    return me + (1 << bit) - (2 << bit) * lax.rem(me // (1 << bit), 2)


def remote(source, target, send_sem, recv_sem, **where):
    return pltpu.make_async_remote_copy(
        src_ref=source, dst_ref=target, send_sem=send_sem, recv_sem=recv_sem,
        device_id=where, device_id_type=pl.DeviceIdType.MESH,
    )


def greet(barrier, **where):
    pl.semaphore_signal(barrier, inc=1, device_id=where, device_id_type=pl.DeviceIdType.MESH)


def run_kernel(body, steps, ins, weights, outs, scratch, flops, collective=None):
    anywhere = pl.BlockSpec(memory_space=pl.ANY)
    names = [name for name, *_ in ins] + [name + "_hbm" for name, *_ in weights]
    names += [name for name, *_ in outs]
    names += [name + "_vmem" for name, *_ in weights] + ["weight_sems"]
    names += [name for name, _ in scratch]

    def kernel(*refs):
        r = Refs(names, refs)
        lates = []
        for number, (name, _, step) in enumerate(weights):
            late = Late(
                getattr(r, name + "_hbm"), getattr(r, name + "_vmem"), r.weight_sems.at[number], step
            )
            lates.append(late)
            setattr(r, name, late)

        @pl.when(pl.program_id(0) == 0)
        def _():
            for late in lates:
                if late.step == 0:
                    late.copy.start()

        body(r)

        @pl.when(pl.program_id(0) == 0)
        def _():
            for late in lates:
                if late.step > 0:
                    late.copy.start()

    arrays = [array for _, array, _ in ins] + [array for _, array, _ in weights]
    shapes = [shape for _, shape, _ in outs]
    touched = sum(math.prod(a.shape) * a.dtype.itemsize for a in arrays + shapes)
    params = {} if collective is None else {"collective_id": collective, "has_side_effects": True}
    done = pl.pallas_call(
        kernel,
        grid=(steps,),
        in_specs=[spec for *_, spec in ins] + [anywhere] * len(weights),
        out_specs=[spec or anywhere for *_, spec in outs],
        out_shape=shapes,
        scratch_shapes=[pltpu.VMEM(a.shape, a.dtype) for _, a, _ in weights]
        + [pltpu.SemaphoreType.DMA((max(len(weights), 1),))]
        + [shape for _, shape in scratch],
        compiler_params=pltpu.CompilerParams(vmem_limit_bytes=VMEM_LIMIT, **params),
        cost_estimate=pl.CostEstimate(flops=flops, bytes_accessed=touched, transcendentals=0),
    )(*arrays)
    return Refs([name for name, *_ in outs], done)


def clip_spec(array, first, clips, depth=None):
    rest = array.shape[1:]
    mode = {} if depth is None else {"pipeline_mode": pl.Buffered(depth)}
    return pl.BlockSpec(
        (1,) + rest, lambda s: (jnp.clip(s - first, 0, clips - 1),) + (0,) * len(rest), **mode
    )


def spatial_forward(r, heads, clip):
    width = r.tokens.shape[-1]
    rows = r.tokens.shape[1]
    mod = r.mod
    inputs = r.tokens[0].astype(F32)
    normed, _ = norm(inputs)
    hidden = (normed * (1.0 + mod[0, 1:2]) + mod[0, 0:1]).astype(BF16)
    r.hidden_a[0] = hidden
    for part in range(3):
        cols = slice(part * width, (part + 1) * width)
        r.qkv_a[0, :, cols] = dot(hidden, r.w_qkv_a[:, cols]).astype(BF16)
    scaled, plain = side_masks(BF16, HEAD_DIM**-0.5), side_masks(BF16, 1.0)
    for first in range(0, heads // 2, 3):
        pairs = range(first, min(first + 3, heads // 2))
        scores, softs = [], []
        for pair in pairs:
            query, key = (columns(r.qkv_a, part, pair) for part in (0, 1))
            scores.append(dot_nt(both_sides(key, scaled), query))
        for pair, score in zip(pairs, scores):
            halves = []
            for side in range(2):
                mine = score[side * rows : (side + 1) * rows]
                top = jnp.max(mine, axis=0, keepdims=True)
                grown = jnp.exp(mine - top)
                total = jnp.sum(grown, axis=0, keepdims=True)
                halves.append((grown * (1.0 / total)).astype(BF16))
                head = 2 * pair + side
                r.lse[0, head : head + 1] = top + jnp.log(total)
            softs.append(jnp.concatenate(halves, axis=0))
        for pair, soft in zip(pairs, softs):
            value = columns(r.qkv_a, 2, pair)
            r.mixed_a[0, :, pair * LANES : (pair + 1) * LANES] = dot_tn(
                soft, both_sides(value, plain)
            ).astype(BF16)
    branch_a = dot(r.mixed_a[0], r.w_out_a[...])
    r.branch_a[0] = branch_a.astype(BF16)
    after_a = inputs + mod[0, 2:3] * branch_a
    r.after_held[clip] = after_a
    normed_b, _ = norm(after_a)
    r.hidden_held[clip] = (
        normed_b * (1.0 + mod[0, 4:5]) + (mod[0, 3:4] + r.posenc[0])
    ).astype(BF16)


def both_sides(array, masks):
    return jnp.concatenate((array * masks[0], array * masks[1]), axis=0)


def columns(ref, part, pair):
    start = part * (ref.shape[-1] // 3) + pair * LANES
    return ref[0, :, start : start + LANES]


def by_head(left, right, to_heads):
    return dot(left * right, to_heads)


def middle(r, clip, rows_at):
    width = r.target.shape[-1]
    rows = r.target.shape[1]
    ff = r.act.shape[-1]
    scale_qk = HEAD_DIM**-0.5
    mod = r.mod
    own_rows = pl.ds(rows_at, rows)
    store = r.w_qkv_a_vmem

    def kept(number, part):
        return store[number * rows : (number + 1) * rows, part * width : (part + 1) * width]

    three = jnp.concatenate((r.hidden_prev[clip], r.hidden_held[clip], r.hidden_next[clip]), axis=0)
    for part in range(3):
        cols = slice(part * width, (part + 1) * width)
        value = dot(three, r.w_qkv_b[:, cols]).astype(BF16)
        store[:, cols] = value
        if part == 0:
            for number, out in enumerate((r.q_prev, r.q_own, r.q_next)):
                out[0] = value[number * rows : (number + 1) * rows]
    scores = []
    for number in range(3):
        raw = by_head(kept(1, 0), kept(number, 1), r.to_heads[...]) * scale_qk
        scores.append(raw + r.masks[number : number + 1])
    top = jnp.maximum(jnp.maximum(scores[0], scores[1]), scores[2])
    grown = [jnp.exp(entry - top) for entry in scores]
    inverse = 1.0 / (grown[0] + grown[1] + grown[2])
    soft = [entry * inverse for entry in grown]
    soft_low = [entry.astype(BF16) for entry in soft]
    to_width = r.spread[LANES : 2 * LANES]
    total = None
    for number in range(3):
        term = dot(soft_low[number], to_width) * kept(number, 2).astype(F32)
        total = term if total is None else total + term
    mixed = total.astype(BF16)
    r.mixed_b[0] = mixed
    branch_b = dot(mixed, r.w_out_b[...])
    r.grad_b[0] = branch_b
    after_b = r.after_held[clip] + mod[0, 5:6] * branch_b
    normed_c, inv_c = norm(after_b)
    hidden = (normed_c * (1.0 + mod[0, 7:8]) + mod[0, 6:7]).astype(BF16)
    r.hidden_c[own_rows, :] = hidden
    parts = ff // width
    ahead = dot(hidden, r.w_in[:, :width])
    for part in range(parts):
        cols = slice(part * width, (part + 1) * width)
        upward = ahead
        if part + 1 < parts:
            ahead = dot(hidden, r.w_in[:, (part + 1) * width : (part + 2) * width])
        squared = upward * upward
        bent = jnp.tanh(upward * (GELU_A + (GELU_A * GELU_B) * squared))
        share = 0.5 + 0.5 * bent
        r.act[own_rows, cols] = (upward * share).astype(BF16)
        steep = (1.0 - bent * bent) * (0.5 * GELU_A + (1.5 * GELU_A * GELU_B) * squared)
        r.grad_up[own_rows, cols] = (share + upward * steep).astype(BF16)
    branch_c = dot(r.act[own_rows, :], r.w_mlp[...])
    result = after_b + mod[0, 8:9] * branch_c
    r.output[0] = result.astype(BF16)
    grad_result = r.weight[0, :, :1] * (result - r.target[0].astype(F32))
    r.sums[0, 2:3] = column_sum(grad_result * branch_c)
    low_c = (mod[0, 8:9] * grad_result).astype(BF16)
    r.grad_branch_c[own_rows, :] = low_c
    ahead = dot_nt(low_c, r.w_mlp[:width, :])
    for part in range(parts):
        cols = slice(part * width, (part + 1) * width)
        grad_act = ahead
        if part + 1 < parts:
            ahead = dot_nt(low_c, r.w_mlp[(part + 1) * width : (part + 2) * width, :])
        r.grad_up[own_rows, cols] = (grad_act * r.grad_up[own_rows, cols].astype(F32)).astype(BF16)
    grad_hidden = dot_nt(r.grad_up[own_rows, :], r.w_in[...])
    r.sums[0, 0:1] = column_sum(grad_hidden)
    r.sums[0, 1:2] = column_sum(grad_hidden * normed_c)
    grad_after = grad_result + norm_back(grad_hidden, normed_c, inv_c, 1.0 + mod[0, 7:8])
    r.sums[0, 3:4] = column_sum(grad_after * r.grad_b[0])
    r.grad_b[0] = grad_after
    low_b = (mod[0, 5:6] * grad_after).astype(BF16)
    r.grad_branch_b[0] = low_b
    grad_mixed = dot_nt(low_b, r.w_out_b[...]).astype(BF16)
    grad_soft = [by_head(grad_mixed, kept(number, 2), r.to_heads[...]) for number in range(3)]
    inner = soft[0] * grad_soft[0] + soft[1] * grad_soft[1] + soft[2] * grad_soft[2]
    grad_scores = [(soft[number] * (grad_soft[number] - inner)).astype(BF16) for number in range(3)]
    total = None
    for number in range(3):
        term = dot(grad_scores[number], to_width) * kept(number, 1).astype(F32)
        total = term if total is None else total + term
    r.grad_q[0] = (total * scale_qk).astype(BF16)
    r.sent_held[clip, :, :width] = grad_mixed
    r.sent_held[clip, :, width:] = dot(
        jnp.concatenate(soft_low + grad_scores, axis=1), r.pack[...]
    ).astype(BF16)


def share_rows(number, keep, share):
    core = lax.rem(lax.axis_index("clip"), 2)
    spot = 2 * number + (core if keep else 1 - core)
    return pl.ds(pl.multiple_of(spot * share, share), share)


def forward_kernel(heads, clips, n, r):
    step = pl.program_id(0)
    rows, width = r.tokens.shape[1:]
    ff = r.act.shape[-1]
    in_steps = ff // width
    out_steps = n // 2
    share = ff // n
    last = 2 * clips + in_steps + out_steps - 1
    frame = lax.axis_index("frame")
    has_prev = frame > 0
    has_next = frame < lax.axis_size("frame") - 1
    no_prev = jnp.logical_not(has_prev)
    no_next = jnp.logical_not(has_next)
    core = lax.rem(lax.axis_index("clip"), 2)
    sibling = partner("clip", 0)
    barrier = pltpu.get_barrier_semaphore()

    def halo(way, clip):
        return remote(
            r.hidden_held.at[clip], (r.hidden_prev, r.hidden_next)[way].at[clip],
            r.halo_send.at[way, clip], r.halo_recv.at[way, clip],
            frame=frame + 1 if way == 0 else frame - 1,
        )

    def packet(way, clip):
        return remote(
            r.sent_held.at[clip], (r.sent_prev, r.sent_next)[way].at[clip],
            r.sent_send.at[way, clip], r.sent_recv.at[way, clip],
            frame=frame + 1 if way == 0 else frame - 1,
        )

    low_share = width // n

    def in_tile(tile):
        return [
            remote(
                r.stage.at[lax.rem(tile, 2), share_rows(number, False, low_share)],
                r.came_in.at[tile, number],
                r.in_send.at[tile, number], r.in_recv.at[tile, number], clip=sibling,
            )
            for number in range(n // 2)
        ]

    def in_kept(tile):
        return [
            pltpu.make_async_copy(
                r.stage.at[lax.rem(tile, 2), share_rows(number, True, low_share)],
                r.keep_in.at[tile, number], r.in_keep.at[tile, number],
            )
            for number in range(n // 2)
        ]

    def in_sent(tile):
        for copy in in_tile(tile):
            copy.wait_send()
        for copy in in_kept(tile):
            copy.wait()

    def out_part(tile, which):
        return r.stage.at[
            lax.rem(tile + in_steps, 2), pl.ds(pl.multiple_of(which * share, share), share)
        ]

    def out_tile(tile):
        return remote(
            out_part(tile, 1 - core), r.came_out.at[tile],
            r.out_send.at[tile], r.out_recv.at[tile], clip=sibling,
        )

    def out_kept(tile):
        return pltpu.make_async_copy(
            out_part(tile, core), r.keep_out.at[tile], r.out_keep.at[tile]
        )

    def save(clip):
        return [
            pltpu.make_async_copy(r.after_held.at[clip], r.after_a.at[clip], r.save_sems.at[0, clip]),
            pltpu.make_async_copy(
                r.hidden_held.at[clip], r.hidden_b.at[clip], r.save_sems.at[1, clip]
            ),
        ]

    def save_sent(clip):
        return pltpu.make_async_copy(r.sent_held.at[clip], r.sent.at[clip], r.save_sems.at[2, clip])

    def fill(way, clip):
        zeros = (r.hidden_prev, r.hidden_next)[way].at[clip]
        target = (r.sent_prev, r.sent_next)[way].at[clip]
        return [
            pltpu.make_async_copy(zeros, target.at[:, pl.ds(0, width)], r.save_sems.at[3, clip]),
            pltpu.make_async_copy(
                zeros.at[:, pl.ds(0, LANES)], target.at[:, pl.ds(width, LANES)],
                r.save_sems.at[4, clip],
            ),
        ]

    @pl.when(step == 0)
    def _():
        greet(barrier, clip=sibling)
        pl.when(has_prev)(lambda: greet(barrier, frame=frame - 1))
        pl.when(has_next)(lambda: greet(barrier, frame=frame + 1))

        @pl.when(no_prev)
        def _():
            r.hidden_prev[...] = jnp.zeros_like(r.hidden_prev)
            for clip in range(clips):
                for copy in fill(0, clip):
                    copy.start()

        @pl.when(no_next)
        def _():
            r.hidden_next[...] = jnp.zeros_like(r.hidden_next)
            for clip in range(clips):
                for copy in fill(1, clip):
                    copy.start()

    @pl.when(step < clips)
    def _():
        spatial_forward(r, heads, step)

        @pl.when(step == 0)
        def _():
            pl.semaphore_wait(
                barrier, 1 + jnp.where(has_prev, 1, 0) + jnp.where(has_next, 1, 0)
            )

        pl.when(has_next)(lambda: halo(0, step).start())
        pl.when(has_prev)(lambda: halo(1, step).start())
        for copy in save(step):
            copy.start()

    @pl.when((step >= clips) & (step < 2 * clips))
    def _():
        clip = step - clips
        pl.when(has_prev)(lambda: halo(0, clip).wait_recv())
        pl.when(has_next)(lambda: halo(1, clip).wait_recv())
        middle(r, clip, pl.multiple_of(clip * rows, rows))
        pl.when(has_next)(lambda: packet(0, clip).start())
        pl.when(has_prev)(lambda: packet(1, clip).start())
        save_sent(clip).start()

    @pl.when((step >= 2 * clips) & (step < 2 * clips + in_steps))
    def _():
        tile = step - 2 * clips

        pl.when(tile >= 2)(lambda: in_sent(tile - 2))
        cols = pl.ds(pl.multiple_of(tile * width, width), width)
        r.stage[lax.rem(tile, 2), :width] = dot_tn(r.hidden_c[...], r.grad_up[:, cols]).astype(BF16)
        for copy in in_tile(tile) + in_kept(tile):
            copy.start()

    @pl.when(step >= 2 * clips + in_steps)
    def _():
        tile = step - 2 * clips - in_steps

        pl.when(tile < 2)(lambda: in_sent(in_steps + tile - 2))

        @pl.when(tile >= 2)
        def _():
            out_tile(tile - 2).wait_send()
            out_kept(tile - 2).wait()

        cols = pl.ds(pl.multiple_of(tile * 2 * share, 2 * share), 2 * share)
        r.stage[lax.rem(tile + in_steps, 2), : 2 * share] = dot_tn(
            r.act[:, cols], r.grad_branch_c[...]
        ).astype(BF16)
        out_tile(tile).start()
        out_kept(tile).start()

    @pl.when(step == last)
    def _():
        for clip in range(clips):
            for copy in save(clip):
                copy.wait()
            save_sent(clip).wait()

            @pl.when(has_next)
            def _():
                halo(0, clip).wait_send()
                packet(0, clip).wait_send()
                packet(1, clip).wait_recv()

            @pl.when(has_prev)
            def _():
                halo(1, clip).wait_send()
                packet(1, clip).wait_send()
                packet(0, clip).wait_recv()

            for way, absent in ((0, no_prev), (1, no_next)):

                @pl.when(absent)
                def _():
                    for copy in fill(way, clip):
                        copy.wait()

        for tile in range(in_steps):
            for copy in in_tile(tile):
                copy.wait_recv()
        for tile in range(out_steps):
            out_tile(tile).wait_recv()
        for tile in range(out_steps - 2, out_steps):
            out_tile(tile).wait_send()
            out_kept(tile).wait()


def forward_call(tok, target, mod, posenc, weight, masks, tables, weights, n):
    clips, rows, width = tok.shape
    ff = weights["mlp_in"].shape[1]
    heads = width // HEAD_DIM
    tokens_here = clips * rows
    in_steps, out_steps, share = ff // width, n // 2, ff // n
    to_heads, spread, pack = tables

    def struct(last, dtype=BF16):
        return jax.ShapeDtypeStruct((clips, rows, last), dtype)

    def early(array):
        return clip_spec(array, 0, clips)

    def late(array):
        return clip_spec(array, clips, clips)

    mod_spec = pl.BlockSpec(
        (1,) + mod.shape[1:],
        lambda s: (jnp.where(s < clips, s, jnp.minimum(s - clips, clips - 1)), 0, 0),
    )
    ins = [
        ("tokens", tok, early(tok)), ("posenc", posenc, early(posenc)), ("mod", mod, mod_spec),
        ("target", target, clip_spec(target, clips, clips, 1)), ("weight", weight, late(weight)),
    ]
    held = [
        ("w_qkv_a", weights["spatial_qkv"], 0), ("w_out_a", weights["spatial_out"], 0),
        ("w_qkv_b", weights["temporal_qkv"], clips), ("to_heads", to_heads, clips),
        ("masks", masks, clips), ("spread", spread, clips), ("w_out_b", weights["temporal_out"], clips),
        ("w_in", weights["mlp_in"], clips), ("w_mlp", weights["mlp_out"], clips), ("pack", pack, clips),
    ]
    outs = []
    for name, shape in (
        ("hidden_a", struct(width)), ("qkv_a", struct(3 * width)), ("mixed_a", struct(width)),
        ("branch_a", struct(width)),
        ("lse", jax.ShapeDtypeStruct((clips, -(-heads // 8) * 8, rows), F32)),
    ):
        outs.append((name, shape, clip_spec(shape, 0, clips, 1)))
    for name, shape in (
        ("output", struct(width)), ("grad_b", struct(width, F32)), ("mixed_b", struct(width)),
        ("grad_branch_b", struct(width)), ("q_own", struct(width)), ("q_prev", struct(width)),
        ("q_next", struct(width)), ("grad_q", struct(width)),
        ("sums", jax.ShapeDtypeStruct((clips, 8, width), F32)),
    ):
        outs.append((name, shape, clip_spec(shape, clips, clips, 1)))
    outs += [
        ("after_a", struct(width, F32), None), ("hidden_b", struct(width), None),
        ("sent", struct(width + LANES), None), ("sent_prev", struct(width + LANES), None),
        ("sent_next", struct(width + LANES), None),
    ]
    tile_in = jax.ShapeDtypeStruct((in_steps, n // 2, width // n, width), BF16)
    tile_out = jax.ShapeDtypeStruct((out_steps, share, width), BF16)
    outs += [
        ("keep_in", tile_in, None), ("came_in", tile_in, None), ("keep_out", tile_out, None),
        ("came_out", tile_out, None),
    ]
    dma = pltpu.SemaphoreType.DMA
    scratch = [
        ("after_held", pltpu.VMEM((clips, rows, width), F32)),
        ("hidden_held", pltpu.VMEM((clips, rows, width), BF16)),
        ("hidden_prev", pltpu.VMEM((clips, rows, width), BF16)),
        ("hidden_next", pltpu.VMEM((clips, rows, width), BF16)),
        ("sent_held", pltpu.VMEM((clips, rows, width + LANES), BF16)),
        ("act", pltpu.VMEM((tokens_here, ff), BF16)),
        ("grad_up", pltpu.VMEM((tokens_here, ff), BF16)),
        ("hidden_c", pltpu.VMEM((tokens_here, width), BF16)),
        ("grad_branch_c", pltpu.VMEM((tokens_here, width), BF16)),
        ("stage", pltpu.VMEM((2, max(width, 2 * share), width), BF16)),
        ("halo_send", dma((2, clips))), ("halo_recv", dma((2, clips))),
        ("sent_send", dma((2, clips))), ("sent_recv", dma((2, clips))),
        ("in_send", dma((in_steps, n // 2))), ("in_recv", dma((in_steps, n // 2))),
        ("in_keep", dma((in_steps, n // 2))), ("out_send", dma((out_steps,))),
        ("out_recv", dma((out_steps,))), ("out_keep", dma((out_steps,))),
        ("save_sems", dma((5, clips))),
    ]
    return run_kernel(
        functools.partial(forward_kernel, heads, clips, n), 2 * clips + in_steps + out_steps,
        ins, held, outs, scratch, 2 * tokens_here * width * width * 46, collective=1,
    )


def temporal_backward(r, clip, rows_at):
    width = r.tokens.shape[-1]
    rows = r.tokens.shape[1]
    scale_qk = HEAD_DIM**-0.5
    own_rows = pl.ds(rows_at, rows)
    grad_key = None
    grad_value = None
    for number, (source, query) in enumerate(
        ((r.sent_prev, r.q_prev), (r.sent, r.q_own), (r.sent_next, r.q_next))
    ):
        other = 2 - number
        table = source[0, :, width:]
        low = LANES - SLOT * other
        soft = dot(table, r.spread[low : low + LANES])
        low = LANES - SLOT * (3 + other)
        score = dot(table, r.spread[low : low + LANES])
        key_term = score * query[0].astype(F32)
        value_term = soft * source[0, :, :width].astype(F32)
        grad_key = key_term if grad_key is None else grad_key + key_term
        grad_value = value_term if grad_value is None else grad_value + value_term
    r.grad_qkv[own_rows, :width] = r.grad_q[0]
    r.grad_qkv[own_rows, width : 2 * width] = (grad_key * scale_qk).astype(BF16)
    r.grad_qkv[own_rows, 2 * width :] = grad_value.astype(BF16)
    grad_hidden = dot_nt(r.grad_qkv[own_rows, :], r.w_qkv_b[...])
    normed_b, inv_b = norm(r.after_a[0])
    r.mods[3, pl.ds(clip, 1)] = column_sum(grad_hidden)
    r.mods[4, pl.ds(clip, 1)] = column_sum(grad_hidden * normed_b)
    r.grad_a[clip] = r.grad_b[0] + norm_back(grad_hidden, normed_b, inv_b, 1.0 + r.mod[0, 4:5])


def spatial_backward(r, heads, clip, rows_at):
    width = r.tokens.shape[-1]
    rows = r.tokens.shape[1]
    scale_qk = HEAD_DIM**-0.5
    own_rows = pl.ds(rows_at, rows)
    mod = r.mod
    r.mods[2, pl.ds(clip, 1)] = column_sum(r.grad_a[clip] * r.branch_a[0].astype(F32))
    low_a = (mod[0, 2:3] * r.grad_a[clip]).astype(BF16)
    r.grad_branch[own_rows, :] = low_a
    grad_mixed = dot_nt(low_a, r.w_out_a[...]).astype(BF16)
    scaled, plain = side_masks(BF16, scale_qk), side_masks(BF16, 1.0)
    lane = lax.broadcasted_iota(jnp.int32, (1, LANES), 1)
    for first in range(0, heads // 2, GROUP):
        pairs = range(first, min(first + GROUP, heads // 2))
        scores, grads, softs, backs = [], [], [], []
        for pair in pairs:
            gm = grad_mixed[:, pair * LANES : (pair + 1) * LANES]
            scores.append(
                dot_nt(both_sides(columns(r.qkv_a, 1, pair), scaled), columns(r.qkv_a, 0, pair))
            )
            grads.append(dot_nt(both_sides(columns(r.qkv_a, 2, pair), plain), gm))
        for pair, score, grad in zip(pairs, scores, grads):
            low, back = [], []
            for side in range(2):
                mine = slice(side * rows, (side + 1) * rows)
                head = 2 * pair + side
                soft = jnp.exp(score[mine] - r.lse[0, head : head + 1])
                inner = jnp.sum(soft * grad[mine], axis=0, keepdims=True)
                back.append((soft * (grad[mine] - inner)).astype(BF16))
                low.append(soft.astype(BF16))
            softs.append(jnp.concatenate(low, axis=0))
            backs.append(jnp.concatenate(back, axis=0))
        for pair, soft, back in zip(pairs, softs, backs):
            gm = grad_mixed[:, pair * LANES : (pair + 1) * LANES]
            query, key = (columns(r.qkv_a, part, pair) for part in (0, 1))
            start = pair * LANES
            r.grad_qkv[own_rows, start : start + LANES] = dot_tn(
                back, both_sides(key, scaled)
            ).astype(BF16)
            for part, total, factor in ((1, dot(back, query), scale_qk), (2, dot(soft, gm), 1.0)):
                joined = jnp.where(lane < HEAD_DIM, total[:rows], total[rows:])
                start = part * width + pair * LANES
                r.grad_qkv[own_rows, start : start + LANES] = (joined * factor).astype(BF16)
    grad_hidden = dot_nt(r.grad_qkv[own_rows, :], r.w_qkv_a[...])
    normed_a, inv_a = norm(r.tokens[0].astype(F32))
    r.mods[0, pl.ds(clip, 1)] = column_sum(grad_hidden)
    r.mods[1, pl.ds(clip, 1)] = column_sum(grad_hidden * normed_a)
    r.grad_tokens[0] = r.grad_a[clip] + norm_back(
        grad_hidden, normed_a, inv_a, 1.0 + mod[0, 1:2]
    )


class Halving:
    def __init__(self, sums, landings, sends, recvs, bits):
        self.sums, self.landings, self.sends, self.recvs = sums, landings, sends, recvs
        self.bits = bits

    def share(self, stage, number, keep):
        me = lax.axis_index("clip")
        later = sorted(self.bits[stage + 1 :])
        spot = sum(((number >> i) & 1) << (bit - 1) for i, bit in enumerate(later))
        for bit in self.bits[: stage + 1]:
            mine = lax.rem(me // (1 << bit), 2)
            if bit == self.bits[stage] and not keep:
                mine = 1 - mine
            spot = spot + mine * (1 << (bit - 1))
        return spot

    def count(self, stage):
        return 1 << (len(self.bits) - 1 - stage)

    def copy(self, stage, number):
        at = sum(self.count(i) for i in range(stage)) + number
        return remote(
            self.sums.at[:, self.share(stage, number, False)],
            self.landings.at[:, at], self.sends.at[at], self.recvs.at[at],
            clip=partner("clip", self.bits[stage]),
        )

    def send(self, stage):
        for number in range(self.count(stage)):
            self.copy(stage, number).start()

    def fold(self, stage):
        for number in range(self.count(stage)):
            self.copy(stage, number).wait_recv()
            at = sum(self.count(i) for i in range(stage)) + number
            spot = self.share(stage, number, True)
            self.sums[:, spot] = (
                self.sums[:, spot].astype(F32) + self.landings[:, at].astype(F32)
            ).astype(BF16)

    def own(self):
        return self.sums[:, self.share(len(self.bits) - 1, 0, True)]

    def drain(self):
        for stage in range(len(self.bits)):
            for number in range(self.count(stage)):
                self.copy(stage, number).wait_send()


class Frames:
    def __init__(self, away, landing, sends, recvs):
        self.away, self.landing, self.sends, self.recvs = away, landing, sends, recvs

    def copy(self, distance):
        count = self.away.shape[0]
        frame = lax.rem(lax.axis_index("frame") + distance, count)
        return remote(
            self.away.at[frame], self.landing.at[distance - 1],
            self.sends.at[distance - 1], self.recvs.at[distance - 1], frame=frame,
        )

    def send(self, piece):
        count = self.away.shape[0]
        for frame in range(count):
            self.away[frame] = piece(frame)
        for distance in range(1, count):
            self.copy(distance).start()

    def finish(self):
        total = self.away[lax.axis_index("frame")].astype(F32)
        for distance in range(1, self.away.shape[0]):
            self.copy(distance).wait_recv()
            total = total + self.landing[distance - 1].astype(F32)
        return total

    def drain(self):
        for distance in range(1, self.away.shape[0]):
            self.copy(distance).wait_send()


def cut(array, number, count):
    cols = array.shape[1] // count
    return array[:, number * cols : (number + 1) * cols]


def thirds_in_rows(values):
    high = values.astype(BF16).astype(F32)
    mid = (values - high).astype(BF16).astype(F32)
    low = (values - high) - mid
    return jnp.concatenate((high, mid, low, jnp.zeros_like(low)), axis=0).astype(BF16)


def side_by_side(tiles):
    return jnp.concatenate([tiles[i] for i in range(tiles.shape[0])], axis=1)


def backward_kernel(heads, clips, n, n_frame, r):
    step = pl.program_id(0)
    rows, width = r.tokens.shape[1:]
    tiles = 4
    half = n // 2
    share = width // n
    first_t = clips
    first_s = clips + tiles
    first_w = 2 * clips + tiles
    last = first_w + tiles - 1
    sibling = partner("clip", 0)
    barrier = pltpu.get_barrier_semaphore()
    bits = list(range(1, n.bit_length() - 1))
    frame = lax.axis_index("frame")
    place = lax.axis_index("clip")

    feed_in = Halving(r.sum_in, r.land_in, r.in_send, r.in_recv, bits)
    feed_out = Halving(r.sum_out, r.land_out, r.out_send, r.out_recv, bits[::-1])

    def units_of(name):
        sums, land = getattr(r, "sum_" + name), getattr(r, "land_" + name)
        sends, recvs = getattr(r, name + "_send"), getattr(r, name + "_recv")
        return [
            Halving(
                sums.at[pl.ds(i, 1)], land.at[pl.ds(i, 1)], sends.at[i], recvs.at[i],
                bits[:: 1 - 2 * (i % 2)],
            )
            for i in range(tiles)
        ]

    temporal, spatial = units_of("t"), units_of("s")
    stages = len(bits)

    regions = {"t": r.w_qkv_a_vmem, "s": r.w_qkv_b_vmem}

    def tile_cols(tile):
        return pl.ds(pl.multiple_of(lax.rem(tile, 3) * width, width), width)

    def tile_copies(name, tile):
        sends, recvs = getattr(r, name + "_core_send"), getattr(r, name + "_core_recv")
        return [
            remote(
                regions[name].at[share_rows(number, False, share), tile_cols(tile)],
                getattr(r, "core_" + name).at[tile, number],
                sends.at[tile, number], recvs.at[tile, number], clip=sibling,
            )
            for number in range(half)
        ]

    def tile_sent(name, tile):
        for copy in tile_copies(name, tile):
            copy.wait_send()

    def fold_core(name, which):
        sums, core = getattr(r, "sum_" + name), getattr(r, "core_" + name)
        for tile in which:
            for copy in tile_copies(name, tile):
                copy.wait_recv()
            sums[tile] = (sums[tile].astype(F32) + core[tile].astype(F32)).astype(BF16)

    frames = {
        name: Frames(
            getattr(r, "away_" + name), getattr(r, "near_" + name),
            getattr(r, name + "_z_send"), getattr(r, name + "_z_recv"),
        )
        for name in ("in", "out", "t", "s", "mod")
    }

    spaces = (r.left, r.left_out, r.grad_branch)

    def mod_tile(part):
        return pltpu.make_async_copy(
            r.w_mod.at[:, pl.ds(part * width, width)],
            spaces[part % 3].at[pl.ds(0, width)], r.mod_sems.at[part],
        )

    def mod_sums():
        total = None
        for part in range(9):
            mod_tile(part).wait()
            term = dot_nt(thirds_in_rows(r.mods[part]), spaces[part % 3][:width])
            total = term if total is None else total + term
            if part + 3 < 9:
                mod_tile(part + 3).start()
        pad = r.mods.shape[1]
        total = total[:pad] + total[pad : 2 * pad] + total[2 * pad : 3 * pad]
        joined = side_by_side(r.mods)
        total = total * r.silu_grad[...]
        frames["mod"].send(
            lambda other: jnp.concatenate((total, cut(joined, other, n_frame)), axis=1)
        )

    def spread_mods(distance):
        return remote(
            r.mod_share, r.gathered.at[place], r.mod_send.at[distance - 1],
            r.mod_recv.at[distance - 1], clip=lax.rem(place + distance, n),
        )

    own_mods = pltpu.make_async_copy(r.mod_share, r.gathered.at[place], r.mod_sems.at[9])

    def to_frames(units, name):
        owned = [unit.own()[0] for unit in units]
        wide = jnp.concatenate(owned[:-1], axis=1)
        frames[name].send(
            lambda other: jnp.concatenate(
                (cut(wide, other, n_frame), cut(owned[-1], other, n_frame)), axis=1
            )
        )

    def from_frames(name, wide, narrow):
        total = frames[name].finish()
        wide[...] = total[:, : wide.shape[1]]
        narrow[...] = total[:, wide.shape[1] :]

    def two_high(array):
        rows = array.shape[0] // 2
        return jnp.concatenate((array[:rows], array[rows:]), axis=1)

    loads = [
        pltpu.make_async_copy(r.keep_in, r.sum_in, r.load_sems.at[0]),
        pltpu.make_async_copy(r.came_in, r.core_t, r.load_sems.at[1]),
        pltpu.make_async_copy(r.keep_out, r.sum_out, r.load_sems.at[2]),
        pltpu.make_async_copy(r.came_out, r.core_s, r.load_sems.at[3]),
    ]
    lefts_t = [
        pltpu.make_async_copy(r.hidden_b, r.left, r.load_sems.at[4]),
        pltpu.make_async_copy(r.mixed_b, r.left_out, r.load_sems.at[5]),
        pltpu.make_async_copy(r.grad_branch_b, r.grad_branch, r.load_sems.at[6]),
    ]
    lefts_s = [
        pltpu.make_async_copy(r.hidden_a, r.left, r.load_sems.at[7]),
        pltpu.make_async_copy(r.mixed_a, r.left_out, r.load_sems.at[8]),
    ]
    r.w_qkv_a = Late(r.w_qkv_a_hbm, r.w_qkv_a_vmem, r.load_sems.at[9], first_s)

    @pl.when(step == 0)
    def _():
        for distance in range(1, n):
            greet(barrier, clip=lax.rem(place + distance, n))
        for distance in range(1, n_frame):
            greet(barrier, frame=lax.rem(frame + distance, n_frame))
        for copy in loads + lefts_t:
            copy.start()
        r.mods[...] = jnp.zeros_like(r.mods)
        for clip in range(clips):
            for row, part in enumerate((6, 7, 8, 5)):
                r.mods[part, clip : clip + 1] = r.sums[clip, row : row + 1]

    @pl.when(step < clips)
    def _():
        temporal_backward(r, step, pl.multiple_of(step * rows, rows))

    @pl.when(step == 0)
    def _():
        for copy in loads:
            copy.wait()
        for tile in range(tiles):
            r.sum_in[tile] = (
                r.sum_in[tile].astype(F32) + r.core_t[tile].astype(F32)
            ).astype(BF16)
        per = r.sum_out.shape[1] // tiles
        for tile in range(tiles):
            which = slice(tile * per, (tile + 1) * per)
            came = r.core_s[tile].reshape(r.sum_out[0, which].shape)
            r.sum_out[0, which] = (
                r.sum_out[0, which].astype(F32) + came.astype(F32)
            ).astype(BF16)
        pl.semaphore_wait(barrier, n - 1 + n_frame - 1)
        pl.semaphore_signal(
            r.free, inc=1, device_id={"clip": sibling}, device_id_type=pl.DeviceIdType.MESH
        )
        feed_in.send(0)
        feed_out.send(0)

    def weight_tile(name, tile):
        region = regions[name]

        @pl.when(tile < tiles - 1)
        def _():
            cols = pl.ds(pl.multiple_of(tile * width, width), width)
            region[:, tile_cols(tile)] = dot_tn(r.left[...], r.grad_qkv[:, cols]).astype(BF16)

        @pl.when(tile == tiles - 1)
        def _():
            region[:, tile_cols(tile)] = dot_tn(r.left_out[...], r.grad_branch[...]).astype(BF16)

        for copy in tile_copies(name, tile):
            copy.start()
        for number in range(half):
            getattr(r, "sum_" + name)[tile, number] = region[
                share_rows(number, True, share), tile_cols(tile)
            ]

    @pl.when((step >= first_t) & (step < first_s))
    def _():
        tile = step - first_t

        @pl.when(tile == 0)
        def _():
            for copy in lefts_t:
                copy.wait()
            pl.semaphore_wait(r.free, 1)

        pl.when(tile == 3)(lambda: tile_sent("t", 0))
        weight_tile("t", tile)

        @pl.when(tile == tiles - 1)
        def _():
            for copy in lefts_s:
                copy.start()

    @pl.when((step >= first_s) & (step < first_w))
    def _():
        clip = step - first_s

        @pl.when(clip == 0)
        def _():
            for tile in range(1, tiles):
                tile_sent("t", tile)
            r.w_qkv_a.copy.start()

        spatial_backward(r, heads, clip, pl.multiple_of(clip * rows, rows))

    @pl.when(step == first_s - 1)
    def _():
        for unit in (feed_in, feed_out):
            unit.fold(0)
            if stages > 1:
                unit.send(1)

    @pl.when(step == first_s)
    def _():
        for tile, unit in enumerate(temporal):
            fold_core("t", (tile,))
            unit.send(0)

    @pl.when(step == first_s + 1)
    def _():
        for stage in range(1, stages):
            for unit in (feed_in, feed_out):
                unit.fold(stage)
                if stage + 1 < stages:
                    unit.send(stage + 1)
        owned_in, owned_out = side_by_side(feed_in.own()), feed_out.own()[0]
        frames["in"].send(lambda other: cut(owned_in, other, n_frame))
        frames["out"].send(lambda other: two_high(cut(owned_out, other, n_frame)))

    @pl.when(step == first_s + 2)
    def _():
        for unit in temporal:
            unit.fold(0)
            if stages > 1:
                unit.send(1)

    @pl.when(step == first_s + 3)
    def _():
        for stage in range(1, stages):
            for unit in temporal:
                unit.fold(stage)
                if stage + 1 < stages:
                    unit.send(stage + 1)
        to_frames(temporal, "t")

    @pl.when(step >= first_w)
    def _():
        tile = step - first_w

        @pl.when(tile == 0)
        def _():
            for copy in lefts_s:
                copy.wait()

        pl.when(tile == 3)(lambda: tile_sent("s", 0))
        weight_tile("s", tile)

    for tile in range(tiles - 1):

        @pl.when(step == first_w + 1 + tile)
        def _():
            fold_core("s", (tile,))
            spatial[tile].send(0)

    @pl.when(step == last)
    def _():
        fold_core("s", (tiles - 1,))
        spatial[tiles - 1].send(0)
        for part in range(3):
            mod_tile(part).start()
        mod_sums()
        r.done_in[...] = frames["in"].finish()
        total = frames["out"].finish()
        high = total.shape[0]
        r.done_out[:high] = cut(total, 0, 2)
        r.done_out[high:] = cut(total, 1, 2)
        from_frames("t", r.done_tq, r.done_to)
        for stage in range(stages):
            for unit in spatial:
                unit.fold(stage)
                if stage + 1 < stages:
                    unit.send(stage + 1)
            if stage == 0:
                r.mod_share[...] = frames["mod"].finish()
                for distance in range(1, n):
                    spread_mods(distance).start()
                own_mods.start()
        to_frames(spatial, "s")
        from_frames("s", r.done_sq, r.done_so)
        own_mods.wait()
        for distance in range(1, n):
            spread_mods(distance).wait()
        for unit in (feed_in, feed_out, *temporal, *spatial):
            unit.drain()
        for name in frames:
            frames[name].drain()
        for tile in range(1, tiles):
            tile_sent("s", tile)


def backward_call(fwd, tok, mod, spread, weights, modulate_w, silu_grad, n, n_frame):
    clips, rows, width = tok.shape
    ff = weights["mlp_in"].shape[1]
    heads = width // HEAD_DIM
    tokens_here = clips * rows
    tiles = 4
    half, share, tall = n // 2, width // n, ff // n
    first_s, first_w = clips + tiles, 2 * clips + tiles

    def struct(last, dtype=BF16):
        return jax.ShapeDtypeStruct((clips, rows, last), dtype)

    mod_spec = pl.BlockSpec(
        (1,) + mod.shape[1:],
        lambda s: (
            jnp.where(s < first_s, jnp.minimum(s, clips - 1), jnp.minimum(s - first_s, clips - 1)),
            0, 0,
        ),
    )
    anywhere = pl.BlockSpec(memory_space=pl.ANY)
    pad, mod_cols = silu_grad.shape[0], width + 9 * width // n_frame
    whole = pl.BlockSpec(fwd.sums.shape, lambda s: (0, 0, 0), pipeline_mode=pl.Buffered(1))
    whole_grad = pl.BlockSpec(silu_grad.shape, lambda s: (0, 0), pipeline_mode=pl.Buffered(1))
    ins = [
        ("mod", mod, mod_spec), ("sums", fwd.sums, whole), ("silu_grad", silu_grad, whole_grad),
        ("w_mod", modulate_w, anywhere),
    ]
    for name in ("q_prev", "q_own", "q_next", "sent_prev", "sent", "sent_next", "grad_q", "grad_b", "after_a"):
        array = getattr(fwd, name)
        ins.append((name, array, clip_spec(array, 0, clips, 1 if name in ("grad_q", "grad_b", "after_a") else 2)))
    for name, array in (
        ("tokens", tok), ("branch_a", fwd.branch_a), ("qkv_a", fwd.qkv_a), ("lse", fwd.lse)
    ):
        ins.append((name, array, clip_spec(array, first_s, clips, 1)))
    flat = (tokens_here, width)
    for name in ("hidden_b", "mixed_b", "grad_branch_b", "hidden_a", "mixed_a"):
        ins.append((name, getattr(fwd, name).reshape(flat), anywhere))
    core_shape = (tiles, half, share, width)
    ins += [
        ("keep_in", fwd.keep_in.reshape(core_shape), anywhere),
        ("came_in", fwd.came_in.reshape(core_shape), anywhere),
        ("keep_out", fwd.keep_out.reshape(1, half, tall, width), anywhere),
        ("came_out", fwd.came_out.reshape(core_shape), anywhere),
        ("w_qkv_a_hbm", weights["spatial_qkv"], anywhere),
    ]
    held = [
        ("spread", spread, 0), ("w_qkv_b", weights["temporal_qkv"], 0),
        ("w_out_a", weights["spatial_out"], first_s),
    ]
    grad_tokens = struct(width, F32)
    outs = [
        ("grad_tokens", grad_tokens, clip_spec(grad_tokens, first_s, clips, 1)),
        ("gathered", jax.ShapeDtypeStruct((n, pad, mod_cols), F32), None),
    ]
    dma = pltpu.SemaphoreType.DMA
    pieces = {
        "in": (share, ff // n_frame), "out": (tall, width // n_frame),
        "tq": (share, 3 * width // n_frame), "to": (share, width // n_frame),
        "sq": (share, 3 * width // n_frame), "so": (share, width // n_frame),
    }
    moved = half - 1
    scratch = [
        ("grad_a", pltpu.VMEM((clips, rows, width), F32)),
        ("grad_qkv", pltpu.VMEM((tokens_here, 3 * width), BF16)),
        ("grad_branch", pltpu.VMEM(flat, BF16)), ("left", pltpu.VMEM(flat, BF16)),
        ("left_out", pltpu.VMEM(flat, BF16)),
        ("w_qkv_a_vmem", pltpu.VMEM(weights["spatial_qkv"].shape, BF16)),
        ("sum_in", pltpu.VMEM(core_shape, BF16)), ("land_in", pltpu.VMEM((tiles, moved, share, width), BF16)),
        ("in_send", dma((moved,))), ("in_recv", dma((moved,))),
        ("sum_out", pltpu.VMEM((1, half, tall, width), BF16)),
        ("land_out", pltpu.VMEM((1, moved, tall, width), BF16)),
        ("out_send", dma((moved,))), ("out_recv", dma((moved,))),
        ("load_sems", dma((10,))), ("free", pltpu.SemaphoreType.REGULAR),
        ("mods", pltpu.VMEM((9, pad, width), F32)), ("mod_sems", dma((10,))),
        ("mod_share", pltpu.VMEM((pad, mod_cols), F32)),
        ("mod_send", dma((n - 1,))), ("mod_recv", dma((n - 1,))),
    ]
    for name in ("t", "s"):
        scratch += [
            ("sum_" + name, pltpu.VMEM(core_shape, BF16)), ("core_" + name, pltpu.VMEM(core_shape, BF16)),
            ("land_" + name, pltpu.VMEM((tiles, moved, share, width), BF16)),
            (name + "_send", dma((tiles, moved))), (name + "_recv", dma((tiles, moved))),
            (name + "_core_send", dma((tiles, half))), (name + "_core_recv", dma((tiles, half))),
        ]
    for name, dims in pieces.items():
        shape = jax.ShapeDtypeStruct(dims, F32)
        outs.append(("done_" + name, shape, pl.BlockSpec(shape.shape, lambda s: (0, 0))))
    packed = {
        "in": (share, ff // n_frame), "out": (tall // 2, 2 * width // n_frame),
        "t": (share, 4 * width // n_frame), "s": (share, 4 * width // n_frame),
        "mod": (pad, mod_cols),
    }
    for name, dims in packed.items():
        kind = F32 if name == "mod" else BF16
        scratch += [
            ("away_" + name, pltpu.VMEM((n_frame, *dims), kind)),
            ("near_" + name, pltpu.VMEM((n_frame - 1, *dims), kind)),
            (name + "_z_send", dma((n_frame - 1,))), (name + "_z_recv", dma((n_frame - 1,))),
        ]
    return run_kernel(
        functools.partial(backward_kernel, heads, clips, n, n_frame), first_w + tiles,
        ins, held, outs, scratch, 2 * tokens_here * width * width * 20, collective=2,
    )


def thirds(values):
    high = values.astype(BF16)
    rest = values - high.astype(F32)
    mid = rest.astype(BF16)
    low = (rest - mid.astype(F32)).astype(BF16)
    return jnp.concatenate((high, mid, low), axis=0)


def local(
    tokens, target, loss_weight, timesteps, offsets, cond_table, modulate_w,
    spatial_qkv, spatial_out, temporal_qkv, temporal_out, mlp_in, mlp_out,
):
    clips, frames, patches, width = tokens.shape
    steps = cond_table.shape[0]
    heads = width // HEAD_DIM
    n_clip = lax.axis_size("clip")
    n_frame = lax.axis_size("frame")
    clip_at = lax.axis_index("clip")
    frame_at = lax.axis_index("frame")
    flat = (clips, patches, width)
    tok = tokens.reshape(flat)
    tgt = target.reshape(flat)

    condition = jnp.take(cond_table, timesteps, axis=0, mode="clip")
    cond_low = jax.nn.silu(condition).astype(BF16)
    cond_here = lax.dynamic_slice_in_dim(condition, clip_at * clips, clips)
    _, silu_pull = jax.vjp(jax.nn.silu, cond_here)
    low_here = lax.dynamic_slice_in_dim(cond_low, clip_at * clips, clips)
    mod = jnp.dot(low_here, modulate_w, preferred_element_type=F32).reshape(clips, 9, width)

    half = width // 2
    positions = (offsets + frame_at).astype(F32)
    freqs = jnp.exp(jnp.arange(half, dtype=F32) * (-math.log(10000.0) / half))
    angles = positions[:, None] * freqs
    posenc = jnp.concatenate((jnp.sin(angles), jnp.cos(angles)), axis=-1)[:, None, :]

    head_of = np.arange(width) // HEAD_DIM
    lane_ids = np.arange(LANES)
    to_heads = jnp.asarray((head_of[:, None] == lane_ids[None, :]).astype(BF16))
    tall = np.arange(2 * LANES) - LANES
    spread = jnp.asarray((tall[:, None] == head_of[None, :]).astype(BF16))
    group, inside = np.divmod(np.arange(6 * LANES), LANES)
    slot_at = np.where(inside < heads, group * SLOT + inside, -1)
    pack = jnp.asarray((slot_at[:, None] == lane_ids[None, :]).astype(BF16))
    side_ok = jnp.stack((frame_at > 0, frame_at >= 0, frame_at < n_frame - 1))
    masks = jnp.where(side_ok[:, None], 0.0, NO_KEY) * jnp.ones((1, LANES), F32)
    masks = jnp.pad(masks, ((0, 5), (0, 0)))
    weight = jnp.broadcast_to(loss_weight[:, None, None], (clips, 1, LANES))

    weights = {
        "spatial_qkv": spatial_qkv, "spatial_out": spatial_out, "temporal_qkv": temporal_qkv,
        "temporal_out": temporal_out, "mlp_in": mlp_in, "mlp_out": mlp_out,
    }
    fwd = forward_call(
        tok, tgt, mod, posenc, weight, masks, (to_heads, spread, pack), weights, n_clip
    )

    pad = -(-clips // 8) * 8
    silu_grad = jnp.pad(silu_pull(jnp.ones_like(cond_here))[0], ((0, pad - clips), (0, 0)))
    bwd = backward_call(fwd, tok, mod, spread, weights, modulate_w, silu_grad, n_clip, n_frame)
    gathered = bwd.gathered[:, :clips].reshape(n_clip * clips, -1)
    onehot = (timesteps[:, None] == jnp.arange(steps, dtype=jnp.int32)[None, :]).astype(BF16)
    grad_table = dot_tn(jnp.concatenate((onehot,) * 3, axis=0), thirds(gathered[:, :width]))
    mod_rows = width // n_clip
    low_rows = lax.dynamic_slice_in_dim(cond_low, clip_at * mod_rows, mod_rows, axis=1)
    grad_modulate = dot_tn(jnp.concatenate((low_rows,) * 3, axis=0), thirds(gathered[:, width:]))
    return (
        fwd.output.reshape(tokens.shape),
        bwd.grad_tokens.reshape(tokens.shape),
        grad_table,
        grad_modulate,
        bwd.done_sq,
        bwd.done_so,
        bwd.done_tq,
        bwd.done_to,
        bwd.done_in,
        bwd.done_out,
    )


def solution(mesh):
    placed = (
        P("clip", "frame", None, None), P("clip", "frame", None, None), P("clip"), P(), P("clip"),
    ) + (P(),) * 8
    return jax.shard_map(
        local,
        mesh=mesh,
        in_specs=placed,
        out_specs=(
            P("clip", "frame", None, None), P("clip", "frame", None, None), P(),
        ) + (P("clip", "frame"),) * 7,
        check_vma=False,
    )
```

```python
import functools
import math

import jax
import jax.numpy as jnp
import numpy as np
from jax import lax
from jax.experimental import pallas as pl
from jax.experimental.pallas import tpu as pltpu
from jax.sharding import PartitionSpec as P

HEAD_DIM = 64
NORM_EPSILON = 1e-06
F32 = jnp.float32
BF16 = jnp.bfloat16
LANES = 128
SLOT = 16
NO_KEY = -1e30
VMEM_LIMIT = 60 * 2**20
GROUP = 2
GELU_A = math.sqrt(2.0 / math.pi)
GELU_B = 0.044715


def dot(left, right):
    return lax.dot_general(left, right, (((1,), (0,)), ((), ())), preferred_element_type=F32)


def dot_nt(left, right):
    return lax.dot_general(left, right, (((1,), (1,)), ((), ())), preferred_element_type=F32)


def dot_tn(left, right):
    return lax.dot_general(left, right, (((0,), (0,)), ((), ())), preferred_element_type=F32)


def norm(values):
    centred = values - jnp.mean(values, axis=-1, keepdims=True)
    inv_std = lax.rsqrt(jnp.mean(centred * centred, axis=-1, keepdims=True) + NORM_EPSILON)
    return centred * inv_std, inv_std


def norm_back(grad_hidden, normed, inv_std, scale_plus):
    grad_normed = grad_hidden * scale_plus
    mean_grad = jnp.mean(grad_normed, axis=-1, keepdims=True)
    mean_cross = jnp.mean(grad_normed * normed, axis=-1, keepdims=True)
    return inv_std * (grad_normed - mean_grad - normed * mean_cross)


def column_sum(values):
    return jnp.sum(values, axis=0, keepdims=True)


def side_masks(dtype, value):
    lane = lax.broadcasted_iota(jnp.int32, (1, LANES), 1)
    return [jnp.where((lane < HEAD_DIM) == (side == 0), value, 0.0).astype(dtype) for side in (0, 1)]


class Refs:
    def __init__(self, names, refs):
        self.__dict__.update(zip(names, refs, strict=True))


class Late:
    def __init__(self, source, ref, sem, step):
        self.ref = ref
        self.copy = pltpu.make_async_copy(source, ref, sem)
        self.step = step
        self.waited = False

    def __getitem__(self, index):
        if not self.waited:
            pl.when(pl.program_id(0) == self.step)(self.copy.wait)
            self.waited = True
        return self.ref[index]


def partner(axis, bit):
    me = lax.axis_index(axis)
    return me + (1 << bit) - (2 << bit) * lax.rem(me // (1 << bit), 2)


def remote(source, target, send_sem, recv_sem, **where):
    return pltpu.make_async_remote_copy(
        src_ref=source, dst_ref=target, send_sem=send_sem, recv_sem=recv_sem,
        device_id=where, device_id_type=pl.DeviceIdType.MESH,
    )


def greet(barrier, **where):
    pl.semaphore_signal(barrier, inc=1, device_id=where, device_id_type=pl.DeviceIdType.MESH)


def run_kernel(body, steps, ins, weights, outs, scratch, flops, collective=None):
    anywhere = pl.BlockSpec(memory_space=pl.ANY)
    names = [name for name, *_ in ins] + [name + "_hbm" for name, *_ in weights]
    names += [name for name, *_ in outs]
    names += [name + "_vmem" for name, *_ in weights] + ["weight_sems"]
    names += [name for name, _ in scratch]

    def kernel(*refs):
        r = Refs(names, refs)
        lates = []
        for number, (name, _, step) in enumerate(weights):
            late = Late(
                getattr(r, name + "_hbm"), getattr(r, name + "_vmem"), r.weight_sems.at[number], step
            )
            lates.append(late)
            setattr(r, name, late)

        @pl.when(pl.program_id(0) == 0)
        def _():
            for late in lates:
                if late.step == 0:
                    late.copy.start()

        body(r)

        @pl.when(pl.program_id(0) == 0)
        def _():
            for late in lates:
                if late.step > 0:
                    late.copy.start()

    arrays = [array for _, array, _ in ins] + [array for _, array, _ in weights]
    shapes = [shape for _, shape, _ in outs]
    touched = sum(math.prod(a.shape) * a.dtype.itemsize for a in arrays + shapes)
    params = {} if collective is None else {"collective_id": collective, "has_side_effects": True}
    done = pl.pallas_call(
        kernel,
        grid=(steps,),
        in_specs=[spec for *_, spec in ins] + [anywhere] * len(weights),
        out_specs=[spec or anywhere for *_, spec in outs],
        out_shape=shapes,
        scratch_shapes=[pltpu.VMEM(a.shape, a.dtype) for _, a, _ in weights]
        + [pltpu.SemaphoreType.DMA((max(len(weights), 1),))]
        + [shape for _, shape in scratch],
        compiler_params=pltpu.CompilerParams(vmem_limit_bytes=VMEM_LIMIT, **params),
        cost_estimate=pl.CostEstimate(flops=flops, bytes_accessed=touched, transcendentals=0),
    )(*arrays)
    return Refs([name for name, *_ in outs], done)


def clip_spec(array, first, clips, depth=None):
    rest = array.shape[1:]
    mode = {} if depth is None else {"pipeline_mode": pl.Buffered(depth)}
    return pl.BlockSpec(
        (1,) + rest, lambda s: (jnp.clip(s - first, 0, clips - 1),) + (0,) * len(rest), **mode
    )


def spatial_forward(r, heads, clip):
    width = r.tokens.shape[-1]
    rows = r.tokens.shape[1]
    mod = r.mod
    inputs = r.tokens[0].astype(F32)
    normed, _ = norm(inputs)
    hidden = (normed * (1.0 + mod[0, 1:2]) + mod[0, 0:1]).astype(BF16)
    r.hidden_a[0] = hidden
    for part in range(3):
        cols = slice(part * width, (part + 1) * width)
        r.qkv_a[0, :, cols] = dot(hidden, r.w_qkv_a[:, cols]).astype(BF16)
    scaled, plain = side_masks(BF16, HEAD_DIM**-0.5), side_masks(BF16, 1.0)
    for first in range(0, heads // 2, 3):
        pairs = range(first, min(first + 3, heads // 2))
        scores, softs = [], []
        for pair in pairs:
            query, key = (columns(r.qkv_a, part, pair) for part in (0, 1))
            scores.append(dot_nt(both_sides(key, scaled), query))
        for pair, score in zip(pairs, scores):
            halves = []
            for side in range(2):
                mine = score[side * rows : (side + 1) * rows]
                top = jnp.max(mine, axis=0, keepdims=True)
                grown = jnp.exp(mine - top)
                total = jnp.sum(grown, axis=0, keepdims=True)
                halves.append((grown * (1.0 / total)).astype(BF16))
                head = 2 * pair + side
                r.lse[0, head : head + 1] = top + jnp.log(total)
            softs.append(jnp.concatenate(halves, axis=0))
        for pair, soft in zip(pairs, softs):
            value = columns(r.qkv_a, 2, pair)
            r.mixed_a[0, :, pair * LANES : (pair + 1) * LANES] = dot_tn(
                soft, both_sides(value, plain)
            ).astype(BF16)
    branch_a = dot(r.mixed_a[0], r.w_out_a[...])
    r.branch_a[0] = branch_a.astype(BF16)
    after_a = inputs + mod[0, 2:3] * branch_a
    r.after_held[clip] = after_a
    normed_b, _ = norm(after_a)
    r.hidden_held[clip] = (
        normed_b * (1.0 + mod[0, 4:5]) + (mod[0, 3:4] + r.posenc[0])
    ).astype(BF16)


def both_sides(array, masks):
    return jnp.concatenate((array * masks[0], array * masks[1]), axis=0)


def columns(ref, part, pair):
    start = part * (ref.shape[-1] // 3) + pair * LANES
    return ref[0, :, start : start + LANES]


def by_head(left, right, to_heads):
    return dot(left * right, to_heads)


def middle(r, clip, rows_at):
    width = r.target.shape[-1]
    rows = r.target.shape[1]
    ff = r.act.shape[-1]
    scale_qk = HEAD_DIM**-0.5
    mod = r.mod
    own_rows = pl.ds(rows_at, rows)
    store = r.w_qkv_a_vmem

    def kept(number, part):
        return store[number * rows : (number + 1) * rows, part * width : (part + 1) * width]

    three = jnp.concatenate((r.hidden_prev[clip], r.hidden_held[clip], r.hidden_next[clip]), axis=0)
    for part in range(3):
        cols = slice(part * width, (part + 1) * width)
        value = dot(three, r.w_qkv_b[:, cols]).astype(BF16)
        store[:, cols] = value
        if part == 0:
            for number, out in enumerate((r.q_prev, r.q_own, r.q_next)):
                out[0] = value[number * rows : (number + 1) * rows]
    frame = lax.axis_index("frame")
    absent = (frame == 0, None, frame == lax.axis_size("frame") - 1)
    scores = []
    for number in range(3):
        raw = by_head(kept(1, 0), kept(number, 1), r.to_heads[...]) * scale_qk
        if absent[number] is not None:
            raw = raw + jnp.where(absent[number], NO_KEY, 0.0)
        scores.append(raw)
    top = jnp.maximum(jnp.maximum(scores[0], scores[1]), scores[2])
    grown = [jnp.exp(entry - top) for entry in scores]
    inverse = 1.0 / (grown[0] + grown[1] + grown[2])
    soft = [entry * inverse for entry in grown]
    soft_low = [entry.astype(BF16) for entry in soft]
    to_width = r.spread[LANES : 2 * LANES]
    total = None
    for number in range(3):
        term = dot(soft_low[number], to_width) * kept(number, 2).astype(F32)
        total = term if total is None else total + term
    mixed = total.astype(BF16)
    r.mixed_b[0] = mixed
    branch_b = dot(mixed, r.w_out_b[...])
    r.grad_b[0] = branch_b
    after_b = r.after_held[clip] + mod[0, 5:6] * branch_b
    normed_c, inv_c = norm(after_b)
    hidden = (normed_c * (1.0 + mod[0, 7:8]) + mod[0, 6:7]).astype(BF16)
    r.hidden_c[own_rows, :] = hidden
    parts = ff // width
    ahead = dot(hidden, r.w_in[:, :width])
    for part in range(parts):
        cols = slice(part * width, (part + 1) * width)
        upward = ahead
        if part + 1 < parts:
            ahead = dot(hidden, r.w_in[:, (part + 1) * width : (part + 2) * width])
        squared = upward * upward
        bent = jnp.tanh(upward * (GELU_A + (GELU_A * GELU_B) * squared))
        share = 0.5 + 0.5 * bent
        r.act[own_rows, cols] = (upward * share).astype(BF16)
        steep = (1.0 - bent * bent) * (0.5 * GELU_A + (1.5 * GELU_A * GELU_B) * squared)
        r.grad_up[own_rows, cols] = (share + upward * steep).astype(BF16)
    branch_c = dot(r.act[own_rows, :], r.w_mlp[...])
    result = after_b + mod[0, 8:9] * branch_c
    r.output[0] = result.astype(BF16)
    grad_result = r.weight[clip] * (result - r.target[0].astype(F32))
    r.sums[0, 2:3] = column_sum(grad_result * branch_c)
    low_c = (mod[0, 8:9] * grad_result).astype(BF16)
    r.grad_branch_c[own_rows, :] = low_c
    ahead = dot_nt(low_c, r.w_mlp[:width, :])
    for part in range(parts):
        cols = slice(part * width, (part + 1) * width)
        grad_act = ahead
        if part + 1 < parts:
            ahead = dot_nt(low_c, r.w_mlp[(part + 1) * width : (part + 2) * width, :])
        r.grad_up[own_rows, cols] = (grad_act * r.grad_up[own_rows, cols].astype(F32)).astype(BF16)
    grad_hidden = dot_nt(r.grad_up[own_rows, :], r.w_in[...])
    r.sums[0, 0:1] = column_sum(grad_hidden)
    r.sums[0, 1:2] = column_sum(grad_hidden * normed_c)
    grad_after = grad_result + norm_back(grad_hidden, normed_c, inv_c, 1.0 + mod[0, 7:8])
    r.sums[0, 3:4] = column_sum(grad_after * r.grad_b[0])
    r.grad_b[0] = grad_after
    low_b = (mod[0, 5:6] * grad_after).astype(BF16)
    r.grad_branch_b[0] = low_b
    grad_mixed = dot_nt(low_b, r.w_out_b[...]).astype(BF16)
    grad_soft = [by_head(grad_mixed, kept(number, 2), r.to_heads[...]) for number in range(3)]
    inner = soft[0] * grad_soft[0] + soft[1] * grad_soft[1] + soft[2] * grad_soft[2]
    grad_scores = [(soft[number] * (grad_soft[number] - inner)).astype(BF16) for number in range(3)]
    total = None
    for number in range(3):
        term = dot(grad_scores[number], to_width) * kept(number, 1).astype(F32)
        total = term if total is None else total + term
    r.grad_q[0] = (total * scale_qk).astype(BF16)
    r.sent_held[clip, :, :width] = grad_mixed
    r.sent_held[clip, :, width:] = dot(
        jnp.concatenate(soft_low + grad_scores, axis=1), r.pack[...]
    ).astype(BF16)


def share_rows(number, keep, share):
    core = lax.rem(lax.axis_index("clip"), 2)
    spot = 2 * number + (core if keep else 1 - core)
    return pl.ds(pl.multiple_of(spot * share, share), share)


def forward_kernel(heads, clips, n, r):
    step = pl.program_id(0)
    rows, width = r.tokens.shape[1:]
    ff = r.act.shape[-1]
    in_steps = ff // width
    out_steps = n // 2
    share = ff // n
    last = 2 * clips + in_steps + out_steps - 1
    frame = lax.axis_index("frame")
    has_prev = frame > 0
    has_next = frame < lax.axis_size("frame") - 1
    no_prev = jnp.logical_not(has_prev)
    no_next = jnp.logical_not(has_next)
    core = lax.rem(lax.axis_index("clip"), 2)
    sibling = partner("clip", 0)
    barrier = pltpu.get_barrier_semaphore()

    def halo(way, clip):
        return remote(
            r.hidden_held.at[clip], (r.hidden_prev, r.hidden_next)[way].at[clip],
            r.halo_send.at[way, clip], r.halo_recv.at[way, clip],
            frame=frame + 1 if way == 0 else frame - 1,
        )

    def packet(way, clip):
        return remote(
            r.sent_held.at[clip], (r.sent_prev, r.sent_next)[way].at[clip],
            r.sent_send.at[way, clip], r.sent_recv.at[way, clip],
            frame=frame + 1 if way == 0 else frame - 1,
        )

    low_share = width // n

    def in_tile(tile):
        return [
            remote(
                r.stage.at[lax.rem(tile, 2), share_rows(number, False, low_share)],
                r.came_in.at[tile, number],
                r.in_send.at[tile, number], r.in_recv.at[tile, number], clip=sibling,
            )
            for number in range(n // 2)
        ]

    def in_kept(tile):
        return [
            pltpu.make_async_copy(
                r.stage.at[lax.rem(tile, 2), share_rows(number, True, low_share)],
                r.keep_in.at[tile, number], r.in_keep.at[tile, number],
            )
            for number in range(n // 2)
        ]

    def in_sent(tile):
        for copy in in_tile(tile):
            copy.wait_send()
        for copy in in_kept(tile):
            copy.wait()

    def out_part(tile, which):
        return r.stage.at[
            lax.rem(tile + in_steps, 2), pl.ds(pl.multiple_of(which * share, share), share)
        ]

    def out_tile(tile):
        return remote(
            out_part(tile, 1 - core), r.came_out.at[tile],
            r.out_send.at[tile], r.out_recv.at[tile], clip=sibling,
        )

    def out_kept(tile):
        return pltpu.make_async_copy(
            out_part(tile, core), r.keep_out.at[tile], r.out_keep.at[tile]
        )

    def save(clip):
        return [
            pltpu.make_async_copy(r.after_held.at[clip], r.after_a.at[clip], r.save_sems.at[0, clip]),
            pltpu.make_async_copy(
                r.hidden_held.at[clip], r.hidden_b.at[clip], r.save_sems.at[1, clip]
            ),
        ]

    def save_sent(clip):
        return pltpu.make_async_copy(r.sent_held.at[clip], r.sent.at[clip], r.save_sems.at[2, clip])

    def fill(way, clip):
        zeros = (r.hidden_prev, r.hidden_next)[way].at[clip]
        target = (r.sent_prev, r.sent_next)[way].at[clip]
        return [
            pltpu.make_async_copy(zeros, target.at[:, pl.ds(0, width)], r.save_sems.at[3, clip]),
            pltpu.make_async_copy(
                zeros.at[:, pl.ds(0, LANES)], target.at[:, pl.ds(width, LANES)],
                r.save_sems.at[4, clip],
            ),
        ]

    @pl.when(step == 0)
    def _():
        greet(barrier, clip=sibling)
        pl.when(has_prev)(lambda: greet(barrier, frame=frame - 1))
        pl.when(has_next)(lambda: greet(barrier, frame=frame + 1))

        @pl.when(no_prev)
        def _():
            r.hidden_prev[...] = jnp.zeros_like(r.hidden_prev)
            for clip in range(clips):
                for copy in fill(0, clip):
                    copy.start()

        @pl.when(no_next)
        def _():
            r.hidden_next[...] = jnp.zeros_like(r.hidden_next)
            for clip in range(clips):
                for copy in fill(1, clip):
                    copy.start()

    @pl.when(step < clips)
    def _():
        spatial_forward(r, heads, step)

        @pl.when(step == 0)
        def _():
            pl.semaphore_wait(
                barrier, 1 + jnp.where(has_prev, 1, 0) + jnp.where(has_next, 1, 0)
            )

        pl.when(has_next)(lambda: halo(0, step).start())
        pl.when(has_prev)(lambda: halo(1, step).start())
        for copy in save(step):
            copy.start()

    @pl.when((step >= clips) & (step < 2 * clips))
    def _():
        clip = step - clips
        pl.when(has_prev)(lambda: halo(0, clip).wait_recv())
        pl.when(has_next)(lambda: halo(1, clip).wait_recv())
        middle(r, clip, pl.multiple_of(clip * rows, rows))
        pl.when(has_next)(lambda: packet(0, clip).start())
        pl.when(has_prev)(lambda: packet(1, clip).start())
        save_sent(clip).start()

    @pl.when((step >= 2 * clips) & (step < 2 * clips + in_steps))
    def _():
        tile = step - 2 * clips

        pl.when(tile >= 2)(lambda: in_sent(tile - 2))
        cols = pl.ds(pl.multiple_of(tile * width, width), width)
        r.stage[lax.rem(tile, 2), :width] = dot_tn(r.hidden_c[...], r.grad_up[:, cols]).astype(BF16)
        for copy in in_tile(tile) + in_kept(tile):
            copy.start()

    @pl.when(step >= 2 * clips + in_steps)
    def _():
        tile = step - 2 * clips - in_steps

        pl.when(tile < 2)(lambda: in_sent(in_steps + tile - 2))

        @pl.when(tile >= 2)
        def _():
            out_tile(tile - 2).wait_send()
            out_kept(tile - 2).wait()

        cols = pl.ds(pl.multiple_of(tile * 2 * share, 2 * share), 2 * share)
        r.stage[lax.rem(tile + in_steps, 2), : 2 * share] = dot_tn(
            r.act[:, cols], r.grad_branch_c[...]
        ).astype(BF16)
        out_tile(tile).start()
        out_kept(tile).start()

    @pl.when(step == last)
    def _():
        for clip in range(clips):
            for copy in save(clip):
                copy.wait()
            save_sent(clip).wait()

            @pl.when(has_next)
            def _():
                halo(0, clip).wait_send()
                packet(0, clip).wait_send()
                packet(1, clip).wait_recv()

            @pl.when(has_prev)
            def _():
                halo(1, clip).wait_send()
                packet(1, clip).wait_send()
                packet(0, clip).wait_recv()

            for way, absent in ((0, no_prev), (1, no_next)):

                @pl.when(absent)
                def _():
                    for copy in fill(way, clip):
                        copy.wait()

        for tile in range(in_steps):
            for copy in in_tile(tile):
                copy.wait_recv()
        for tile in range(out_steps):
            out_tile(tile).wait_recv()
        for tile in range(out_steps - 2, out_steps):
            out_tile(tile).wait_send()
            out_kept(tile).wait()


def forward_call(tok, target, mod, posenc, weight, tables, weights, n):
    clips, rows, width = tok.shape
    ff = weights["mlp_in"].shape[1]
    heads = width // HEAD_DIM
    tokens_here = clips * rows
    in_steps, out_steps, share = ff // width, n // 2, ff // n
    to_heads, spread, pack = tables

    def struct(last, dtype=BF16):
        return jax.ShapeDtypeStruct((clips, rows, last), dtype)

    def early(array):
        return clip_spec(array, 0, clips)

    def late(array):
        return clip_spec(array, clips, clips)

    mod_spec = pl.BlockSpec(
        (1,) + mod.shape[1:],
        lambda s: (jnp.where(s < clips, s, jnp.minimum(s - clips, clips - 1)), 0, 0),
    )
    ins = [
        ("tokens", tok, early(tok)), ("posenc", posenc, early(posenc)), ("mod", mod, mod_spec),
        ("target", target, clip_spec(target, clips, clips, 1)), ("weight", weight, pl.BlockSpec(memory_space=pltpu.SMEM)),
    ]
    held = [
        ("w_qkv_a", weights["spatial_qkv"], 0), ("w_out_a", weights["spatial_out"], 0),
        ("w_qkv_b", weights["temporal_qkv"], clips), ("to_heads", to_heads, clips),
        ("spread", spread, clips), ("w_out_b", weights["temporal_out"], clips),
        ("w_in", weights["mlp_in"], clips), ("w_mlp", weights["mlp_out"], clips), ("pack", pack, clips),
    ]
    outs = []
    for name, shape in (
        ("hidden_a", struct(width)), ("qkv_a", struct(3 * width)), ("mixed_a", struct(width)),
        ("branch_a", struct(width)),
        ("lse", jax.ShapeDtypeStruct((clips, -(-heads // 8) * 8, rows), F32)),
    ):
        outs.append((name, shape, clip_spec(shape, 0, clips, 1)))
    for name, shape in (
        ("output", struct(width)), ("grad_b", struct(width, F32)), ("mixed_b", struct(width)),
        ("grad_branch_b", struct(width)), ("q_own", struct(width)), ("q_prev", struct(width)),
        ("q_next", struct(width)), ("grad_q", struct(width)),
        ("sums", jax.ShapeDtypeStruct((clips, 8, width), F32)),
    ):
        outs.append((name, shape, clip_spec(shape, clips, clips, 1)))
    outs += [
        ("after_a", struct(width, F32), None), ("hidden_b", struct(width), None),
        ("sent", struct(width + LANES), None), ("sent_prev", struct(width + LANES), None),
        ("sent_next", struct(width + LANES), None),
    ]
    tile_in = jax.ShapeDtypeStruct((in_steps, n // 2, width // n, width), BF16)
    tile_out = jax.ShapeDtypeStruct((out_steps, share, width), BF16)
    outs += [
        ("keep_in", tile_in, None), ("came_in", tile_in, None), ("keep_out", tile_out, None),
        ("came_out", tile_out, None),
    ]
    dma = pltpu.SemaphoreType.DMA
    scratch = [
        ("after_held", pltpu.VMEM((clips, rows, width), F32)),
        ("hidden_held", pltpu.VMEM((clips, rows, width), BF16)),
        ("hidden_prev", pltpu.VMEM((clips, rows, width), BF16)),
        ("hidden_next", pltpu.VMEM((clips, rows, width), BF16)),
        ("sent_held", pltpu.VMEM((clips, rows, width + LANES), BF16)),
        ("act", pltpu.VMEM((tokens_here, ff), BF16)),
        ("grad_up", pltpu.VMEM((tokens_here, ff), BF16)),
        ("hidden_c", pltpu.VMEM((tokens_here, width), BF16)),
        ("grad_branch_c", pltpu.VMEM((tokens_here, width), BF16)),
        ("stage", pltpu.VMEM((2, max(width, 2 * share), width), BF16)),
        ("halo_send", dma((2, clips))), ("halo_recv", dma((2, clips))),
        ("sent_send", dma((2, clips))), ("sent_recv", dma((2, clips))),
        ("in_send", dma((in_steps, n // 2))), ("in_recv", dma((in_steps, n // 2))),
        ("in_keep", dma((in_steps, n // 2))), ("out_send", dma((out_steps,))),
        ("out_recv", dma((out_steps,))), ("out_keep", dma((out_steps,))),
        ("save_sems", dma((5, clips))),
    ]
    return run_kernel(
        functools.partial(forward_kernel, heads, clips, n), 2 * clips + in_steps + out_steps,
        ins, held, outs, scratch, 2 * tokens_here * width * width * 46, collective=1,
    )


def temporal_backward(r, clip, rows_at):
    width = r.tokens.shape[-1]
    rows = r.tokens.shape[1]
    scale_qk = HEAD_DIM**-0.5
    own_rows = pl.ds(rows_at, rows)
    grad_key = None
    grad_value = None
    for number, (source, query) in enumerate(
        ((r.sent_prev, r.q_prev), (r.sent, r.q_own), (r.sent_next, r.q_next))
    ):
        other = 2 - number
        table = source[0, :, width:]
        low = LANES - SLOT * other
        soft = dot(table, r.spread[low : low + LANES])
        low = LANES - SLOT * (3 + other)
        score = dot(table, r.spread[low : low + LANES])
        key_term = score * query[0].astype(F32)
        value_term = soft * source[0, :, :width].astype(F32)
        grad_key = key_term if grad_key is None else grad_key + key_term
        grad_value = value_term if grad_value is None else grad_value + value_term
    r.grad_qkv[own_rows, :width] = r.grad_q[0]
    r.grad_qkv[own_rows, width : 2 * width] = (grad_key * scale_qk).astype(BF16)
    r.grad_qkv[own_rows, 2 * width :] = grad_value.astype(BF16)
    grad_hidden = dot_nt(r.grad_qkv[own_rows, :], r.w_qkv_b[...])
    normed_b, inv_b = norm(r.after_a[0])
    r.mods[3, pl.ds(clip, 1)] = column_sum(grad_hidden)
    r.mods[4, pl.ds(clip, 1)] = column_sum(grad_hidden * normed_b)
    r.grad_a[clip] = r.grad_b[0] + norm_back(grad_hidden, normed_b, inv_b, 1.0 + r.mod[0, 4:5])


def spatial_backward(r, heads, clip, rows_at):
    width = r.tokens.shape[-1]
    rows = r.tokens.shape[1]
    scale_qk = HEAD_DIM**-0.5
    own_rows = pl.ds(rows_at, rows)
    mod = r.mod
    r.mods[2, pl.ds(clip, 1)] = column_sum(r.grad_a[clip] * r.branch_a[0].astype(F32))
    low_a = (mod[0, 2:3] * r.grad_a[clip]).astype(BF16)
    r.grad_branch[own_rows, :] = low_a
    grad_mixed = dot_nt(low_a, r.w_out_a[...]).astype(BF16)
    scaled, plain = side_masks(BF16, scale_qk), side_masks(BF16, 1.0)
    lane = lax.broadcasted_iota(jnp.int32, (1, LANES), 1)
    for first in range(0, heads // 2, GROUP):
        pairs = range(first, min(first + GROUP, heads // 2))
        scores, grads, softs, backs = [], [], [], []
        for pair in pairs:
            gm = grad_mixed[:, pair * LANES : (pair + 1) * LANES]
            scores.append(
                dot_nt(both_sides(columns(r.qkv_a, 1, pair), scaled), columns(r.qkv_a, 0, pair))
            )
            grads.append(dot_nt(both_sides(columns(r.qkv_a, 2, pair), plain), gm))
        for pair, score, grad in zip(pairs, scores, grads):
            low, back = [], []
            for side in range(2):
                mine = slice(side * rows, (side + 1) * rows)
                head = 2 * pair + side
                soft = jnp.exp(score[mine] - r.lse[0, head : head + 1])
                inner = jnp.sum(soft * grad[mine], axis=0, keepdims=True)
                back.append((soft * (grad[mine] - inner)).astype(BF16))
                low.append(soft.astype(BF16))
            softs.append(jnp.concatenate(low, axis=0))
            backs.append(jnp.concatenate(back, axis=0))
        for pair, soft, back in zip(pairs, softs, backs):
            gm = grad_mixed[:, pair * LANES : (pair + 1) * LANES]
            query, key = (columns(r.qkv_a, part, pair) for part in (0, 1))
            start = pair * LANES
            r.grad_qkv[own_rows, start : start + LANES] = dot_tn(
                back, both_sides(key, scaled)
            ).astype(BF16)
            for part, total, factor in ((1, dot(back, query), scale_qk), (2, dot(soft, gm), 1.0)):
                joined = jnp.where(lane < HEAD_DIM, total[:rows], total[rows:])
                start = part * width + pair * LANES
                r.grad_qkv[own_rows, start : start + LANES] = (joined * factor).astype(BF16)
    grad_hidden = dot_nt(r.grad_qkv[own_rows, :], r.w_qkv_a[...])
    normed_a, inv_a = norm(r.tokens[0].astype(F32))
    r.mods[0, pl.ds(clip, 1)] = column_sum(grad_hidden)
    r.mods[1, pl.ds(clip, 1)] = column_sum(grad_hidden * normed_a)
    r.grad_tokens[0] = r.grad_a[clip] + norm_back(
        grad_hidden, normed_a, inv_a, 1.0 + mod[0, 1:2]
    )


class Halving:
    def __init__(self, sums, landings, sends, recvs, bits):
        self.sums, self.landings, self.sends, self.recvs = sums, landings, sends, recvs
        self.bits = bits

    def share(self, stage, number, keep):
        me = lax.axis_index("clip")
        later = sorted(self.bits[stage + 1 :])
        spot = sum(((number >> i) & 1) << (bit - 1) for i, bit in enumerate(later))
        for bit in self.bits[: stage + 1]:
            mine = lax.rem(me // (1 << bit), 2)
            if bit == self.bits[stage] and not keep:
                mine = 1 - mine
            spot = spot + mine * (1 << (bit - 1))
        return spot

    def count(self, stage):
        return 1 << (len(self.bits) - 1 - stage)

    def copy(self, stage, number):
        at = sum(self.count(i) for i in range(stage)) + number
        return remote(
            self.sums.at[:, self.share(stage, number, False)],
            self.landings.at[:, at], self.sends.at[at], self.recvs.at[at],
            clip=partner("clip", self.bits[stage]),
        )

    def send(self, stage):
        for number in range(self.count(stage)):
            self.copy(stage, number).start()

    def fold(self, stage):
        for number in range(self.count(stage)):
            self.copy(stage, number).wait_recv()
            at = sum(self.count(i) for i in range(stage)) + number
            spot = self.share(stage, number, True)
            self.sums[:, spot] = (
                self.sums[:, spot].astype(F32) + self.landings[:, at].astype(F32)
            ).astype(BF16)

    def own(self):
        return self.sums[:, self.share(len(self.bits) - 1, 0, True)]

    def drain(self):
        for stage in range(len(self.bits)):
            for number in range(self.count(stage)):
                self.copy(stage, number).wait_send()


class Frames:
    def __init__(self, away, landing, sends, recvs):
        self.away, self.landing, self.sends, self.recvs = away, landing, sends, recvs

    def copy(self, distance):
        count = self.away.shape[0]
        frame = lax.rem(lax.axis_index("frame") + distance, count)
        return remote(
            self.away.at[frame], self.landing.at[distance - 1],
            self.sends.at[distance - 1], self.recvs.at[distance - 1], frame=frame,
        )

    def send(self, piece):
        count = self.away.shape[0]
        for frame in range(count):
            self.away[frame] = piece(frame)
        for distance in range(1, count):
            self.copy(distance).start()

    def send_one(self, frame, piece):
        count = self.away.shape[0]
        me = lax.axis_index("frame")
        self.away[frame] = piece
        distance = lax.rem(frame - me + count, count)

        @pl.when(frame != me)
        def _():
            remote(
                self.away.at[frame], self.landing.at[distance - 1],
                self.sends.at[distance - 1], self.recvs.at[distance - 1], frame=frame,
            ).start()

    def finish(self):
        total = self.away[lax.axis_index("frame")].astype(F32)
        for distance in range(1, self.away.shape[0]):
            self.copy(distance).wait_recv()
            total = total + self.landing[distance - 1].astype(F32)
        return total

    def drain(self):
        for distance in range(1, self.away.shape[0]):
            self.copy(distance).wait_send()


def run_of(ref, number, count):
    cols = ref.shape[1] // count
    low = number * cols // LANES * LANES
    high = -(-(number + 1) * cols // LANES) * LANES
    return ref[:, low:high][:, number * cols - low : (number + 1) * cols - low]


def cut(array, number, count):
    cols = array.shape[1] // count
    return array[:, number * cols : (number + 1) * cols]


def thirds_in_rows(values):
    high = values.astype(BF16).astype(F32)
    mid = (values - high).astype(BF16).astype(F32)
    low = (values - high) - mid
    return jnp.concatenate((high, mid, low, jnp.zeros_like(low)), axis=0).astype(BF16)


def side_by_side(tiles):
    return jnp.concatenate([tiles[i] for i in range(tiles.shape[0])], axis=1)


def backward_kernel(heads, clips, n, n_frame, r):
    step = pl.program_id(0)
    rows, width = r.tokens.shape[1:]
    tiles = 4
    half = n // 2
    share = width // n
    first_t = clips
    first_s = clips + tiles
    first_w = 2 * clips + tiles
    last = first_w + tiles - 1
    sibling = partner("clip", 0)
    barrier = pltpu.get_barrier_semaphore()
    bits = list(range(1, n.bit_length() - 1))
    frame = lax.axis_index("frame")
    place = lax.axis_index("clip")

    feed_in = Halving(r.sum_in, r.land_in, r.in_send, r.in_recv, bits)
    feed_out = Halving(r.sum_out, r.land_out, r.out_send, r.out_recv, bits[::-1])

    def units_of(name):
        sums, land = getattr(r, "sum_" + name), getattr(r, "land_" + name)
        sends, recvs = getattr(r, name + "_send"), getattr(r, name + "_recv")
        return [
            Halving(
                sums.at[pl.ds(i, 1)], land.at[pl.ds(i, 1)], sends.at[i], recvs.at[i],
                bits[:: 1 - 2 * (i % 2)],
            )
            for i in range(tiles)
        ]

    temporal, spatial = units_of("t"), units_of("s")
    stages = len(bits)

    regions = {"t": r.w_qkv_a_vmem, "s": r.w_qkv_b_vmem}

    def tile_cols(tile):
        return pl.ds(pl.multiple_of(lax.rem(tile, 3) * width, width), width)

    def tile_copies(name, tile):
        sends, recvs = getattr(r, name + "_core_send"), getattr(r, name + "_core_recv")
        return [
            remote(
                regions[name].at[share_rows(number, False, share), tile_cols(tile)],
                getattr(r, "core_" + name).at[tile, number],
                sends.at[tile, number], recvs.at[tile, number], clip=sibling,
            )
            for number in range(half)
        ]

    def tile_sent(name, tile):
        for copy in tile_copies(name, tile):
            copy.wait_send()

    def fold_core(name, which):
        sums, core = getattr(r, "sum_" + name), getattr(r, "core_" + name)
        for tile in which:
            for copy in tile_copies(name, tile):
                copy.wait_recv()
            sums[tile] = (sums[tile].astype(F32) + core[tile].astype(F32)).astype(BF16)

    frames = {
        name: Frames(
            getattr(r, "away_" + name), getattr(r, "near_" + name),
            getattr(r, name + "_z_send"), getattr(r, name + "_z_recv"),
        )
        for name in ("in", "out", "t", "s", "mod")
    }

    spaces = (r.left, r.left_out, r.grad_branch)

    def mod_tile(part):
        return pltpu.make_async_copy(
            r.w_mod.at[:, pl.ds(part * width, width)],
            spaces[part % 3].at[pl.ds(0, width)], r.mod_sems.at[part],
        )

    def mod_sums(total, parts):
        for part in parts:
            mod_tile(part).wait()
            term = dot_nt(thirds_in_rows(r.mods[part]), spaces[part % 3][:width])
            total = term if total is None else total + term
            if part + 3 < 9:
                mod_tile(part + 3).start()
        return total

    def send_mods(total):
        pad = r.mods.shape[1]
        total = total[:pad] + total[pad : 2 * pad] + total[2 * pad : 3 * pad]
        joined = side_by_side(r.mods)
        total = total * r.silu_grad[...]
        frames["mod"].send(
            lambda other: jnp.concatenate((total, cut(joined, other, n_frame)), axis=1)
        )

    def spread_mods(distance):
        return remote(
            r.mod_share, r.gathered.at[place], r.mod_send.at[distance - 1],
            r.mod_recv.at[distance - 1], clip=lax.rem(place + distance, n),
        )

    own_mods = pltpu.make_async_copy(r.mod_share, r.gathered.at[place], r.mod_sems.at[9])

    def to_frames(units, name, tile):
        owned = units[tile].own()[0]
        wide, narrow = owned[:, : 3 * width // tiles], owned[:, 3 * width // tiles :]
        count = n_frame // tiles
        for number in range(count):
            frames[name].send_one(
                tile * count + number,
                jnp.concatenate((cut(wide, number, count), cut(narrow, number, count)), axis=1),
            )

    def from_frames(name, wide, narrow):
        total = frames[name].finish()
        wide[...] = total[:, : wide.shape[1]]
        narrow[...] = total[:, wide.shape[1] :]

    def two_high(array):
        rows = array.shape[0] // 2
        return jnp.concatenate((array[:rows], array[rows:]), axis=1)

    loads = [
        pltpu.make_async_copy(r.keep_in, r.sum_in, r.load_sems.at[0]),
        pltpu.make_async_copy(r.came_in, r.core_t, r.load_sems.at[1]),
        pltpu.make_async_copy(r.keep_out, r.sum_out, r.load_sems.at[2]),
        pltpu.make_async_copy(r.came_out, r.core_s, r.load_sems.at[3]),
    ]
    lefts_t = [
        pltpu.make_async_copy(r.hidden_b, r.left, r.load_sems.at[4]),
        pltpu.make_async_copy(r.mixed_b, r.left_out, r.load_sems.at[5]),
        pltpu.make_async_copy(r.grad_branch_b, r.grad_branch, r.load_sems.at[6]),
    ]
    lefts_s = [
        pltpu.make_async_copy(r.hidden_a, r.left, r.load_sems.at[7]),
        pltpu.make_async_copy(r.mixed_a, r.left_out, r.load_sems.at[8]),
    ]
    r.w_qkv_a = Late(r.w_qkv_a_hbm, r.w_qkv_a_vmem, r.load_sems.at[9], first_s)

    @pl.when(step == 0)
    def _():
        for distance in range(1, n):
            greet(barrier, clip=lax.rem(place + distance, n))
        for distance in range(1, n_frame):
            greet(barrier, frame=lax.rem(frame + distance, n_frame))
        for copy in loads + lefts_t:
            copy.start()
        r.mods[...] = jnp.zeros_like(r.mods)
        for clip in range(clips):
            for row, part in enumerate((6, 7, 8, 5)):
                r.mods[part, clip : clip + 1] = r.sums[clip, row : row + 1]

    @pl.when(step < clips)
    def _():
        temporal_backward(r, step, pl.multiple_of(step * rows, rows))

    @pl.when(step == 0)
    def _():
        for copy in loads:
            copy.wait()
        for tile in range(tiles):
            r.sum_in[tile] = (
                r.sum_in[tile].astype(F32) + r.core_t[tile].astype(F32)
            ).astype(BF16)
        per = r.sum_out.shape[1] // tiles
        for tile in range(tiles):
            which = slice(tile * per, (tile + 1) * per)
            came = r.core_s[tile].reshape(r.sum_out[0, which].shape)
            r.sum_out[0, which] = (
                r.sum_out[0, which].astype(F32) + came.astype(F32)
            ).astype(BF16)
        pl.semaphore_wait(barrier, n - 1 + n_frame - 1)
        pl.semaphore_signal(
            r.free, inc=1, device_id={"clip": sibling}, device_id_type=pl.DeviceIdType.MESH
        )
        feed_in.send(0)
        feed_out.send(0)

    def weight_tile(name, tile):
        region = regions[name]
        for number in range(tiles):

            @pl.when(tile == number)
            def _():
                region[:, number % 3 * width : (number % 3 + 1) * width] = jnp.concatenate(
                    (
                        dot_tn(r.left[...], run_of(r.grad_qkv, number, tiles)),
                        dot_tn(r.left_out[...], run_of(r.grad_branch, number, tiles)),
                    ),
                    axis=1,
                ).astype(BF16)

        for copy in tile_copies(name, tile):
            copy.start()
        for number in range(half):
            getattr(r, "sum_" + name)[tile, number] = region[
                share_rows(number, True, share), tile_cols(tile)
            ]

    @pl.when((step >= first_t) & (step < first_s))
    def _():
        tile = step - first_t

        @pl.when(tile == 0)
        def _():
            for copy in lefts_t:
                copy.wait()
            pl.semaphore_wait(r.free, 1)

        pl.when(tile == 3)(lambda: tile_sent("t", 0))
        weight_tile("t", tile)

        @pl.when(tile == tiles - 1)
        def _():
            for copy in lefts_s:
                copy.start()

    @pl.when((step >= first_s) & (step < first_w))
    def _():
        clip = step - first_s

        @pl.when(clip == 0)
        def _():
            for tile in range(1, tiles):
                tile_sent("t", tile)
            r.w_qkv_a.copy.start()

        spatial_backward(r, heads, clip, pl.multiple_of(clip * rows, rows))

    @pl.when(step == first_s - 1)
    def _():
        for unit in (feed_in, feed_out):
            unit.fold(0)
            if stages > 1:
                unit.send(1)

    @pl.when(step == first_s)
    def _():
        for tile, unit in enumerate(temporal):
            fold_core("t", (tile,))
            unit.send(0)

    @pl.when(step == first_s + 1)
    def _():
        for stage in range(1, stages):
            for unit in (feed_in, feed_out):
                unit.fold(stage)
                if stage + 1 < stages:
                    unit.send(stage + 1)
        owned_in, owned_out = side_by_side(feed_in.own()), feed_out.own()[0]
        frames["in"].send(lambda other: cut(owned_in, other, n_frame))
        frames["out"].send(lambda other: two_high(cut(owned_out, other, n_frame)))

    @pl.when(step == first_s + 2)
    def _():
        for unit in temporal:
            unit.fold(0)
            if stages > 1:
                unit.send(1)

    @pl.when(step == first_s + 3)
    def _():
        for stage in range(1, stages):
            for tile, unit in enumerate(temporal):
                unit.fold(stage)
                if stage + 1 < stages:
                    unit.send(stage + 1)
                else:
                    to_frames(temporal, "t", tile)

    @pl.when(step >= first_w)
    def _():
        tile = step - first_w

        @pl.when(tile == 0)
        def _():
            for copy in lefts_s:
                copy.wait()

        pl.when(tile == 3)(lambda: tile_sent("s", 0))
        weight_tile("s", tile)

    for tile in range(tiles - 1):

        @pl.when(step == first_w + 1 + tile)
        def _():
            fold_core("s", (tile,))
            spatial[tile].send(0)

    @pl.when(step == last)
    def _():
        fold_core("s", (tiles - 1,))
        spatial[tiles - 1].send(0)
        for part in range(3):
            mod_tile(part).start()
        total = mod_sums(None, range(0, 3))
        for stage in range(stages):
            if stage == 1:
                total = mod_sums(total, range(3, 6))
            for tile, unit in enumerate(spatial):
                unit.fold(stage)
                if stage + 1 < stages:
                    unit.send(stage + 1)
                else:
                    to_frames(spatial, "s", tile)
                if stage == 0 and tile == 1:
                    r.done_in[...] = frames["in"].finish()
        total = mod_sums(total, range(3 if stages < 2 else 6, 9))
        send_mods(total)
        flat = frames["out"].finish()
        high = flat.shape[0]
        r.done_out[:high] = cut(flat, 0, 2)
        r.done_out[high:] = cut(flat, 1, 2)
        from_frames("t", r.done_tq, r.done_to)
        r.mod_share[...] = frames["mod"].finish()
        for distance in range(1, n):
            spread_mods(distance).start()
        own_mods.start()
        from_frames("s", r.done_sq, r.done_so)
        own_mods.wait()
        for distance in range(1, n):
            spread_mods(distance).wait()
        for unit in (feed_in, feed_out, *temporal, *spatial):
            unit.drain()
        for name in frames:
            frames[name].drain()
        for tile in range(1, tiles):
            tile_sent("s", tile)


def backward_call(fwd, tok, mod, spread, weights, modulate_w, silu_grad, n, n_frame):
    clips, rows, width = tok.shape
    ff = weights["mlp_in"].shape[1]
    heads = width // HEAD_DIM
    tokens_here = clips * rows
    tiles = 4
    half, share, tall = n // 2, width // n, ff // n
    first_s, first_w = clips + tiles, 2 * clips + tiles

    def struct(last, dtype=BF16):
        return jax.ShapeDtypeStruct((clips, rows, last), dtype)

    mod_spec = pl.BlockSpec(
        (1,) + mod.shape[1:],
        lambda s: (
            jnp.where(s < first_s, jnp.minimum(s, clips - 1), jnp.minimum(s - first_s, clips - 1)),
            0, 0,
        ),
    )
    anywhere = pl.BlockSpec(memory_space=pl.ANY)
    pad, mod_cols = silu_grad.shape[0], width + 9 * width // n_frame
    whole = pl.BlockSpec(fwd.sums.shape, lambda s: (0, 0, 0), pipeline_mode=pl.Buffered(1))
    whole_grad = pl.BlockSpec(silu_grad.shape, lambda s: (0, 0), pipeline_mode=pl.Buffered(1))
    ins = [
        ("mod", mod, mod_spec), ("sums", fwd.sums, whole), ("silu_grad", silu_grad, whole_grad),
        ("w_mod", modulate_w, anywhere),
    ]
    for name in ("q_prev", "q_own", "q_next", "sent_prev", "sent", "sent_next", "grad_q", "grad_b", "after_a"):
        array = getattr(fwd, name)
        ins.append((name, array, clip_spec(array, 0, clips, 1 if name in ("grad_q", "grad_b", "after_a") else 2)))
    for name, array in (
        ("tokens", tok), ("branch_a", fwd.branch_a), ("qkv_a", fwd.qkv_a), ("lse", fwd.lse)
    ):
        ins.append((name, array, clip_spec(array, first_s, clips, 1)))
    flat = (tokens_here, width)
    for name in ("hidden_b", "mixed_b", "grad_branch_b", "hidden_a", "mixed_a"):
        ins.append((name, getattr(fwd, name).reshape(flat), anywhere))
    core_shape = (tiles, half, share, width)
    ins += [
        ("keep_in", fwd.keep_in.reshape(core_shape), anywhere),
        ("came_in", fwd.came_in.reshape(core_shape), anywhere),
        ("keep_out", fwd.keep_out.reshape(1, half, tall, width), anywhere),
        ("came_out", fwd.came_out.reshape(core_shape), anywhere),
        ("w_qkv_a_hbm", weights["spatial_qkv"], anywhere),
    ]
    held = [
        ("spread", spread, 0), ("w_qkv_b", weights["temporal_qkv"], 0),
        ("w_out_a", weights["spatial_out"], first_s),
    ]
    grad_tokens = struct(width, F32)
    outs = [
        ("grad_tokens", grad_tokens, clip_spec(grad_tokens, first_s, clips, 1)),
        ("gathered", jax.ShapeDtypeStruct((n, pad, mod_cols), F32), None),
    ]
    dma = pltpu.SemaphoreType.DMA
    pieces = {
        "in": (share, ff // n_frame), "out": (tall, width // n_frame),
        "tq": (share, 3 * width // n_frame), "to": (share, width // n_frame),
        "sq": (share, 3 * width // n_frame), "so": (share, width // n_frame),
    }
    moved = half - 1
    scratch = [
        ("grad_a", pltpu.VMEM((clips, rows, width), F32)),
        ("grad_qkv", pltpu.VMEM((tokens_here, 3 * width), BF16)),
        ("grad_branch", pltpu.VMEM(flat, BF16)), ("left", pltpu.VMEM(flat, BF16)),
        ("left_out", pltpu.VMEM(flat, BF16)),
        ("w_qkv_a_vmem", pltpu.VMEM(weights["spatial_qkv"].shape, BF16)),
        ("sum_in", pltpu.VMEM(core_shape, BF16)), ("land_in", pltpu.VMEM((tiles, moved, share, width), BF16)),
        ("in_send", dma((moved,))), ("in_recv", dma((moved,))),
        ("sum_out", pltpu.VMEM((1, half, tall, width), BF16)),
        ("land_out", pltpu.VMEM((1, moved, tall, width), BF16)),
        ("out_send", dma((moved,))), ("out_recv", dma((moved,))),
        ("load_sems", dma((10,))), ("free", pltpu.SemaphoreType.REGULAR),
        ("mods", pltpu.VMEM((9, pad, width), F32)), ("mod_sems", dma((10,))),
        ("mod_share", pltpu.VMEM((pad, mod_cols), F32)),
        ("mod_send", dma((n - 1,))), ("mod_recv", dma((n - 1,))),
    ]
    for name in ("t", "s"):
        scratch += [
            ("sum_" + name, pltpu.VMEM(core_shape, BF16)), ("core_" + name, pltpu.VMEM(core_shape, BF16)),
            ("land_" + name, pltpu.VMEM((tiles, moved, share, width), BF16)),
            (name + "_send", dma((tiles, moved))), (name + "_recv", dma((tiles, moved))),
            (name + "_core_send", dma((tiles, half))), (name + "_core_recv", dma((tiles, half))),
        ]
    for name, dims in pieces.items():
        shape = jax.ShapeDtypeStruct(dims, F32)
        outs.append(("done_" + name, shape, pl.BlockSpec(shape.shape, lambda s: (0, 0))))
    packed = {
        "in": (share, ff // n_frame), "out": (tall // 2, 2 * width // n_frame),
        "t": (share, 4 * width // n_frame), "s": (share, 4 * width // n_frame),
        "mod": (pad, mod_cols),
    }
    for name, dims in packed.items():
        kind = F32 if name == "mod" else BF16
        scratch += [
            ("away_" + name, pltpu.VMEM((n_frame, *dims), kind)),
            ("near_" + name, pltpu.VMEM((n_frame - 1, *dims), kind)),
            (name + "_z_send", dma((n_frame - 1,))), (name + "_z_recv", dma((n_frame - 1,))),
        ]
    return run_kernel(
        functools.partial(backward_kernel, heads, clips, n, n_frame), first_w + tiles,
        ins, held, outs, scratch, 2 * tokens_here * width * width * 20, collective=2,
    )


def thirds(values):
    high = values.astype(BF16)
    rest = values - high.astype(F32)
    mid = rest.astype(BF16)
    low = (rest - mid.astype(F32)).astype(BF16)
    return jnp.concatenate((high, mid, low), axis=0)


def local(
    tokens, target, loss_weight, timesteps, offsets, cond_table, modulate_w,
    spatial_qkv, spatial_out, temporal_qkv, temporal_out, mlp_in, mlp_out,
):
    clips, frames, patches, width = tokens.shape
    steps = cond_table.shape[0]
    heads = width // HEAD_DIM
    n_clip = lax.axis_size("clip")
    n_frame = lax.axis_size("frame")
    clip_at = lax.axis_index("clip")
    frame_at = lax.axis_index("frame")
    flat = (clips, patches, width)
    tok = tokens.reshape(flat)
    tgt = target.reshape(flat)

    condition = jnp.take(cond_table, timesteps, axis=0, mode="clip")
    cond_low = jax.nn.silu(condition).astype(BF16)
    cond_here = lax.dynamic_slice_in_dim(condition, clip_at * clips, clips)
    _, silu_pull = jax.vjp(jax.nn.silu, cond_here)
    low_here = lax.dynamic_slice_in_dim(cond_low, clip_at * clips, clips)
    mod = jnp.dot(low_here, modulate_w, preferred_element_type=F32).reshape(clips, 9, width)

    half = width // 2
    positions = (offsets + frame_at).astype(F32)
    freqs = jnp.exp(jnp.arange(half, dtype=F32) * (-math.log(10000.0) / half))
    angles = positions[:, None] * freqs
    posenc = jnp.concatenate((jnp.sin(angles), jnp.cos(angles)), axis=-1)[:, None, :]

    head_of = np.arange(width) // HEAD_DIM
    lane_ids = np.arange(LANES)
    to_heads = jnp.asarray((head_of[:, None] == lane_ids[None, :]).astype(BF16))
    tall = np.arange(2 * LANES) - LANES
    spread = jnp.asarray((tall[:, None] == head_of[None, :]).astype(BF16))
    group, inside = np.divmod(np.arange(6 * LANES), LANES)
    slot_at = np.where(inside < heads, group * SLOT + inside, -1)
    pack = jnp.asarray((slot_at[:, None] == lane_ids[None, :]).astype(BF16))
    weights = {
        "spatial_qkv": spatial_qkv, "spatial_out": spatial_out, "temporal_qkv": temporal_qkv,
        "temporal_out": temporal_out, "mlp_in": mlp_in, "mlp_out": mlp_out,
    }
    fwd = forward_call(
        tok, tgt, mod, posenc, loss_weight, (to_heads, spread, pack), weights, n_clip
    )

    pad = -(-clips // 8) * 8
    silu_grad = jnp.pad(silu_pull(jnp.ones_like(cond_here))[0], ((0, pad - clips), (0, 0)))
    bwd = backward_call(fwd, tok, mod, spread, weights, modulate_w, silu_grad, n_clip, n_frame)
    gathered = bwd.gathered[:, :clips].reshape(n_clip * clips, -1)
    onehot = (timesteps[:, None] == jnp.arange(steps, dtype=jnp.int32)[None, :]).astype(BF16)
    grad_table = dot_tn(jnp.concatenate((onehot,) * 3, axis=0), thirds(gathered[:, :width]))
    mod_rows = width // n_clip
    low_rows = lax.dynamic_slice_in_dim(cond_low, clip_at * mod_rows, mod_rows, axis=1)
    grad_modulate = dot_tn(jnp.concatenate((low_rows,) * 3, axis=0), thirds(gathered[:, width:]))
    return (
        fwd.output.reshape(tokens.shape),
        bwd.grad_tokens.reshape(tokens.shape),
        grad_table,
        grad_modulate,
        bwd.done_sq,
        bwd.done_so,
        bwd.done_tq,
        bwd.done_to,
        bwd.done_in,
        bwd.done_out,
    )


def solution(mesh):
    placed = (
        P("clip", "frame", None, None), P("clip", "frame", None, None), P("clip"), P(), P("clip"),
    ) + (P(),) * 8
    return jax.shard_map(
        local,
        mesh=mesh,
        in_specs=placed,
        out_specs=(
            P("clip", "frame", None, None), P("clip", "frame", None, None), P(),
        ) + (P("clip", "frame"),) * 7,
        check_vma=False,
    )
```

```python
import functools
import math

import jax
import jax.numpy as jnp
import numpy as np
from jax import lax
from jax.experimental import pallas as pl
from jax.experimental.pallas import tpu as pltpu
from jax.sharding import PartitionSpec as P

HEAD_DIM = 64
NORM_EPSILON = 1e-06
F32 = jnp.float32
BF16 = jnp.bfloat16
LANES = 128
SLOT = 16
NO_KEY = -1e30
VMEM_LIMIT = 60 * 2**20
GROUP = 2
GELU_A = math.sqrt(2.0 / math.pi)
GELU_B = 0.044715


def dot(left, right):
    return lax.dot_general(left, right, (((1,), (0,)), ((), ())), preferred_element_type=F32)


def dot_nt(left, right):
    return lax.dot_general(left, right, (((1,), (1,)), ((), ())), preferred_element_type=F32)


def dot_tn(left, right):
    return lax.dot_general(left, right, (((0,), (0,)), ((), ())), preferred_element_type=F32)


def norm(values):
    centred = values - jnp.mean(values, axis=-1, keepdims=True)
    inv_std = lax.rsqrt(jnp.mean(centred * centred, axis=-1, keepdims=True) + NORM_EPSILON)
    return centred * inv_std, inv_std


def norm_back(grad_hidden, normed, inv_std, scale_plus):
    grad_normed = grad_hidden * scale_plus
    mean_grad = jnp.mean(grad_normed, axis=-1, keepdims=True)
    mean_cross = jnp.mean(grad_normed * normed, axis=-1, keepdims=True)
    return inv_std * (grad_normed - mean_grad - normed * mean_cross)


def column_sum(values):
    return jnp.sum(values, axis=0, keepdims=True)


def side_masks(dtype, value):
    lane = lax.broadcasted_iota(jnp.int32, (1, LANES), 1)
    return [jnp.where((lane < HEAD_DIM) == (side == 0), value, 0.0).astype(dtype) for side in (0, 1)]


class Refs:
    def __init__(self, names, refs):
        self.__dict__.update(zip(names, refs, strict=True))


class Late:
    def __init__(self, source, ref, sem, step):
        self.ref = ref
        self.copy = pltpu.make_async_copy(source, ref, sem)
        self.step = step
        self.waited = False

    def __getitem__(self, index):
        if not self.waited:
            pl.when(pl.program_id(0) == self.step)(self.copy.wait)
            self.waited = True
        return self.ref[index]


def partner(axis, bit):
    me = lax.axis_index(axis)
    return me + (1 << bit) - (2 << bit) * lax.rem(me // (1 << bit), 2)


def remote(source, target, send_sem, recv_sem, **where):
    return pltpu.make_async_remote_copy(
        src_ref=source, dst_ref=target, send_sem=send_sem, recv_sem=recv_sem,
        device_id=where, device_id_type=pl.DeviceIdType.MESH,
    )


def greet(barrier, **where):
    pl.semaphore_signal(barrier, inc=1, device_id=where, device_id_type=pl.DeviceIdType.MESH)


def run_kernel(body, steps, ins, weights, outs, scratch, flops, collective=None):
    anywhere = pl.BlockSpec(memory_space=pl.ANY)
    names = [name for name, *_ in ins] + [name + "_hbm" for name, *_ in weights]
    names += [name for name, *_ in outs]
    names += [name + "_vmem" for name, *_ in weights] + ["weight_sems"]
    names += [name for name, _ in scratch]

    def kernel(*refs):
        r = Refs(names, refs)
        lates = []
        for number, (name, _, step) in enumerate(weights):
            late = Late(
                getattr(r, name + "_hbm"), getattr(r, name + "_vmem"), r.weight_sems.at[number], step
            )
            lates.append(late)
            setattr(r, name, late)

        @pl.when(pl.program_id(0) == 0)
        def _():
            for late in lates:
                if late.step == 0:
                    late.copy.start()

        body(r)

        @pl.when(pl.program_id(0) == 0)
        def _():
            for late in lates:
                if late.step > 0:
                    late.copy.start()

    arrays = [array for _, array, _ in ins] + [array for _, array, _ in weights]
    shapes = [shape for _, shape, _ in outs]
    touched = sum(math.prod(a.shape) * a.dtype.itemsize for a in arrays + shapes)
    params = {} if collective is None else {"collective_id": collective, "has_side_effects": True}
    done = pl.pallas_call(
        kernel,
        grid=(steps,),
        in_specs=[spec for *_, spec in ins] + [anywhere] * len(weights),
        out_specs=[spec or anywhere for *_, spec in outs],
        out_shape=shapes,
        scratch_shapes=[pltpu.VMEM(a.shape, a.dtype) for _, a, _ in weights]
        + [pltpu.SemaphoreType.DMA((max(len(weights), 1),))]
        + [shape for _, shape in scratch],
        compiler_params=pltpu.CompilerParams(vmem_limit_bytes=VMEM_LIMIT, **params),
        cost_estimate=pl.CostEstimate(flops=flops, bytes_accessed=touched, transcendentals=0),
    )(*arrays)
    return Refs([name for name, *_ in outs], done)


def clip_spec(array, first, clips, depth=None):
    rest = array.shape[1:]
    mode = {} if depth is None else {"pipeline_mode": pl.Buffered(depth)}
    return pl.BlockSpec(
        (1,) + rest, lambda s: (jnp.clip(s - first, 0, clips - 1),) + (0,) * len(rest), **mode
    )


def spatial_forward(r, heads, clip):
    width = r.tokens.shape[-1]
    rows = r.tokens.shape[1]
    mod = r.mod
    inputs = r.tokens[0].astype(F32)
    normed, _ = norm(inputs)
    hidden = (normed * (1.0 + mod[0, 1:2]) + mod[0, 0:1]).astype(BF16)
    r.hidden_a[0] = hidden
    for part in range(3):
        cols = slice(part * width, (part + 1) * width)
        r.qkv_a[0, :, cols] = dot(hidden, r.w_qkv_a[:, cols]).astype(BF16)
    scaled, plain = side_masks(BF16, HEAD_DIM**-0.5), side_masks(BF16, 1.0)
    for first in range(0, heads // 2, 3):
        pairs = range(first, min(first + 3, heads // 2))
        scores, softs = [], []
        for pair in pairs:
            query, key = (columns(r.qkv_a, part, pair) for part in (0, 1))
            scores.append(dot_nt(both_sides(key, scaled), query))
        for pair, score in zip(pairs, scores):
            halves = []
            for side in range(2):
                mine = score[side * rows : (side + 1) * rows]
                top = jnp.max(mine, axis=0, keepdims=True)
                grown = jnp.exp(mine - top)
                total = jnp.sum(grown, axis=0, keepdims=True)
                halves.append((grown * (1.0 / total)).astype(BF16))
                head = 2 * pair + side
                r.lse[0, head : head + 1] = top + jnp.log(total)
            softs.append(jnp.concatenate(halves, axis=0))
        for pair, soft in zip(pairs, softs):
            value = columns(r.qkv_a, 2, pair)
            r.mixed_a[0, :, pair * LANES : (pair + 1) * LANES] = dot_tn(
                soft, both_sides(value, plain)
            ).astype(BF16)
    branch_a = dot(r.mixed_a[0], r.w_out_a[...])
    r.branch_a[0] = branch_a.astype(BF16)
    after_a = inputs + mod[0, 2:3] * branch_a
    r.after_held[clip] = after_a
    normed_b, _ = norm(after_a)
    r.hidden_held[clip] = (
        normed_b * (1.0 + mod[0, 4:5]) + (mod[0, 3:4] + r.posenc[0])
    ).astype(BF16)


def both_sides(array, masks):
    return jnp.concatenate((array * masks[0], array * masks[1]), axis=0)


def columns(ref, part, pair):
    start = part * (ref.shape[-1] // 3) + pair * LANES
    return ref[0, :, start : start + LANES]


def by_head(left, right, to_heads):
    return dot(left * right, to_heads)


def middle(r, clip, rows_at):
    width = r.target.shape[-1]
    rows = r.target.shape[1]
    ff = r.act.shape[-1]
    scale_qk = HEAD_DIM**-0.5
    mod = r.mod
    own_rows = pl.ds(rows_at, rows)
    store = r.w_qkv_a_vmem

    def kept(number, part):
        return store[number * rows : (number + 1) * rows, part * width : (part + 1) * width]

    three = jnp.concatenate((r.hidden_prev[clip], r.hidden_held[clip], r.hidden_next[clip]), axis=0)
    for part in range(3):
        cols = slice(part * width, (part + 1) * width)
        value = dot(three, r.w_qkv_b[:, cols]).astype(BF16)
        store[:, cols] = value
        if part == 0:
            for number, out in enumerate((r.q_prev, r.q_own, r.q_next)):
                out[0] = value[number * rows : (number + 1) * rows]
    frame = lax.axis_index("frame")
    absent = (frame == 0, None, frame == lax.axis_size("frame") - 1)
    scores = []
    for number in range(3):
        raw = by_head(kept(1, 0), kept(number, 1), r.to_heads[...]) * scale_qk
        if absent[number] is not None:
            raw = raw + jnp.where(absent[number], NO_KEY, 0.0)
        scores.append(raw)
    top = jnp.maximum(jnp.maximum(scores[0], scores[1]), scores[2])
    grown = [jnp.exp(entry - top) for entry in scores]
    inverse = 1.0 / (grown[0] + grown[1] + grown[2])
    soft = [entry * inverse for entry in grown]
    soft_low = [entry.astype(BF16) for entry in soft]
    to_width = r.spread[LANES : 2 * LANES]
    total = None
    for number in range(3):
        term = dot(soft_low[number], to_width) * kept(number, 2).astype(F32)
        total = term if total is None else total + term
    mixed = total.astype(BF16)
    r.mixed_b[0] = mixed
    branch_b = dot(mixed, r.w_out_b[...])
    r.grad_b[0] = branch_b
    after_b = r.after_held[clip] + mod[0, 5:6] * branch_b
    normed_c, inv_c = norm(after_b)
    hidden = (normed_c * (1.0 + mod[0, 7:8]) + mod[0, 6:7]).astype(BF16)
    r.hidden_c[own_rows, :] = hidden
    parts = ff // width
    ahead = dot(hidden, r.w_in[:, :width])
    for part in range(parts):
        cols = slice(part * width, (part + 1) * width)
        upward = ahead
        if part + 1 < parts:
            ahead = dot(hidden, r.w_in[:, (part + 1) * width : (part + 2) * width])
        squared = upward * upward
        bent = jnp.tanh(upward * (GELU_A + (GELU_A * GELU_B) * squared))
        share = 0.5 + 0.5 * bent
        r.act[own_rows, cols] = (upward * share).astype(BF16)
        steep = (1.0 - bent * bent) * (0.5 * GELU_A + (1.5 * GELU_A * GELU_B) * squared)
        r.grad_up[own_rows, cols] = (share + upward * steep).astype(BF16)
    branch_c = dot(r.act[own_rows, :], r.w_mlp[...])
    result = after_b + mod[0, 8:9] * branch_c
    r.output[0] = result.astype(BF16)
    grad_result = r.weight[clip] * (result - r.target[0].astype(F32))
    r.sums[0, 2:3] = column_sum(grad_result * branch_c)
    low_c = (mod[0, 8:9] * grad_result).astype(BF16)
    r.grad_branch_c[own_rows, :] = low_c
    ahead = dot_nt(low_c, r.w_mlp[:width, :])
    for part in range(parts):
        cols = slice(part * width, (part + 1) * width)
        grad_act = ahead
        if part + 1 < parts:
            ahead = dot_nt(low_c, r.w_mlp[(part + 1) * width : (part + 2) * width, :])
        r.grad_up[own_rows, cols] = (grad_act * r.grad_up[own_rows, cols].astype(F32)).astype(BF16)
    grad_hidden = dot_nt(r.grad_up[own_rows, :], r.w_in[...])
    r.sums[0, 0:1] = column_sum(grad_hidden)
    r.sums[0, 1:2] = column_sum(grad_hidden * normed_c)
    grad_after = grad_result + norm_back(grad_hidden, normed_c, inv_c, 1.0 + mod[0, 7:8])
    r.sums[0, 3:4] = column_sum(grad_after * r.grad_b[0])
    r.grad_b[0] = grad_after
    low_b = (mod[0, 5:6] * grad_after).astype(BF16)
    r.grad_branch_b[0] = low_b
    grad_mixed = dot_nt(low_b, r.w_out_b[...]).astype(BF16)
    grad_soft = [by_head(grad_mixed, kept(number, 2), r.to_heads[...]) for number in range(3)]
    inner = soft[0] * grad_soft[0] + soft[1] * grad_soft[1] + soft[2] * grad_soft[2]
    grad_scores = [(soft[number] * (grad_soft[number] - inner)).astype(BF16) for number in range(3)]
    total = None
    for number in range(3):
        term = dot(grad_scores[number], to_width) * kept(number, 1).astype(F32)
        total = term if total is None else total + term
    r.grad_q[0] = (total * scale_qk).astype(BF16)
    r.sent_held[clip, :, :width] = grad_mixed
    r.sent_held[clip, :, width:] = dot(
        jnp.concatenate(soft_low + grad_scores, axis=1), r.pack[...]
    ).astype(BF16)


def share_rows(number, keep, share):
    core = lax.rem(lax.axis_index("clip"), 2)
    spot = 2 * number + (core if keep else 1 - core)
    return pl.ds(pl.multiple_of(spot * share, share), share)


def forward_kernel(heads, clips, n, r):
    step = pl.program_id(0)
    rows, width = r.tokens.shape[1:]
    ff = r.act.shape[-1]
    in_steps = ff // width
    out_steps = n // 2
    share = ff // n
    last = 2 * clips + in_steps + out_steps - 1
    frame = lax.axis_index("frame")
    has_prev = frame > 0
    has_next = frame < lax.axis_size("frame") - 1
    no_prev = jnp.logical_not(has_prev)
    no_next = jnp.logical_not(has_next)
    core = lax.rem(lax.axis_index("clip"), 2)
    sibling = partner("clip", 0)
    barrier = pltpu.get_barrier_semaphore()

    def halo(way, clip):
        return remote(
            r.hidden_held.at[clip], (r.hidden_prev, r.hidden_next)[way].at[clip],
            r.halo_send.at[way, clip], r.halo_recv.at[way, clip],
            frame=frame + 1 if way == 0 else frame - 1,
        )

    def packet(way, clip):
        return remote(
            r.sent_held.at[clip], (r.sent_prev, r.sent_next)[way].at[clip],
            r.sent_send.at[way, clip], r.sent_recv.at[way, clip],
            frame=frame + 1 if way == 0 else frame - 1,
        )

    low_share = width // n

    def in_tile(tile):
        return [
            remote(
                r.stage.at[lax.rem(tile, 2), share_rows(number, False, low_share)],
                r.came_in.at[tile, number],
                r.in_send.at[tile, number], r.in_recv.at[tile, number], clip=sibling,
            )
            for number in range(n // 2)
        ]

    def in_kept(tile):
        return [
            pltpu.make_async_copy(
                r.stage.at[lax.rem(tile, 2), share_rows(number, True, low_share)],
                r.keep_in.at[tile, number], r.in_keep.at[tile, number],
            )
            for number in range(n // 2)
        ]

    def in_sent(tile):
        for copy in in_tile(tile):
            copy.wait_send()
        for copy in in_kept(tile):
            copy.wait()

    def out_part(tile, which):
        return r.stage.at[
            lax.rem(tile + in_steps, 2), pl.ds(pl.multiple_of(which * share, share), share)
        ]

    def out_tile(tile):
        return remote(
            out_part(tile, 1 - core), r.came_out.at[tile],
            r.out_send.at[tile], r.out_recv.at[tile], clip=sibling,
        )

    def out_kept(tile):
        return pltpu.make_async_copy(
            out_part(tile, core), r.keep_out.at[tile], r.out_keep.at[tile]
        )

    def save(clip):
        return [
            pltpu.make_async_copy(r.after_held.at[clip], r.after_a.at[clip], r.save_sems.at[0, clip]),
            pltpu.make_async_copy(
                r.hidden_held.at[clip], r.hidden_b.at[clip], r.save_sems.at[1, clip]
            ),
        ]

    def save_sent(clip):
        return pltpu.make_async_copy(r.sent_held.at[clip], r.sent.at[clip], r.save_sems.at[2, clip])

    def fill(way, clip):
        zeros = (r.hidden_prev, r.hidden_next)[way].at[clip]
        target = (r.sent_prev, r.sent_next)[way].at[clip]
        return [
            pltpu.make_async_copy(zeros, target.at[:, pl.ds(0, width)], r.save_sems.at[3, clip]),
            pltpu.make_async_copy(
                zeros.at[:, pl.ds(0, LANES)], target.at[:, pl.ds(width, LANES)],
                r.save_sems.at[4, clip],
            ),
        ]

    @pl.when(step == 0)
    def _():
        greet(barrier, clip=sibling)
        pl.when(has_prev)(lambda: greet(barrier, frame=frame - 1))
        pl.when(has_next)(lambda: greet(barrier, frame=frame + 1))

        @pl.when(no_prev)
        def _():
            r.hidden_prev[...] = jnp.zeros_like(r.hidden_prev)
            for clip in range(clips):
                for copy in fill(0, clip):
                    copy.start()

        @pl.when(no_next)
        def _():
            r.hidden_next[...] = jnp.zeros_like(r.hidden_next)
            for clip in range(clips):
                for copy in fill(1, clip):
                    copy.start()

    @pl.when(step < clips)
    def _():
        spatial_forward(r, heads, step)

        @pl.when(step == 0)
        def _():
            pl.semaphore_wait(
                barrier, 1 + jnp.where(has_prev, 1, 0) + jnp.where(has_next, 1, 0)
            )

        pl.when(has_next)(lambda: halo(0, step).start())
        pl.when(has_prev)(lambda: halo(1, step).start())
        for copy in save(step):
            copy.start()

    @pl.when((step >= clips) & (step < 2 * clips))
    def _():
        clip = step - clips
        pl.when(has_prev)(lambda: halo(0, clip).wait_recv())
        pl.when(has_next)(lambda: halo(1, clip).wait_recv())
        middle(r, clip, pl.multiple_of(clip * rows, rows))
        pl.when(has_next)(lambda: packet(0, clip).start())
        pl.when(has_prev)(lambda: packet(1, clip).start())
        save_sent(clip).start()

    @pl.when((step >= 2 * clips) & (step < 2 * clips + in_steps))
    def _():
        tile = step - 2 * clips

        pl.when(tile >= 2)(lambda: in_sent(tile - 2))
        cols = pl.ds(pl.multiple_of(tile * width, width), width)
        r.stage[lax.rem(tile, 2), :width] = dot_tn(r.hidden_c[...], r.grad_up[:, cols]).astype(BF16)
        for copy in in_tile(tile) + in_kept(tile):
            copy.start()

    @pl.when(step >= 2 * clips + in_steps)
    def _():
        tile = step - 2 * clips - in_steps

        pl.when(tile < 2)(lambda: in_sent(in_steps + tile - 2))

        @pl.when(tile >= 2)
        def _():
            out_tile(tile - 2).wait_send()
            out_kept(tile - 2).wait()

        cols = pl.ds(pl.multiple_of(tile * 2 * share, 2 * share), 2 * share)
        r.stage[lax.rem(tile + in_steps, 2), : 2 * share] = dot_tn(
            r.act[:, cols], r.grad_branch_c[...]
        ).astype(BF16)
        out_tile(tile).start()
        out_kept(tile).start()

    @pl.when(step == last)
    def _():
        for clip in range(clips):
            for copy in save(clip):
                copy.wait()
            save_sent(clip).wait()

            @pl.when(has_next)
            def _():
                halo(0, clip).wait_send()
                packet(0, clip).wait_send()
                packet(1, clip).wait_recv()

            @pl.when(has_prev)
            def _():
                halo(1, clip).wait_send()
                packet(1, clip).wait_send()
                packet(0, clip).wait_recv()

            for way, absent in ((0, no_prev), (1, no_next)):

                @pl.when(absent)
                def _():
                    for copy in fill(way, clip):
                        copy.wait()

        for tile in range(in_steps):
            for copy in in_tile(tile):
                copy.wait_recv()
        for tile in range(out_steps):
            out_tile(tile).wait_recv()
        for tile in range(out_steps - 2, out_steps):
            out_tile(tile).wait_send()
            out_kept(tile).wait()


def forward_call(tok, target, mod, posenc, weight, tables, weights, n):
    clips, rows, width = tok.shape
    ff = weights["mlp_in"].shape[1]
    heads = width // HEAD_DIM
    tokens_here = clips * rows
    in_steps, out_steps, share = ff // width, n // 2, ff // n
    to_heads, spread, pack = tables

    def struct(last, dtype=BF16):
        return jax.ShapeDtypeStruct((clips, rows, last), dtype)

    def early(array):
        return clip_spec(array, 0, clips)

    def late(array):
        return clip_spec(array, clips, clips)

    mod_spec = pl.BlockSpec(
        (1,) + mod.shape[1:],
        lambda s: (jnp.where(s < clips, s, jnp.minimum(s - clips, clips - 1)), 0, 0),
    )
    ins = [
        ("tokens", tok, early(tok)), ("posenc", posenc, early(posenc)), ("mod", mod, mod_spec),
        ("target", target, clip_spec(target, clips, clips, 1)), ("weight", weight, pl.BlockSpec(memory_space=pltpu.SMEM)),
    ]
    held = [
        ("w_qkv_a", weights["spatial_qkv"], 0), ("w_out_a", weights["spatial_out"], 0),
        ("w_qkv_b", weights["temporal_qkv"], clips), ("to_heads", to_heads, clips),
        ("spread", spread, clips), ("w_out_b", weights["temporal_out"], clips),
        ("w_in", weights["mlp_in"], clips), ("w_mlp", weights["mlp_out"], clips), ("pack", pack, clips),
    ]
    outs = []
    for name, shape in (
        ("hidden_a", struct(width)), ("qkv_a", struct(3 * width)), ("mixed_a", struct(width)),
        ("branch_a", struct(width)),
        ("lse", jax.ShapeDtypeStruct((clips, -(-heads // 8) * 8, rows), F32)),
    ):
        outs.append((name, shape, clip_spec(shape, 0, clips, 1)))
    for name, shape in (
        ("output", struct(width)), ("grad_b", struct(width, F32)), ("mixed_b", struct(width)),
        ("grad_branch_b", struct(width)), ("q_own", struct(width)), ("q_prev", struct(width)),
        ("q_next", struct(width)), ("grad_q", struct(width)),
        ("sums", jax.ShapeDtypeStruct((clips, 8, width), F32)),
    ):
        outs.append((name, shape, clip_spec(shape, clips, clips, 1)))
    outs += [
        ("after_a", struct(width, F32), None), ("hidden_b", struct(width), None),
        ("sent", struct(width + LANES), None), ("sent_prev", struct(width + LANES), None),
        ("sent_next", struct(width + LANES), None),
    ]
    tile_in = jax.ShapeDtypeStruct((in_steps, n // 2, width // n, width), BF16)
    tile_out = jax.ShapeDtypeStruct((out_steps, share, width), BF16)
    outs += [
        ("keep_in", tile_in, None), ("came_in", tile_in, None), ("keep_out", tile_out, None),
        ("came_out", tile_out, None),
    ]
    dma = pltpu.SemaphoreType.DMA
    scratch = [
        ("after_held", pltpu.VMEM((clips, rows, width), F32)),
        ("hidden_held", pltpu.VMEM((clips, rows, width), BF16)),
        ("hidden_prev", pltpu.VMEM((clips, rows, width), BF16)),
        ("hidden_next", pltpu.VMEM((clips, rows, width), BF16)),
        ("sent_held", pltpu.VMEM((clips, rows, width + LANES), BF16)),
        ("act", pltpu.VMEM((tokens_here, ff), BF16)),
        ("grad_up", pltpu.VMEM((tokens_here, ff), BF16)),
        ("hidden_c", pltpu.VMEM((tokens_here, width), BF16)),
        ("grad_branch_c", pltpu.VMEM((tokens_here, width), BF16)),
        ("stage", pltpu.VMEM((2, max(width, 2 * share), width), BF16)),
        ("halo_send", dma((2, clips))), ("halo_recv", dma((2, clips))),
        ("sent_send", dma((2, clips))), ("sent_recv", dma((2, clips))),
        ("in_send", dma((in_steps, n // 2))), ("in_recv", dma((in_steps, n // 2))),
        ("in_keep", dma((in_steps, n // 2))), ("out_send", dma((out_steps,))),
        ("out_recv", dma((out_steps,))), ("out_keep", dma((out_steps,))),
        ("save_sems", dma((5, clips))),
    ]
    return run_kernel(
        functools.partial(forward_kernel, heads, clips, n), 2 * clips + in_steps + out_steps,
        ins, held, outs, scratch, 2 * tokens_here * width * width * 46, collective=1,
    )


def temporal_backward(r, clip, rows_at):
    width = r.tokens.shape[-1]
    rows = r.tokens.shape[1]
    scale_qk = HEAD_DIM**-0.5
    own_rows = pl.ds(rows_at, rows)
    grad_key = None
    grad_value = None
    for number, (source, query) in enumerate(
        ((r.sent_prev, r.q_prev), (r.sent, r.q_own), (r.sent_next, r.q_next))
    ):
        other = 2 - number
        table = source[0, :, width:]
        low = LANES - SLOT * other
        soft = dot(table, r.spread[low : low + LANES])
        low = LANES - SLOT * (3 + other)
        score = dot(table, r.spread[low : low + LANES])
        key_term = score * query[0].astype(F32)
        value_term = soft * source[0, :, :width].astype(F32)
        grad_key = key_term if grad_key is None else grad_key + key_term
        grad_value = value_term if grad_value is None else grad_value + value_term
    r.grad_qkv[own_rows, :width] = r.grad_q[0]
    r.grad_qkv[own_rows, width : 2 * width] = (grad_key * scale_qk).astype(BF16)
    r.grad_qkv[own_rows, 2 * width :] = grad_value.astype(BF16)
    grad_hidden = dot_nt(r.grad_qkv[own_rows, :], r.w_qkv_b[...])
    normed_b, inv_b = norm(r.after_a[0])
    r.mods[3, pl.ds(clip, 1)] = column_sum(grad_hidden)
    r.mods[4, pl.ds(clip, 1)] = column_sum(grad_hidden * normed_b)
    r.grad_a[clip] = r.grad_b[0] + norm_back(grad_hidden, normed_b, inv_b, 1.0 + r.mod[0, 4:5])


def spatial_backward(r, heads, clip, rows_at):
    width = r.tokens.shape[-1]
    rows = r.tokens.shape[1]
    scale_qk = HEAD_DIM**-0.5
    own_rows = pl.ds(rows_at, rows)
    mod = r.mod
    r.mods[2, pl.ds(clip, 1)] = column_sum(r.grad_a[clip] * r.branch_a[0].astype(F32))
    low_a = (mod[0, 2:3] * r.grad_a[clip]).astype(BF16)
    r.grad_branch[own_rows, :] = low_a
    grad_mixed = dot_nt(low_a, r.w_out_a[...]).astype(BF16)
    scaled, plain = side_masks(BF16, scale_qk), side_masks(BF16, 1.0)
    lane = lax.broadcasted_iota(jnp.int32, (1, LANES), 1)
    for first in range(0, heads // 2, GROUP):
        pairs = range(first, min(first + GROUP, heads // 2))
        scores, grads, softs, backs = [], [], [], []
        for pair in pairs:
            gm = grad_mixed[:, pair * LANES : (pair + 1) * LANES]
            scores.append(
                dot_nt(both_sides(columns(r.qkv_a, 1, pair), scaled), columns(r.qkv_a, 0, pair))
            )
            grads.append(dot_nt(both_sides(columns(r.qkv_a, 2, pair), plain), gm))
        for pair, score, grad in zip(pairs, scores, grads):
            low, back = [], []
            for side in range(2):
                mine = slice(side * rows, (side + 1) * rows)
                head = 2 * pair + side
                soft = jnp.exp(score[mine] - r.lse[0, head : head + 1])
                inner = jnp.sum(soft * grad[mine], axis=0, keepdims=True)
                back.append((soft * (grad[mine] - inner)).astype(BF16))
                low.append(soft.astype(BF16))
            softs.append(jnp.concatenate(low, axis=0))
            backs.append(jnp.concatenate(back, axis=0))
        for pair, soft, back in zip(pairs, softs, backs):
            gm = grad_mixed[:, pair * LANES : (pair + 1) * LANES]
            query, key = (columns(r.qkv_a, part, pair) for part in (0, 1))
            start = pair * LANES
            r.grad_qkv[own_rows, start : start + LANES] = dot_tn(
                back, both_sides(key, scaled)
            ).astype(BF16)
            for part, total, factor in ((1, dot(back, query), scale_qk), (2, dot(soft, gm), 1.0)):
                joined = jnp.where(lane < HEAD_DIM, total[:rows], total[rows:])
                start = part * width + pair * LANES
                r.grad_qkv[own_rows, start : start + LANES] = (joined * factor).astype(BF16)
    grad_hidden = dot_nt(r.grad_qkv[own_rows, :], r.w_qkv_a[...])
    normed_a, inv_a = norm(r.tokens[0].astype(F32))
    r.mods[0, pl.ds(clip, 1)] = column_sum(grad_hidden)
    r.mods[1, pl.ds(clip, 1)] = column_sum(grad_hidden * normed_a)
    r.grad_tokens[0] = r.grad_a[clip] + norm_back(
        grad_hidden, normed_a, inv_a, 1.0 + mod[0, 1:2]
    )


class Halving:
    def __init__(self, sums, landings, sends, recvs, bits):
        self.sums, self.landings, self.sends, self.recvs = sums, landings, sends, recvs
        self.bits = bits

    def share(self, stage, number, keep):
        me = lax.axis_index("clip")
        later = sorted(self.bits[stage + 1 :])
        spot = sum(((number >> i) & 1) << (bit - 1) for i, bit in enumerate(later))
        for bit in self.bits[: stage + 1]:
            mine = lax.rem(me // (1 << bit), 2)
            if bit == self.bits[stage] and not keep:
                mine = 1 - mine
            spot = spot + mine * (1 << (bit - 1))
        return spot

    def count(self, stage):
        return 1 << (len(self.bits) - 1 - stage)

    def copy(self, stage, number):
        at = sum(self.count(i) for i in range(stage)) + number
        return remote(
            self.sums.at[:, self.share(stage, number, False)],
            self.landings.at[:, at], self.sends.at[at], self.recvs.at[at],
            clip=partner("clip", self.bits[stage]),
        )

    def send(self, stage):
        for number in range(self.count(stage)):
            self.copy(stage, number).start()

    def fold(self, stage):
        for number in range(self.count(stage)):
            self.copy(stage, number).wait_recv()
            at = sum(self.count(i) for i in range(stage)) + number
            spot = self.share(stage, number, True)
            self.sums[:, spot] = (
                self.sums[:, spot].astype(F32) + self.landings[:, at].astype(F32)
            ).astype(BF16)

    def own(self):
        return self.sums[:, self.share(len(self.bits) - 1, 0, True)]

    def drain(self):
        for stage in range(len(self.bits)):
            for number in range(self.count(stage)):
                self.copy(stage, number).wait_send()


class Frames:
    def __init__(self, away, landing, sends, recvs):
        self.away, self.landing, self.sends, self.recvs = away, landing, sends, recvs

    def copy(self, distance):
        count = self.away.shape[0]
        frame = lax.rem(lax.axis_index("frame") + distance, count)
        return remote(
            self.away.at[frame], self.landing.at[distance - 1],
            self.sends.at[distance - 1], self.recvs.at[distance - 1], frame=frame,
        )

    def send(self, piece):
        count = self.away.shape[0]
        for frame in range(count):
            self.away[frame] = piece(frame)
        for distance in range(1, count):
            self.copy(distance).start()

    def send_one(self, frame, piece):
        count = self.away.shape[0]
        me = lax.axis_index("frame")
        self.away[frame] = piece
        distance = lax.rem(frame - me + count, count)

        @pl.when(frame != me)
        def _():
            remote(
                self.away.at[frame], self.landing.at[distance - 1],
                self.sends.at[distance - 1], self.recvs.at[distance - 1], frame=frame,
            ).start()

    def finish(self):
        total = self.away[lax.axis_index("frame")].astype(F32)
        for distance in range(1, self.away.shape[0]):
            self.copy(distance).wait_recv()
            total = total + self.landing[distance - 1].astype(F32)
        return total

    def drain(self):
        for distance in range(1, self.away.shape[0]):
            self.copy(distance).wait_send()


def cut(array, number, count):
    cols = array.shape[1] // count
    return array[:, number * cols : (number + 1) * cols]


def thirds_in_rows(values):
    high = values.astype(BF16).astype(F32)
    mid = (values - high).astype(BF16).astype(F32)
    low = (values - high) - mid
    return jnp.concatenate((high, mid, low, jnp.zeros_like(low)), axis=0).astype(BF16)


def side_by_side(tiles):
    return jnp.concatenate([tiles[i] for i in range(tiles.shape[0])], axis=1)


def backward_kernel(heads, clips, n, n_frame, r):
    step = pl.program_id(0)
    rows, width = r.tokens.shape[1:]
    tiles = 4
    half = n // 2
    share = width // n
    first_t = clips
    first_s = clips + tiles
    first_w = 2 * clips + tiles
    last = first_w + tiles - 1
    sibling = partner("clip", 0)
    barrier = pltpu.get_barrier_semaphore()
    bits = list(range(1, n.bit_length() - 1))
    frame = lax.axis_index("frame")
    place = lax.axis_index("clip")

    feed_in = Halving(r.sum_in, r.land_in, r.in_send, r.in_recv, bits)
    feed_out = Halving(r.sum_out, r.land_out, r.out_send, r.out_recv, bits[::-1])

    def units_of(name):
        sums, land = getattr(r, "sum_" + name), getattr(r, "land_" + name)
        sends, recvs = getattr(r, name + "_send"), getattr(r, name + "_recv")
        return [
            Halving(
                sums.at[pl.ds(i, 1)], land.at[pl.ds(i, 1)], sends.at[i], recvs.at[i],
                bits[:: 1 - 2 * (i % 2)],
            )
            for i in range(tiles)
        ]

    temporal, spatial = units_of("t"), units_of("s")
    stages = len(bits)

    regions = {"t": r.w_qkv_a_vmem, "s": r.w_qkv_b_vmem}

    def tile_cols(tile):
        return pl.ds(pl.multiple_of(lax.rem(tile, 3) * width, width), width)

    def tile_copies(name, tile):
        sends, recvs = getattr(r, name + "_core_send"), getattr(r, name + "_core_recv")
        return [
            remote(
                regions[name].at[share_rows(number, False, share), tile_cols(tile)],
                getattr(r, "core_" + name).at[tile, number],
                sends.at[tile, number], recvs.at[tile, number], clip=sibling,
            )
            for number in range(half)
        ]

    def tile_sent(name, tile):
        for copy in tile_copies(name, tile):
            copy.wait_send()

    def fold_core(name, which):
        sums, core = getattr(r, "sum_" + name), getattr(r, "core_" + name)
        for tile in which:
            for copy in tile_copies(name, tile):
                copy.wait_recv()
            sums[tile] = (sums[tile].astype(F32) + core[tile].astype(F32)).astype(BF16)

    frames = {
        name: Frames(
            getattr(r, "away_" + name), getattr(r, "near_" + name),
            getattr(r, name + "_z_send"), getattr(r, name + "_z_recv"),
        )
        for name in ("in", "out", "t", "s", "mod")
    }

    spaces = (r.left, r.left_out, r.grad_branch)

    def mod_tile(part):
        return pltpu.make_async_copy(
            r.w_mod.at[:, pl.ds(part * width, width)],
            spaces[part % 3].at[pl.ds(0, width)], r.mod_sems.at[part],
        )

    def mod_sums(total, parts):
        for part in parts:
            mod_tile(part).wait()
            term = dot_nt(thirds_in_rows(r.mods[part]), spaces[part % 3][:width])
            total = term if total is None else total + term
            if part + 3 < 9:
                mod_tile(part + 3).start()
        return total

    def send_mods(total):
        pad = r.mods.shape[1]
        total = total[:pad] + total[pad : 2 * pad] + total[2 * pad : 3 * pad]
        joined = side_by_side(r.mods)
        total = total * r.silu_grad[...]
        frames["mod"].send(
            lambda other: jnp.concatenate((total, cut(joined, other, n_frame)), axis=1)
        )

    def spread_mods(distance):
        return remote(
            r.mod_share, r.gathered.at[place], r.mod_send.at[distance - 1],
            r.mod_recv.at[distance - 1], clip=lax.rem(place + distance, n),
        )

    own_mods = pltpu.make_async_copy(r.mod_share, r.gathered.at[place], r.mod_sems.at[9])

    def to_frames(units, name, side):
        owned = jnp.concatenate([units[2 * side + i].own()[0] for i in range(2)], axis=1)
        wide, narrow = owned[:, : 3 * width // 2], owned[:, 3 * width // 2 :]
        count = n_frame // 2
        for number in range(count):
            frames[name].send_one(
                side * count + number,
                jnp.concatenate((cut(wide, number, count), cut(narrow, number, count)), axis=1),
            )

    def from_frames(name, wide, narrow):
        total = frames[name].finish()
        wide[...] = total[:, : wide.shape[1]]
        narrow[...] = total[:, wide.shape[1] :]

    def two_high(array):
        rows = array.shape[0] // 2
        return jnp.concatenate((array[:rows], array[rows:]), axis=1)

    loads = [
        pltpu.make_async_copy(r.keep_in, r.sum_in, r.load_sems.at[0]),
        pltpu.make_async_copy(r.came_in, r.core_t, r.load_sems.at[1]),
        pltpu.make_async_copy(r.keep_out, r.sum_out, r.load_sems.at[2]),
        pltpu.make_async_copy(r.came_out, r.core_s, r.load_sems.at[3]),
    ]
    lefts_t = [
        pltpu.make_async_copy(r.hidden_b, r.left, r.load_sems.at[4]),
        pltpu.make_async_copy(r.mixed_b, r.left_out, r.load_sems.at[5]),
        pltpu.make_async_copy(r.grad_branch_b, r.grad_branch, r.load_sems.at[6]),
    ]
    lefts_s = [
        pltpu.make_async_copy(r.hidden_a, r.left, r.load_sems.at[7]),
        pltpu.make_async_copy(r.mixed_a, r.left_out, r.load_sems.at[8]),
    ]
    r.w_qkv_a = Late(r.w_qkv_a_hbm, r.w_qkv_a_vmem, r.load_sems.at[9], first_s)

    @pl.when(step == 0)
    def _():
        for distance in range(1, n):
            greet(barrier, clip=lax.rem(place + distance, n))
        for distance in range(1, n_frame):
            greet(barrier, frame=lax.rem(frame + distance, n_frame))
        for copy in loads + lefts_t:
            copy.start()
        r.mods[...] = jnp.zeros_like(r.mods)
        for clip in range(clips):
            for row, part in enumerate((6, 7, 8, 5)):
                r.mods[part, clip : clip + 1] = r.sums[clip, row : row + 1]

    @pl.when(step < clips)
    def _():
        temporal_backward(r, step, pl.multiple_of(step * rows, rows))

    @pl.when(step == 0)
    def _():
        for copy in loads:
            copy.wait()
        for tile in range(tiles):
            r.sum_in[tile] = (
                r.sum_in[tile].astype(F32) + r.core_t[tile].astype(F32)
            ).astype(BF16)
        per = r.sum_out.shape[1] // tiles
        for tile in range(tiles):
            which = slice(tile * per, (tile + 1) * per)
            came = r.core_s[tile].reshape(r.sum_out[0, which].shape)
            r.sum_out[0, which] = (
                r.sum_out[0, which].astype(F32) + came.astype(F32)
            ).astype(BF16)
        pl.semaphore_wait(barrier, n - 1 + n_frame - 1)
        pl.semaphore_signal(
            r.free, inc=1, device_id={"clip": sibling}, device_id_type=pl.DeviceIdType.MESH
        )
        feed_in.send(0)
        feed_out.send(0)

    def weight_tile(name, tile):
        region = regions[name]
        side = tile // 2
        wide, narrow = 3 * width // 2, width // 2

        @pl.when(lax.rem(tile, 2) == 0)
        def _():
            cols = pl.ds(pl.multiple_of(side * wide, LANES), width)
            region[:, tile_cols(tile)] = dot_tn(r.left[...], r.grad_qkv[:, cols]).astype(BF16)

        @pl.when(lax.rem(tile, 2) == 1)
        def _():
            cols = pl.ds(pl.multiple_of(side * wide + width, LANES), wide - width)
            last_cols = pl.ds(pl.multiple_of(side * narrow, LANES), narrow)
            region[:, tile_cols(tile)] = jnp.concatenate(
                (
                    dot_tn(r.left[...], r.grad_qkv[:, cols]),
                    dot_tn(r.left_out[...], r.grad_branch[:, last_cols]),
                ),
                axis=1,
            ).astype(BF16)

        for copy in tile_copies(name, tile):
            copy.start()
        for number in range(half):
            getattr(r, "sum_" + name)[tile, number] = region[
                share_rows(number, True, share), tile_cols(tile)
            ]

    @pl.when((step >= first_t) & (step < first_s))
    def _():
        tile = step - first_t

        @pl.when(tile == 0)
        def _():
            for copy in lefts_t:
                copy.wait()
            pl.semaphore_wait(r.free, 1)

        pl.when(tile == 3)(lambda: tile_sent("t", 0))
        weight_tile("t", tile)

        @pl.when(tile == tiles - 1)
        def _():
            for copy in lefts_s:
                copy.start()

    @pl.when((step >= first_s) & (step < first_w))
    def _():
        clip = step - first_s

        @pl.when(clip == 0)
        def _():
            for tile in range(1, tiles):
                tile_sent("t", tile)
            r.w_qkv_a.copy.start()

        spatial_backward(r, heads, clip, pl.multiple_of(clip * rows, rows))

    @pl.when(step == first_s - 1)
    def _():
        for unit in (feed_in, feed_out):
            unit.fold(0)
            if stages > 1:
                unit.send(1)

    @pl.when(step == first_s)
    def _():
        for tile, unit in enumerate(temporal):
            fold_core("t", (tile,))
            unit.send(0)

    @pl.when(step == first_s + 1)
    def _():
        for stage in range(1, stages):
            for unit in (feed_in, feed_out):
                unit.fold(stage)
                if stage + 1 < stages:
                    unit.send(stage + 1)
        owned_in, owned_out = side_by_side(feed_in.own()), feed_out.own()[0]
        frames["in"].send(lambda other: cut(owned_in, other, n_frame))
        frames["out"].send(lambda other: two_high(cut(owned_out, other, n_frame)))

    @pl.when(step == first_s + 2)
    def _():
        for unit in temporal:
            unit.fold(0)
            if stages > 1:
                unit.send(1)

    @pl.when(step == first_s + 3)
    def _():
        for stage in range(1, stages):
            for tile, unit in enumerate(temporal):
                unit.fold(stage)
                if stage + 1 < stages:
                    unit.send(stage + 1)
                elif tile % 2 == 1:
                    to_frames(temporal, "t", tile // 2)

    @pl.when(step >= first_w)
    def _():
        tile = step - first_w

        @pl.when(tile == 0)
        def _():
            for copy in lefts_s:
                copy.wait()

        pl.when(tile == 3)(lambda: tile_sent("s", 0))
        weight_tile("s", tile)

    for tile in range(tiles - 1):

        @pl.when(step == first_w + 1 + tile)
        def _():
            fold_core("s", (tile,))
            spatial[tile].send(0)

    @pl.when(step == last)
    def _():
        fold_core("s", (tiles - 1,))
        spatial[tiles - 1].send(0)
        for part in range(3):
            mod_tile(part).start()
        total = mod_sums(None, range(0, 3))
        for stage in range(stages):
            for tile, unit in enumerate(spatial):
                unit.fold(stage)
                if stage + 1 < stages:
                    unit.send(stage + 1)
                elif tile % 2 == 1:
                    to_frames(spatial, "s", tile // 2)
                if stage == 0 and tile == 1:
                    total = mod_sums(total, range(3, 6))
            if stage == 0:
                r.done_in[...] = frames["in"].finish()
        total = mod_sums(total, range(6, 9))
        send_mods(total)
        flat = frames["out"].finish()
        high = flat.shape[0]
        r.done_out[:high] = cut(flat, 0, 2)
        r.done_out[high:] = cut(flat, 1, 2)
        from_frames("t", r.done_tq, r.done_to)
        r.mod_share[...] = frames["mod"].finish()
        for distance in range(1, n):
            spread_mods(distance).start()
        own_mods.start()
        from_frames("s", r.done_sq, r.done_so)
        own_mods.wait()
        for distance in range(1, n):
            spread_mods(distance).wait()
        for unit in (feed_in, feed_out, *temporal, *spatial):
            unit.drain()
        for name in frames:
            frames[name].drain()
        for tile in range(1, tiles):
            tile_sent("s", tile)


def backward_call(fwd, tok, mod, spread, weights, modulate_w, silu_grad, n, n_frame):
    clips, rows, width = tok.shape
    ff = weights["mlp_in"].shape[1]
    heads = width // HEAD_DIM
    tokens_here = clips * rows
    tiles = 4
    half, share, tall = n // 2, width // n, ff // n
    first_s, first_w = clips + tiles, 2 * clips + tiles

    def struct(last, dtype=BF16):
        return jax.ShapeDtypeStruct((clips, rows, last), dtype)

    mod_spec = pl.BlockSpec(
        (1,) + mod.shape[1:],
        lambda s: (
            jnp.where(s < first_s, jnp.minimum(s, clips - 1), jnp.minimum(s - first_s, clips - 1)),
            0, 0,
        ),
    )
    anywhere = pl.BlockSpec(memory_space=pl.ANY)
    pad, mod_cols = silu_grad.shape[0], width + 9 * width // n_frame
    whole = pl.BlockSpec(fwd.sums.shape, lambda s: (0, 0, 0), pipeline_mode=pl.Buffered(1))
    whole_grad = pl.BlockSpec(silu_grad.shape, lambda s: (0, 0), pipeline_mode=pl.Buffered(1))
    ins = [
        ("mod", mod, mod_spec), ("sums", fwd.sums, whole), ("silu_grad", silu_grad, whole_grad),
        ("w_mod", modulate_w, anywhere),
    ]
    for name in ("q_prev", "q_own", "q_next", "sent_prev", "sent", "sent_next", "grad_q", "grad_b", "after_a"):
        array = getattr(fwd, name)
        ins.append((name, array, clip_spec(array, 0, clips, 1 if name in ("grad_q", "grad_b", "after_a") else 2)))
    for name, array in (
        ("tokens", tok), ("branch_a", fwd.branch_a), ("qkv_a", fwd.qkv_a), ("lse", fwd.lse)
    ):
        ins.append((name, array, clip_spec(array, first_s, clips, 1)))
    flat = (tokens_here, width)
    for name in ("hidden_b", "mixed_b", "grad_branch_b", "hidden_a", "mixed_a"):
        ins.append((name, getattr(fwd, name).reshape(flat), anywhere))
    core_shape = (tiles, half, share, width)
    ins += [
        ("keep_in", fwd.keep_in.reshape(core_shape), anywhere),
        ("came_in", fwd.came_in.reshape(core_shape), anywhere),
        ("keep_out", fwd.keep_out.reshape(1, half, tall, width), anywhere),
        ("came_out", fwd.came_out.reshape(core_shape), anywhere),
        ("w_qkv_a_hbm", weights["spatial_qkv"], anywhere),
    ]
    held = [
        ("spread", spread, 0), ("w_qkv_b", weights["temporal_qkv"], 0),
        ("w_out_a", weights["spatial_out"], first_s),
    ]
    grad_tokens = struct(width, F32)
    outs = [
        ("grad_tokens", grad_tokens, clip_spec(grad_tokens, first_s, clips, 1)),
        ("gathered", jax.ShapeDtypeStruct((n, pad, mod_cols), F32), None),
    ]
    dma = pltpu.SemaphoreType.DMA
    pieces = {
        "in": (share, ff // n_frame), "out": (tall, width // n_frame),
        "tq": (share, 3 * width // n_frame), "to": (share, width // n_frame),
        "sq": (share, 3 * width // n_frame), "so": (share, width // n_frame),
    }
    moved = half - 1
    scratch = [
        ("grad_a", pltpu.VMEM((clips, rows, width), F32)),
        ("grad_qkv", pltpu.VMEM((tokens_here, 3 * width), BF16)),
        ("grad_branch", pltpu.VMEM(flat, BF16)), ("left", pltpu.VMEM(flat, BF16)),
        ("left_out", pltpu.VMEM(flat, BF16)),
        ("w_qkv_a_vmem", pltpu.VMEM(weights["spatial_qkv"].shape, BF16)),
        ("sum_in", pltpu.VMEM(core_shape, BF16)), ("land_in", pltpu.VMEM((tiles, moved, share, width), BF16)),
        ("in_send", dma((moved,))), ("in_recv", dma((moved,))),
        ("sum_out", pltpu.VMEM((1, half, tall, width), BF16)),
        ("land_out", pltpu.VMEM((1, moved, tall, width), BF16)),
        ("out_send", dma((moved,))), ("out_recv", dma((moved,))),
        ("load_sems", dma((10,))), ("free", pltpu.SemaphoreType.REGULAR),
        ("mods", pltpu.VMEM((9, pad, width), F32)), ("mod_sems", dma((10,))),
        ("mod_share", pltpu.VMEM((pad, mod_cols), F32)),
        ("mod_send", dma((n - 1,))), ("mod_recv", dma((n - 1,))),
    ]
    for name in ("t", "s"):
        scratch += [
            ("sum_" + name, pltpu.VMEM(core_shape, BF16)), ("core_" + name, pltpu.VMEM(core_shape, BF16)),
            ("land_" + name, pltpu.VMEM((tiles, moved, share, width), BF16)),
            (name + "_send", dma((tiles, moved))), (name + "_recv", dma((tiles, moved))),
            (name + "_core_send", dma((tiles, half))), (name + "_core_recv", dma((tiles, half))),
        ]
    for name, dims in pieces.items():
        shape = jax.ShapeDtypeStruct(dims, F32)
        outs.append(("done_" + name, shape, pl.BlockSpec(shape.shape, lambda s: (0, 0))))
    packed = {
        "in": (share, ff // n_frame), "out": (tall // 2, 2 * width // n_frame),
        "t": (share, 4 * width // n_frame), "s": (share, 4 * width // n_frame),
        "mod": (pad, mod_cols),
    }
    for name, dims in packed.items():
        kind = F32 if name == "mod" else BF16
        scratch += [
            ("away_" + name, pltpu.VMEM((n_frame, *dims), kind)),
            ("near_" + name, pltpu.VMEM((n_frame - 1, *dims), kind)),
            (name + "_z_send", dma((n_frame - 1,))), (name + "_z_recv", dma((n_frame - 1,))),
        ]
    return run_kernel(
        functools.partial(backward_kernel, heads, clips, n, n_frame), first_w + tiles,
        ins, held, outs, scratch, 2 * tokens_here * width * width * 20, collective=2,
    )


def thirds(values):
    high = values.astype(BF16)
    rest = values - high.astype(F32)
    mid = rest.astype(BF16)
    low = (rest - mid.astype(F32)).astype(BF16)
    return jnp.concatenate((high, mid, low), axis=0)


def local(
    tokens, target, loss_weight, timesteps, offsets, cond_table, modulate_w,
    spatial_qkv, spatial_out, temporal_qkv, temporal_out, mlp_in, mlp_out,
):
    clips, frames, patches, width = tokens.shape
    steps = cond_table.shape[0]
    heads = width // HEAD_DIM
    n_clip = lax.axis_size("clip")
    n_frame = lax.axis_size("frame")
    clip_at = lax.axis_index("clip")
    frame_at = lax.axis_index("frame")
    flat = (clips, patches, width)
    tok = tokens.reshape(flat)
    tgt = target.reshape(flat)

    condition = jnp.take(cond_table, timesteps, axis=0, mode="clip")
    cond_low = jax.nn.silu(condition).astype(BF16)
    cond_here = lax.dynamic_slice_in_dim(condition, clip_at * clips, clips)
    _, silu_pull = jax.vjp(jax.nn.silu, cond_here)
    low_here = lax.dynamic_slice_in_dim(cond_low, clip_at * clips, clips)
    mod = jnp.dot(low_here, modulate_w, preferred_element_type=F32).reshape(clips, 9, width)

    half = width // 2
    positions = (offsets + frame_at).astype(F32)
    freqs = jnp.exp(jnp.arange(half, dtype=F32) * (-math.log(10000.0) / half))
    angles = positions[:, None] * freqs
    posenc = jnp.concatenate((jnp.sin(angles), jnp.cos(angles)), axis=-1)[:, None, :]

    head_of = np.arange(width) // HEAD_DIM
    lane_ids = np.arange(LANES)
    to_heads = jnp.asarray((head_of[:, None] == lane_ids[None, :]).astype(BF16))
    tall = np.arange(2 * LANES) - LANES
    spread = jnp.asarray((tall[:, None] == head_of[None, :]).astype(BF16))
    group, inside = np.divmod(np.arange(6 * LANES), LANES)
    slot_at = np.where(inside < heads, group * SLOT + inside, -1)
    pack = jnp.asarray((slot_at[:, None] == lane_ids[None, :]).astype(BF16))
    weights = {
        "spatial_qkv": spatial_qkv, "spatial_out": spatial_out, "temporal_qkv": temporal_qkv,
        "temporal_out": temporal_out, "mlp_in": mlp_in, "mlp_out": mlp_out,
    }
    fwd = forward_call(
        tok, tgt, mod, posenc, loss_weight, (to_heads, spread, pack), weights, n_clip
    )

    pad = -(-clips // 8) * 8
    silu_grad = jnp.pad(silu_pull(jnp.ones_like(cond_here))[0], ((0, pad - clips), (0, 0)))
    bwd = backward_call(fwd, tok, mod, spread, weights, modulate_w, silu_grad, n_clip, n_frame)
    gathered = bwd.gathered[:, :clips].reshape(n_clip * clips, -1)
    onehot = (timesteps[:, None] == jnp.arange(steps, dtype=jnp.int32)[None, :]).astype(BF16)
    grad_table = dot_tn(jnp.concatenate((onehot,) * 3, axis=0), thirds(gathered[:, :width]))
    mod_rows = width // n_clip
    low_rows = lax.dynamic_slice_in_dim(cond_low, clip_at * mod_rows, mod_rows, axis=1)
    grad_modulate = dot_tn(jnp.concatenate((low_rows,) * 3, axis=0), thirds(gathered[:, width:]))
    return (
        fwd.output.reshape(tokens.shape),
        bwd.grad_tokens.reshape(tokens.shape),
        grad_table,
        grad_modulate,
        bwd.done_sq,
        bwd.done_so,
        bwd.done_tq,
        bwd.done_to,
        bwd.done_in,
        bwd.done_out,
    )


def solution(mesh):
    placed = (
        P("clip", "frame", None, None), P("clip", "frame", None, None), P("clip"), P(), P("clip"),
    ) + (P(),) * 8
    return jax.shard_map(
        local,
        mesh=mesh,
        in_specs=placed,
        out_specs=(
            P("clip", "frame", None, None), P("clip", "frame", None, None), P(),
        ) + (P("clip", "frame"),) * 7,
        check_vma=False,
    )
```

```python
import functools
import math

import jax
import jax.numpy as jnp
import numpy as np
from jax import lax
from jax.experimental import pallas as pl
from jax.experimental.pallas import tpu as pltpu
from jax.sharding import PartitionSpec as P

HEAD_DIM = 64
NORM_EPSILON = 1e-06
F32 = jnp.float32
BF16 = jnp.bfloat16
LANES = 128
SLOT = 16
NO_KEY = -1e30
VMEM_LIMIT = 60 * 2**20
GROUP = 2
GELU_A = math.sqrt(2.0 / math.pi)
GELU_B = 0.044715


def dot(left, right):
    return lax.dot_general(left, right, (((1,), (0,)), ((), ())), preferred_element_type=F32)


def dot_nt(left, right):
    return lax.dot_general(left, right, (((1,), (1,)), ((), ())), preferred_element_type=F32)


def dot_tn(left, right):
    return lax.dot_general(left, right, (((0,), (0,)), ((), ())), preferred_element_type=F32)


def norm(values):
    centred = values - jnp.mean(values, axis=-1, keepdims=True)
    inv_std = lax.rsqrt(jnp.mean(centred * centred, axis=-1, keepdims=True) + NORM_EPSILON)
    return centred * inv_std, inv_std


def norm_back(grad_hidden, normed, inv_std, scale_plus):
    grad_normed = grad_hidden * scale_plus
    mean_grad = jnp.mean(grad_normed, axis=-1, keepdims=True)
    mean_cross = jnp.mean(grad_normed * normed, axis=-1, keepdims=True)
    return inv_std * (grad_normed - mean_grad - normed * mean_cross)


def column_sum(values):
    return jnp.sum(values, axis=0, keepdims=True)


def side_masks(dtype, value):
    lane = lax.broadcasted_iota(jnp.int32, (1, LANES), 1)
    return [jnp.where((lane < HEAD_DIM) == (side == 0), value, 0.0).astype(dtype) for side in (0, 1)]


class Refs:
    def __init__(self, names, refs):
        self.__dict__.update(zip(names, refs, strict=True))


class Late:
    def __init__(self, source, ref, sem, step):
        self.ref = ref
        self.copy = pltpu.make_async_copy(source, ref, sem)
        self.step = step
        self.waited = False

    def __getitem__(self, index):
        if not self.waited:
            pl.when(pl.program_id(0) == self.step)(self.copy.wait)
            self.waited = True
        return self.ref[index]


def partner(axis, bit):
    me = lax.axis_index(axis)
    return me + (1 << bit) - (2 << bit) * lax.rem(me // (1 << bit), 2)


def remote(source, target, send_sem, recv_sem, **where):
    return pltpu.make_async_remote_copy(
        src_ref=source, dst_ref=target, send_sem=send_sem, recv_sem=recv_sem,
        device_id=where, device_id_type=pl.DeviceIdType.MESH,
    )


def greet(barrier, **where):
    pl.semaphore_signal(barrier, inc=1, device_id=where, device_id_type=pl.DeviceIdType.MESH)


def run_kernel(body, steps, ins, weights, outs, scratch, flops, collective=None):
    anywhere = pl.BlockSpec(memory_space=pl.ANY)
    names = [name for name, *_ in ins] + [name + "_hbm" for name, *_ in weights]
    names += [name for name, *_ in outs]
    names += [name + "_vmem" for name, *_ in weights] + ["weight_sems"]
    names += [name for name, _ in scratch]

    def kernel(*refs):
        r = Refs(names, refs)
        lates = []
        for number, (name, _, step) in enumerate(weights):
            late = Late(
                getattr(r, name + "_hbm"), getattr(r, name + "_vmem"), r.weight_sems.at[number], step
            )
            lates.append(late)
            setattr(r, name, late)

        @pl.when(pl.program_id(0) == 0)
        def _():
            for late in lates:
                if late.step == 0:
                    late.copy.start()

        body(r)

        @pl.when(pl.program_id(0) == 0)
        def _():
            for late in lates:
                if late.step > 0:
                    late.copy.start()

    arrays = [array for _, array, _ in ins] + [array for _, array, _ in weights]
    shapes = [shape for _, shape, _ in outs]
    touched = sum(math.prod(a.shape) * a.dtype.itemsize for a in arrays + shapes)
    params = {} if collective is None else {"collective_id": collective, "has_side_effects": True}
    done = pl.pallas_call(
        kernel,
        grid=(steps,),
        in_specs=[spec for *_, spec in ins] + [anywhere] * len(weights),
        out_specs=[spec or anywhere for *_, spec in outs],
        out_shape=shapes,
        scratch_shapes=[pltpu.VMEM(a.shape, a.dtype) for _, a, _ in weights]
        + [pltpu.SemaphoreType.DMA((max(len(weights), 1),))]
        + [shape for _, shape in scratch],
        compiler_params=pltpu.CompilerParams(vmem_limit_bytes=VMEM_LIMIT, **params),
        cost_estimate=pl.CostEstimate(flops=flops, bytes_accessed=touched, transcendentals=0),
    )(*arrays)
    return Refs([name for name, *_ in outs], done)


def clip_spec(array, first, clips, depth=None):
    rest = array.shape[1:]
    mode = {} if depth is None else {"pipeline_mode": pl.Buffered(depth)}
    return pl.BlockSpec(
        (1,) + rest, lambda s: (jnp.clip(s - first, 0, clips - 1),) + (0,) * len(rest), **mode
    )


def spatial_forward(r, heads, clip):
    width = r.tokens.shape[-1]
    rows = r.tokens.shape[1]
    mod = r.mod
    inputs = r.tokens[0].astype(F32)
    normed, _ = norm(inputs)
    hidden = (normed * (1.0 + mod[0, 1:2]) + mod[0, 0:1]).astype(BF16)
    r.hidden_a[0] = hidden
    for part in range(3):
        cols = slice(part * width, (part + 1) * width)
        r.qkv_a[0, :, cols] = dot(hidden, r.w_qkv_a[:, cols]).astype(BF16)
    scaled, plain = side_masks(BF16, HEAD_DIM**-0.5), side_masks(BF16, 1.0)
    for first in range(0, heads // 2, 3):
        pairs = range(first, min(first + 3, heads // 2))
        scores, softs = [], []
        for pair in pairs:
            query, key = (columns(r.qkv_a, part, pair) for part in (0, 1))
            scores.append(dot_nt(both_sides(key, scaled), query))
        for pair, score in zip(pairs, scores):
            halves = []
            for side in range(2):
                mine = score[side * rows : (side + 1) * rows]
                top = jnp.max(mine, axis=0, keepdims=True)
                grown = jnp.exp(mine - top)
                total = jnp.sum(grown, axis=0, keepdims=True)
                halves.append((grown * (1.0 / total)).astype(BF16))
                head = 2 * pair + side
                r.lse[0, head : head + 1] = top + jnp.log(total)
            softs.append(jnp.concatenate(halves, axis=0))
        for pair, soft in zip(pairs, softs):
            value = columns(r.qkv_a, 2, pair)
            r.mixed_a[0, :, pair * LANES : (pair + 1) * LANES] = dot_tn(
                soft, both_sides(value, plain)
            ).astype(BF16)
    branch_a = dot(r.mixed_a[0], r.w_out_a[...])
    r.branch_a[0] = branch_a.astype(BF16)
    after_a = inputs + mod[0, 2:3] * branch_a
    r.after_held[clip] = after_a
    normed_b, _ = norm(after_a)
    r.hidden_held[clip] = (
        normed_b * (1.0 + mod[0, 4:5]) + (mod[0, 3:4] + r.posenc[0])
    ).astype(BF16)


def both_sides(array, masks):
    return jnp.concatenate((array * masks[0], array * masks[1]), axis=0)


def columns(ref, part, pair):
    start = part * (ref.shape[-1] // 3) + pair * LANES
    return ref[0, :, start : start + LANES]


def by_head(left, right, to_heads):
    return dot(left * right, to_heads)


def middle(r, clip, rows_at):
    width = r.target.shape[-1]
    rows = r.target.shape[1]
    ff = r.act.shape[-1]
    scale_qk = HEAD_DIM**-0.5
    mod = r.mod
    own_rows = pl.ds(rows_at, rows)
    store = r.w_qkv_a_vmem

    def kept(number, part):
        return store[number * rows : (number + 1) * rows, part * width : (part + 1) * width]

    three = jnp.concatenate((r.hidden_prev[clip], r.hidden_held[clip], r.hidden_next[clip]), axis=0)
    for part in range(3):
        cols = slice(part * width, (part + 1) * width)
        value = dot(three, r.w_qkv_b[:, cols]).astype(BF16)
        store[:, cols] = value
        if part == 0:
            for number, out in enumerate((r.q_prev, r.q_own, r.q_next)):
                out[0] = value[number * rows : (number + 1) * rows]
    frame = lax.axis_index("frame")
    absent = (frame == 0, None, frame == lax.axis_size("frame") - 1)
    scores = []
    for number in range(3):
        raw = by_head(kept(1, 0), kept(number, 1), r.to_heads[...]) * scale_qk
        if absent[number] is not None:
            raw = raw + jnp.where(absent[number], NO_KEY, 0.0)
        scores.append(raw)
    top = jnp.maximum(jnp.maximum(scores[0], scores[1]), scores[2])
    grown = [jnp.exp(entry - top) for entry in scores]
    inverse = 1.0 / (grown[0] + grown[1] + grown[2])
    soft = [entry * inverse for entry in grown]
    soft_low = [entry.astype(BF16) for entry in soft]
    to_width = r.spread[LANES : 2 * LANES]
    total = None
    for number in range(3):
        term = dot(soft_low[number], to_width) * kept(number, 2).astype(F32)
        total = term if total is None else total + term
    mixed = total.astype(BF16)
    r.mixed_b[0] = mixed
    branch_b = dot(mixed, r.w_out_b[...])
    r.grad_b[0] = branch_b
    after_b = r.after_held[clip] + mod[0, 5:6] * branch_b
    normed_c, inv_c = norm(after_b)
    hidden = (normed_c * (1.0 + mod[0, 7:8]) + mod[0, 6:7]).astype(BF16)
    r.hidden_c[own_rows, :] = hidden
    parts = ff // width
    ahead = dot(hidden, r.w_in[:, :width])
    for part in range(parts):
        cols = slice(part * width, (part + 1) * width)
        upward = ahead
        if part + 1 < parts:
            ahead = dot(hidden, r.w_in[:, (part + 1) * width : (part + 2) * width])
        squared = upward * upward
        bent = jnp.tanh(upward * (GELU_A + (GELU_A * GELU_B) * squared))
        share = 0.5 + 0.5 * bent
        r.act[own_rows, cols] = (upward * share).astype(BF16)
        steep = (1.0 - bent * bent) * (0.5 * GELU_A + (1.5 * GELU_A * GELU_B) * squared)
        r.grad_up[own_rows, cols] = (share + upward * steep).astype(BF16)
    branch_c = dot(r.act[own_rows, :], r.w_mlp[...])
    result = after_b + mod[0, 8:9] * branch_c
    r.output[0] = result.astype(BF16)
    grad_result = r.weight[clip] * (result - r.target[0].astype(F32))
    r.sums[0, 2:3] = column_sum(grad_result * branch_c)
    low_c = (mod[0, 8:9] * grad_result).astype(BF16)
    r.grad_branch_c[own_rows, :] = low_c
    ahead = dot_nt(low_c, r.w_mlp[:width, :])
    for part in range(parts):
        cols = slice(part * width, (part + 1) * width)
        grad_act = ahead
        if part + 1 < parts:
            ahead = dot_nt(low_c, r.w_mlp[(part + 1) * width : (part + 2) * width, :])
        r.grad_up[own_rows, cols] = (grad_act * r.grad_up[own_rows, cols].astype(F32)).astype(BF16)
    grad_hidden = dot_nt(r.grad_up[own_rows, :], r.w_in[...])
    r.sums[0, 0:1] = column_sum(grad_hidden)
    r.sums[0, 1:2] = column_sum(grad_hidden * normed_c)
    grad_after = grad_result + norm_back(grad_hidden, normed_c, inv_c, 1.0 + mod[0, 7:8])
    r.sums[0, 3:4] = column_sum(grad_after * r.grad_b[0])
    r.grad_b[0] = grad_after
    low_b = (mod[0, 5:6] * grad_after).astype(BF16)
    r.grad_branch_b[0] = low_b
    grad_mixed = dot_nt(low_b, r.w_out_b[...]).astype(BF16)
    grad_soft = [by_head(grad_mixed, kept(number, 2), r.to_heads[...]) for number in range(3)]
    inner = soft[0] * grad_soft[0] + soft[1] * grad_soft[1] + soft[2] * grad_soft[2]
    grad_scores = [(soft[number] * (grad_soft[number] - inner)).astype(BF16) for number in range(3)]
    total = None
    for number in range(3):
        term = dot(grad_scores[number], to_width) * kept(number, 1).astype(F32)
        total = term if total is None else total + term
    r.grad_q[0] = (total * scale_qk).astype(BF16)
    r.sent_held[clip, :, :width] = grad_mixed
    r.sent_held[clip, :, width:] = dot(
        jnp.concatenate(soft_low + grad_scores, axis=1), r.pack[...]
    ).astype(BF16)


def share_rows(number, keep, share):
    core = lax.rem(lax.axis_index("clip"), 2)
    spot = 2 * number + (core if keep else 1 - core)
    return pl.ds(pl.multiple_of(spot * share, share), share)


def forward_kernel(heads, clips, n, r):
    step = pl.program_id(0)
    rows, width = r.tokens.shape[1:]
    ff = r.act.shape[-1]
    in_steps = ff // width
    out_steps = n // 2
    share = ff // n
    last = 2 * clips + in_steps + out_steps - 1
    frame = lax.axis_index("frame")
    has_prev = frame > 0
    has_next = frame < lax.axis_size("frame") - 1
    no_prev = jnp.logical_not(has_prev)
    no_next = jnp.logical_not(has_next)
    core = lax.rem(lax.axis_index("clip"), 2)
    sibling = partner("clip", 0)
    barrier = pltpu.get_barrier_semaphore()

    def halo(way, clip):
        return remote(
            r.hidden_held.at[clip], (r.hidden_prev, r.hidden_next)[way].at[clip],
            r.halo_send.at[way, clip], r.halo_recv.at[way, clip],
            frame=frame + 1 if way == 0 else frame - 1,
        )

    def packet(way, clip):
        return remote(
            r.sent_held.at[clip], (r.sent_prev, r.sent_next)[way].at[clip],
            r.sent_send.at[way, clip], r.sent_recv.at[way, clip],
            frame=frame + 1 if way == 0 else frame - 1,
        )

    low_share = width // n

    def in_tile(tile):
        return [
            remote(
                r.stage.at[lax.rem(tile, 2), share_rows(number, False, low_share)],
                r.came_in.at[tile, number],
                r.in_send.at[tile, number], r.in_recv.at[tile, number], clip=sibling,
            )
            for number in range(n // 2)
        ]

    def in_kept(tile):
        return [
            pltpu.make_async_copy(
                r.stage.at[lax.rem(tile, 2), share_rows(number, True, low_share)],
                r.keep_in.at[tile, number], r.in_keep.at[tile, number],
            )
            for number in range(n // 2)
        ]

    def in_sent(tile):
        for copy in in_tile(tile):
            copy.wait_send()
        for copy in in_kept(tile):
            copy.wait()

    def out_part(tile, which):
        return r.stage.at[
            lax.rem(tile + in_steps, 2), pl.ds(pl.multiple_of(which * share, share), share)
        ]

    def out_tile(tile):
        return remote(
            out_part(tile, 1 - core), r.came_out.at[tile],
            r.out_send.at[tile], r.out_recv.at[tile], clip=sibling,
        )

    def out_kept(tile):
        return pltpu.make_async_copy(
            out_part(tile, core), r.keep_out.at[tile], r.out_keep.at[tile]
        )

    def save(clip):
        return [
            pltpu.make_async_copy(r.after_held.at[clip], r.after_a.at[clip], r.save_sems.at[0, clip]),
            pltpu.make_async_copy(
                r.hidden_held.at[clip], r.hidden_b.at[clip], r.save_sems.at[1, clip]
            ),
        ]

    def save_sent(clip):
        return pltpu.make_async_copy(r.sent_held.at[clip], r.sent.at[clip], r.save_sems.at[2, clip])

    def fill(way, clip):
        zeros = (r.hidden_prev, r.hidden_next)[way].at[clip]
        target = (r.sent_prev, r.sent_next)[way].at[clip]
        return [
            pltpu.make_async_copy(zeros, target.at[:, pl.ds(0, width)], r.save_sems.at[3, clip]),
            pltpu.make_async_copy(
                zeros.at[:, pl.ds(0, LANES)], target.at[:, pl.ds(width, LANES)],
                r.save_sems.at[4, clip],
            ),
        ]

    @pl.when(step == 0)
    def _():
        greet(barrier, clip=sibling)
        pl.when(has_prev)(lambda: greet(barrier, frame=frame - 1))
        pl.when(has_next)(lambda: greet(barrier, frame=frame + 1))

        @pl.when(no_prev)
        def _():
            r.hidden_prev[...] = jnp.zeros_like(r.hidden_prev)
            for clip in range(clips):
                for copy in fill(0, clip):
                    copy.start()

        @pl.when(no_next)
        def _():
            r.hidden_next[...] = jnp.zeros_like(r.hidden_next)
            for clip in range(clips):
                for copy in fill(1, clip):
                    copy.start()

    @pl.when(step < clips)
    def _():
        spatial_forward(r, heads, step)

        @pl.when(step == 0)
        def _():
            pl.semaphore_wait(
                barrier, 1 + jnp.where(has_prev, 1, 0) + jnp.where(has_next, 1, 0)
            )

        pl.when(has_next)(lambda: halo(0, step).start())
        pl.when(has_prev)(lambda: halo(1, step).start())
        for copy in save(step):
            copy.start()

    @pl.when((step >= clips) & (step < 2 * clips))
    def _():
        clip = step - clips
        pl.when(has_prev)(lambda: halo(0, clip).wait_recv())
        pl.when(has_next)(lambda: halo(1, clip).wait_recv())
        middle(r, clip, pl.multiple_of(clip * rows, rows))
        pl.when(has_next)(lambda: packet(0, clip).start())
        pl.when(has_prev)(lambda: packet(1, clip).start())
        save_sent(clip).start()

    @pl.when((step >= 2 * clips) & (step < 2 * clips + in_steps))
    def _():
        tile = step - 2 * clips

        pl.when(tile >= 2)(lambda: in_sent(tile - 2))
        cols = pl.ds(pl.multiple_of(tile * width, width), width)
        r.stage[lax.rem(tile, 2), :width] = dot_tn(r.hidden_c[...], r.grad_up[:, cols]).astype(BF16)
        for copy in in_tile(tile) + in_kept(tile):
            copy.start()

    @pl.when(step >= 2 * clips + in_steps)
    def _():
        tile = step - 2 * clips - in_steps

        pl.when(tile < 2)(lambda: in_sent(in_steps + tile - 2))

        @pl.when(tile >= 2)
        def _():
            out_tile(tile - 2).wait_send()
            out_kept(tile - 2).wait()

        cols = pl.ds(pl.multiple_of(tile * 2 * share, 2 * share), 2 * share)
        r.stage[lax.rem(tile + in_steps, 2), : 2 * share] = dot_tn(
            r.act[:, cols], r.grad_branch_c[...]
        ).astype(BF16)
        out_tile(tile).start()
        out_kept(tile).start()

    @pl.when(step == last)
    def _():
        for clip in range(clips):
            for copy in save(clip):
                copy.wait()
            save_sent(clip).wait()

            @pl.when(has_next)
            def _():
                halo(0, clip).wait_send()
                packet(0, clip).wait_send()
                packet(1, clip).wait_recv()

            @pl.when(has_prev)
            def _():
                halo(1, clip).wait_send()
                packet(1, clip).wait_send()
                packet(0, clip).wait_recv()

            for way, absent in ((0, no_prev), (1, no_next)):

                @pl.when(absent)
                def _():
                    for copy in fill(way, clip):
                        copy.wait()

        for tile in range(in_steps):
            for copy in in_tile(tile):
                copy.wait_recv()
        for tile in range(out_steps):
            out_tile(tile).wait_recv()
        for tile in range(out_steps - 2, out_steps):
            out_tile(tile).wait_send()
            out_kept(tile).wait()


def forward_call(tok, target, mod, posenc, weight, tables, weights, n):
    clips, rows, width = tok.shape
    ff = weights["mlp_in"].shape[1]
    heads = width // HEAD_DIM
    tokens_here = clips * rows
    in_steps, out_steps, share = ff // width, n // 2, ff // n
    to_heads, spread, pack = tables

    def struct(last, dtype=BF16):
        return jax.ShapeDtypeStruct((clips, rows, last), dtype)

    def early(array):
        return clip_spec(array, 0, clips)

    def late(array):
        return clip_spec(array, clips, clips)

    mod_spec = pl.BlockSpec(
        (1,) + mod.shape[1:],
        lambda s: (jnp.where(s < clips, s, jnp.minimum(s - clips, clips - 1)), 0, 0),
    )
    ins = [
        ("tokens", tok, early(tok)), ("posenc", posenc, early(posenc)), ("mod", mod, mod_spec),
        ("target", target, clip_spec(target, clips, clips, 1)), ("weight", weight, pl.BlockSpec(memory_space=pltpu.SMEM)),
    ]
    held = [
        ("w_qkv_a", weights["spatial_qkv"], 0), ("w_out_a", weights["spatial_out"], 0),
        ("w_qkv_b", weights["temporal_qkv"], clips), ("to_heads", to_heads, clips),
        ("spread", spread, clips), ("w_out_b", weights["temporal_out"], clips),
        ("w_in", weights["mlp_in"], clips), ("w_mlp", weights["mlp_out"], clips), ("pack", pack, clips),
    ]
    outs = []
    for name, shape in (
        ("hidden_a", struct(width)), ("qkv_a", struct(3 * width)), ("mixed_a", struct(width)),
        ("branch_a", struct(width)),
        ("lse", jax.ShapeDtypeStruct((clips, -(-heads // 8) * 8, rows), F32)),
    ):
        outs.append((name, shape, clip_spec(shape, 0, clips, 1)))
    for name, shape in (
        ("output", struct(width)), ("grad_b", struct(width, F32)), ("mixed_b", struct(width)),
        ("grad_branch_b", struct(width)), ("q_own", struct(width)), ("q_prev", struct(width)),
        ("q_next", struct(width)), ("grad_q", struct(width)),
        ("sums", jax.ShapeDtypeStruct((clips, 8, width), F32)),
    ):
        outs.append((name, shape, clip_spec(shape, clips, clips, 1)))
    outs += [
        ("after_a", struct(width, F32), None), ("hidden_b", struct(width), None),
        ("sent", struct(width + LANES), None), ("sent_prev", struct(width + LANES), None),
        ("sent_next", struct(width + LANES), None),
    ]
    tile_in = jax.ShapeDtypeStruct((in_steps, n // 2, width // n, width), BF16)
    tile_out = jax.ShapeDtypeStruct((out_steps, share, width), BF16)
    outs += [
        ("keep_in", tile_in, None), ("came_in", tile_in, None), ("keep_out", tile_out, None),
        ("came_out", tile_out, None),
    ]
    dma = pltpu.SemaphoreType.DMA
    scratch = [
        ("after_held", pltpu.VMEM((clips, rows, width), F32)),
        ("hidden_held", pltpu.VMEM((clips, rows, width), BF16)),
        ("hidden_prev", pltpu.VMEM((clips, rows, width), BF16)),
        ("hidden_next", pltpu.VMEM((clips, rows, width), BF16)),
        ("sent_held", pltpu.VMEM((clips, rows, width + LANES), BF16)),
        ("act", pltpu.VMEM((tokens_here, ff), BF16)),
        ("grad_up", pltpu.VMEM((tokens_here, ff), BF16)),
        ("hidden_c", pltpu.VMEM((tokens_here, width), BF16)),
        ("grad_branch_c", pltpu.VMEM((tokens_here, width), BF16)),
        ("stage", pltpu.VMEM((2, max(width, 2 * share), width), BF16)),
        ("halo_send", dma((2, clips))), ("halo_recv", dma((2, clips))),
        ("sent_send", dma((2, clips))), ("sent_recv", dma((2, clips))),
        ("in_send", dma((in_steps, n // 2))), ("in_recv", dma((in_steps, n // 2))),
        ("in_keep", dma((in_steps, n // 2))), ("out_send", dma((out_steps,))),
        ("out_recv", dma((out_steps,))), ("out_keep", dma((out_steps,))),
        ("save_sems", dma((5, clips))),
    ]
    return run_kernel(
        functools.partial(forward_kernel, heads, clips, n), 2 * clips + in_steps + out_steps,
        ins, held, outs, scratch, 2 * tokens_here * width * width * 46, collective=1,
    )


def temporal_backward(r, clip, rows_at):
    width = r.tokens.shape[-1]
    rows = r.tokens.shape[1]
    scale_qk = HEAD_DIM**-0.5
    own_rows = pl.ds(rows_at, rows)
    grad_key = None
    grad_value = None
    for number, (source, query) in enumerate(
        ((r.sent_prev, r.q_prev), (r.sent, r.q_own), (r.sent_next, r.q_next))
    ):
        other = 2 - number
        table = source[0, :, width:]
        low = LANES - SLOT * other
        soft = dot(table, r.spread[low : low + LANES])
        low = LANES - SLOT * (3 + other)
        score = dot(table, r.spread[low : low + LANES])
        key_term = score * query[0].astype(F32)
        value_term = soft * source[0, :, :width].astype(F32)
        grad_key = key_term if grad_key is None else grad_key + key_term
        grad_value = value_term if grad_value is None else grad_value + value_term
    r.grad_qkv[own_rows, :width] = r.grad_q[0]
    r.grad_qkv[own_rows, width : 2 * width] = (grad_key * scale_qk).astype(BF16)
    r.grad_qkv[own_rows, 2 * width :] = grad_value.astype(BF16)
    grad_hidden = dot_nt(r.grad_qkv[own_rows, :], r.w_qkv_b[...])
    normed_b, inv_b = norm(r.after_a[0])
    r.mods[3, pl.ds(clip, 1)] = column_sum(grad_hidden)
    r.mods[4, pl.ds(clip, 1)] = column_sum(grad_hidden * normed_b)
    r.grad_a[clip] = r.grad_b[0] + norm_back(grad_hidden, normed_b, inv_b, 1.0 + r.mod[0, 4:5])


def spatial_backward(r, heads, clip, rows_at):
    width = r.tokens.shape[-1]
    rows = r.tokens.shape[1]
    scale_qk = HEAD_DIM**-0.5
    own_rows = pl.ds(rows_at, rows)
    mod = r.mod
    r.mods[2, pl.ds(clip, 1)] = column_sum(r.grad_a[clip] * r.branch_a[0].astype(F32))
    low_a = (mod[0, 2:3] * r.grad_a[clip]).astype(BF16)
    r.grad_branch[own_rows, :] = low_a
    grad_mixed = dot_nt(low_a, r.w_out_a[...]).astype(BF16)
    scaled, plain = side_masks(BF16, scale_qk), side_masks(BF16, 1.0)
    lane = lax.broadcasted_iota(jnp.int32, (1, LANES), 1)
    for first in range(0, heads // 2, GROUP):
        pairs = range(first, min(first + GROUP, heads // 2))
        scores, grads, softs, backs = [], [], [], []
        for pair in pairs:
            gm = grad_mixed[:, pair * LANES : (pair + 1) * LANES]
            scores.append(
                dot_nt(both_sides(columns(r.qkv_a, 1, pair), scaled), columns(r.qkv_a, 0, pair))
            )
            grads.append(dot_nt(both_sides(columns(r.qkv_a, 2, pair), plain), gm))
        for pair, score, grad in zip(pairs, scores, grads):
            low, back = [], []
            for side in range(2):
                mine = slice(side * rows, (side + 1) * rows)
                head = 2 * pair + side
                soft = jnp.exp(score[mine] - r.lse[0, head : head + 1])
                inner = jnp.sum(soft * grad[mine], axis=0, keepdims=True)
                back.append((soft * (grad[mine] - inner)).astype(BF16))
                low.append(soft.astype(BF16))
            softs.append(jnp.concatenate(low, axis=0))
            backs.append(jnp.concatenate(back, axis=0))
        for pair, soft, back in zip(pairs, softs, backs):
            gm = grad_mixed[:, pair * LANES : (pair + 1) * LANES]
            query, key = (columns(r.qkv_a, part, pair) for part in (0, 1))
            start = pair * LANES
            r.grad_qkv[own_rows, start : start + LANES] = dot_tn(
                back, both_sides(key, scaled)
            ).astype(BF16)
            for part, total, factor in ((1, dot(back, query), scale_qk), (2, dot(soft, gm), 1.0)):
                joined = jnp.where(lane < HEAD_DIM, total[:rows], total[rows:])
                start = part * width + pair * LANES
                r.grad_qkv[own_rows, start : start + LANES] = (joined * factor).astype(BF16)
    grad_hidden = dot_nt(r.grad_qkv[own_rows, :], r.w_qkv_a[...])
    normed_a, inv_a = norm(r.tokens[0].astype(F32))
    r.mods[0, pl.ds(clip, 1)] = column_sum(grad_hidden)
    r.mods[1, pl.ds(clip, 1)] = column_sum(grad_hidden * normed_a)
    r.grad_tokens[0] = r.grad_a[clip] + norm_back(
        grad_hidden, normed_a, inv_a, 1.0 + mod[0, 1:2]
    )


class Halving:
    def __init__(self, sums, landings, sends, recvs, bits):
        self.sums, self.landings, self.sends, self.recvs = sums, landings, sends, recvs
        self.bits = bits

    def share(self, stage, number, keep):
        me = lax.axis_index("clip")
        later = sorted(self.bits[stage + 1 :])
        spot = sum(((number >> i) & 1) << (bit - 1) for i, bit in enumerate(later))
        for bit in self.bits[: stage + 1]:
            mine = lax.rem(me // (1 << bit), 2)
            if bit == self.bits[stage] and not keep:
                mine = 1 - mine
            spot = spot + mine * (1 << (bit - 1))
        return spot

    def count(self, stage):
        return 1 << (len(self.bits) - 1 - stage)

    def copy(self, stage, number):
        at = sum(self.count(i) for i in range(stage)) + number
        return remote(
            self.sums.at[:, self.share(stage, number, False)],
            self.landings.at[:, at], self.sends.at[at], self.recvs.at[at],
            clip=partner("clip", self.bits[stage]),
        )

    def send(self, stage):
        for number in range(self.count(stage)):
            self.copy(stage, number).start()

    def fold(self, stage):
        for number in range(self.count(stage)):
            self.copy(stage, number).wait_recv()
            at = sum(self.count(i) for i in range(stage)) + number
            spot = self.share(stage, number, True)
            self.sums[:, spot] = (
                self.sums[:, spot].astype(F32) + self.landings[:, at].astype(F32)
            ).astype(BF16)

    def own(self):
        return self.sums[:, self.share(len(self.bits) - 1, 0, True)]

    def drain(self):
        for stage in range(len(self.bits)):
            for number in range(self.count(stage)):
                self.copy(stage, number).wait_send()


class Frames:
    def __init__(self, away, landing, sends, recvs):
        self.away, self.landing, self.sends, self.recvs = away, landing, sends, recvs

    def copy(self, distance):
        count = self.away.shape[0]
        frame = lax.rem(lax.axis_index("frame") + distance, count)
        return remote(
            self.away.at[frame], self.landing.at[distance - 1],
            self.sends.at[distance - 1], self.recvs.at[distance - 1], frame=frame,
        )

    def send(self, piece):
        count = self.away.shape[0]
        for frame in range(count):
            self.away[frame] = piece(frame)
        for distance in range(1, count):
            self.copy(distance).start()

    def finish(self):
        total = self.away[lax.axis_index("frame")].astype(F32)
        for distance in range(1, self.away.shape[0]):
            self.copy(distance).wait_recv()
            total = total + self.landing[distance - 1].astype(F32)
        return total

    def drain(self):
        for distance in range(1, self.away.shape[0]):
            self.copy(distance).wait_send()


def cut(array, number, count):
    cols = array.shape[1] // count
    return array[:, number * cols : (number + 1) * cols]


def thirds_in_rows(values):
    high = values.astype(BF16).astype(F32)
    mid = (values - high).astype(BF16).astype(F32)
    low = (values - high) - mid
    return jnp.concatenate((high, mid, low, jnp.zeros_like(low)), axis=0).astype(BF16)


def side_by_side(tiles):
    return jnp.concatenate([tiles[i] for i in range(tiles.shape[0])], axis=1)


def backward_kernel(heads, clips, n, n_frame, r):
    step = pl.program_id(0)
    rows, width = r.tokens.shape[1:]
    tiles = 4
    half = n // 2
    share = width // n
    first_t = clips
    first_s = clips + tiles
    first_w = 2 * clips + tiles
    last = first_w + tiles - 1
    sibling = partner("clip", 0)
    barrier = pltpu.get_barrier_semaphore()
    bits = list(range(1, n.bit_length() - 1))
    frame = lax.axis_index("frame")
    place = lax.axis_index("clip")

    feed_in = Halving(r.sum_in, r.land_in, r.in_send, r.in_recv, bits)
    feed_out = Halving(r.sum_out, r.land_out, r.out_send, r.out_recv, bits[::-1])

    def units_of(name):
        sums, land = getattr(r, "sum_" + name), getattr(r, "land_" + name)
        sends, recvs = getattr(r, name + "_send"), getattr(r, name + "_recv")
        return [
            Halving(
                sums.at[pl.ds(i, 1)], land.at[pl.ds(i, 1)], sends.at[i], recvs.at[i],
                bits[:: 1 - 2 * (i % 2)],
            )
            for i in range(tiles)
        ]

    temporal, spatial = units_of("t"), units_of("s")
    stages = len(bits)

    regions = {"t": r.w_qkv_a_vmem, "s": r.w_qkv_b_vmem}

    def tile_cols(tile):
        return pl.ds(pl.multiple_of(lax.rem(tile, 3) * width, width), width)

    def tile_copies(name, tile):
        sends, recvs = getattr(r, name + "_core_send"), getattr(r, name + "_core_recv")
        return [
            remote(
                regions[name].at[share_rows(number, False, share), tile_cols(tile)],
                getattr(r, "core_" + name).at[tile, number],
                sends.at[tile, number], recvs.at[tile, number], clip=sibling,
            )
            for number in range(half)
        ]

    def tile_sent(name, tile):
        for copy in tile_copies(name, tile):
            copy.wait_send()

    def fold_core(name, which):
        sums, core = getattr(r, "sum_" + name), getattr(r, "core_" + name)
        for tile in which:
            for copy in tile_copies(name, tile):
                copy.wait_recv()
            sums[tile] = (sums[tile].astype(F32) + core[tile].astype(F32)).astype(BF16)

    frames = {
        name: Frames(
            getattr(r, "away_" + name), getattr(r, "near_" + name),
            getattr(r, name + "_z_send"), getattr(r, name + "_z_recv"),
        )
        for name in ("in", "out", "t", "s", "mod")
    }

    spaces = (r.left, r.left_out, r.grad_branch)

    def mod_tile(part):
        return pltpu.make_async_copy(
            r.w_mod.at[:, pl.ds(part * width, width)],
            spaces[part % 3].at[pl.ds(0, width)], r.mod_sems.at[part],
        )

    def mod_sums():
        total = None
        for part in range(9):
            mod_tile(part).wait()
            term = dot_nt(thirds_in_rows(r.mods[part]), spaces[part % 3][:width])
            total = term if total is None else total + term
            if part + 3 < 9:
                mod_tile(part + 3).start()
        pad = r.mods.shape[1]
        total = total[:pad] + total[pad : 2 * pad] + total[2 * pad : 3 * pad]
        joined = side_by_side(r.mods)
        total = total * r.silu_grad[...]
        frames["mod"].send(
            lambda other: jnp.concatenate((total, cut(joined, other, n_frame)), axis=1)
        )

    def spread_mods(distance):
        return remote(
            r.mod_share, r.gathered.at[place], r.mod_send.at[distance - 1],
            r.mod_recv.at[distance - 1], clip=lax.rem(place + distance, n),
        )

    own_mods = pltpu.make_async_copy(r.mod_share, r.gathered.at[place], r.mod_sems.at[9])

    def to_frames(units, name):
        owned = [unit.own()[0] for unit in units]
        wide = jnp.concatenate(owned[:-1], axis=1)
        frames[name].send(
            lambda other: jnp.concatenate(
                (cut(wide, other, n_frame), cut(owned[-1], other, n_frame)), axis=1
            )
        )

    def from_frames(name, wide, narrow):
        total = frames[name].finish()
        wide[...] = total[:, : wide.shape[1]]
        narrow[...] = total[:, wide.shape[1] :]

    def two_high(array):
        rows = array.shape[0] // 2
        return jnp.concatenate((array[:rows], array[rows:]), axis=1)

    loads = [
        pltpu.make_async_copy(r.keep_in, r.sum_in, r.load_sems.at[0]),
        pltpu.make_async_copy(r.came_in, r.core_t, r.load_sems.at[1]),
        pltpu.make_async_copy(r.keep_out, r.sum_out, r.load_sems.at[2]),
        pltpu.make_async_copy(r.came_out, r.core_s, r.load_sems.at[3]),
    ]
    lefts_t = [
        pltpu.make_async_copy(r.hidden_b, r.left, r.load_sems.at[4]),
        pltpu.make_async_copy(r.mixed_b, r.left_out, r.load_sems.at[5]),
        pltpu.make_async_copy(r.grad_branch_b, r.grad_branch, r.load_sems.at[6]),
    ]
    lefts_s = [
        pltpu.make_async_copy(r.hidden_a, r.left, r.load_sems.at[7]),
        pltpu.make_async_copy(r.mixed_a, r.left_out, r.load_sems.at[8]),
    ]
    r.w_qkv_a = Late(r.w_qkv_a_hbm, r.w_qkv_a_vmem, r.load_sems.at[9], first_s)

    @pl.when(step == 0)
    def _():
        for distance in range(1, n):
            greet(barrier, clip=lax.rem(place + distance, n))
        for distance in range(1, n_frame):
            greet(barrier, frame=lax.rem(frame + distance, n_frame))
        for copy in loads + lefts_t:
            copy.start()
        r.mods[...] = jnp.zeros_like(r.mods)
        for clip in range(clips):
            for row, part in enumerate((6, 7, 8, 5)):
                r.mods[part, clip : clip + 1] = r.sums[clip, row : row + 1]

    @pl.when(step < clips)
    def _():
        temporal_backward(r, step, pl.multiple_of(step * rows, rows))

    @pl.when(step == 0)
    def _():
        for copy in loads:
            copy.wait()
        for tile in range(tiles):
            r.sum_in[tile] = (
                r.sum_in[tile].astype(F32) + r.core_t[tile].astype(F32)
            ).astype(BF16)
        per = r.sum_out.shape[1] // tiles
        for tile in range(tiles):
            which = slice(tile * per, (tile + 1) * per)
            came = r.core_s[tile].reshape(r.sum_out[0, which].shape)
            r.sum_out[0, which] = (
                r.sum_out[0, which].astype(F32) + came.astype(F32)
            ).astype(BF16)
        pl.semaphore_wait(barrier, n - 1 + n_frame - 1)
        pl.semaphore_signal(
            r.free, inc=1, device_id={"clip": sibling}, device_id_type=pl.DeviceIdType.MESH
        )
        feed_in.send(0)
        feed_out.send(0)

    def weight_tile(name, tile):
        region = regions[name]

        @pl.when(tile < tiles - 1)
        def _():
            cols = pl.ds(pl.multiple_of(tile * width, width), width)
            region[:, tile_cols(tile)] = dot_tn(r.left[...], r.grad_qkv[:, cols]).astype(BF16)

        @pl.when(tile == tiles - 1)
        def _():
            region[:, tile_cols(tile)] = dot_tn(r.left_out[...], r.grad_branch[...]).astype(BF16)

        for copy in tile_copies(name, tile):
            copy.start()
        for number in range(half):
            getattr(r, "sum_" + name)[tile, number] = region[
                share_rows(number, True, share), tile_cols(tile)
            ]

    @pl.when((step >= first_t) & (step < first_s))
    def _():
        tile = step - first_t

        @pl.when(tile == 0)
        def _():
            for copy in lefts_t:
                copy.wait()
            pl.semaphore_wait(r.free, 1)

        pl.when(tile == 3)(lambda: tile_sent("t", 0))
        weight_tile("t", tile)

        @pl.when(tile == tiles - 1)
        def _():
            for copy in lefts_s:
                copy.start()

    @pl.when((step >= first_s) & (step < first_w))
    def _():
        clip = step - first_s

        @pl.when(clip == 0)
        def _():
            for tile in range(1, tiles):
                tile_sent("t", tile)
            r.w_qkv_a.copy.start()

        spatial_backward(r, heads, clip, pl.multiple_of(clip * rows, rows))

    @pl.when(step == first_s - 1)
    def _():
        for unit in (feed_in, feed_out):
            unit.fold(0)
            if stages > 1:
                unit.send(1)

    @pl.when(step == first_s)
    def _():
        for tile, unit in enumerate(temporal):
            fold_core("t", (tile,))
            unit.send(0)

    @pl.when(step == first_s + 1)
    def _():
        for stage in range(1, stages):
            for unit in (feed_in, feed_out):
                unit.fold(stage)
                if stage + 1 < stages:
                    unit.send(stage + 1)
        owned_in, owned_out = side_by_side(feed_in.own()), feed_out.own()[0]
        frames["in"].send(lambda other: cut(owned_in, other, n_frame))
        frames["out"].send(lambda other: two_high(cut(owned_out, other, n_frame)))

    @pl.when(step == first_s + 2)
    def _():
        for unit in temporal:
            unit.fold(0)
            if stages > 1:
                unit.send(1)

    @pl.when(step == first_s + 3)
    def _():
        for stage in range(1, stages):
            for unit in temporal:
                unit.fold(stage)
                if stage + 1 < stages:
                    unit.send(stage + 1)
        to_frames(temporal, "t")

    @pl.when(step >= first_w)
    def _():
        tile = step - first_w

        @pl.when(tile == 0)
        def _():
            for copy in lefts_s:
                copy.wait()

        pl.when(tile == 3)(lambda: tile_sent("s", 0))
        weight_tile("s", tile)

    for tile in range(tiles - 1):

        @pl.when(step == first_w + 1 + tile)
        def _():
            fold_core("s", (tile,))
            spatial[tile].send(0)

    @pl.when(step == last)
    def _():
        fold_core("s", (tiles - 1,))
        spatial[tiles - 1].send(0)
        for part in range(3):
            mod_tile(part).start()
        mod_sums()
        r.done_in[...] = frames["in"].finish()
        total = frames["out"].finish()
        high = total.shape[0]
        r.done_out[:high] = cut(total, 0, 2)
        r.done_out[high:] = cut(total, 1, 2)
        from_frames("t", r.done_tq, r.done_to)
        for stage in range(stages):
            for unit in spatial:
                unit.fold(stage)
                if stage + 1 < stages:
                    unit.send(stage + 1)
            if stage == 0:
                r.mod_share[...] = frames["mod"].finish()
                for distance in range(1, n):
                    spread_mods(distance).start()
                own_mods.start()
        to_frames(spatial, "s")
        from_frames("s", r.done_sq, r.done_so)
        own_mods.wait()
        for distance in range(1, n):
            spread_mods(distance).wait()
        for unit in (feed_in, feed_out, *temporal, *spatial):
            unit.drain()
        for name in frames:
            frames[name].drain()
        for tile in range(1, tiles):
            tile_sent("s", tile)


def backward_call(fwd, tok, mod, spread, weights, modulate_w, silu_grad, n, n_frame):
    clips, rows, width = tok.shape
    ff = weights["mlp_in"].shape[1]
    heads = width // HEAD_DIM
    tokens_here = clips * rows
    tiles = 4
    half, share, tall = n // 2, width // n, ff // n
    first_s, first_w = clips + tiles, 2 * clips + tiles

    def struct(last, dtype=BF16):
        return jax.ShapeDtypeStruct((clips, rows, last), dtype)

    mod_spec = pl.BlockSpec(
        (1,) + mod.shape[1:],
        lambda s: (
            jnp.where(s < first_s, jnp.minimum(s, clips - 1), jnp.minimum(s - first_s, clips - 1)),
            0, 0,
        ),
    )
    anywhere = pl.BlockSpec(memory_space=pl.ANY)
    pad, mod_cols = silu_grad.shape[0], width + 9 * width // n_frame
    whole = pl.BlockSpec(fwd.sums.shape, lambda s: (0, 0, 0), pipeline_mode=pl.Buffered(1))
    whole_grad = pl.BlockSpec(silu_grad.shape, lambda s: (0, 0), pipeline_mode=pl.Buffered(1))
    ins = [
        ("mod", mod, mod_spec), ("sums", fwd.sums, whole), ("silu_grad", silu_grad, whole_grad),
        ("w_mod", modulate_w, anywhere),
    ]
    for name in ("q_prev", "q_own", "q_next", "sent_prev", "sent", "sent_next", "grad_q", "grad_b", "after_a"):
        array = getattr(fwd, name)
        ins.append((name, array, clip_spec(array, 0, clips, 1 if name in ("grad_q", "grad_b", "after_a") else 2)))
    for name, array in (
        ("tokens", tok), ("branch_a", fwd.branch_a), ("qkv_a", fwd.qkv_a), ("lse", fwd.lse)
    ):
        ins.append((name, array, clip_spec(array, first_s, clips, 1)))
    flat = (tokens_here, width)
    for name in ("hidden_b", "mixed_b", "grad_branch_b", "hidden_a", "mixed_a"):
        ins.append((name, getattr(fwd, name).reshape(flat), anywhere))
    core_shape = (tiles, half, share, width)
    ins += [
        ("keep_in", fwd.keep_in.reshape(core_shape), anywhere),
        ("came_in", fwd.came_in.reshape(core_shape), anywhere),
        ("keep_out", fwd.keep_out.reshape(1, half, tall, width), anywhere),
        ("came_out", fwd.came_out.reshape(core_shape), anywhere),
        ("w_qkv_a_hbm", weights["spatial_qkv"], anywhere),
    ]
    held = [
        ("spread", spread, 0), ("w_qkv_b", weights["temporal_qkv"], 0),
        ("w_out_a", weights["spatial_out"], first_s),
    ]
    grad_tokens = struct(width, F32)
    outs = [
        ("grad_tokens", grad_tokens, clip_spec(grad_tokens, first_s, clips, 1)),
        ("gathered", jax.ShapeDtypeStruct((n, pad, mod_cols), F32), None),
    ]
    dma = pltpu.SemaphoreType.DMA
    pieces = {
        "in": (share, ff // n_frame), "out": (tall, width // n_frame),
        "tq": (share, 3 * width // n_frame), "to": (share, width // n_frame),
        "sq": (share, 3 * width // n_frame), "so": (share, width // n_frame),
    }
    moved = half - 1
    scratch = [
        ("grad_a", pltpu.VMEM((clips, rows, width), F32)),
        ("grad_qkv", pltpu.VMEM((tokens_here, 3 * width), BF16)),
        ("grad_branch", pltpu.VMEM(flat, BF16)), ("left", pltpu.VMEM(flat, BF16)),
        ("left_out", pltpu.VMEM(flat, BF16)),
        ("w_qkv_a_vmem", pltpu.VMEM(weights["spatial_qkv"].shape, BF16)),
        ("sum_in", pltpu.VMEM(core_shape, BF16)), ("land_in", pltpu.VMEM((tiles, moved, share, width), BF16)),
        ("in_send", dma((moved,))), ("in_recv", dma((moved,))),
        ("sum_out", pltpu.VMEM((1, half, tall, width), BF16)),
        ("land_out", pltpu.VMEM((1, moved, tall, width), BF16)),
        ("out_send", dma((moved,))), ("out_recv", dma((moved,))),
        ("load_sems", dma((10,))), ("free", pltpu.SemaphoreType.REGULAR),
        ("mods", pltpu.VMEM((9, pad, width), F32)), ("mod_sems", dma((10,))),
        ("mod_share", pltpu.VMEM((pad, mod_cols), F32)),
        ("mod_send", dma((n - 1,))), ("mod_recv", dma((n - 1,))),
    ]
    for name in ("t", "s"):
        scratch += [
            ("sum_" + name, pltpu.VMEM(core_shape, BF16)), ("core_" + name, pltpu.VMEM(core_shape, BF16)),
            ("land_" + name, pltpu.VMEM((tiles, moved, share, width), BF16)),
            (name + "_send", dma((tiles, moved))), (name + "_recv", dma((tiles, moved))),
            (name + "_core_send", dma((tiles, half))), (name + "_core_recv", dma((tiles, half))),
        ]
    for name, dims in pieces.items():
        shape = jax.ShapeDtypeStruct(dims, F32)
        outs.append(("done_" + name, shape, pl.BlockSpec(shape.shape, lambda s: (0, 0))))
    packed = {
        "in": (share, ff // n_frame), "out": (tall // 2, 2 * width // n_frame),
        "t": (share, 4 * width // n_frame), "s": (share, 4 * width // n_frame),
        "mod": (pad, mod_cols),
    }
    for name, dims in packed.items():
        kind = F32 if name == "mod" else BF16
        scratch += [
            ("away_" + name, pltpu.VMEM((n_frame, *dims), kind)),
            ("near_" + name, pltpu.VMEM((n_frame - 1, *dims), kind)),
            (name + "_z_send", dma((n_frame - 1,))), (name + "_z_recv", dma((n_frame - 1,))),
        ]
    return run_kernel(
        functools.partial(backward_kernel, heads, clips, n, n_frame), first_w + tiles,
        ins, held, outs, scratch, 2 * tokens_here * width * width * 20, collective=2,
    )


def thirds(values):
    high = values.astype(BF16)
    rest = values - high.astype(F32)
    mid = rest.astype(BF16)
    low = (rest - mid.astype(F32)).astype(BF16)
    return jnp.concatenate((high, mid, low), axis=0)


def local(
    tokens, target, loss_weight, timesteps, offsets, cond_table, modulate_w,
    spatial_qkv, spatial_out, temporal_qkv, temporal_out, mlp_in, mlp_out,
):
    clips, frames, patches, width = tokens.shape
    steps = cond_table.shape[0]
    heads = width // HEAD_DIM
    n_clip = lax.axis_size("clip")
    n_frame = lax.axis_size("frame")
    clip_at = lax.axis_index("clip")
    frame_at = lax.axis_index("frame")
    flat = (clips, patches, width)
    tok = tokens.reshape(flat)
    tgt = target.reshape(flat)

    condition = jnp.take(cond_table, timesteps, axis=0, mode="clip")
    cond_low = jax.nn.silu(condition).astype(BF16)
    cond_here = lax.dynamic_slice_in_dim(condition, clip_at * clips, clips)
    _, silu_pull = jax.vjp(jax.nn.silu, cond_here)
    low_here = lax.dynamic_slice_in_dim(cond_low, clip_at * clips, clips)
    mod = jnp.dot(low_here, modulate_w, preferred_element_type=F32).reshape(clips, 9, width)

    half = width // 2
    positions = (offsets + frame_at).astype(F32)
    freqs = jnp.exp(jnp.arange(half, dtype=F32) * (-math.log(10000.0) / half))
    angles = positions[:, None] * freqs
    posenc = jnp.concatenate((jnp.sin(angles), jnp.cos(angles)), axis=-1)[:, None, :]

    head_of = np.arange(width) // HEAD_DIM
    lane_ids = np.arange(LANES)
    to_heads = jnp.asarray((head_of[:, None] == lane_ids[None, :]).astype(BF16))
    tall = np.arange(2 * LANES) - LANES
    spread = jnp.asarray((tall[:, None] == head_of[None, :]).astype(BF16))
    group, inside = np.divmod(np.arange(6 * LANES), LANES)
    slot_at = np.where(inside < heads, group * SLOT + inside, -1)
    pack = jnp.asarray((slot_at[:, None] == lane_ids[None, :]).astype(BF16))
    weights = {
        "spatial_qkv": spatial_qkv, "spatial_out": spatial_out, "temporal_qkv": temporal_qkv,
        "temporal_out": temporal_out, "mlp_in": mlp_in, "mlp_out": mlp_out,
    }
    fwd = forward_call(
        tok, tgt, mod, posenc, loss_weight, (to_heads, spread, pack), weights, n_clip
    )

    pad = -(-clips // 8) * 8
    silu_grad = jnp.pad(silu_pull(jnp.ones_like(cond_here))[0], ((0, pad - clips), (0, 0)))
    bwd = backward_call(fwd, tok, mod, spread, weights, modulate_w, silu_grad, n_clip, n_frame)
    gathered = bwd.gathered.reshape(n_clip * pad, -1)

    def padded_rows(values):
        split = values.reshape((n_clip, clips) + values.shape[1:])
        sides = ((0, 0), (0, pad - clips)) + ((0, 0),) * (values.ndim - 1)
        return jnp.pad(split, sides).reshape((n_clip * pad,) + values.shape[1:])

    onehot = timesteps[:, None] == jnp.arange(steps, dtype=jnp.int32)[None, :]
    onehot = padded_rows(onehot.astype(BF16))
    grad_table = dot_tn(jnp.concatenate((onehot,) * 3, axis=0), thirds(gathered[:, :width]))
    mod_rows = width // n_clip
    low_rows = lax.dynamic_slice_in_dim(cond_low, clip_at * mod_rows, mod_rows, axis=1)
    low_rows = padded_rows(low_rows)
    grad_modulate = dot_tn(jnp.concatenate((low_rows,) * 3, axis=0), thirds(gathered[:, width:]))
    return (
        fwd.output.reshape(tokens.shape),
        bwd.grad_tokens.reshape(tokens.shape),
        grad_table,
        grad_modulate,
        bwd.done_sq,
        bwd.done_so,
        bwd.done_tq,
        bwd.done_to,
        bwd.done_in,
        bwd.done_out,
    )


def solution(mesh):
    placed = (
        P("clip", "frame", None, None), P("clip", "frame", None, None), P("clip"), P(), P("clip"),
    ) + (P(),) * 8
    return jax.shard_map(
        local,
        mesh=mesh,
        in_specs=placed,
        out_specs=(
            P("clip", "frame", None, None), P("clip", "frame", None, None), P(),
        ) + (P("clip", "frame"),) * 7,
        check_vma=False,
    )
```

```python
import functools
import math

import jax
import jax.numpy as jnp
import numpy as np
from jax import lax
from jax.experimental import pallas as pl
from jax.experimental.pallas import tpu as pltpu
from jax.sharding import PartitionSpec as P

HEAD_DIM = 64
NORM_EPSILON = 1e-06
F32 = jnp.float32
BF16 = jnp.bfloat16
LANES = 128
SLOT = 16
NO_KEY = -1e30
VMEM_LIMIT = 60 * 2**20
GROUP = 2
GELU_A = math.sqrt(2.0 / math.pi)
GELU_B = 0.044715


def dot(left, right):
    return lax.dot_general(left, right, (((1,), (0,)), ((), ())), preferred_element_type=F32)


def dot_nt(left, right):
    return lax.dot_general(left, right, (((1,), (1,)), ((), ())), preferred_element_type=F32)


def dot_tn(left, right):
    return lax.dot_general(left, right, (((0,), (0,)), ((), ())), preferred_element_type=F32)


def norm(values):
    centred = values - jnp.mean(values, axis=-1, keepdims=True)
    inv_std = lax.rsqrt(jnp.mean(centred * centred, axis=-1, keepdims=True) + NORM_EPSILON)
    return centred * inv_std, inv_std


def norm_back(grad_hidden, normed, inv_std, scale_plus):
    grad_normed = grad_hidden * scale_plus
    mean_grad = jnp.mean(grad_normed, axis=-1, keepdims=True)
    mean_cross = jnp.mean(grad_normed * normed, axis=-1, keepdims=True)
    return inv_std * (grad_normed - mean_grad - normed * mean_cross)


def column_sum(values):
    return jnp.sum(values, axis=0, keepdims=True)


def side_masks(dtype, value):
    lane = lax.broadcasted_iota(jnp.int32, (1, LANES), 1)
    return [jnp.where((lane < HEAD_DIM) == (side == 0), value, 0.0).astype(dtype) for side in (0, 1)]


class Refs:
    def __init__(self, names, refs):
        self.__dict__.update(zip(names, refs, strict=True))


class Late:
    def __init__(self, source, ref, sem, step):
        self.ref = ref
        self.copy = pltpu.make_async_copy(source, ref, sem)
        self.step = step
        self.waited = False

    def __getitem__(self, index):
        if not self.waited:
            pl.when(pl.program_id(0) == self.step)(self.copy.wait)
            self.waited = True
        return self.ref[index]


def partner(axis, bit):
    me = lax.axis_index(axis)
    return me + (1 << bit) - (2 << bit) * lax.rem(me // (1 << bit), 2)


def remote(source, target, send_sem, recv_sem, **where):
    return pltpu.make_async_remote_copy(
        src_ref=source, dst_ref=target, send_sem=send_sem, recv_sem=recv_sem,
        device_id=where, device_id_type=pl.DeviceIdType.MESH,
    )


def greet(barrier, **where):
    pl.semaphore_signal(barrier, inc=1, device_id=where, device_id_type=pl.DeviceIdType.MESH)


def run_kernel(body, steps, ins, weights, outs, scratch, flops, collective=None):
    anywhere = pl.BlockSpec(memory_space=pl.ANY)
    names = [name for name, *_ in ins] + [name + "_hbm" for name, *_ in weights]
    names += [name for name, *_ in outs]
    names += [name + "_vmem" for name, *_ in weights] + ["weight_sems"]
    names += [name for name, _ in scratch]

    def kernel(*refs):
        r = Refs(names, refs)
        lates = []
        for number, (name, _, step) in enumerate(weights):
            late = Late(
                getattr(r, name + "_hbm"), getattr(r, name + "_vmem"), r.weight_sems.at[number], step
            )
            lates.append(late)
            setattr(r, name, late)

        @pl.when(pl.program_id(0) == 0)
        def _():
            for late in lates:
                if late.step == 0:
                    late.copy.start()

        body(r)

        @pl.when(pl.program_id(0) == 0)
        def _():
            for late in lates:
                if late.step > 0:
                    late.copy.start()

    arrays = [array for _, array, _ in ins] + [array for _, array, _ in weights]
    shapes = [shape for _, shape, _ in outs]
    touched = sum(math.prod(a.shape) * a.dtype.itemsize for a in arrays + shapes)
    params = {} if collective is None else {"collective_id": collective, "has_side_effects": True}
    done = pl.pallas_call(
        kernel,
        grid=(steps,),
        in_specs=[spec for *_, spec in ins] + [anywhere] * len(weights),
        out_specs=[spec or anywhere for *_, spec in outs],
        out_shape=shapes,
        scratch_shapes=[pltpu.VMEM(a.shape, a.dtype) for _, a, _ in weights]
        + [pltpu.SemaphoreType.DMA((max(len(weights), 1),))]
        + [shape for _, shape in scratch],
        compiler_params=pltpu.CompilerParams(vmem_limit_bytes=VMEM_LIMIT, **params),
        cost_estimate=pl.CostEstimate(flops=flops, bytes_accessed=touched, transcendentals=0),
    )(*arrays)
    return Refs([name for name, *_ in outs], done)


def clip_spec(array, first, clips, depth=None):
    rest = array.shape[1:]
    mode = {} if depth is None else {"pipeline_mode": pl.Buffered(depth)}
    return pl.BlockSpec(
        (1,) + rest, lambda s: (jnp.clip(s - first, 0, clips - 1),) + (0,) * len(rest), **mode
    )


def spatial_forward(r, heads, clip):
    width = r.tokens.shape[-1]
    rows = r.tokens.shape[1]
    mod = r.mod
    inputs = r.tokens[0].astype(F32)
    normed, _ = norm(inputs)
    hidden = (normed * (1.0 + mod[0, 1:2]) + mod[0, 0:1]).astype(BF16)
    r.hidden_a[0] = hidden
    for part in range(3):
        cols = slice(part * width, (part + 1) * width)
        r.qkv_a[0, :, cols] = dot(hidden, r.w_qkv_a[:, cols]).astype(BF16)
    scaled, plain = side_masks(BF16, HEAD_DIM**-0.5), side_masks(BF16, 1.0)
    for first in range(0, heads // 2, 3):
        pairs = range(first, min(first + 3, heads // 2))
        scores, softs = [], []
        for pair in pairs:
            query, key = (columns(r.qkv_a, part, pair) for part in (0, 1))
            scores.append(dot_nt(both_sides(key, scaled), query))
        for pair, score in zip(pairs, scores):
            halves = []
            for side in range(2):
                mine = score[side * rows : (side + 1) * rows]
                top = jnp.max(mine, axis=0, keepdims=True)
                grown = jnp.exp(mine - top)
                total = jnp.sum(grown, axis=0, keepdims=True)
                halves.append((grown * (1.0 / total)).astype(BF16))
                head = 2 * pair + side
                r.lse[0, head : head + 1] = top + jnp.log(total)
            softs.append(jnp.concatenate(halves, axis=0))
        for pair, soft in zip(pairs, softs):
            value = columns(r.qkv_a, 2, pair)
            r.mixed_a[0, :, pair * LANES : (pair + 1) * LANES] = dot_tn(
                soft, both_sides(value, plain)
            ).astype(BF16)
    branch_a = dot(r.mixed_a[0], r.w_out_a[...])
    r.branch_a[0] = branch_a.astype(BF16)
    after_a = inputs + mod[0, 2:3] * branch_a
    r.after_held[clip] = after_a
    normed_b, _ = norm(after_a)
    r.hidden_held[clip] = (
        normed_b * (1.0 + mod[0, 4:5]) + (mod[0, 3:4] + r.posenc[0])
    ).astype(BF16)


def both_sides(array, masks):
    return jnp.concatenate((array * masks[0], array * masks[1]), axis=0)


def columns(ref, part, pair):
    start = part * (ref.shape[-1] // 3) + pair * LANES
    return ref[0, :, start : start + LANES]


def by_head(left, right, to_heads):
    return dot(left * right, to_heads)


def middle(r, clip, rows_at):
    width = r.target.shape[-1]
    rows = r.target.shape[1]
    ff = r.act.shape[-1]
    scale_qk = HEAD_DIM**-0.5
    mod = r.mod
    own_rows = pl.ds(rows_at, rows)
    store = r.w_qkv_a_vmem

    def kept(number, part):
        return store[number * rows : (number + 1) * rows, part * width : (part + 1) * width]

    three = jnp.concatenate((r.hidden_prev[clip], r.hidden_held[clip], r.hidden_next[clip]), axis=0)
    for part in range(3):
        cols = slice(part * width, (part + 1) * width)
        value = dot(three, r.w_qkv_b[:, cols]).astype(BF16)
        store[:, cols] = value
        if part == 0:
            for number, out in enumerate((r.q_prev, r.q_own, r.q_next)):
                out[0] = value[number * rows : (number + 1) * rows]
    frame = lax.axis_index("frame")
    absent = (frame == 0, None, frame == lax.axis_size("frame") - 1)
    scores = []
    for number in range(3):
        raw = by_head(kept(1, 0), kept(number, 1), r.to_heads[...]) * scale_qk
        if absent[number] is not None:
            raw = raw + jnp.where(absent[number], NO_KEY, 0.0)
        scores.append(raw)
    top = jnp.maximum(jnp.maximum(scores[0], scores[1]), scores[2])
    grown = [jnp.exp(entry - top) for entry in scores]
    inverse = 1.0 / (grown[0] + grown[1] + grown[2])
    soft = [entry * inverse for entry in grown]
    soft_low = [entry.astype(BF16) for entry in soft]
    to_width = r.spread[LANES : 2 * LANES]
    total = None
    for number in range(3):
        term = dot(soft_low[number], to_width) * kept(number, 2).astype(F32)
        total = term if total is None else total + term
    mixed = total.astype(BF16)
    r.mixed_b[0] = mixed
    branch_b = dot(mixed, r.w_out_b[...])
    r.grad_b[0] = branch_b
    after_b = r.after_held[clip] + mod[0, 5:6] * branch_b
    normed_c, inv_c = norm(after_b)
    hidden = (normed_c * (1.0 + mod[0, 7:8]) + mod[0, 6:7]).astype(BF16)
    r.hidden_c[own_rows, :] = hidden
    parts = ff // width
    ahead = dot(hidden, r.w_in[:, :width])
    for part in range(parts):
        cols = slice(part * width, (part + 1) * width)
        upward = ahead
        if part + 1 < parts:
            ahead = dot(hidden, r.w_in[:, (part + 1) * width : (part + 2) * width])
        squared = upward * upward
        bent = jnp.tanh(upward * (GELU_A + (GELU_A * GELU_B) * squared))
        share = 0.5 + 0.5 * bent
        r.act[own_rows, cols] = (upward * share).astype(BF16)
        steep = (1.0 - bent * bent) * (0.5 * GELU_A + (1.5 * GELU_A * GELU_B) * squared)
        r.grad_up[own_rows, cols] = (share + upward * steep).astype(BF16)
    branch_c = dot(r.act[own_rows, :], r.w_mlp[...])
    result = after_b + mod[0, 8:9] * branch_c
    r.output[0] = result.astype(BF16)
    grad_result = r.weight[clip] * (result - r.target[0].astype(F32))
    r.sums[0, 2:3] = column_sum(grad_result * branch_c)
    low_c = (mod[0, 8:9] * grad_result).astype(BF16)
    r.grad_branch_c[own_rows, :] = low_c
    ahead = dot_nt(low_c, r.w_mlp[:width, :])
    for part in range(parts):
        cols = slice(part * width, (part + 1) * width)
        grad_act = ahead
        if part + 1 < parts:
            ahead = dot_nt(low_c, r.w_mlp[(part + 1) * width : (part + 2) * width, :])
        r.grad_up[own_rows, cols] = (grad_act * r.grad_up[own_rows, cols].astype(F32)).astype(BF16)
    grad_hidden = dot_nt(r.grad_up[own_rows, :], r.w_in[...])
    r.sums[0, 0:1] = column_sum(grad_hidden)
    r.sums[0, 1:2] = column_sum(grad_hidden * normed_c)
    grad_after = grad_result + norm_back(grad_hidden, normed_c, inv_c, 1.0 + mod[0, 7:8])
    r.sums[0, 3:4] = column_sum(grad_after * r.grad_b[0])
    r.grad_b[0] = grad_after
    low_b = (mod[0, 5:6] * grad_after).astype(BF16)
    r.grad_branch_b[0] = low_b
    grad_mixed = dot_nt(low_b, r.w_out_b[...]).astype(BF16)
    grad_soft = [by_head(grad_mixed, kept(number, 2), r.to_heads[...]) for number in range(3)]
    inner = soft[0] * grad_soft[0] + soft[1] * grad_soft[1] + soft[2] * grad_soft[2]
    grad_scores = [(soft[number] * (grad_soft[number] - inner)).astype(BF16) for number in range(3)]
    total = None
    for number in range(3):
        term = dot(grad_scores[number], to_width) * kept(number, 1).astype(F32)
        total = term if total is None else total + term
    r.grad_q[0] = (total * scale_qk).astype(BF16)
    r.sent_held[clip, :, :width] = grad_mixed
    r.sent_held[clip, :, width:] = dot(
        jnp.concatenate(soft_low + grad_scores, axis=1), r.pack[...]
    ).astype(BF16)


def share_rows(number, keep, share):
    core = lax.rem(lax.axis_index("clip"), 2)
    spot = 2 * number + (core if keep else 1 - core)
    return pl.ds(pl.multiple_of(spot * share, share), share)


def forward_kernel(heads, clips, n, r):
    step = pl.program_id(0)
    rows, width = r.tokens.shape[1:]
    ff = r.act.shape[-1]
    in_steps = ff // width
    out_steps = n // 2
    share = ff // n
    last = 2 * clips + in_steps + out_steps - 1
    frame = lax.axis_index("frame")
    has_prev = frame > 0
    has_next = frame < lax.axis_size("frame") - 1
    no_prev = jnp.logical_not(has_prev)
    no_next = jnp.logical_not(has_next)
    core = lax.rem(lax.axis_index("clip"), 2)
    sibling = partner("clip", 0)
    barrier = pltpu.get_barrier_semaphore()

    def halo(way, clip):
        return remote(
            r.hidden_held.at[clip], (r.hidden_prev, r.hidden_next)[way].at[clip],
            r.halo_send.at[way, clip], r.halo_recv.at[way, clip],
            frame=frame + 1 if way == 0 else frame - 1,
        )

    def packet(way, clip):
        return remote(
            r.sent_held.at[clip], (r.sent_prev, r.sent_next)[way].at[clip],
            r.sent_send.at[way, clip], r.sent_recv.at[way, clip],
            frame=frame + 1 if way == 0 else frame - 1,
        )

    low_share = width // n

    def in_tile(tile):
        return [
            remote(
                r.stage.at[lax.rem(tile, 2), share_rows(number, False, low_share)],
                r.came_in.at[tile, number],
                r.in_send.at[tile, number], r.in_recv.at[tile, number], clip=sibling,
            )
            for number in range(n // 2)
        ]

    def in_kept(tile):
        return [
            pltpu.make_async_copy(
                r.stage.at[lax.rem(tile, 2), share_rows(number, True, low_share)],
                r.keep_in.at[tile, number], r.in_keep.at[tile, number],
            )
            for number in range(n // 2)
        ]

    def in_sent(tile):
        for copy in in_tile(tile):
            copy.wait_send()
        for copy in in_kept(tile):
            copy.wait()

    def out_part(tile, which):
        return r.stage.at[
            lax.rem(tile + in_steps, 2), pl.ds(pl.multiple_of(which * share, share), share)
        ]

    def out_tile(tile):
        return remote(
            out_part(tile, 1 - core), r.came_out.at[tile],
            r.out_send.at[tile], r.out_recv.at[tile], clip=sibling,
        )

    def out_kept(tile):
        return pltpu.make_async_copy(
            out_part(tile, core), r.keep_out.at[tile], r.out_keep.at[tile]
        )

    def save(clip):
        return [
            pltpu.make_async_copy(r.after_held.at[clip], r.after_a.at[clip], r.save_sems.at[0, clip]),
            pltpu.make_async_copy(
                r.hidden_held.at[clip], r.hidden_b.at[clip], r.save_sems.at[1, clip]
            ),
        ]

    def save_sent(clip):
        return pltpu.make_async_copy(r.sent_held.at[clip], r.sent.at[clip], r.save_sems.at[2, clip])

    def fill(way, clip):
        zeros = (r.hidden_prev, r.hidden_next)[way].at[clip]
        target = (r.sent_prev, r.sent_next)[way].at[clip]
        return [
            pltpu.make_async_copy(zeros, target.at[:, pl.ds(0, width)], r.save_sems.at[3, clip]),
            pltpu.make_async_copy(
                zeros.at[:, pl.ds(0, LANES)], target.at[:, pl.ds(width, LANES)],
                r.save_sems.at[4, clip],
            ),
        ]

    @pl.when(step == 0)
    def _():
        greet(barrier, clip=sibling)
        pl.when(has_prev)(lambda: greet(barrier, frame=frame - 1))
        pl.when(has_next)(lambda: greet(barrier, frame=frame + 1))

        @pl.when(no_prev)
        def _():
            r.hidden_prev[...] = jnp.zeros_like(r.hidden_prev)
            for clip in range(clips):
                for copy in fill(0, clip):
                    copy.start()

        @pl.when(no_next)
        def _():
            r.hidden_next[...] = jnp.zeros_like(r.hidden_next)
            for clip in range(clips):
                for copy in fill(1, clip):
                    copy.start()

    @pl.when(step < clips)
    def _():
        spatial_forward(r, heads, step)

        @pl.when(step == 0)
        def _():
            pl.semaphore_wait(
                barrier, 1 + jnp.where(has_prev, 1, 0) + jnp.where(has_next, 1, 0)
            )

        pl.when(has_next)(lambda: halo(0, step).start())
        pl.when(has_prev)(lambda: halo(1, step).start())
        for copy in save(step):
            copy.start()

    @pl.when((step >= clips) & (step < 2 * clips))
    def _():
        clip = step - clips
        pl.when(has_prev)(lambda: halo(0, clip).wait_recv())
        pl.when(has_next)(lambda: halo(1, clip).wait_recv())
        middle(r, clip, pl.multiple_of(clip * rows, rows))
        pl.when(has_next)(lambda: packet(0, clip).start())
        pl.when(has_prev)(lambda: packet(1, clip).start())
        save_sent(clip).start()

    @pl.when((step >= 2 * clips) & (step < 2 * clips + in_steps))
    def _():
        tile = step - 2 * clips

        pl.when(tile >= 2)(lambda: in_sent(tile - 2))
        cols = pl.ds(pl.multiple_of(tile * width, width), width)
        r.stage[lax.rem(tile, 2), :width] = dot_tn(r.hidden_c[...], r.grad_up[:, cols]).astype(BF16)
        for copy in in_tile(tile) + in_kept(tile):
            copy.start()

    @pl.when(step >= 2 * clips + in_steps)
    def _():
        tile = step - 2 * clips - in_steps

        pl.when(tile < 2)(lambda: in_sent(in_steps + tile - 2))

        @pl.when(tile >= 2)
        def _():
            out_tile(tile - 2).wait_send()
            out_kept(tile - 2).wait()

        cols = pl.ds(pl.multiple_of(tile * 2 * share, 2 * share), 2 * share)
        r.stage[lax.rem(tile + in_steps, 2), : 2 * share] = dot_tn(
            r.act[:, cols], r.grad_branch_c[...]
        ).astype(BF16)
        out_tile(tile).start()
        out_kept(tile).start()

    @pl.when(step == last)
    def _():
        for clip in range(clips):
            for copy in save(clip):
                copy.wait()
            save_sent(clip).wait()

            @pl.when(has_next)
            def _():
                halo(0, clip).wait_send()
                packet(0, clip).wait_send()
                packet(1, clip).wait_recv()

            @pl.when(has_prev)
            def _():
                halo(1, clip).wait_send()
                packet(1, clip).wait_send()
                packet(0, clip).wait_recv()

            for way, absent in ((0, no_prev), (1, no_next)):

                @pl.when(absent)
                def _():
                    for copy in fill(way, clip):
                        copy.wait()

        for tile in range(in_steps):
            for copy in in_tile(tile):
                copy.wait_recv()
        for tile in range(out_steps):
            out_tile(tile).wait_recv()
        for tile in range(out_steps - 2, out_steps):
            out_tile(tile).wait_send()
            out_kept(tile).wait()


def forward_call(tok, target, mod, posenc, weight, tables, weights, n):
    clips, rows, width = tok.shape
    ff = weights["mlp_in"].shape[1]
    heads = width // HEAD_DIM
    tokens_here = clips * rows
    in_steps, out_steps, share = ff // width, n // 2, ff // n
    to_heads, spread, pack = tables

    def struct(last, dtype=BF16):
        return jax.ShapeDtypeStruct((clips, rows, last), dtype)

    def early(array):
        return clip_spec(array, 0, clips)

    def late(array):
        return clip_spec(array, clips, clips)

    mod_spec = pl.BlockSpec(
        (1,) + mod.shape[1:],
        lambda s: (jnp.where(s < clips, s, jnp.minimum(s - clips, clips - 1)), 0, 0),
    )
    ins = [
        ("tokens", tok, early(tok)), ("posenc", posenc, early(posenc)), ("mod", mod, mod_spec),
        ("target", target, clip_spec(target, clips, clips, 1)), ("weight", weight, pl.BlockSpec(memory_space=pltpu.SMEM)),
    ]
    held = [
        ("w_qkv_a", weights["spatial_qkv"], 0), ("w_out_a", weights["spatial_out"], 0),
        ("w_qkv_b", weights["temporal_qkv"], clips), ("to_heads", to_heads, clips),
        ("spread", spread, clips), ("w_out_b", weights["temporal_out"], clips),
        ("w_in", weights["mlp_in"], clips), ("w_mlp", weights["mlp_out"], clips), ("pack", pack, clips),
    ]
    outs = []
    for name, shape in (
        ("hidden_a", struct(width)), ("qkv_a", struct(3 * width)), ("mixed_a", struct(width)),
        ("branch_a", struct(width)),
        ("lse", jax.ShapeDtypeStruct((clips, -(-heads // 8) * 8, rows), F32)),
    ):
        outs.append((name, shape, clip_spec(shape, 0, clips, 1)))
    for name, shape in (
        ("output", struct(width)), ("grad_b", struct(width, F32)), ("mixed_b", struct(width)),
        ("grad_branch_b", struct(width)), ("q_own", struct(width)), ("q_prev", struct(width)),
        ("q_next", struct(width)), ("grad_q", struct(width)),
        ("sums", jax.ShapeDtypeStruct((clips, 8, width), F32)),
    ):
        outs.append((name, shape, clip_spec(shape, clips, clips, 1)))
    outs += [
        ("after_a", struct(width, F32), None), ("hidden_b", struct(width), None),
        ("sent", struct(width + LANES), None), ("sent_prev", struct(width + LANES), None),
        ("sent_next", struct(width + LANES), None),
    ]
    tile_in = jax.ShapeDtypeStruct((in_steps, n // 2, width // n, width), BF16)
    tile_out = jax.ShapeDtypeStruct((out_steps, share, width), BF16)
    outs += [
        ("keep_in", tile_in, None), ("came_in", tile_in, None), ("keep_out", tile_out, None),
        ("came_out", tile_out, None),
    ]
    dma = pltpu.SemaphoreType.DMA
    scratch = [
        ("after_held", pltpu.VMEM((clips, rows, width), F32)),
        ("hidden_held", pltpu.VMEM((clips, rows, width), BF16)),
        ("hidden_prev", pltpu.VMEM((clips, rows, width), BF16)),
        ("hidden_next", pltpu.VMEM((clips, rows, width), BF16)),
        ("sent_held", pltpu.VMEM((clips, rows, width + LANES), BF16)),
        ("act", pltpu.VMEM((tokens_here, ff), BF16)),
        ("grad_up", pltpu.VMEM((tokens_here, ff), BF16)),
        ("hidden_c", pltpu.VMEM((tokens_here, width), BF16)),
        ("grad_branch_c", pltpu.VMEM((tokens_here, width), BF16)),
        ("stage", pltpu.VMEM((2, max(width, 2 * share), width), BF16)),
        ("halo_send", dma((2, clips))), ("halo_recv", dma((2, clips))),
        ("sent_send", dma((2, clips))), ("sent_recv", dma((2, clips))),
        ("in_send", dma((in_steps, n // 2))), ("in_recv", dma((in_steps, n // 2))),
        ("in_keep", dma((in_steps, n // 2))), ("out_send", dma((out_steps,))),
        ("out_recv", dma((out_steps,))), ("out_keep", dma((out_steps,))),
        ("save_sems", dma((5, clips))),
    ]
    return run_kernel(
        functools.partial(forward_kernel, heads, clips, n), 2 * clips + in_steps + out_steps,
        ins, held, outs, scratch, 2 * tokens_here * width * width * 46, collective=1,
    )


def temporal_backward(r, clip, rows_at):
    width = r.tokens.shape[-1]
    rows = r.tokens.shape[1]
    scale_qk = HEAD_DIM**-0.5
    own_rows = pl.ds(rows_at, rows)
    grad_key = None
    grad_value = None
    for number, (source, query) in enumerate(
        ((r.sent_prev, r.q_prev), (r.sent, r.q_own), (r.sent_next, r.q_next))
    ):
        other = 2 - number
        table = source[0, :, width:]
        low = LANES - SLOT * other
        soft = dot(table, r.spread[low : low + LANES])
        low = LANES - SLOT * (3 + other)
        score = dot(table, r.spread[low : low + LANES])
        key_term = score * query[0].astype(F32)
        value_term = soft * source[0, :, :width].astype(F32)
        grad_key = key_term if grad_key is None else grad_key + key_term
        grad_value = value_term if grad_value is None else grad_value + value_term
    r.grad_qkv[own_rows, :width] = r.grad_q[0]
    r.grad_qkv[own_rows, width : 2 * width] = (grad_key * scale_qk).astype(BF16)
    r.grad_qkv[own_rows, 2 * width :] = grad_value.astype(BF16)
    grad_hidden = dot_nt(r.grad_qkv[own_rows, :], r.w_qkv_b[...])
    normed_b, inv_b = norm(r.after_a[0])
    r.mods[3, pl.ds(clip, 1)] = column_sum(grad_hidden)
    r.mods[4, pl.ds(clip, 1)] = column_sum(grad_hidden * normed_b)
    r.grad_a[clip] = r.grad_b[0] + norm_back(grad_hidden, normed_b, inv_b, 1.0 + r.mod[0, 4:5])


def spatial_backward(r, heads, clip, rows_at):
    width = r.tokens.shape[-1]
    rows = r.tokens.shape[1]
    scale_qk = HEAD_DIM**-0.5
    own_rows = pl.ds(rows_at, rows)
    mod = r.mod
    r.mods[2, pl.ds(clip, 1)] = column_sum(r.grad_a[clip] * r.branch_a[0].astype(F32))
    low_a = (mod[0, 2:3] * r.grad_a[clip]).astype(BF16)
    r.grad_branch[own_rows, :] = low_a
    grad_mixed = dot_nt(low_a, r.w_out_a[...]).astype(BF16)
    scaled, plain = side_masks(BF16, scale_qk), side_masks(BF16, 1.0)
    lane = lax.broadcasted_iota(jnp.int32, (1, LANES), 1)
    for first in range(0, heads // 2, GROUP):
        pairs = range(first, min(first + GROUP, heads // 2))
        scores, grads, softs, backs = [], [], [], []
        for pair in pairs:
            gm = grad_mixed[:, pair * LANES : (pair + 1) * LANES]
            scores.append(
                dot_nt(both_sides(columns(r.qkv_a, 1, pair), scaled), columns(r.qkv_a, 0, pair))
            )
            grads.append(dot_nt(both_sides(columns(r.qkv_a, 2, pair), plain), gm))
        for pair, score, grad in zip(pairs, scores, grads):
            low, back = [], []
            for side in range(2):
                mine = slice(side * rows, (side + 1) * rows)
                head = 2 * pair + side
                soft = jnp.exp(score[mine] - r.lse[0, head : head + 1])
                inner = jnp.sum(soft * grad[mine], axis=0, keepdims=True)
                back.append((soft * (grad[mine] - inner)).astype(BF16))
                low.append(soft.astype(BF16))
            softs.append(jnp.concatenate(low, axis=0))
            backs.append(jnp.concatenate(back, axis=0))
        for pair, soft, back in zip(pairs, softs, backs):
            gm = grad_mixed[:, pair * LANES : (pair + 1) * LANES]
            query, key = (columns(r.qkv_a, part, pair) for part in (0, 1))
            start = pair * LANES
            r.grad_qkv[own_rows, start : start + LANES] = dot_tn(
                back, both_sides(key, scaled)
            ).astype(BF16)
            for part, total, factor in ((1, dot(back, query), scale_qk), (2, dot(soft, gm), 1.0)):
                joined = jnp.where(lane < HEAD_DIM, total[:rows], total[rows:])
                start = part * width + pair * LANES
                r.grad_qkv[own_rows, start : start + LANES] = (joined * factor).astype(BF16)
    grad_hidden = dot_nt(r.grad_qkv[own_rows, :], r.w_qkv_a[...])
    normed_a, inv_a = norm(r.tokens[0].astype(F32))
    r.mods[0, pl.ds(clip, 1)] = column_sum(grad_hidden)
    r.mods[1, pl.ds(clip, 1)] = column_sum(grad_hidden * normed_a)
    r.grad_tokens[0] = r.grad_a[clip] + norm_back(
        grad_hidden, normed_a, inv_a, 1.0 + mod[0, 1:2]
    )


class Halving:
    def __init__(self, sums, landings, sends, recvs, bits):
        self.sums, self.landings, self.sends, self.recvs = sums, landings, sends, recvs
        self.bits = bits

    def share(self, stage, number, keep):
        me = lax.axis_index("clip")
        later = sorted(self.bits[stage + 1 :])
        spot = sum(((number >> i) & 1) << (bit - 1) for i, bit in enumerate(later))
        for bit in self.bits[: stage + 1]:
            mine = lax.rem(me // (1 << bit), 2)
            if bit == self.bits[stage] and not keep:
                mine = 1 - mine
            spot = spot + mine * (1 << (bit - 1))
        return spot

    def count(self, stage):
        return 1 << (len(self.bits) - 1 - stage)

    def copy(self, stage, number):
        at = sum(self.count(i) for i in range(stage)) + number
        return remote(
            self.sums.at[:, self.share(stage, number, False)],
            self.landings.at[:, at], self.sends.at[at], self.recvs.at[at],
            clip=partner("clip", self.bits[stage]),
        )

    def send(self, stage):
        for number in range(self.count(stage)):
            self.copy(stage, number).start()

    def fold(self, stage):
        for number in range(self.count(stage)):
            self.copy(stage, number).wait_recv()
            at = sum(self.count(i) for i in range(stage)) + number
            spot = self.share(stage, number, True)
            self.sums[:, spot] = (
                self.sums[:, spot].astype(F32) + self.landings[:, at].astype(F32)
            ).astype(BF16)

    def own(self):
        return self.sums[:, self.share(len(self.bits) - 1, 0, True)]

    def drain(self):
        for stage in range(len(self.bits)):
            for number in range(self.count(stage)):
                self.copy(stage, number).wait_send()


class Frames:
    def __init__(self, away, landing, sends, recvs):
        self.away, self.landing, self.sends, self.recvs = away, landing, sends, recvs

    def copy(self, distance):
        count = self.away.shape[0]
        frame = lax.rem(lax.axis_index("frame") + distance, count)
        return remote(
            self.away.at[frame], self.landing.at[distance - 1],
            self.sends.at[distance - 1], self.recvs.at[distance - 1], frame=frame,
        )

    def send(self, piece):
        count = self.away.shape[0]
        for frame in range(count):
            self.away[frame] = piece(frame)
        for distance in range(1, count):
            self.copy(distance).start()

    def finish(self):
        total = self.away[lax.axis_index("frame")].astype(F32)
        for distance in range(1, self.away.shape[0]):
            self.copy(distance).wait_recv()
            total = total + self.landing[distance - 1].astype(F32)
        return total

    def drain(self):
        for distance in range(1, self.away.shape[0]):
            self.copy(distance).wait_send()


def cut(array, number, count):
    cols = array.shape[1] // count
    return array[:, number * cols : (number + 1) * cols]


def thirds_in_rows(values):
    high = values.astype(BF16).astype(F32)
    mid = (values - high).astype(BF16).astype(F32)
    low = (values - high) - mid
    return jnp.concatenate((high, mid, low, jnp.zeros_like(low)), axis=0).astype(BF16)


def side_by_side(tiles):
    return jnp.concatenate([tiles[i] for i in range(tiles.shape[0])], axis=1)


def backward_kernel(heads, clips, n, n_frame, r):
    step = pl.program_id(0)
    rows, width = r.tokens.shape[1:]
    tiles = 4
    half = n // 2
    share = width // n
    first_t = clips
    first_s = clips + tiles
    first_w = 2 * clips + tiles
    last = first_w + tiles - 1
    sibling = partner("clip", 0)
    barrier = pltpu.get_barrier_semaphore()
    bits = list(range(1, n.bit_length() - 1))
    frame = lax.axis_index("frame")
    place = lax.axis_index("clip")

    feed_in = Halving(r.sum_in, r.land_in, r.in_send, r.in_recv, bits)
    feed_out = Halving(r.sum_out, r.land_out, r.out_send, r.out_recv, bits[::-1])

    def units_of(name):
        sums, land = getattr(r, "sum_" + name), getattr(r, "land_" + name)
        sends, recvs = getattr(r, name + "_send"), getattr(r, name + "_recv")
        return [
            Halving(
                sums.at[pl.ds(i, 1)], land.at[pl.ds(i, 1)], sends.at[i], recvs.at[i],
                bits[:: 1 - 2 * (i % 2)],
            )
            for i in range(tiles)
        ]

    temporal, spatial = units_of("t"), units_of("s")
    stages = len(bits)

    regions = {"t": r.w_qkv_a_vmem, "s": r.w_qkv_b_vmem}

    def tile_cols(tile):
        return pl.ds(pl.multiple_of(lax.rem(tile, 3) * width, width), width)

    def tile_copies(name, tile):
        sends, recvs = getattr(r, name + "_core_send"), getattr(r, name + "_core_recv")
        return [
            remote(
                regions[name].at[share_rows(number, False, share), tile_cols(tile)],
                getattr(r, "core_" + name).at[tile, number],
                sends.at[tile, number], recvs.at[tile, number], clip=sibling,
            )
            for number in range(half)
        ]

    def tile_sent(name, tile):
        for copy in tile_copies(name, tile):
            copy.wait_send()

    def fold_core(name, which):
        sums, core = getattr(r, "sum_" + name), getattr(r, "core_" + name)
        for tile in which:
            for copy in tile_copies(name, tile):
                copy.wait_recv()
            sums[tile] = (sums[tile].astype(F32) + core[tile].astype(F32)).astype(BF16)

    frames = {
        name: Frames(
            getattr(r, "away_" + name), getattr(r, "near_" + name),
            getattr(r, name + "_z_send"), getattr(r, name + "_z_recv"),
        )
        for name in ("in", "out", "t", "s", "mod")
    }

    spaces = (r.left, r.left_out, r.grad_branch)

    def mod_tile(part):
        return pltpu.make_async_copy(
            r.w_mod.at[:, pl.ds(part * width, width)],
            spaces[part % 3].at[pl.ds(0, width)], r.mod_sems.at[part],
        )

    def mod_sums():
        total = None
        for part in range(9):
            mod_tile(part).wait()
            term = dot_nt(thirds_in_rows(r.mods[part]), spaces[part % 3][:width])
            total = term if total is None else total + term
            if part + 3 < 9:
                mod_tile(part + 3).start()
        pad = r.mods.shape[1]
        total = total[:pad] + total[pad : 2 * pad] + total[2 * pad : 3 * pad]
        joined = side_by_side(r.mods)
        total = total * r.silu_grad[...]
        frames["mod"].send(
            lambda other: jnp.concatenate((total, cut(joined, other, n_frame)), axis=1)
        )

    def spread_mods(distance):
        return remote(
            r.mod_share, r.gathered.at[place], r.mod_send.at[distance - 1],
            r.mod_recv.at[distance - 1], clip=lax.rem(place + distance, n),
        )

    own_mods = pltpu.make_async_copy(r.mod_share, r.gathered.at[place], r.mod_sems.at[9])

    def to_frames(units, name):
        owned = [unit.own()[0] for unit in units]
        wide = jnp.concatenate(owned[:-1], axis=1)
        frames[name].send(
            lambda other: jnp.concatenate(
                (cut(wide, other, n_frame), cut(owned[-1], other, n_frame)), axis=1
            )
        )

    def from_frames(name, wide, narrow):
        total = frames[name].finish()
        wide[...] = total[:, : wide.shape[1]]
        narrow[...] = total[:, wide.shape[1] :]

    def two_high(array):
        rows = array.shape[0] // 2
        return jnp.concatenate((array[:rows], array[rows:]), axis=1)

    loads = [
        pltpu.make_async_copy(r.keep_in, r.sum_in, r.load_sems.at[0]),
        pltpu.make_async_copy(r.came_in, r.core_t, r.load_sems.at[1]),
        pltpu.make_async_copy(r.keep_out, r.sum_out, r.load_sems.at[2]),
        pltpu.make_async_copy(r.came_out, r.core_s, r.load_sems.at[3]),
    ]
    lefts_t = [
        pltpu.make_async_copy(r.hidden_b, r.left, r.load_sems.at[4]),
        pltpu.make_async_copy(r.mixed_b, r.left_out, r.load_sems.at[5]),
        pltpu.make_async_copy(r.grad_branch_b, r.grad_branch, r.load_sems.at[6]),
    ]
    lefts_s = [
        pltpu.make_async_copy(r.hidden_a, r.left, r.load_sems.at[7]),
        pltpu.make_async_copy(r.mixed_a, r.left_out, r.load_sems.at[8]),
    ]
    r.w_qkv_a = Late(r.w_qkv_a_hbm, r.w_qkv_a_vmem, r.load_sems.at[9], first_s)

    @pl.when(step == 0)
    def _():
        for distance in range(1, n):
            greet(barrier, clip=lax.rem(place + distance, n))
        for distance in range(1, n_frame):
            greet(barrier, frame=lax.rem(frame + distance, n_frame))
        for copy in loads + lefts_t:
            copy.start()
        r.mods[...] = jnp.zeros_like(r.mods)
        for clip in range(clips):
            for row, part in enumerate((6, 7, 8, 5)):
                r.mods[part, clip : clip + 1] = r.sums[clip, row : row + 1]

    @pl.when(step < clips)
    def _():
        temporal_backward(r, step, pl.multiple_of(step * rows, rows))

    @pl.when(step == 0)
    def _():
        for copy in loads:
            copy.wait()
        for tile in range(tiles):
            r.sum_in[tile] = (
                r.sum_in[tile].astype(F32) + r.core_t[tile].astype(F32)
            ).astype(BF16)
        per = r.sum_out.shape[1] // tiles
        for tile in range(tiles):
            which = slice(tile * per, (tile + 1) * per)
            came = r.core_s[tile].reshape(r.sum_out[0, which].shape)
            r.sum_out[0, which] = (
                r.sum_out[0, which].astype(F32) + came.astype(F32)
            ).astype(BF16)
        pl.semaphore_wait(barrier, n - 1 + n_frame - 1)
        pl.semaphore_signal(
            r.free, inc=1, device_id={"clip": sibling}, device_id_type=pl.DeviceIdType.MESH
        )
        feed_in.send(0)
        feed_out.send(0)

    def weight_tile(name, tile):
        region = regions[name]

        @pl.when(tile < tiles - 1)
        def _():
            cols = pl.ds(pl.multiple_of(tile * width, width), width)
            region[:, tile_cols(tile)] = dot_tn(r.left[...], r.grad_qkv[:, cols]).astype(BF16)

        @pl.when(tile == tiles - 1)
        def _():
            region[:, tile_cols(tile)] = dot_tn(r.left_out[...], r.grad_branch[...]).astype(BF16)

        for copy in tile_copies(name, tile):
            copy.start()
        for number in range(half):
            getattr(r, "sum_" + name)[tile, number] = region[
                share_rows(number, True, share), tile_cols(tile)
            ]

    @pl.when((step >= first_t) & (step < first_s))
    def _():
        tile = step - first_t

        @pl.when(tile == 0)
        def _():
            for copy in lefts_t:
                copy.wait()
            pl.semaphore_wait(r.free, 1)

        pl.when(tile == 3)(lambda: tile_sent("t", 0))
        weight_tile("t", tile)

        @pl.when(tile == tiles - 1)
        def _():
            for copy in lefts_s:
                copy.start()

    @pl.when((step >= first_s) & (step < first_w))
    def _():
        clip = step - first_s

        @pl.when(clip == 0)
        def _():
            for tile in range(1, tiles):
                tile_sent("t", tile)
            r.w_qkv_a.copy.start()

        spatial_backward(r, heads, clip, pl.multiple_of(clip * rows, rows))

    @pl.when(step == first_s - 1)
    def _():
        for unit in (feed_in, feed_out):
            unit.fold(0)
            if stages > 1:
                unit.send(1)

    @pl.when(step == first_s)
    def _():
        for tile, unit in enumerate(temporal):
            fold_core("t", (tile,))
            unit.send(0)

    @pl.when(step == first_s + 1)
    def _():
        for stage in range(1, stages):
            for unit in (feed_in, feed_out):
                unit.fold(stage)
                if stage + 1 < stages:
                    unit.send(stage + 1)
        owned_in, owned_out = side_by_side(feed_in.own()), feed_out.own()[0]
        frames["in"].send(lambda other: cut(owned_in, other, n_frame))
        frames["out"].send(lambda other: two_high(cut(owned_out, other, n_frame)))

    @pl.when(step == first_s + 2)
    def _():
        for unit in temporal:
            unit.fold(0)
            if stages > 1:
                unit.send(1)

    @pl.when(step == first_s + 3)
    def _():
        for stage in range(1, stages):
            for unit in temporal:
                unit.fold(stage)
                if stage + 1 < stages:
                    unit.send(stage + 1)
        to_frames(temporal, "t")

    @pl.when(step >= first_w)
    def _():
        tile = step - first_w

        @pl.when(tile == 0)
        def _():
            for copy in lefts_s:
                copy.wait()

        pl.when(tile == 3)(lambda: tile_sent("s", 0))
        weight_tile("s", tile)

    for tile in range(tiles - 1):

        @pl.when(step == first_w + 1 + tile)
        def _():
            fold_core("s", (tile,))
            spatial[tile].send(0)

    @pl.when(step == last)
    def _():
        fold_core("s", (tiles - 1,))
        spatial[tiles - 1].send(0)
        for part in range(3):
            mod_tile(part).start()
        mod_sums()
        for stage in range(stages):
            for unit in spatial:
                unit.fold(stage)
                if stage + 1 < stages:
                    unit.send(stage + 1)
        to_frames(spatial, "s")
        r.mod_share[...] = frames["mod"].finish()
        for distance in range(1, n):
            spread_mods(distance).start()
        own_mods.start()
        r.done_in[...] = frames["in"].finish()
        total = frames["out"].finish()
        high = total.shape[0]
        r.done_out[:high] = cut(total, 0, 2)
        r.done_out[high:] = cut(total, 1, 2)
        from_frames("t", r.done_tq, r.done_to)
        from_frames("s", r.done_sq, r.done_so)
        own_mods.wait()
        for distance in range(1, n):
            spread_mods(distance).wait()
        for unit in (feed_in, feed_out, *temporal, *spatial):
            unit.drain()
        for name in frames:
            frames[name].drain()
        for tile in range(1, tiles):
            tile_sent("s", tile)


def backward_call(fwd, tok, mod, spread, weights, modulate_w, silu_grad, n, n_frame):
    clips, rows, width = tok.shape
    ff = weights["mlp_in"].shape[1]
    heads = width // HEAD_DIM
    tokens_here = clips * rows
    tiles = 4
    half, share, tall = n // 2, width // n, ff // n
    first_s, first_w = clips + tiles, 2 * clips + tiles

    def struct(last, dtype=BF16):
        return jax.ShapeDtypeStruct((clips, rows, last), dtype)

    mod_spec = pl.BlockSpec(
        (1,) + mod.shape[1:],
        lambda s: (
            jnp.where(s < first_s, jnp.minimum(s, clips - 1), jnp.minimum(s - first_s, clips - 1)),
            0, 0,
        ),
    )
    anywhere = pl.BlockSpec(memory_space=pl.ANY)
    pad, mod_cols = silu_grad.shape[0], width + 9 * width // n_frame
    whole = pl.BlockSpec(fwd.sums.shape, lambda s: (0, 0, 0), pipeline_mode=pl.Buffered(1))
    whole_grad = pl.BlockSpec(silu_grad.shape, lambda s: (0, 0), pipeline_mode=pl.Buffered(1))
    ins = [
        ("mod", mod, mod_spec), ("sums", fwd.sums, whole), ("silu_grad", silu_grad, whole_grad),
        ("w_mod", modulate_w, anywhere),
    ]
    for name in ("q_prev", "q_own", "q_next", "sent_prev", "sent", "sent_next", "grad_q", "grad_b", "after_a"):
        array = getattr(fwd, name)
        ins.append((name, array, clip_spec(array, 0, clips, 1 if name in ("grad_q", "grad_b", "after_a") else 2)))
    for name, array in (
        ("tokens", tok), ("branch_a", fwd.branch_a), ("qkv_a", fwd.qkv_a), ("lse", fwd.lse)
    ):
        ins.append((name, array, clip_spec(array, first_s, clips, 1)))
    flat = (tokens_here, width)
    for name in ("hidden_b", "mixed_b", "grad_branch_b", "hidden_a", "mixed_a"):
        ins.append((name, getattr(fwd, name).reshape(flat), anywhere))
    core_shape = (tiles, half, share, width)
    ins += [
        ("keep_in", fwd.keep_in.reshape(core_shape), anywhere),
        ("came_in", fwd.came_in.reshape(core_shape), anywhere),
        ("keep_out", fwd.keep_out.reshape(1, half, tall, width), anywhere),
        ("came_out", fwd.came_out.reshape(core_shape), anywhere),
        ("w_qkv_a_hbm", weights["spatial_qkv"], anywhere),
    ]
    held = [
        ("spread", spread, 0), ("w_qkv_b", weights["temporal_qkv"], 0),
        ("w_out_a", weights["spatial_out"], first_s),
    ]
    grad_tokens = struct(width, F32)
    outs = [
        ("grad_tokens", grad_tokens, clip_spec(grad_tokens, first_s, clips, 1)),
        ("gathered", jax.ShapeDtypeStruct((n, pad, mod_cols), F32), None),
    ]
    dma = pltpu.SemaphoreType.DMA
    pieces = {
        "in": (share, ff // n_frame), "out": (tall, width // n_frame),
        "tq": (share, 3 * width // n_frame), "to": (share, width // n_frame),
        "sq": (share, 3 * width // n_frame), "so": (share, width // n_frame),
    }
    moved = half - 1
    scratch = [
        ("grad_a", pltpu.VMEM((clips, rows, width), F32)),
        ("grad_qkv", pltpu.VMEM((tokens_here, 3 * width), BF16)),
        ("grad_branch", pltpu.VMEM(flat, BF16)), ("left", pltpu.VMEM(flat, BF16)),
        ("left_out", pltpu.VMEM(flat, BF16)),
        ("w_qkv_a_vmem", pltpu.VMEM(weights["spatial_qkv"].shape, BF16)),
        ("sum_in", pltpu.VMEM(core_shape, BF16)), ("land_in", pltpu.VMEM((tiles, moved, share, width), BF16)),
        ("in_send", dma((moved,))), ("in_recv", dma((moved,))),
        ("sum_out", pltpu.VMEM((1, half, tall, width), BF16)),
        ("land_out", pltpu.VMEM((1, moved, tall, width), BF16)),
        ("out_send", dma((moved,))), ("out_recv", dma((moved,))),
        ("load_sems", dma((10,))), ("free", pltpu.SemaphoreType.REGULAR),
        ("mods", pltpu.VMEM((9, pad, width), F32)), ("mod_sems", dma((10,))),
        ("mod_share", pltpu.VMEM((pad, mod_cols), F32)),
        ("mod_send", dma((n - 1,))), ("mod_recv", dma((n - 1,))),
    ]
    for name in ("t", "s"):
        scratch += [
            ("sum_" + name, pltpu.VMEM(core_shape, BF16)), ("core_" + name, pltpu.VMEM(core_shape, BF16)),
            ("land_" + name, pltpu.VMEM((tiles, moved, share, width), BF16)),
            (name + "_send", dma((tiles, moved))), (name + "_recv", dma((tiles, moved))),
            (name + "_core_send", dma((tiles, half))), (name + "_core_recv", dma((tiles, half))),
        ]
    for name, dims in pieces.items():
        shape = jax.ShapeDtypeStruct(dims, F32)
        outs.append(("done_" + name, shape, pl.BlockSpec(shape.shape, lambda s: (0, 0))))
    packed = {
        "in": (share, ff // n_frame), "out": (tall // 2, 2 * width // n_frame),
        "t": (share, 4 * width // n_frame), "s": (share, 4 * width // n_frame),
        "mod": (pad, mod_cols),
    }
    for name, dims in packed.items():
        kind = F32 if name == "mod" else BF16
        scratch += [
            ("away_" + name, pltpu.VMEM((n_frame, *dims), kind)),
            ("near_" + name, pltpu.VMEM((n_frame - 1, *dims), kind)),
            (name + "_z_send", dma((n_frame - 1,))), (name + "_z_recv", dma((n_frame - 1,))),
        ]
    return run_kernel(
        functools.partial(backward_kernel, heads, clips, n, n_frame), first_w + tiles,
        ins, held, outs, scratch, 2 * tokens_here * width * width * 20, collective=2,
    )


def thirds(values):
    high = values.astype(BF16)
    rest = values - high.astype(F32)
    mid = rest.astype(BF16)
    low = (rest - mid.astype(F32)).astype(BF16)
    return jnp.concatenate((high, mid, low), axis=0)


def local(
    tokens, target, loss_weight, timesteps, offsets, cond_table, modulate_w,
    spatial_qkv, spatial_out, temporal_qkv, temporal_out, mlp_in, mlp_out,
):
    clips, frames, patches, width = tokens.shape
    steps = cond_table.shape[0]
    heads = width // HEAD_DIM
    n_clip = lax.axis_size("clip")
    n_frame = lax.axis_size("frame")
    clip_at = lax.axis_index("clip")
    frame_at = lax.axis_index("frame")
    flat = (clips, patches, width)
    tok = tokens.reshape(flat)
    tgt = target.reshape(flat)

    condition = jnp.take(cond_table, timesteps, axis=0, mode="clip")
    cond_low = jax.nn.silu(condition).astype(BF16)
    cond_here = lax.dynamic_slice_in_dim(condition, clip_at * clips, clips)
    _, silu_pull = jax.vjp(jax.nn.silu, cond_here)
    low_here = lax.dynamic_slice_in_dim(cond_low, clip_at * clips, clips)
    mod = jnp.dot(low_here, modulate_w, preferred_element_type=F32).reshape(clips, 9, width)

    half = width // 2
    positions = (offsets + frame_at).astype(F32)
    freqs = jnp.exp(jnp.arange(half, dtype=F32) * (-math.log(10000.0) / half))
    angles = positions[:, None] * freqs
    posenc = jnp.concatenate((jnp.sin(angles), jnp.cos(angles)), axis=-1)[:, None, :]

    head_of = np.arange(width) // HEAD_DIM
    lane_ids = np.arange(LANES)
    to_heads = jnp.asarray((head_of[:, None] == lane_ids[None, :]).astype(BF16))
    tall = np.arange(2 * LANES) - LANES
    spread = jnp.asarray((tall[:, None] == head_of[None, :]).astype(BF16))
    group, inside = np.divmod(np.arange(6 * LANES), LANES)
    slot_at = np.where(inside < heads, group * SLOT + inside, -1)
    pack = jnp.asarray((slot_at[:, None] == lane_ids[None, :]).astype(BF16))
    weights = {
        "spatial_qkv": spatial_qkv, "spatial_out": spatial_out, "temporal_qkv": temporal_qkv,
        "temporal_out": temporal_out, "mlp_in": mlp_in, "mlp_out": mlp_out,
    }
    fwd = forward_call(
        tok, tgt, mod, posenc, loss_weight, (to_heads, spread, pack), weights, n_clip
    )

    pad = -(-clips // 8) * 8
    silu_grad = jnp.pad(silu_pull(jnp.ones_like(cond_here))[0], ((0, pad - clips), (0, 0)))
    bwd = backward_call(fwd, tok, mod, spread, weights, modulate_w, silu_grad, n_clip, n_frame)
    gathered = bwd.gathered.reshape(n_clip * pad, -1)

    def padded_rows(values):
        split = values.reshape((n_clip, clips) + values.shape[1:])
        sides = ((0, 0), (0, pad - clips)) + ((0, 0),) * (values.ndim - 1)
        return jnp.pad(split, sides).reshape((n_clip * pad,) + values.shape[1:])

    onehot = timesteps[:, None] == jnp.arange(steps, dtype=jnp.int32)[None, :]
    onehot = padded_rows(onehot.astype(BF16))
    grad_table = dot_tn(jnp.concatenate((onehot,) * 3, axis=0), thirds(gathered[:, :width]))
    mod_rows = width // n_clip
    low_rows = lax.dynamic_slice_in_dim(cond_low, clip_at * mod_rows, mod_rows, axis=1)
    low_rows = padded_rows(low_rows)
    grad_modulate = dot_tn(jnp.concatenate((low_rows,) * 3, axis=0), thirds(gathered[:, width:]))
    return (
        fwd.output.reshape(tokens.shape),
        bwd.grad_tokens.reshape(tokens.shape),
        grad_table,
        grad_modulate,
        bwd.done_sq,
        bwd.done_so,
        bwd.done_tq,
        bwd.done_to,
        bwd.done_in,
        bwd.done_out,
    )


def solution(mesh):
    placed = (
        P("clip", "frame", None, None), P("clip", "frame", None, None), P("clip"), P(), P("clip"),
    ) + (P(),) * 8
    return jax.shard_map(
        local,
        mesh=mesh,
        in_specs=placed,
        out_specs=(
            P("clip", "frame", None, None), P("clip", "frame", None, None), P(),
        ) + (P("clip", "frame"),) * 7,
        check_vma=False,
    )
```

```python
import functools
import math

import jax
import jax.numpy as jnp
import numpy as np
from jax import lax
from jax.experimental import pallas as pl
from jax.experimental.pallas import tpu as pltpu
from jax.sharding import PartitionSpec as P

HEAD_DIM = 64
NORM_EPSILON = 1e-06
F32 = jnp.float32
BF16 = jnp.bfloat16
LANES = 128
SLOT = 16
NO_KEY = -1e30
VMEM_LIMIT = 60 * 2**20
GROUP = 2
GELU_A = math.sqrt(2.0 / math.pi)
GELU_B = 0.044715


def dot(left, right):
    return lax.dot_general(left, right, (((1,), (0,)), ((), ())), preferred_element_type=F32)


def dot_nt(left, right):
    return lax.dot_general(left, right, (((1,), (1,)), ((), ())), preferred_element_type=F32)


def dot_tn(left, right):
    return lax.dot_general(left, right, (((0,), (0,)), ((), ())), preferred_element_type=F32)


def norm(values):
    centred = values - jnp.mean(values, axis=-1, keepdims=True)
    inv_std = lax.rsqrt(jnp.mean(centred * centred, axis=-1, keepdims=True) + NORM_EPSILON)
    return centred * inv_std, inv_std


def norm_back(grad_hidden, normed, inv_std, scale_plus):
    grad_normed = grad_hidden * scale_plus
    mean_grad = jnp.mean(grad_normed, axis=-1, keepdims=True)
    mean_cross = jnp.mean(grad_normed * normed, axis=-1, keepdims=True)
    return inv_std * (grad_normed - mean_grad - normed * mean_cross)


def column_sum(values):
    return jnp.sum(values, axis=0, keepdims=True)


def side_masks(dtype, value):
    lane = lax.broadcasted_iota(jnp.int32, (1, LANES), 1)
    return [jnp.where((lane < HEAD_DIM) == (side == 0), value, 0.0).astype(dtype) for side in (0, 1)]


class Refs:
    def __init__(self, names, refs):
        self.__dict__.update(zip(names, refs, strict=True))


class Late:
    def __init__(self, source, ref, sem, step):
        self.ref = ref
        self.copy = pltpu.make_async_copy(source, ref, sem)
        self.step = step
        self.waited = False

    def __getitem__(self, index):
        if not self.waited:
            pl.when(pl.program_id(0) == self.step)(self.copy.wait)
            self.waited = True
        return self.ref[index]


def partner(axis, bit):
    me = lax.axis_index(axis)
    return me + (1 << bit) - (2 << bit) * lax.rem(me // (1 << bit), 2)


def remote(source, target, send_sem, recv_sem, **where):
    return pltpu.make_async_remote_copy(
        src_ref=source, dst_ref=target, send_sem=send_sem, recv_sem=recv_sem,
        device_id=where, device_id_type=pl.DeviceIdType.MESH,
    )


def greet(barrier, **where):
    pl.semaphore_signal(barrier, inc=1, device_id=where, device_id_type=pl.DeviceIdType.MESH)


def run_kernel(body, steps, ins, weights, outs, scratch, flops, collective=None):
    anywhere = pl.BlockSpec(memory_space=pl.ANY)
    names = [name for name, *_ in ins] + [name + "_hbm" for name, *_ in weights]
    names += [name for name, *_ in outs]
    names += [name + "_vmem" for name, *_ in weights] + ["weight_sems"]
    names += [name for name, _ in scratch]

    def kernel(*refs):
        r = Refs(names, refs)
        lates = []
        for number, (name, _, step) in enumerate(weights):
            late = Late(
                getattr(r, name + "_hbm"), getattr(r, name + "_vmem"), r.weight_sems.at[number], step
            )
            lates.append(late)
            setattr(r, name, late)

        @pl.when(pl.program_id(0) == 0)
        def _():
            for late in lates:
                if late.step == 0:
                    late.copy.start()

        body(r)

        @pl.when(pl.program_id(0) == 0)
        def _():
            for late in lates:
                if late.step > 0:
                    late.copy.start()

    arrays = [array for _, array, _ in ins] + [array for _, array, _ in weights]
    shapes = [shape for _, shape, _ in outs]
    touched = sum(math.prod(a.shape) * a.dtype.itemsize for a in arrays + shapes)
    params = {} if collective is None else {"collective_id": collective, "has_side_effects": True}
    done = pl.pallas_call(
        kernel,
        grid=(steps,),
        in_specs=[spec for *_, spec in ins] + [anywhere] * len(weights),
        out_specs=[spec or anywhere for *_, spec in outs],
        out_shape=shapes,
        scratch_shapes=[pltpu.VMEM(a.shape, a.dtype) for _, a, _ in weights]
        + [pltpu.SemaphoreType.DMA((max(len(weights), 1),))]
        + [shape for _, shape in scratch],
        compiler_params=pltpu.CompilerParams(vmem_limit_bytes=VMEM_LIMIT, **params),
        cost_estimate=pl.CostEstimate(flops=flops, bytes_accessed=touched, transcendentals=0),
    )(*arrays)
    return Refs([name for name, *_ in outs], done)


def clip_spec(array, first, clips, depth=None):
    rest = array.shape[1:]
    mode = {} if depth is None else {"pipeline_mode": pl.Buffered(depth)}
    return pl.BlockSpec(
        (1,) + rest, lambda s: (jnp.clip(s - first, 0, clips - 1),) + (0,) * len(rest), **mode
    )


def spatial_forward(r, heads, clip):
    width = r.tokens.shape[-1]
    rows = r.tokens.shape[1]
    mod = r.mod
    inputs = r.tokens[0].astype(F32)
    normed, _ = norm(inputs)
    hidden = (normed * (1.0 + mod[0, 1:2]) + mod[0, 0:1]).astype(BF16)
    r.hidden_a[0] = hidden
    for part in range(3):
        cols = slice(part * width, (part + 1) * width)
        r.qkv_a[0, :, cols] = dot(hidden, r.w_qkv_a[:, cols]).astype(BF16)
    scaled, plain = side_masks(BF16, HEAD_DIM**-0.5), side_masks(BF16, 1.0)
    for first in range(0, heads // 2, 3):
        pairs = range(first, min(first + 3, heads // 2))
        scores, softs = [], []
        for pair in pairs:
            query, key = (columns(r.qkv_a, part, pair) for part in (0, 1))
            scores.append(dot_nt(both_sides(key, scaled), query))
        for pair, score in zip(pairs, scores):
            halves = []
            for side in range(2):
                mine = score[side * rows : (side + 1) * rows]
                top = jnp.max(mine, axis=0, keepdims=True)
                grown = jnp.exp(mine - top)
                total = jnp.sum(grown, axis=0, keepdims=True)
                halves.append((grown * (1.0 / total)).astype(BF16))
                head = 2 * pair + side
                r.lse[0, head : head + 1] = top + jnp.log(total)
            softs.append(jnp.concatenate(halves, axis=0))
        for pair, soft in zip(pairs, softs):
            value = columns(r.qkv_a, 2, pair)
            r.mixed_a[0, :, pair * LANES : (pair + 1) * LANES] = dot_tn(
                soft, both_sides(value, plain)
            ).astype(BF16)
    branch_a = dot(r.mixed_a[0], r.w_out_a[...])
    r.branch_a[0] = branch_a.astype(BF16)
    after_a = inputs + mod[0, 2:3] * branch_a
    r.after_held[clip] = after_a
    normed_b, _ = norm(after_a)
    r.hidden_held[clip] = (
        normed_b * (1.0 + mod[0, 4:5]) + (mod[0, 3:4] + r.posenc[0])
    ).astype(BF16)


def both_sides(array, masks):
    return jnp.concatenate((array * masks[0], array * masks[1]), axis=0)


def columns(ref, part, pair):
    start = part * (ref.shape[-1] // 3) + pair * LANES
    return ref[0, :, start : start + LANES]


def by_head(left, right, to_heads):
    return dot(left * right, to_heads)


def middle(r, clip, rows_at):
    width = r.target.shape[-1]
    rows = r.target.shape[1]
    ff = r.act.shape[-1]
    scale_qk = HEAD_DIM**-0.5
    mod = r.mod
    own_rows = pl.ds(rows_at, rows)
    store = r.w_qkv_a_vmem

    def kept(number, part):
        return store[number * rows : (number + 1) * rows, part * width : (part + 1) * width]

    three = jnp.concatenate((r.hidden_prev[clip], r.hidden_held[clip], r.hidden_next[clip]), axis=0)
    for part in range(3):
        cols = slice(part * width, (part + 1) * width)
        value = dot(three, r.w_qkv_b[:, cols]).astype(BF16)
        store[:, cols] = value
        if part == 0:
            for number, out in enumerate((r.q_prev, r.q_own, r.q_next)):
                out[0] = value[number * rows : (number + 1) * rows]
    frame = lax.axis_index("frame")
    absent = (frame == 0, None, frame == lax.axis_size("frame") - 1)
    scores = []
    for number in range(3):
        raw = by_head(kept(1, 0), kept(number, 1), r.to_heads[...]) * scale_qk
        if absent[number] is not None:
            raw = raw + jnp.where(absent[number], NO_KEY, 0.0)
        scores.append(raw)
    top = jnp.maximum(jnp.maximum(scores[0], scores[1]), scores[2])
    grown = [jnp.exp(entry - top) for entry in scores]
    inverse = 1.0 / (grown[0] + grown[1] + grown[2])
    soft = [entry * inverse for entry in grown]
    soft_low = [entry.astype(BF16) for entry in soft]
    to_width = r.spread[LANES : 2 * LANES]
    total = None
    for number in range(3):
        term = dot(soft_low[number], to_width) * kept(number, 2).astype(F32)
        total = term if total is None else total + term
    mixed = total.astype(BF16)
    r.mixed_b[0] = mixed
    branch_b = dot(mixed, r.w_out_b[...])
    r.grad_b[0] = branch_b
    after_b = r.after_held[clip] + mod[0, 5:6] * branch_b
    normed_c, inv_c = norm(after_b)
    hidden = (normed_c * (1.0 + mod[0, 7:8]) + mod[0, 6:7]).astype(BF16)
    r.hidden_c[own_rows, :] = hidden
    parts = ff // width
    ahead = dot(hidden, r.w_in[:, :width])
    for part in range(parts):
        cols = slice(part * width, (part + 1) * width)
        upward = ahead
        if part + 1 < parts:
            ahead = dot(hidden, r.w_in[:, (part + 1) * width : (part + 2) * width])
        squared = upward * upward
        bent = jnp.tanh(upward * (GELU_A + (GELU_A * GELU_B) * squared))
        share = 0.5 + 0.5 * bent
        r.act[own_rows, cols] = (upward * share).astype(BF16)
        steep = (1.0 - bent * bent) * (0.5 * GELU_A + (1.5 * GELU_A * GELU_B) * squared)
        r.grad_up[own_rows, cols] = (share + upward * steep).astype(BF16)
    branch_c = dot(r.act[own_rows, :], r.w_mlp[...])
    result = after_b + mod[0, 8:9] * branch_c
    r.output[0] = result.astype(BF16)
    grad_result = r.weight[clip] * (result - r.target[0].astype(F32))
    r.sums[0, 2:3] = column_sum(grad_result * branch_c)
    low_c = (mod[0, 8:9] * grad_result).astype(BF16)
    r.grad_branch_c[own_rows, :] = low_c
    ahead = dot_nt(low_c, r.w_mlp[:width, :])
    for part in range(parts):
        cols = slice(part * width, (part + 1) * width)
        grad_act = ahead
        if part + 1 < parts:
            ahead = dot_nt(low_c, r.w_mlp[(part + 1) * width : (part + 2) * width, :])
        r.grad_up[own_rows, cols] = (grad_act * r.grad_up[own_rows, cols].astype(F32)).astype(BF16)
    grad_hidden = dot_nt(r.grad_up[own_rows, :], r.w_in[...])
    r.sums[0, 0:1] = column_sum(grad_hidden)
    r.sums[0, 1:2] = column_sum(grad_hidden * normed_c)
    grad_after = grad_result + norm_back(grad_hidden, normed_c, inv_c, 1.0 + mod[0, 7:8])
    r.sums[0, 3:4] = column_sum(grad_after * r.grad_b[0])
    r.grad_b[0] = grad_after
    low_b = (mod[0, 5:6] * grad_after).astype(BF16)
    r.grad_branch_b[0] = low_b
    grad_mixed = dot_nt(low_b, r.w_out_b[...]).astype(BF16)
    grad_soft = [by_head(grad_mixed, kept(number, 2), r.to_heads[...]) for number in range(3)]
    inner = soft[0] * grad_soft[0] + soft[1] * grad_soft[1] + soft[2] * grad_soft[2]
    grad_scores = [(soft[number] * (grad_soft[number] - inner)).astype(BF16) for number in range(3)]
    total = None
    for number in range(3):
        term = dot(grad_scores[number], to_width) * kept(number, 1).astype(F32)
        total = term if total is None else total + term
    r.grad_q[0] = (total * scale_qk).astype(BF16)
    r.sent_held[clip, :, :width] = grad_mixed
    r.sent_held[clip, :, width:] = dot(
        jnp.concatenate(soft_low + grad_scores, axis=1), r.pack[...]
    ).astype(BF16)


def share_rows(number, keep, share):
    core = lax.rem(lax.axis_index("clip"), 2)
    spot = 2 * number + (core if keep else 1 - core)
    return pl.ds(pl.multiple_of(spot * share, share), share)


def forward_kernel(heads, clips, n, r):
    step = pl.program_id(0)
    rows, width = r.tokens.shape[1:]
    ff = r.act.shape[-1]
    in_steps = ff // width
    out_steps = n // 2
    share = ff // n
    last = 2 * clips + in_steps + out_steps - 1
    frame = lax.axis_index("frame")
    has_prev = frame > 0
    has_next = frame < lax.axis_size("frame") - 1
    no_prev = jnp.logical_not(has_prev)
    no_next = jnp.logical_not(has_next)
    core = lax.rem(lax.axis_index("clip"), 2)
    sibling = partner("clip", 0)
    barrier = pltpu.get_barrier_semaphore()

    def halo(way, clip):
        return remote(
            r.hidden_held.at[clip], (r.hidden_prev, r.hidden_next)[way].at[clip],
            r.halo_send.at[way, clip], r.halo_recv.at[way, clip],
            frame=frame + 1 if way == 0 else frame - 1,
        )

    def packet(way, clip):
        return remote(
            r.sent_held.at[clip], (r.sent_prev, r.sent_next)[way].at[clip],
            r.sent_send.at[way, clip], r.sent_recv.at[way, clip],
            frame=frame + 1 if way == 0 else frame - 1,
        )

    low_share = width // n

    def in_tile(tile):
        return [
            remote(
                r.stage.at[lax.rem(tile, 2), share_rows(number, False, low_share)],
                r.came_in.at[tile, number],
                r.in_send.at[tile, number], r.in_recv.at[tile, number], clip=sibling,
            )
            for number in range(n // 2)
        ]

    def in_kept(tile):
        return [
            pltpu.make_async_copy(
                r.stage.at[lax.rem(tile, 2), share_rows(number, True, low_share)],
                r.keep_in.at[tile, number], r.in_keep.at[tile, number],
            )
            for number in range(n // 2)
        ]

    def in_sent(tile):
        for copy in in_tile(tile):
            copy.wait_send()
        for copy in in_kept(tile):
            copy.wait()

    def out_part(tile, which):
        return r.stage.at[
            lax.rem(tile + in_steps, 2), pl.ds(pl.multiple_of(which * share, share), share)
        ]

    def out_tile(tile):
        return remote(
            out_part(tile, 1 - core), r.came_out.at[tile],
            r.out_send.at[tile], r.out_recv.at[tile], clip=sibling,
        )

    def out_kept(tile):
        return pltpu.make_async_copy(
            out_part(tile, core), r.keep_out.at[tile], r.out_keep.at[tile]
        )

    def save(clip):
        return [
            pltpu.make_async_copy(r.after_held.at[clip], r.after_a.at[clip], r.save_sems.at[0, clip]),
            pltpu.make_async_copy(
                r.hidden_held.at[clip], r.hidden_b.at[clip], r.save_sems.at[1, clip]
            ),
        ]

    def save_sent(clip):
        return pltpu.make_async_copy(r.sent_held.at[clip], r.sent.at[clip], r.save_sems.at[2, clip])

    def fill(way, clip):
        zeros = (r.hidden_prev, r.hidden_next)[way].at[clip]
        target = (r.sent_prev, r.sent_next)[way].at[clip]
        return [
            pltpu.make_async_copy(zeros, target.at[:, pl.ds(0, width)], r.save_sems.at[3, clip]),
            pltpu.make_async_copy(
                zeros.at[:, pl.ds(0, LANES)], target.at[:, pl.ds(width, LANES)],
                r.save_sems.at[4, clip],
            ),
        ]

    @pl.when(step == 0)
    def _():
        greet(barrier, clip=sibling)
        pl.when(has_prev)(lambda: greet(barrier, frame=frame - 1))
        pl.when(has_next)(lambda: greet(barrier, frame=frame + 1))

        @pl.when(no_prev)
        def _():
            r.hidden_prev[...] = jnp.zeros_like(r.hidden_prev)
            for clip in range(clips):
                for copy in fill(0, clip):
                    copy.start()

        @pl.when(no_next)
        def _():
            r.hidden_next[...] = jnp.zeros_like(r.hidden_next)
            for clip in range(clips):
                for copy in fill(1, clip):
                    copy.start()

    @pl.when(step < clips)
    def _():
        spatial_forward(r, heads, step)

        @pl.when(step == 0)
        def _():
            pl.semaphore_wait(
                barrier, 1 + jnp.where(has_prev, 1, 0) + jnp.where(has_next, 1, 0)
            )

        pl.when(has_next)(lambda: halo(0, step).start())
        pl.when(has_prev)(lambda: halo(1, step).start())
        for copy in save(step):
            copy.start()

    @pl.when((step >= clips) & (step < 2 * clips))
    def _():
        clip = step - clips
        pl.when(has_prev)(lambda: halo(0, clip).wait_recv())
        pl.when(has_next)(lambda: halo(1, clip).wait_recv())
        middle(r, clip, pl.multiple_of(clip * rows, rows))
        pl.when(has_next)(lambda: packet(0, clip).start())
        pl.when(has_prev)(lambda: packet(1, clip).start())
        save_sent(clip).start()

    @pl.when((step >= 2 * clips) & (step < 2 * clips + in_steps))
    def _():
        tile = step - 2 * clips

        pl.when(tile >= 2)(lambda: in_sent(tile - 2))
        cols = pl.ds(pl.multiple_of(tile * width, width), width)
        r.stage[lax.rem(tile, 2), :width] = dot_tn(r.hidden_c[...], r.grad_up[:, cols]).astype(BF16)
        for copy in in_tile(tile) + in_kept(tile):
            copy.start()

    @pl.when(step >= 2 * clips + in_steps)
    def _():
        tile = step - 2 * clips - in_steps

        pl.when(tile < 2)(lambda: in_sent(in_steps + tile - 2))

        @pl.when(tile >= 2)
        def _():
            out_tile(tile - 2).wait_send()
            out_kept(tile - 2).wait()

        cols = pl.ds(pl.multiple_of(tile * 2 * share, 2 * share), 2 * share)
        r.stage[lax.rem(tile + in_steps, 2), : 2 * share] = dot_tn(
            r.act[:, cols], r.grad_branch_c[...]
        ).astype(BF16)
        out_tile(tile).start()
        out_kept(tile).start()

    @pl.when(step == last)
    def _():
        for clip in range(clips):
            for copy in save(clip):
                copy.wait()
            save_sent(clip).wait()

            @pl.when(has_next)
            def _():
                halo(0, clip).wait_send()
                packet(0, clip).wait_send()
                packet(1, clip).wait_recv()

            @pl.when(has_prev)
            def _():
                halo(1, clip).wait_send()
                packet(1, clip).wait_send()
                packet(0, clip).wait_recv()

            for way, absent in ((0, no_prev), (1, no_next)):

                @pl.when(absent)
                def _():
                    for copy in fill(way, clip):
                        copy.wait()

        for tile in range(in_steps):
            for copy in in_tile(tile):
                copy.wait_recv()
        for tile in range(out_steps):
            out_tile(tile).wait_recv()
        for tile in range(out_steps - 2, out_steps):
            out_tile(tile).wait_send()
            out_kept(tile).wait()


def forward_call(tok, target, mod, posenc, weight, tables, weights, n):
    clips, rows, width = tok.shape
    ff = weights["mlp_in"].shape[1]
    heads = width // HEAD_DIM
    tokens_here = clips * rows
    in_steps, out_steps, share = ff // width, n // 2, ff // n
    to_heads, spread, pack = tables

    def struct(last, dtype=BF16):
        return jax.ShapeDtypeStruct((clips, rows, last), dtype)

    def early(array):
        return clip_spec(array, 0, clips)

    def late(array):
        return clip_spec(array, clips, clips)

    mod_spec = pl.BlockSpec(
        (1,) + mod.shape[1:],
        lambda s: (jnp.where(s < clips, s, jnp.minimum(s - clips, clips - 1)), 0, 0),
    )
    ins = [
        ("tokens", tok, early(tok)), ("posenc", posenc, early(posenc)), ("mod", mod, mod_spec),
        ("target", target, clip_spec(target, clips, clips, 1)), ("weight", weight, pl.BlockSpec(memory_space=pltpu.SMEM)),
    ]
    held = [
        ("w_qkv_a", weights["spatial_qkv"], 0), ("w_out_a", weights["spatial_out"], 0),
        ("w_qkv_b", weights["temporal_qkv"], clips), ("to_heads", to_heads, clips),
        ("spread", spread, clips), ("w_out_b", weights["temporal_out"], clips),
        ("w_in", weights["mlp_in"], clips), ("w_mlp", weights["mlp_out"], clips), ("pack", pack, clips),
    ]
    outs = []
    for name, shape in (
        ("hidden_a", struct(width)), ("qkv_a", struct(3 * width)), ("mixed_a", struct(width)),
        ("branch_a", struct(width)),
        ("lse", jax.ShapeDtypeStruct((clips, -(-heads // 8) * 8, rows), F32)),
    ):
        outs.append((name, shape, clip_spec(shape, 0, clips, 1)))
    for name, shape in (
        ("output", struct(width)), ("grad_b", struct(width, F32)), ("mixed_b", struct(width)),
        ("grad_branch_b", struct(width)), ("q_own", struct(width)), ("q_prev", struct(width)),
        ("q_next", struct(width)), ("grad_q", struct(width)),
        ("sums", jax.ShapeDtypeStruct((clips, 8, width), F32)),
    ):
        outs.append((name, shape, clip_spec(shape, clips, clips, 1)))
    outs += [
        ("after_a", struct(width, F32), None), ("hidden_b", struct(width), None),
        ("sent", struct(width + LANES), None), ("sent_prev", struct(width + LANES), None),
        ("sent_next", struct(width + LANES), None),
    ]
    tile_in = jax.ShapeDtypeStruct((in_steps, n // 2, width // n, width), BF16)
    tile_out = jax.ShapeDtypeStruct((out_steps, share, width), BF16)
    outs += [
        ("keep_in", tile_in, None), ("came_in", tile_in, None), ("keep_out", tile_out, None),
        ("came_out", tile_out, None),
    ]
    dma = pltpu.SemaphoreType.DMA
    scratch = [
        ("after_held", pltpu.VMEM((clips, rows, width), F32)),
        ("hidden_held", pltpu.VMEM((clips, rows, width), BF16)),
        ("hidden_prev", pltpu.VMEM((clips, rows, width), BF16)),
        ("hidden_next", pltpu.VMEM((clips, rows, width), BF16)),
        ("sent_held", pltpu.VMEM((clips, rows, width + LANES), BF16)),
        ("act", pltpu.VMEM((tokens_here, ff), BF16)),
        ("grad_up", pltpu.VMEM((tokens_here, ff), BF16)),
        ("hidden_c", pltpu.VMEM((tokens_here, width), BF16)),
        ("grad_branch_c", pltpu.VMEM((tokens_here, width), BF16)),
        ("stage", pltpu.VMEM((2, max(width, 2 * share), width), BF16)),
        ("halo_send", dma((2, clips))), ("halo_recv", dma((2, clips))),
        ("sent_send", dma((2, clips))), ("sent_recv", dma((2, clips))),
        ("in_send", dma((in_steps, n // 2))), ("in_recv", dma((in_steps, n // 2))),
        ("in_keep", dma((in_steps, n // 2))), ("out_send", dma((out_steps,))),
        ("out_recv", dma((out_steps,))), ("out_keep", dma((out_steps,))),
        ("save_sems", dma((5, clips))),
    ]
    return run_kernel(
        functools.partial(forward_kernel, heads, clips, n), 2 * clips + in_steps + out_steps,
        ins, held, outs, scratch, 2 * tokens_here * width * width * 46, collective=1,
    )


def temporal_backward(r, clip, rows_at):
    width = r.tokens.shape[-1]
    rows = r.tokens.shape[1]
    scale_qk = HEAD_DIM**-0.5
    own_rows = pl.ds(rows_at, rows)
    grad_key = None
    grad_value = None
    for number, (source, query) in enumerate(
        ((r.sent_prev, r.q_prev), (r.sent, r.q_own), (r.sent_next, r.q_next))
    ):
        other = 2 - number
        table = source[0, :, width:]
        low = LANES - SLOT * other
        soft = dot(table, r.spread[low : low + LANES])
        low = LANES - SLOT * (3 + other)
        score = dot(table, r.spread[low : low + LANES])
        key_term = score * query[0].astype(F32)
        value_term = soft * source[0, :, :width].astype(F32)
        grad_key = key_term if grad_key is None else grad_key + key_term
        grad_value = value_term if grad_value is None else grad_value + value_term
    r.grad_qkv[own_rows, :width] = r.grad_q[0]
    r.grad_qkv[own_rows, width : 2 * width] = (grad_key * scale_qk).astype(BF16)
    r.grad_qkv[own_rows, 2 * width :] = grad_value.astype(BF16)
    grad_hidden = dot_nt(r.grad_qkv[own_rows, :], r.w_qkv_b[...])
    normed_b, inv_b = norm(r.after_a[0])
    r.mods[3, pl.ds(clip, 1)] = column_sum(grad_hidden)
    r.mods[4, pl.ds(clip, 1)] = column_sum(grad_hidden * normed_b)
    r.grad_a[clip] = r.grad_b[0] + norm_back(grad_hidden, normed_b, inv_b, 1.0 + r.mod[0, 4:5])


def spatial_backward(r, heads, clip, rows_at):
    width = r.tokens.shape[-1]
    rows = r.tokens.shape[1]
    scale_qk = HEAD_DIM**-0.5
    own_rows = pl.ds(rows_at, rows)
    mod = r.mod
    r.mods[2, pl.ds(clip, 1)] = column_sum(r.grad_a[clip] * r.branch_a[0].astype(F32))
    low_a = (mod[0, 2:3] * r.grad_a[clip]).astype(BF16)
    r.grad_branch[own_rows, :] = low_a
    grad_mixed = dot_nt(low_a, r.w_out_a[...]).astype(BF16)
    scaled, plain = side_masks(BF16, scale_qk), side_masks(BF16, 1.0)
    lane = lax.broadcasted_iota(jnp.int32, (1, LANES), 1)
    for first in range(0, heads // 2, GROUP):
        pairs = range(first, min(first + GROUP, heads // 2))
        scores, grads, softs, backs = [], [], [], []
        for pair in pairs:
            gm = grad_mixed[:, pair * LANES : (pair + 1) * LANES]
            scores.append(
                dot_nt(both_sides(columns(r.qkv_a, 1, pair), scaled), columns(r.qkv_a, 0, pair))
            )
            grads.append(dot_nt(both_sides(columns(r.qkv_a, 2, pair), plain), gm))
        for pair, score, grad in zip(pairs, scores, grads):
            low, back = [], []
            for side in range(2):
                mine = slice(side * rows, (side + 1) * rows)
                head = 2 * pair + side
                soft = jnp.exp(score[mine] - r.lse[0, head : head + 1])
                inner = jnp.sum(soft * grad[mine], axis=0, keepdims=True)
                back.append((soft * (grad[mine] - inner)).astype(BF16))
                low.append(soft.astype(BF16))
            softs.append(jnp.concatenate(low, axis=0))
            backs.append(jnp.concatenate(back, axis=0))
        for pair, soft, back in zip(pairs, softs, backs):
            gm = grad_mixed[:, pair * LANES : (pair + 1) * LANES]
            query, key = (columns(r.qkv_a, part, pair) for part in (0, 1))
            start = pair * LANES
            r.grad_qkv[own_rows, start : start + LANES] = dot_tn(
                back, both_sides(key, scaled)
            ).astype(BF16)
            for part, total, factor in ((1, dot(back, query), scale_qk), (2, dot(soft, gm), 1.0)):
                joined = jnp.where(lane < HEAD_DIM, total[:rows], total[rows:])
                start = part * width + pair * LANES
                r.grad_qkv[own_rows, start : start + LANES] = (joined * factor).astype(BF16)
    grad_hidden = dot_nt(r.grad_qkv[own_rows, :], r.w_qkv_a[...])
    normed_a, inv_a = norm(r.tokens[0].astype(F32))
    r.mods[0, pl.ds(clip, 1)] = column_sum(grad_hidden)
    r.mods[1, pl.ds(clip, 1)] = column_sum(grad_hidden * normed_a)
    r.grad_tokens[0] = r.grad_a[clip] + norm_back(
        grad_hidden, normed_a, inv_a, 1.0 + mod[0, 1:2]
    )


class Halving:
    def __init__(self, sums, landings, sends, recvs, bits):
        self.sums, self.landings, self.sends, self.recvs = sums, landings, sends, recvs
        self.bits = bits

    def share(self, stage, number, keep):
        me = lax.axis_index("clip")
        later = sorted(self.bits[stage + 1 :])
        spot = sum(((number >> i) & 1) << (bit - 1) for i, bit in enumerate(later))
        for bit in self.bits[: stage + 1]:
            mine = lax.rem(me // (1 << bit), 2)
            if bit == self.bits[stage] and not keep:
                mine = 1 - mine
            spot = spot + mine * (1 << (bit - 1))
        return spot

    def count(self, stage):
        return 1 << (len(self.bits) - 1 - stage)

    def copy(self, stage, number):
        at = sum(self.count(i) for i in range(stage)) + number
        return remote(
            self.sums.at[:, self.share(stage, number, False)],
            self.landings.at[:, at], self.sends.at[at], self.recvs.at[at],
            clip=partner("clip", self.bits[stage]),
        )

    def send(self, stage):
        for number in range(self.count(stage)):
            self.copy(stage, number).start()

    def fold(self, stage):
        for number in range(self.count(stage)):
            self.copy(stage, number).wait_recv()
            at = sum(self.count(i) for i in range(stage)) + number
            spot = self.share(stage, number, True)
            self.sums[:, spot] = (
                self.sums[:, spot].astype(F32) + self.landings[:, at].astype(F32)
            ).astype(BF16)

    def own(self):
        return self.sums[:, self.share(len(self.bits) - 1, 0, True)]

    def drain(self):
        for stage in range(len(self.bits)):
            for number in range(self.count(stage)):
                self.copy(stage, number).wait_send()


class Frames:
    def __init__(self, away, landing, sends, recvs):
        self.away, self.landing, self.sends, self.recvs = away, landing, sends, recvs

    def copy(self, distance):
        count = self.away.shape[0]
        frame = lax.rem(lax.axis_index("frame") + distance, count)
        return remote(
            self.away.at[frame], self.landing.at[distance - 1],
            self.sends.at[distance - 1], self.recvs.at[distance - 1], frame=frame,
        )

    def send(self, piece):
        count = self.away.shape[0]
        for frame in range(count):
            self.away[frame] = piece(frame)
        for distance in range(1, count):
            self.copy(distance).start()

    def finish(self):
        total = self.away[lax.axis_index("frame")].astype(F32)
        for distance in range(1, self.away.shape[0]):
            self.copy(distance).wait_recv()
            total = total + self.landing[distance - 1].astype(F32)
        return total

    def drain(self):
        for distance in range(1, self.away.shape[0]):
            self.copy(distance).wait_send()


def cut(array, number, count):
    cols = array.shape[1] // count
    return array[:, number * cols : (number + 1) * cols]


def thirds_in_rows(values):
    high = values.astype(BF16).astype(F32)
    mid = (values - high).astype(BF16).astype(F32)
    low = (values - high) - mid
    return jnp.concatenate((high, mid, low, jnp.zeros_like(low)), axis=0).astype(BF16)


def side_by_side(tiles):
    return jnp.concatenate([tiles[i] for i in range(tiles.shape[0])], axis=1)


def backward_kernel(heads, clips, n, n_frame, r):
    step = pl.program_id(0)
    rows, width = r.tokens.shape[1:]
    tiles = 4
    half = n // 2
    share = width // n
    first_t = clips
    first_s = clips + tiles
    first_w = 2 * clips + tiles
    last = first_w + tiles - 1
    sibling = partner("clip", 0)
    barrier = pltpu.get_barrier_semaphore()
    bits = list(range(1, n.bit_length() - 1))
    frame = lax.axis_index("frame")
    place = lax.axis_index("clip")

    feed_in = Halving(r.sum_in, r.land_in, r.in_send, r.in_recv, bits)
    feed_out = Halving(r.sum_out, r.land_out, r.out_send, r.out_recv, bits[::-1])

    def units_of(name):
        sums, land = getattr(r, "sum_" + name), getattr(r, "land_" + name)
        sends, recvs = getattr(r, name + "_send"), getattr(r, name + "_recv")
        return [
            Halving(
                sums.at[pl.ds(i, 1)], land.at[pl.ds(i, 1)], sends.at[i], recvs.at[i],
                bits[:: 1 - 2 * (i % 2)],
            )
            for i in range(tiles)
        ]

    temporal, spatial = units_of("t"), units_of("s")
    stages = len(bits)

    regions = {"t": r.w_qkv_a_vmem, "s": r.w_qkv_b_vmem}

    def tile_cols(tile):
        return pl.ds(pl.multiple_of(lax.rem(tile, 3) * width, width), width)

    def tile_copies(name, tile):
        sends, recvs = getattr(r, name + "_core_send"), getattr(r, name + "_core_recv")
        return [
            remote(
                regions[name].at[share_rows(number, False, share), tile_cols(tile)],
                getattr(r, "core_" + name).at[tile, number],
                sends.at[tile, number], recvs.at[tile, number], clip=sibling,
            )
            for number in range(half)
        ]

    def tile_sent(name, tile):
        for copy in tile_copies(name, tile):
            copy.wait_send()

    def fold_core(name, which):
        sums, core = getattr(r, "sum_" + name), getattr(r, "core_" + name)
        for tile in which:
            for copy in tile_copies(name, tile):
                copy.wait_recv()
            sums[tile] = (sums[tile].astype(F32) + core[tile].astype(F32)).astype(BF16)

    frames = {
        name: Frames(
            getattr(r, "away_" + name), getattr(r, "near_" + name),
            getattr(r, name + "_z_send"), getattr(r, name + "_z_recv"),
        )
        for name in ("in", "out", "t", "s", "mod")
    }

    spaces = (r.left, r.left_out, r.grad_branch)

    def mod_tile(part):
        return pltpu.make_async_copy(
            r.w_mod.at[:, pl.ds(part * width, width)],
            spaces[part % 3].at[pl.ds(0, width)], r.mod_sems.at[part],
        )

    def mod_sums():
        total = None
        for part in range(9):
            mod_tile(part).wait()
            term = dot_nt(thirds_in_rows(r.mods[part]), spaces[part % 3][:width])
            total = term if total is None else total + term
            if part + 3 < 9:
                mod_tile(part + 3).start()
        pad = r.mods.shape[1]
        total = total[:pad] + total[pad : 2 * pad] + total[2 * pad : 3 * pad]
        joined = side_by_side(r.mods)
        total = total * r.silu_grad[...]
        frames["mod"].send(
            lambda other: jnp.concatenate((total, cut(joined, other, n_frame)), axis=1)
        )

    def spread_mods(distance):
        return remote(
            r.mod_share, r.gathered.at[place], r.mod_send.at[distance - 1],
            r.mod_recv.at[distance - 1], clip=lax.rem(place + distance, n),
        )

    own_mods = pltpu.make_async_copy(r.mod_share, r.gathered.at[place], r.mod_sems.at[9])

    def to_frames(units, name):
        owned = [unit.own()[0] for unit in units]
        wide = jnp.concatenate(owned[:-1], axis=1)
        frames[name].send(
            lambda other: jnp.concatenate(
                (cut(wide, other, n_frame), cut(owned[-1], other, n_frame)), axis=1
            )
        )

    def from_frames(name, wide, narrow):
        total = frames[name].finish()
        wide[...] = total[:, : wide.shape[1]]
        narrow[...] = total[:, wide.shape[1] :]

    def two_high(array):
        rows = array.shape[0] // 2
        return jnp.concatenate((array[:rows], array[rows:]), axis=1)

    loads = [
        pltpu.make_async_copy(r.keep_in, r.sum_in, r.load_sems.at[0]),
        pltpu.make_async_copy(r.came_in, r.core_t, r.load_sems.at[1]),
        pltpu.make_async_copy(r.keep_out, r.sum_out, r.load_sems.at[2]),
        pltpu.make_async_copy(r.came_out, r.core_s, r.load_sems.at[3]),
    ]
    lefts_t = [
        pltpu.make_async_copy(r.hidden_b, r.left, r.load_sems.at[4]),
        pltpu.make_async_copy(r.mixed_b, r.left_out, r.load_sems.at[5]),
        pltpu.make_async_copy(r.grad_branch_b, r.grad_branch, r.load_sems.at[6]),
    ]
    lefts_s = [
        pltpu.make_async_copy(r.hidden_a, r.left, r.load_sems.at[7]),
        pltpu.make_async_copy(r.mixed_a, r.left_out, r.load_sems.at[8]),
    ]
    r.w_qkv_a = Late(r.w_qkv_a_hbm, r.w_qkv_a_vmem, r.load_sems.at[9], first_s)

    @pl.when(step == 0)
    def _():
        for distance in range(1, n):
            greet(barrier, clip=lax.rem(place + distance, n))
        for distance in range(1, n_frame):
            greet(barrier, frame=lax.rem(frame + distance, n_frame))
        for copy in loads + lefts_t:
            copy.start()
        r.mods[...] = jnp.zeros_like(r.mods)
        for clip in range(clips):
            for row, part in enumerate((6, 7, 8, 5)):
                r.mods[part, clip : clip + 1] = r.sums[clip, row : row + 1]

    @pl.when(step < clips)
    def _():
        temporal_backward(r, step, pl.multiple_of(step * rows, rows))

    @pl.when(step == 0)
    def _():
        for copy in loads:
            copy.wait()
        for tile in range(tiles):
            r.sum_in[tile] = (
                r.sum_in[tile].astype(F32) + r.core_t[tile].astype(F32)
            ).astype(BF16)
        per = r.sum_out.shape[1] // tiles
        for tile in range(tiles):
            which = slice(tile * per, (tile + 1) * per)
            came = r.core_s[tile].reshape(r.sum_out[0, which].shape)
            r.sum_out[0, which] = (
                r.sum_out[0, which].astype(F32) + came.astype(F32)
            ).astype(BF16)
        pl.semaphore_wait(barrier, n - 1 + n_frame - 1)
        pl.semaphore_signal(
            r.free, inc=1, device_id={"clip": sibling}, device_id_type=pl.DeviceIdType.MESH
        )
        feed_in.send(0)
        feed_out.send(0)

    def weight_tile(name, tile):
        region = regions[name]

        @pl.when(tile < tiles - 1)
        def _():
            cols = pl.ds(pl.multiple_of(tile * width, width), width)
            region[:, tile_cols(tile)] = dot_tn(r.left[...], r.grad_qkv[:, cols]).astype(BF16)

        @pl.when(tile == tiles - 1)
        def _():
            region[:, tile_cols(tile)] = dot_tn(r.left_out[...], r.grad_branch[...]).astype(BF16)

        for copy in tile_copies(name, tile):
            copy.start()
        for number in range(half):
            getattr(r, "sum_" + name)[tile, number] = region[
                share_rows(number, True, share), tile_cols(tile)
            ]

    @pl.when((step >= first_t) & (step < first_s))
    def _():
        tile = step - first_t

        @pl.when(tile == 0)
        def _():
            for copy in lefts_t:
                copy.wait()
            pl.semaphore_wait(r.free, 1)

        pl.when(tile == 3)(lambda: tile_sent("t", 0))
        weight_tile("t", tile)

        @pl.when(tile == tiles - 1)
        def _():
            for copy in lefts_s:
                copy.start()

    @pl.when((step >= first_s) & (step < first_w))
    def _():
        clip = step - first_s

        @pl.when(clip == 0)
        def _():
            for tile in range(1, tiles):
                tile_sent("t", tile)
            r.w_qkv_a.copy.start()

        spatial_backward(r, heads, clip, pl.multiple_of(clip * rows, rows))

    @pl.when(step == first_s - 1)
    def _():
        for unit in (feed_in, feed_out):
            unit.fold(0)
            if stages > 1:
                unit.send(1)

    @pl.when(step == first_s)
    def _():
        for tile, unit in enumerate(temporal):
            fold_core("t", (tile,))
            unit.send(0)

    @pl.when(step == first_s + 1)
    def _():
        for stage in range(1, stages):
            for unit in (feed_in, feed_out):
                unit.fold(stage)
                if stage + 1 < stages:
                    unit.send(stage + 1)
        owned_in, owned_out = side_by_side(feed_in.own()), feed_out.own()[0]
        frames["in"].send(lambda other: cut(owned_in, other, n_frame))
        frames["out"].send(lambda other: two_high(cut(owned_out, other, n_frame)))

    @pl.when(step == first_s + 2)
    def _():
        for unit in temporal:
            unit.fold(0)
            if stages > 1:
                unit.send(1)

    @pl.when(step == first_s + 3)
    def _():
        for stage in range(1, stages):
            for unit in temporal:
                unit.fold(stage)
                if stage + 1 < stages:
                    unit.send(stage + 1)
        to_frames(temporal, "t")

    @pl.when(step >= first_w)
    def _():
        tile = step - first_w

        @pl.when(tile == 0)
        def _():
            for copy in lefts_s:
                copy.wait()

        pl.when(tile == 3)(lambda: tile_sent("s", 0))
        weight_tile("s", tile)

    for tile in range(tiles - 1):

        @pl.when(step == first_w + 1 + tile)
        def _():
            fold_core("s", (tile,))
            spatial[tile].send(0)

    @pl.when(step == last)
    def _():
        fold_core("s", (tiles - 1,))
        spatial[tiles - 1].send(0)
        for part in range(3):
            mod_tile(part).start()
        for stage in range(stages):
            for number, unit in enumerate(spatial):
                unit.fold(stage)
                if stage + 1 < stages:
                    unit.send(stage + 1)
                if stage == 0 and number == 1:
                    mod_sums()
        to_frames(spatial, "s")
        r.mod_share[...] = frames["mod"].finish()
        for distance in range(1, n):
            spread_mods(distance).start()
        own_mods.start()
        r.done_in[...] = frames["in"].finish()
        total = frames["out"].finish()
        high = total.shape[0]
        r.done_out[:high] = cut(total, 0, 2)
        r.done_out[high:] = cut(total, 1, 2)
        from_frames("t", r.done_tq, r.done_to)
        from_frames("s", r.done_sq, r.done_so)
        own_mods.wait()
        for distance in range(1, n):
            spread_mods(distance).wait()
        for unit in (feed_in, feed_out, *temporal, *spatial):
            unit.drain()
        for name in frames:
            frames[name].drain()
        for tile in range(1, tiles):
            tile_sent("s", tile)


def backward_call(fwd, tok, mod, spread, weights, modulate_w, silu_grad, n, n_frame):
    clips, rows, width = tok.shape
    ff = weights["mlp_in"].shape[1]
    heads = width // HEAD_DIM
    tokens_here = clips * rows
    tiles = 4
    half, share, tall = n // 2, width // n, ff // n
    first_s, first_w = clips + tiles, 2 * clips + tiles

    def struct(last, dtype=BF16):
        return jax.ShapeDtypeStruct((clips, rows, last), dtype)

    mod_spec = pl.BlockSpec(
        (1,) + mod.shape[1:],
        lambda s: (
            jnp.where(s < first_s, jnp.minimum(s, clips - 1), jnp.minimum(s - first_s, clips - 1)),
            0, 0,
        ),
    )
    anywhere = pl.BlockSpec(memory_space=pl.ANY)
    pad, mod_cols = silu_grad.shape[0], width + 9 * width // n_frame
    whole = pl.BlockSpec(fwd.sums.shape, lambda s: (0, 0, 0), pipeline_mode=pl.Buffered(1))
    whole_grad = pl.BlockSpec(silu_grad.shape, lambda s: (0, 0), pipeline_mode=pl.Buffered(1))
    ins = [
        ("mod", mod, mod_spec), ("sums", fwd.sums, whole), ("silu_grad", silu_grad, whole_grad),
        ("w_mod", modulate_w, anywhere),
    ]
    for name in ("q_prev", "q_own", "q_next", "sent_prev", "sent", "sent_next", "grad_q", "grad_b", "after_a"):
        array = getattr(fwd, name)
        ins.append((name, array, clip_spec(array, 0, clips, 1 if name in ("grad_q", "grad_b", "after_a") else 2)))
    for name, array in (
        ("tokens", tok), ("branch_a", fwd.branch_a), ("qkv_a", fwd.qkv_a), ("lse", fwd.lse)
    ):
        ins.append((name, array, clip_spec(array, first_s, clips, 1)))
    flat = (tokens_here, width)
    for name in ("hidden_b", "mixed_b", "grad_branch_b", "hidden_a", "mixed_a"):
        ins.append((name, getattr(fwd, name).reshape(flat), anywhere))
    core_shape = (tiles, half, share, width)
    ins += [
        ("keep_in", fwd.keep_in.reshape(core_shape), anywhere),
        ("came_in", fwd.came_in.reshape(core_shape), anywhere),
        ("keep_out", fwd.keep_out.reshape(1, half, tall, width), anywhere),
        ("came_out", fwd.came_out.reshape(core_shape), anywhere),
        ("w_qkv_a_hbm", weights["spatial_qkv"], anywhere),
    ]
    held = [
        ("spread", spread, 0), ("w_qkv_b", weights["temporal_qkv"], 0),
        ("w_out_a", weights["spatial_out"], first_s),
    ]
    grad_tokens = struct(width, F32)
    outs = [
        ("grad_tokens", grad_tokens, clip_spec(grad_tokens, first_s, clips, 1)),
        ("gathered", jax.ShapeDtypeStruct((n, pad, mod_cols), F32), None),
    ]
    dma = pltpu.SemaphoreType.DMA
    pieces = {
        "in": (share, ff // n_frame), "out": (tall, width // n_frame),
        "tq": (share, 3 * width // n_frame), "to": (share, width // n_frame),
        "sq": (share, 3 * width // n_frame), "so": (share, width // n_frame),
    }
    moved = half - 1
    scratch = [
        ("grad_a", pltpu.VMEM((clips, rows, width), F32)),
        ("grad_qkv", pltpu.VMEM((tokens_here, 3 * width), BF16)),
        ("grad_branch", pltpu.VMEM(flat, BF16)), ("left", pltpu.VMEM(flat, BF16)),
        ("left_out", pltpu.VMEM(flat, BF16)),
        ("w_qkv_a_vmem", pltpu.VMEM(weights["spatial_qkv"].shape, BF16)),
        ("sum_in", pltpu.VMEM(core_shape, BF16)), ("land_in", pltpu.VMEM((tiles, moved, share, width), BF16)),
        ("in_send", dma((moved,))), ("in_recv", dma((moved,))),
        ("sum_out", pltpu.VMEM((1, half, tall, width), BF16)),
        ("land_out", pltpu.VMEM((1, moved, tall, width), BF16)),
        ("out_send", dma((moved,))), ("out_recv", dma((moved,))),
        ("load_sems", dma((10,))), ("free", pltpu.SemaphoreType.REGULAR),
        ("mods", pltpu.VMEM((9, pad, width), F32)), ("mod_sems", dma((10,))),
        ("mod_share", pltpu.VMEM((pad, mod_cols), F32)),
        ("mod_send", dma((n - 1,))), ("mod_recv", dma((n - 1,))),
    ]
    for name in ("t", "s"):
        scratch += [
            ("sum_" + name, pltpu.VMEM(core_shape, BF16)), ("core_" + name, pltpu.VMEM(core_shape, BF16)),
            ("land_" + name, pltpu.VMEM((tiles, moved, share, width), BF16)),
            (name + "_send", dma((tiles, moved))), (name + "_recv", dma((tiles, moved))),
            (name + "_core_send", dma((tiles, half))), (name + "_core_recv", dma((tiles, half))),
        ]
    for name, dims in pieces.items():
        shape = jax.ShapeDtypeStruct(dims, F32)
        outs.append(("done_" + name, shape, pl.BlockSpec(shape.shape, lambda s: (0, 0))))
    packed = {
        "in": (share, ff // n_frame), "out": (tall // 2, 2 * width // n_frame),
        "t": (share, 4 * width // n_frame), "s": (share, 4 * width // n_frame),
        "mod": (pad, mod_cols),
    }
    for name, dims in packed.items():
        kind = F32 if name == "mod" else BF16
        scratch += [
            ("away_" + name, pltpu.VMEM((n_frame, *dims), kind)),
            ("near_" + name, pltpu.VMEM((n_frame - 1, *dims), kind)),
            (name + "_z_send", dma((n_frame - 1,))), (name + "_z_recv", dma((n_frame - 1,))),
        ]
    return run_kernel(
        functools.partial(backward_kernel, heads, clips, n, n_frame), first_w + tiles,
        ins, held, outs, scratch, 2 * tokens_here * width * width * 20, collective=2,
    )


def thirds(values):
    high = values.astype(BF16)
    rest = values - high.astype(F32)
    mid = rest.astype(BF16)
    low = (rest - mid.astype(F32)).astype(BF16)
    return jnp.concatenate((high, mid, low), axis=0)


def local(
    tokens, target, loss_weight, timesteps, offsets, cond_table, modulate_w,
    spatial_qkv, spatial_out, temporal_qkv, temporal_out, mlp_in, mlp_out,
):
    clips, frames, patches, width = tokens.shape
    steps = cond_table.shape[0]
    heads = width // HEAD_DIM
    n_clip = lax.axis_size("clip")
    n_frame = lax.axis_size("frame")
    clip_at = lax.axis_index("clip")
    frame_at = lax.axis_index("frame")
    flat = (clips, patches, width)
    tok = tokens.reshape(flat)
    tgt = target.reshape(flat)

    condition = jnp.take(cond_table, timesteps, axis=0, mode="clip")
    cond_low = jax.nn.silu(condition).astype(BF16)
    cond_here = lax.dynamic_slice_in_dim(condition, clip_at * clips, clips)
    _, silu_pull = jax.vjp(jax.nn.silu, cond_here)
    low_here = lax.dynamic_slice_in_dim(cond_low, clip_at * clips, clips)
    mod = jnp.dot(low_here, modulate_w, preferred_element_type=F32).reshape(clips, 9, width)

    half = width // 2
    positions = (offsets + frame_at).astype(F32)
    freqs = jnp.exp(jnp.arange(half, dtype=F32) * (-math.log(10000.0) / half))
    angles = positions[:, None] * freqs
    posenc = jnp.concatenate((jnp.sin(angles), jnp.cos(angles)), axis=-1)[:, None, :]

    head_of = np.arange(width) // HEAD_DIM
    lane_ids = np.arange(LANES)
    to_heads = jnp.asarray((head_of[:, None] == lane_ids[None, :]).astype(BF16))
    tall = np.arange(2 * LANES) - LANES
    spread = jnp.asarray((tall[:, None] == head_of[None, :]).astype(BF16))
    group, inside = np.divmod(np.arange(6 * LANES), LANES)
    slot_at = np.where(inside < heads, group * SLOT + inside, -1)
    pack = jnp.asarray((slot_at[:, None] == lane_ids[None, :]).astype(BF16))
    weights = {
        "spatial_qkv": spatial_qkv, "spatial_out": spatial_out, "temporal_qkv": temporal_qkv,
        "temporal_out": temporal_out, "mlp_in": mlp_in, "mlp_out": mlp_out,
    }
    fwd = forward_call(
        tok, tgt, mod, posenc, loss_weight, (to_heads, spread, pack), weights, n_clip
    )

    pad = -(-clips // 8) * 8
    silu_grad = jnp.pad(silu_pull(jnp.ones_like(cond_here))[0], ((0, pad - clips), (0, 0)))
    bwd = backward_call(fwd, tok, mod, spread, weights, modulate_w, silu_grad, n_clip, n_frame)
    gathered = bwd.gathered.reshape(n_clip * pad, -1)

    def padded_rows(values):
        split = values.reshape((n_clip, clips) + values.shape[1:])
        sides = ((0, 0), (0, pad - clips)) + ((0, 0),) * (values.ndim - 1)
        return jnp.pad(split, sides).reshape((n_clip * pad,) + values.shape[1:])

    onehot = timesteps[:, None] == jnp.arange(steps, dtype=jnp.int32)[None, :]
    onehot = padded_rows(onehot.astype(BF16))
    grad_table = dot_tn(jnp.concatenate((onehot,) * 3, axis=0), thirds(gathered[:, :width]))
    mod_rows = width // n_clip
    low_rows = lax.dynamic_slice_in_dim(cond_low, clip_at * mod_rows, mod_rows, axis=1)
    low_rows = padded_rows(low_rows)
    grad_modulate = dot_tn(jnp.concatenate((low_rows,) * 3, axis=0), thirds(gathered[:, width:]))
    return (
        fwd.output.reshape(tokens.shape),
        bwd.grad_tokens.reshape(tokens.shape),
        grad_table,
        grad_modulate,
        bwd.done_sq,
        bwd.done_so,
        bwd.done_tq,
        bwd.done_to,
        bwd.done_in,
        bwd.done_out,
    )


def solution(mesh):
    placed = (
        P("clip", "frame", None, None), P("clip", "frame", None, None), P("clip"), P(), P("clip"),
    ) + (P(),) * 8
    return jax.shard_map(
        local,
        mesh=mesh,
        in_specs=placed,
        out_specs=(
            P("clip", "frame", None, None), P("clip", "frame", None, None), P(),
        ) + (P("clip", "frame"),) * 7,
        check_vma=False,
    )
```
